32 devices in a mesh: member: 2 (over y), polar: 4 (over z), azimuth: 4 (over x, core).
Axes of the slice: x: 2, y: 2, z: 4, core: 2. Of those that a mesh axis runs over, the one named last changes fastest.
Arguments:
- conv_out: bfloat16 [32, 720, 640], P(('member', 'polar'), 'azimuth'), parts along dimension 0, may hold values from -6 to 6
- grad_out: bfloat16 [32, 720, 640], P(('member', 'polar'), 'azimuth'), parts along dimension 0, may hold values from -6 to 6
- w_in: bfloat16 [640, 1280], replicated, may hold values from -0.25 to 0.25
- b_in: float32 [1280], replicated, may hold values from -4 to 4
- w_out: bfloat16 [1280, 640], replicated, may hold values from -0.15625 to 0.15625
- basis_weight: float32 [9, 640], replicated, may hold values from -1 to 1
- filt: bfloat16 [9, 16, 640], replicated, may hold values from -2 to 2
- offsets: int32 [16, 9], replicated, may hold values from 0 to 15, as said below
Outputs:
- grad_in: bfloat16 [32, 720, 640], P(('member', 'polar'), 'azimuth'), parts along dimension 0
The draws below stay inside these ranges and needn't reach their ends.
There are 2 independent parts, one for each index of `member`. The reference program is written for one: setup_inputs(seed, part) draws one part's arguments, and reference() takes and returns one part's arrays. A program takes and returns all parts, laid end to end along the dimension named above; an argument that names none is the same for every part. Nothing has to cross between parts.
Inputs may be any that keep to these rules, and one draw needn't show every extreme that they name: offsets[i, k] lies within 3 rows of i; column 0 is i, column 1 is min(i + 3, 15), column 2 is max(i - 3, 0).
All inputs are finite; a program needn't handle non-finite values.
Results may differ from the reference program's by a relative error of at most 0.006.
Values may be sent and summed in bfloat16 or wider, within the bound.
No kernel may reach another device: no remote copies, remote signals or barrier semaphores. Data moves between devices by JAX's collectives and lax.ppermute only.
A program may use at most 64 MiB of HBM per device.

```python
import math
import jax
import jax.numpy as jnp
from jax import lax

CHANNELS = 640
HIDDEN_SIZE = 1280
NLON = 720
MODES = 320
BASES = 9
REACH = 3
NLAT = 16


def draw_offsets(key, part):
    rows = jnp.arange(NLAT, dtype=jnp.int32)[:, None]
    column = jnp.arange(BASES, dtype=jnp.int32)[None, :]
    drawn = jax.random.randint(jax.random.fold_in(key, 17), (NLAT, BASES), -REACH, REACH + 1, dtype=jnp.int32)
    shift_rows = jnp.where(column == 0, 0, jnp.where(column == 1, REACH, jnp.where(column == 2, -REACH, drawn)))
    return jnp.clip(rows + shift_rows, 0, NLAT - 1).astype(jnp.int32)


def shard_levels(stream_key, shape, shards, low, largest):
    gain = 1.0
    for axis_at, blocks in shards:
        draws = jax.random.uniform(jax.random.fold_in(jax.random.fold_in(stream_key, 6), axis_at), (blocks,), jnp.float32, low / len(shards), largest / len(shards))
        gain = gain * jnp.repeat(jnp.exp(draws), shape[axis_at] // blocks).reshape((-1,) + (1,) * (len(shape) - 1 - axis_at))
    return gain


def normal_values(key, dims, scale, limit, pieces=(), held_as=jnp.bfloat16):
    values = scale * jax.random.normal(key, dims, jnp.float32)
    if pieces:
        values = values * shard_levels(key, dims, pieces, -0.22, 0.18)
    return jnp.clip(values, -limit, limit).astype(held_as)


def setup_inputs(seed: int = 0, part: int = 0) -> dict:
    key_list = jax.random.split(jax.random.key(seed), 9)
    part_keys = jax.random.split(jax.random.fold_in(key_list[8], part), 9)
    conv_out = normal_values(part_keys[0], (NLAT, NLON, CHANNELS), 1.0, 6.0, ((0, 4), (1, 4)))
    grad_out = normal_values(part_keys[1], (NLAT, NLON, CHANNELS), 1.0, 6.0, ((0, 4), (1, 4)))
    w_in = normal_values(key_list[2], (CHANNELS, HIDDEN_SIZE), CHANNELS ** -0.5, 0.25)
    b_in = normal_values(key_list[3], (HIDDEN_SIZE,), 1.0, 4.0, (), jnp.float32)
    w_out = normal_values(key_list[4], (HIDDEN_SIZE, CHANNELS), HIDDEN_SIZE ** -0.5, 0.15625)
    basis_weight = jnp.clip(jax.random.uniform(key_list[5], (BASES, CHANNELS), jnp.float32, -1.0, 1.0), -1.0, 1.0)
    filt = normal_values(key_list[6], (BASES, NLAT, 2 * MODES), 0.33, 2.0)
    offsets = draw_offsets(jax.random.fold_in(key_list[8], 71), part)
    return {"conv_out": conv_out, "grad_out": grad_out, "w_in": w_in, "b_in": b_in, "w_out": w_out, "basis_weight": basis_weight, "filt": filt, "offsets": offsets}


def gelu_slope(values):
    normal_cdf = 0.5 * (1.0 + jax.scipy.special.erf(values / math.sqrt(2.0)))
    density = jnp.exp(-0.5 * values * values) / math.sqrt(2.0 * math.pi)
    return normal_cdf + values * density

def fourier_tables(length, modes):
    positions = jnp.arange(length, dtype=jnp.int32)
    waves = jnp.arange(modes, dtype=jnp.int32)
    phase = positions[:, None] * waves[None, :] % length
    angle = 2.0 * math.pi / length * phase.astype(jnp.float32)
    scale = 1.0 / math.sqrt(length)
    factor = jnp.where(waves == 0, 1.0, 2.0).astype(jnp.float32)
    analysis = (jnp.concatenate([jnp.cos(angle), -jnp.sin(angle)], axis=1) * scale).astype(jnp.bfloat16)
    synth = jnp.concatenate([jnp.cos(angle) * factor[None, :], -jnp.sin(angle) * factor[None, :]], axis=1) * scale
    return (analysis, jnp.transpose(synth).astype(jnp.bfloat16))

def spectral_term(spectrum, psi, weight):
    half = psi.shape[-1] // 2
    psi_full = psi.astype(jnp.float32)
    psi_real = psi_full[:, None, :half]
    psi_imag = psi_full[:, None, half:]
    spec_real = spectrum[:, :, :half]
    spec_imag = spectrum[:, :, half:]
    real_part = psi_real * spec_real + psi_imag * spec_imag
    imag_part = psi_real * spec_imag - psi_imag * spec_real
    return jnp.concatenate([real_part, imag_part], axis=2) * weight[None, :, None]

def reference(conv_out, grad_out, w_in, b_in, w_out, basis_weight, filt, offsets):

    def mlp_row(pair):
        h_row, g_row = pair
        pre = jnp.dot(h_row, w_in, preferred_element_type=jnp.float32) + b_in[None, :]
        back = lax.dot_general(g_row, w_out, (((1,), (1,)), ((), ())), preferred_element_type=jnp.float32)
        slope_grad = (back * gelu_slope(pre)).astype(jnp.bfloat16)
        hidden = lax.dot_general(slope_grad, w_in, (((1,), (1,)), ((), ())), preferred_element_type=jnp.float32)
        return hidden.astype(jnp.bfloat16)
    hidden_grad = lax.map(mlp_row, (conv_out, grad_out))
    hidden_grad = lax.optimization_barrier(hidden_grad)
    analysis, synthesis = fourier_tables(NLON, MODES)
    spectrum = jnp.einsum('inc,nm->icm', hidden_grad.astype(jnp.float32), analysis.astype(jnp.float32), precision=lax.Precision.HIGHEST)
    outspec = jnp.zeros(spectrum.shape, jnp.float32)
    for basis in range(BASES):
        contrib = spectral_term(spectrum, filt[basis], basis_weight[basis])
        outspec = outspec.at[offsets[:, basis]].add(contrib)
    rounded = lax.optimization_barrier(outspec.astype(jnp.bfloat16))
    conv_grad = jnp.einsum('jcm,mn->jnc', rounded.astype(jnp.float32), synthesis.astype(jnp.float32), precision=lax.Precision.HIGHEST).astype(jnp.bfloat16)
    return (grad_out.astype(jnp.float32) + conv_grad.astype(jnp.float32)).astype(jnp.bfloat16)
```

```python
import functools
import math

import jax
import jax.numpy as jnp
import ml_dtypes
import numpy as np
from jax import lax
from jax.experimental import pallas as pl
from jax.experimental.pallas import tpu as pltpu
from jax.sharding import PartitionSpec as P

REACH = 3
LANES = 128
HALF = 64
TERMS = 3
VMEM = pltpu.MemorySpace.VMEM


def round_up(value, unit):
    return -(-value // unit) * unit


def partner(me, step, count, sign):
    if count & (count - 1) == 0:
        return me ^ step
    return lax.rem(me + sign * step + count, count)


def exchange(block, step, count):
    if step == 0:
        return block
    pairs = [(a, int(partner_static(a, step, count))) for a in range(count)]
    return lax.ppermute(block, "azimuth", pairs)


def partner_static(a, step, count):
    return a ^ step if count & (count - 1) == 0 else (a + step) % count


def tables(count, part, modes):
    length = count * part
    whole = modes // LANES * LANES
    order = np.concatenate(
        [
            np.arange(whole),
            modes + np.arange(whole),
            np.arange(whole, modes),
            modes + np.arange(whole, modes),
        ]
    )
    positions = np.arange(length)
    waves = np.arange(modes)
    phase = (positions[:, None] * waves[None, :]) % length
    angle = (2.0 * math.pi / length) * phase
    scale = 1.0 / math.sqrt(length)
    factor = np.where(waves == 0, 1.0, 2.0)
    analysis = np.concatenate([np.cos(angle), -np.sin(angle)], axis=1) * scale
    synth = np.concatenate([np.cos(angle) * factor, -np.sin(angle) * factor], axis=1) * scale
    analysis = analysis.astype(np.float32).astype(ml_dtypes.bfloat16)[:, order]
    synth = synth.astype(np.float32).astype(ml_dtypes.bfloat16)[:, order]
    wide = round_up(part, HALF)
    window = round_up(HALF + wide, LANES)
    forth = np.zeros((count, HALF + window, 2 * modes), ml_dtypes.bfloat16)
    back = np.zeros((count, wide, 2 * modes), ml_dtypes.bfloat16)
    for s in range(count):
        forth[s, HALF : HALF + part] = analysis[s * part : (s + 1) * part]
        back[s, :part] = synth[s * part : (s + 1) * part]
    return forth, back


def gelu_slope(values):
    normal_cdf = 0.5 * (1.0 + lax.erf(values * math.sqrt(0.5)))
    density = jnp.exp(-0.5 * values * values) * (1.0 / math.sqrt(2.0 * math.pi))
    return normal_cdf + values * density


def dot_nt(left, right):
    return lax.dot_general(left, right, (((1,), (1,)), ((), ())), preferred_element_type=jnp.float32)


def dot_nn(left, right):
    return jnp.dot(left, right, preferred_element_type=jnp.float32)


def mlp_kernel(count, chunks, conv_ref, grad_ref, win_ref, bias_ref, wout_ref, *rest):
    outs, (slope_ref, total_ref) = rest[:-2], rest[-2:]
    step = pl.program_id(0)
    rows, part, channels = conv_ref.shape
    wide = slope_ref.shape[0] // rows
    owned = channels // count
    me = lax.axis_index("azimuth")

    @pl.when(step == 0)
    def _():
        slope_ref[...] = jnp.zeros_like(slope_ref)
        total_ref[...] = jnp.zeros_like(total_ref)

    for row in range(rows):
        pre = dot_nn(conv_ref[row], win_ref[...]) + bias_ref[...]
        back = dot_nt(grad_ref[row], wout_ref[...])
        slope_ref[row * wide : row * wide + part, :] = (back * gelu_slope(pre)).astype(jnp.bfloat16)
    for k in range(count):
        target = partner(me, k, count, 1)
        weight = win_ref[pl.ds(pl.multiple_of(target * owned, 32), owned), :]
        total_ref[k] += dot_nt(weight, slope_ref[...])

    @pl.when(step == pl.num_programs(0) - 1)
    def _():
        at = 0
        for start, size in chunks:
            for k in range(count):
                outs[at][...] = total_ref[k, start : start + size, :].astype(jnp.bfloat16)
                at += 1


def mlp(conv_out, grad_out, w_in, b_in, w_out, count, chunks):
    rows, part, channels = conv_out.shape
    hidden = w_in.shape[1]
    block = 256
    wide = round_up(part, HALF)
    whole = lambda shape: pl.BlockSpec(shape, lambda t: (0,) * len(shape))
    out_shape = [
        jax.ShapeDtypeStruct((size, rows * wide), jnp.bfloat16)
        for _, size in chunks
        for _ in range(count)
    ]
    return pl.pallas_call(
        functools.partial(mlp_kernel, count, chunks),
        grid=(hidden // block,),
        in_specs=[
            whole(conv_out.shape),
            whole(grad_out.shape),
            pl.BlockSpec((channels, block), lambda t: (0, t)),
            pl.BlockSpec((1, block), lambda t: (0, t)),
            pl.BlockSpec((block, channels), lambda t: (t, 0)),
        ],
        out_specs=[whole(s.shape) for s in out_shape],
        out_shape=out_shape,
        scratch_shapes=[
            pltpu.VMEM((rows * wide, block), jnp.bfloat16),
            pltpu.VMEM((count, channels // count, rows * wide), jnp.float32),
        ],
        compiler_params=pltpu.CompilerParams(vmem_limit_bytes=40 * 2**20),
        cost_estimate=pl.CostEstimate(
            flops=6 * rows * part * channels * hidden, bytes_accessed=8 * 2**20, transcendentals=0
        ),
        name="mlp",
    )(conv_out, grad_out, w_in, b_in.reshape(1, -1), w_out)


def analysis_kernel(count, rows, *refs):
    pieces, table_ref = refs[:count], refs[count]
    own_ref, upward_ref, downward_ref = refs[count + 1 :]
    wide = pieces[0].shape[1] // rows
    window = table_ref.shape[1] - HALF
    me = lax.axis_index("azimuth")
    sources = [partner(me, k, count, -1) for k in range(count)]
    for row in range(rows):
        first = row * wide // LANES * LANES
        shift = row * wide - first
        total = None
        for k in range(count):
            term = dot_nn(
                pieces[k][:, first : first + window],
                table_ref[sources[k], HALF - shift : HALF - shift + window, :],
            )
            total = term if total is None else total + term
        own_ref[row] = total
        sent = total.astype(jnp.bfloat16)
        if row >= rows - REACH:
            upward_ref[row - (rows - REACH)] = sent
        if row < REACH:
            downward_ref[row] = sent


def analyze(pieces, table, rows):
    count = len(pieces)
    size = pieces[0].shape[0]
    width = table.shape[2]
    halo = jax.ShapeDtypeStruct((REACH, size, width), jnp.bfloat16)
    return pl.pallas_call(
        functools.partial(analysis_kernel, count, rows),
        in_specs=[pl.BlockSpec(memory_space=VMEM)] * (count + 1),
        out_specs=[pl.BlockSpec(memory_space=VMEM)] * 3,
        out_shape=[jax.ShapeDtypeStruct((rows, size, width), jnp.float32), halo, halo],
        compiler_params=pltpu.CompilerParams(vmem_limit_bytes=24 * 2**20),
        cost_estimate=pl.CostEstimate(
            flops=8 * rows * size * 256 * width, bytes_accessed=4 * 2**20, transcendentals=0
        ),
        name="analysis",
    )(*pieces, table)


def add_pair(acc, spectrum, weight, target_row, filter_row, target):
    masked = jnp.where(target_row == target, weight, 0.0).astype(jnp.bfloat16)
    gain = dot_nn(masked, filter_row)
    whole = (gain.shape[1] // 2) // LANES * LANES - LANES
    spec_re = spectrum[:, :whole]
    spec_im = spectrum[:, whole : 2 * whole]
    spec_x = spectrum[:, 2 * whole :]
    swapped = pltpu.roll(spec_x, HALF, 1)
    gain_re = gain[:, :whole]
    gain_rx = gain[:, whole : whole + LANES]
    gain_im = gain[:, whole + LANES : 2 * whole + LANES]
    gain_ix = gain[:, 2 * whole + LANES :]
    acc_re, acc_im, acc_x = acc
    acc_re = acc_re + (gain_re * spec_re + gain_im * spec_im)
    acc_im = acc_im + (gain_re * spec_im - gain_im * spec_re)
    acc_x = acc_x + (gain_rx * spec_x + gain_ix * swapped)
    return acc_re, acc_im, acc_x


def split_tiles(value):
    whole = (value.shape[1] - LANES) // 2
    return value[:, :whole], value[:, whole : 2 * whole], value[:, 2 * whole :]


def own_kernel(own_ref, weight_ref, target_ref, filter_ref, out_ref):
    rows, size, width = own_ref.shape
    for target in range(rows):
        acc = split_tiles(jnp.zeros((size, width), jnp.float32))
        for row in range(rows):
            if abs(row - target) <= REACH:
                at = row + REACH
                acc = add_pair(
                    acc, own_ref[row], weight_ref[...], target_ref[at : at + 1, :], filter_ref[at], target
                )
        out_ref[target] = jnp.concatenate(acc, axis=1)


def own_terms(own, weight, target, filters):
    return pl.pallas_call(
        own_kernel,
        in_specs=[pl.BlockSpec(memory_space=VMEM)] * 4,
        out_specs=pl.BlockSpec(memory_space=VMEM),
        out_shape=jax.ShapeDtypeStruct(own.shape, jnp.float32),
        compiler_params=pltpu.CompilerParams(vmem_limit_bytes=24 * 2**20),
        cost_estimate=pl.CostEstimate(flops=2 * 10**9, bytes_accessed=4 * 2**20, transcendentals=0),
        name="own_terms",
    )(own, weight, target, filters)


def finish_kernel(count, part_ref, low_ref, high_ref, weight_ref, target_ref, filter_ref, table_ref, *rest):
    outs, stacked_ref = rest[:-1], rest[-1]
    rows, size, width = part_ref.shape
    part = outs[0].shape[0]
    for target in range(rows):
        acc = split_tiles(part_ref[target])
        for side, base in ((low_ref, -REACH), (high_ref, rows)):
            for h in range(REACH):
                row = base + h
                if abs(row - target) <= REACH:
                    at = row + REACH
                    acc = add_pair(
                        acc,
                        side[h].astype(jnp.float32),
                        weight_ref[...],
                        target_ref[at : at + 1, :],
                        filter_ref[at],
                        target,
                    )
        stacked_ref[target * size : (target + 1) * size, :] = jnp.concatenate(acc, axis=1).astype(
            jnp.bfloat16
        )
    me = lax.axis_index("azimuth")
    for k in range(count):
        grid = dot_nt(table_ref[partner(me, k, count, 1)], stacked_ref[...])
        outs[k][...] = grid[:part].astype(jnp.bfloat16)


def finish(own, low, high, weight, target, filters, table, count, part):
    rows, size, width = own.shape
    return pl.pallas_call(
        functools.partial(finish_kernel, count),
        in_specs=[pl.BlockSpec(memory_space=VMEM)] * 7,
        out_specs=[pl.BlockSpec(memory_space=VMEM)] * count,
        out_shape=[jax.ShapeDtypeStruct((part, rows * size), jnp.bfloat16)] * count,
        scratch_shapes=[pltpu.VMEM((rows * size, width), jnp.bfloat16)],
        compiler_params=pltpu.CompilerParams(vmem_limit_bytes=24 * 2**20),
        cost_estimate=pl.CostEstimate(flops=2 * 10**9, bytes_accessed=4 * 2**20, transcendentals=0),
        name="finish",
    )(own, low, high, weight, target, filters, table)


def add_kernel(count, chunks, grad_ref, *refs):
    pieces, out_ref = refs[:-1], refs[-1]
    rows, part, channels = grad_ref.shape
    owned = channels // count
    me = lax.axis_index("azimuth")
    for row in range(rows):
        for k in range(count):
            source = partner(me, k, count, -1)
            block = jnp.concatenate(
                [
                    pieces[q * count + k][:, row * size : (row + 1) * size]
                    for q, (_, size) in enumerate(chunks)
                ],
                axis=1,
            )
            for s in range(count):

                @pl.when(source == s)
                def _(block=block, s=s, row=row):
                    at = slice(s * owned, (s + 1) * owned)
                    out_ref[row, :, at] = (
                        grad_ref[row, :, at].astype(jnp.float32) + block.astype(jnp.float32)
                    ).astype(jnp.bfloat16)


def add_back(grad_out, pieces, count, chunks):
    return pl.pallas_call(
        functools.partial(add_kernel, count, chunks),
        in_specs=[pl.BlockSpec(memory_space=VMEM)] * (1 + len(pieces)),
        out_specs=pl.BlockSpec(memory_space=VMEM),
        out_shape=jax.ShapeDtypeStruct(grad_out.shape, jnp.bfloat16),
        compiler_params=pltpu.CompilerParams(vmem_limit_bytes=24 * 2**20),
        cost_estimate=pl.CostEstimate(flops=10**6, bytes_accessed=4 * 2**20, transcendentals=0),
        name="add_back",
    )(grad_out, *pieces)


def small_tables(basis_weight, filt, offsets, rows, count):
    owned = basis_weight.shape[1] // count
    bases, lats, _ = filt.shape
    modes = filt.shape[2] // 2
    whole = modes // LANES * LANES
    depth = round_up(TERMS * bases, 16)
    start_lat = lax.axis_index("polar") * rows
    start_chan = lax.axis_index("azimuth") * owned
    weights = lax.dynamic_slice_in_dim(basis_weight, start_chan, owned, 1)
    parts = []
    for _ in range(TERMS):
        rounded = lax.reduce_precision(weights, 8, 7)
        parts.append(rounded)
        weights = weights - rounded
    spare = depth - TERMS * bases
    weight = jnp.pad(jnp.concatenate(parts, axis=0), ((0, spare), (0, 0))).T
    lat = start_lat - REACH + jnp.arange(rows + 2 * REACH, dtype=jnp.int32)
    inside = (lat >= 0) & (lat < lats)
    clamped = jnp.clip(lat, 0, lats - 1)
    local = jnp.where(inside[:, None], jnp.take(offsets, clamped, axis=0) - start_lat, -1)
    target = jnp.pad(jnp.tile(local, (1, TERMS)), ((0, 0), (0, spare)), constant_values=-1)
    chosen = jnp.transpose(jnp.take(filt, clamped, axis=1), (1, 0, 2))
    real, imag = chosen[:, :, :modes], chosen[:, :, modes:]
    rest_re, rest_im = real[:, :, whole:], imag[:, :, whole:]
    row = jnp.concatenate(
        [real[:, :, :whole], rest_re, rest_re, imag[:, :, :whole], rest_im, -rest_im], axis=2
    )
    filters = jnp.pad(jnp.tile(row, (1, TERMS, 1)), ((0, 0), (0, spare), (0, 0)))
    return weight, target, filters


def halo(upward, downward):
    count = lax.axis_size("polar")
    forward = [(i, i + 1) for i in range(count - 1)]
    backward = [(i + 1, i) for i in range(count - 1)]
    return lax.ppermute(upward, "polar", forward), lax.ppermute(downward, "polar", backward)


def on_device(chunks, conv_out, grad_out, w_in, b_in, w_out, basis_weight, filt, offsets):
    rows, part, channels = conv_out.shape
    count = lax.axis_size("azimuth")
    forth, back = tables(count, part, filt.shape[2] // 2)
    forth, back = jnp.asarray(forth), jnp.asarray(back)
    blocks = mlp(conv_out, grad_out, w_in, b_in, w_out, count, chunks)
    weight, target, filters = small_tables(basis_weight, filt, offsets, rows, count)
    returned = []
    for q, (start, size) in enumerate(chunks):
        pieces = [exchange(blocks[q * count + k], k, count) for k in range(count)]
        own, upward, downward = analyze(pieces, forth, rows)
        low, high = halo(upward, downward)
        part_weight = weight[start : start + size]
        own = own_terms(own, part_weight, target, filters)
        grids = finish(own, low, high, part_weight, target, filters, back, count, part)
        returned += [exchange(grids[k], k, count) for k in range(count)]
    return add_back(grad_out, returned, count, chunks)


def solution(mesh):
    grid = P(("member", "polar"), "azimuth", None)

    def run(conv_out, grad_out, *others):
        owned = conv_out.shape[2] // mesh.shape["azimuth"]
        chunks = ((0, owned),)
        return jax.shard_map(
            functools.partial(on_device, chunks),
            mesh=mesh,
            in_specs=(grid, grid) + (P(),) * 6,
            out_specs=grid,
            check_vma=False,
        )(conv_out, grad_out, *others)

    return run
```

```python
import functools
import math

import jax
import jax.numpy as jnp
import ml_dtypes
import numpy as np
from jax import lax
from jax.experimental import pallas as pl
from jax.experimental.pallas import tpu as pltpu
from jax.sharding import PartitionSpec as P

REACH = 3
LANES = 128
HALF = 64
TERMS = 3
VMEM = pltpu.MemorySpace.VMEM


def round_up(value, unit):
    return -(-value // unit) * unit


def partner(me, step, count, sign):
    if count & (count - 1) == 0:
        return me ^ step
    return lax.rem(me + sign * step + count, count)


def exchange(block, step, count):
    if step == 0:
        return block
    pairs = [(a, int(partner_static(a, step, count))) for a in range(count)]
    return lax.ppermute(block, "azimuth", pairs)


def partner_static(a, step, count):
    return a ^ step if count & (count - 1) == 0 else (a + step) % count


def tables(count, part, modes):
    length = count * part
    whole = modes // LANES * LANES
    order = np.concatenate(
        [
            np.arange(whole),
            modes + np.arange(whole),
            np.arange(whole, modes),
            modes + np.arange(whole, modes),
        ]
    )
    positions = np.arange(length)
    waves = np.arange(modes)
    phase = (positions[:, None] * waves[None, :]) % length
    angle = (2.0 * math.pi / length) * phase
    scale = 1.0 / math.sqrt(length)
    factor = np.where(waves == 0, 1.0, 2.0)
    analysis = np.concatenate([np.cos(angle), -np.sin(angle)], axis=1) * scale
    synth = np.concatenate([np.cos(angle) * factor, -np.sin(angle) * factor], axis=1) * scale
    analysis = analysis.astype(np.float32).astype(ml_dtypes.bfloat16)[:, order]
    synth = synth.astype(np.float32).astype(ml_dtypes.bfloat16)[:, order]
    wide = round_up(part, HALF)
    window = round_up(HALF + wide, LANES)
    forth = np.zeros((count, HALF + window, 2 * modes), ml_dtypes.bfloat16)
    back = np.zeros((count, wide, 2 * modes), ml_dtypes.bfloat16)
    for s in range(count):
        forth[s, HALF : HALF + part] = analysis[s * part : (s + 1) * part]
        back[s, :part] = synth[s * part : (s + 1) * part]
    return forth, back


def gelu_slope(values):
    normal_cdf = 0.5 * (1.0 + lax.erf(values * math.sqrt(0.5)))
    density = jnp.exp(-0.5 * values * values) * (1.0 / math.sqrt(2.0 * math.pi))
    return normal_cdf + values * density


def dot_nt(left, right):
    return lax.dot_general(left, right, (((1,), (1,)), ((), ())), preferred_element_type=jnp.float32)


def dot_nn(left, right):
    return jnp.dot(left, right, preferred_element_type=jnp.float32)


def mlp_kernel(count, chunks, conv_ref, grad_ref, win_ref, bias_ref, wout_ref, *rest):
    outs, (slope_ref, total_ref) = rest[:-2], rest[-2:]
    step = pl.program_id(0)
    rows, part, channels = conv_ref.shape
    wide = slope_ref.shape[0] // rows
    owned = channels // count
    me = lax.axis_index("azimuth")

    @pl.when(step == 0)
    def _():
        slope_ref[...] = jnp.zeros_like(slope_ref)
        total_ref[...] = jnp.zeros_like(total_ref)

    block = win_ref.shape[1]
    bias = bias_ref[pl.ds(pl.multiple_of(step * block, block), block)].reshape(1, block)
    for row in range(rows):
        pre = dot_nn(conv_ref[row], win_ref[...]) + bias
        back = dot_nt(grad_ref[row], wout_ref[...])
        slope_ref[row * wide : row * wide + part, :] = (back * gelu_slope(pre)).astype(jnp.bfloat16)
    for k in range(count):
        target = partner(me, k, count, 1)
        weight = win_ref[pl.ds(pl.multiple_of(target * owned, 32), owned), :]
        total_ref[k] += dot_nt(weight, slope_ref[...])

    @pl.when(step == pl.num_programs(0) - 1)
    def _():
        at = 0
        for start, size in chunks:
            for k in range(count):
                outs[at][...] = total_ref[k, start : start + size, :].astype(jnp.bfloat16)
                at += 1


def mlp(conv_out, grad_out, w_in, b_in, w_out, count, chunks):
    rows, part, channels = conv_out.shape
    hidden = w_in.shape[1]
    block = 256
    wide = round_up(part, HALF)
    whole = lambda shape: pl.BlockSpec(shape, lambda t: (0,) * len(shape))
    out_shape = [
        jax.ShapeDtypeStruct((size, rows * wide), jnp.bfloat16)
        for _, size in chunks
        for _ in range(count)
    ]
    return pl.pallas_call(
        functools.partial(mlp_kernel, count, chunks),
        grid=(hidden // block,),
        in_specs=[
            whole(conv_out.shape),
            whole(grad_out.shape),
            pl.BlockSpec((channels, block), lambda t: (0, t)),
            whole(b_in.shape),
            pl.BlockSpec((block, channels), lambda t: (t, 0)),
        ],
        out_specs=[whole(s.shape) for s in out_shape],
        out_shape=out_shape,
        scratch_shapes=[
            pltpu.VMEM((rows * wide, block), jnp.bfloat16),
            pltpu.VMEM((count, channels // count, rows * wide), jnp.float32),
        ],
        compiler_params=pltpu.CompilerParams(vmem_limit_bytes=16 * 2**20),
        cost_estimate=pl.CostEstimate(
            flops=6 * rows * part * channels * hidden, bytes_accessed=8 * 2**20, transcendentals=0
        ),
        name="mlp",
    )(conv_out, grad_out, w_in, b_in, w_out)


def analysis_kernel(count, rows, *refs):
    pieces, table_ref = refs[:count], refs[count]
    own_ref, upward_ref, downward_ref = refs[count + 1 :]
    wide = pieces[0].shape[1] // rows
    window = table_ref.shape[1] - HALF
    me = lax.axis_index("azimuth")
    sources = [partner(me, k, count, -1) for k in range(count)]
    for row in range(rows):
        first = row * wide // LANES * LANES
        shift = row * wide - first
        total = None
        for k in range(count):
            term = dot_nn(
                pieces[k][:, first : first + window],
                table_ref[sources[k], HALF - shift : HALF - shift + window, :],
            )
            total = term if total is None else total + term
        own_ref[row] = total
        sent = total.astype(jnp.bfloat16)
        if row >= rows - REACH:
            upward_ref[row - (rows - REACH)] = sent
        if row < REACH:
            downward_ref[row] = sent


def analyze(pieces, table, rows):
    count = len(pieces)
    size = pieces[0].shape[0]
    width = table.shape[2]
    halo = jax.ShapeDtypeStruct((REACH, size, width), jnp.bfloat16)
    return pl.pallas_call(
        functools.partial(analysis_kernel, count, rows),
        in_specs=[pl.BlockSpec(memory_space=VMEM)] * (count + 1),
        out_specs=[pl.BlockSpec(memory_space=VMEM)] * 3,
        out_shape=[jax.ShapeDtypeStruct((rows, size, width), jnp.float32), halo, halo],
        compiler_params=pltpu.CompilerParams(vmem_limit_bytes=12 * 2**20),
        cost_estimate=pl.CostEstimate(
            flops=8 * rows * size * 256 * width, bytes_accessed=4 * 2**20, transcendentals=0
        ),
        name="analysis",
    )(*pieces, table)


def add_pair(acc, spectrum, weight, target_row, filter_row, target):
    masked = jnp.where(target_row == target, weight, 0.0).astype(jnp.bfloat16)
    gain = dot_nn(masked, filter_row)
    whole = (gain.shape[1] // 2) // LANES * LANES - LANES
    spec_re = spectrum[:, :whole]
    spec_im = spectrum[:, whole : 2 * whole]
    spec_x = spectrum[:, 2 * whole :]
    swapped = pltpu.roll(spec_x, HALF, 1)
    gain_re = gain[:, :whole]
    gain_rx = gain[:, whole : whole + LANES]
    gain_im = gain[:, whole + LANES : 2 * whole + LANES]
    gain_ix = gain[:, 2 * whole + LANES :]
    acc_re, acc_im, acc_x = acc
    acc_re = acc_re + (gain_re * spec_re + gain_im * spec_im)
    acc_im = acc_im + (gain_re * spec_im - gain_im * spec_re)
    acc_x = acc_x + (gain_rx * spec_x + gain_ix * swapped)
    return acc_re, acc_im, acc_x


def split_tiles(value):
    whole = (value.shape[1] - LANES) // 2
    return value[:, :whole], value[:, whole : 2 * whole], value[:, 2 * whole :]


def own_kernel(own_ref, weight_ref, target_ref, filter_ref, out_ref):
    rows, size, width = own_ref.shape
    for target in range(rows):
        acc = split_tiles(jnp.zeros((size, width), jnp.float32))
        for row in range(rows):
            if abs(row - target) <= REACH:
                at = row + REACH
                acc = add_pair(
                    acc, own_ref[row], weight_ref[...], target_ref[at : at + 1, :], filter_ref[at], target
                )
        out_ref[target] = jnp.concatenate(acc, axis=1)


def own_terms(own, weight, target, filters):
    return pl.pallas_call(
        own_kernel,
        in_specs=[pl.BlockSpec(memory_space=VMEM)] * 4,
        out_specs=pl.BlockSpec(memory_space=VMEM),
        out_shape=jax.ShapeDtypeStruct(own.shape, jnp.float32),
        compiler_params=pltpu.CompilerParams(vmem_limit_bytes=12 * 2**20),
        cost_estimate=pl.CostEstimate(flops=2 * 10**9, bytes_accessed=4 * 2**20, transcendentals=0),
        name="own_terms",
    )(own, weight, target, filters)


def finish_kernel(count, part_ref, low_ref, high_ref, weight_ref, target_ref, filter_ref, table_ref, *rest):
    outs, stacked_ref = rest[:-1], rest[-1]
    rows, size, width = part_ref.shape
    part = outs[0].shape[0]
    for target in range(rows):
        acc = split_tiles(part_ref[target])
        for side, base in ((low_ref, -REACH), (high_ref, rows)):
            for h in range(REACH):
                row = base + h
                if abs(row - target) <= REACH:
                    at = row + REACH
                    acc = add_pair(
                        acc,
                        side[h].astype(jnp.float32),
                        weight_ref[...],
                        target_ref[at : at + 1, :],
                        filter_ref[at],
                        target,
                    )
        stacked_ref[target * size : (target + 1) * size, :] = jnp.concatenate(acc, axis=1).astype(
            jnp.bfloat16
        )
    me = lax.axis_index("azimuth")
    for k in range(count):
        grid = dot_nt(table_ref[partner(me, k, count, 1)], stacked_ref[...])
        outs[k][...] = grid[:part].astype(jnp.bfloat16)


def finish(own, low, high, weight, target, filters, table, count, part):
    rows, size, width = own.shape
    return pl.pallas_call(
        functools.partial(finish_kernel, count),
        in_specs=[pl.BlockSpec(memory_space=VMEM)] * 7,
        out_specs=[pl.BlockSpec(memory_space=VMEM)] * count,
        out_shape=[jax.ShapeDtypeStruct((part, rows * size), jnp.bfloat16)] * count,
        scratch_shapes=[pltpu.VMEM((rows * size, width), jnp.bfloat16)],
        compiler_params=pltpu.CompilerParams(vmem_limit_bytes=12 * 2**20),
        cost_estimate=pl.CostEstimate(flops=2 * 10**9, bytes_accessed=4 * 2**20, transcendentals=0),
        name="finish",
    )(own, low, high, weight, target, filters, table)


def add_kernel(count, chunks, grad_ref, *refs):
    pieces, out_ref = refs[:-1], refs[-1]
    rows, part, channels = grad_ref.shape
    owned = channels // count
    me = lax.axis_index("azimuth")
    for row in range(rows):
        for k in range(count):
            source = partner(me, k, count, -1)
            block = jnp.concatenate(
                [
                    pieces[q * count + k][:, row * size : (row + 1) * size]
                    for q, (_, size) in enumerate(chunks)
                ],
                axis=1,
            )
            for s in range(count):

                @pl.when(source == s)
                def _(block=block, s=s, row=row):
                    at = slice(s * owned, (s + 1) * owned)
                    out_ref[row, :, at] = (
                        grad_ref[row, :, at].astype(jnp.float32) + block.astype(jnp.float32)
                    ).astype(jnp.bfloat16)


def add_back(grad_out, pieces, count, chunks):
    return pl.pallas_call(
        functools.partial(add_kernel, count, chunks),
        in_specs=[pl.BlockSpec(memory_space=VMEM)] * (1 + len(pieces)),
        out_specs=pl.BlockSpec(memory_space=VMEM),
        out_shape=jax.ShapeDtypeStruct(grad_out.shape, jnp.bfloat16),
        compiler_params=pltpu.CompilerParams(vmem_limit_bytes=12 * 2**20),
        cost_estimate=pl.CostEstimate(flops=10**6, bytes_accessed=4 * 2**20, transcendentals=0),
        name="add_back",
    )(grad_out, *pieces)


def prepare_kernel(count, chunks, weight_ref, filt_ref, offset_ref, forth_ref, back_ref, *outs):
    filter_out, target_out, forth_out, back_out = outs[:4]
    forth_out[...] = forth_ref[...]
    back_out[...] = back_ref[...]
    bases, channels = weight_ref.shape
    lats, width = filt_ref.shape[1:]
    ext, depth = target_out.shape
    rows = ext - 2 * REACH
    modes = width // 2
    whole = modes // LANES * LANES
    used = TERMS * bases
    weight = pltpu.roll(
        weight_ref[...], lax.rem(count - lax.axis_index("azimuth"), count) * (channels // count), 1
    )[:, : channels // count]
    parts = []
    for _ in range(TERMS):
        rounded = weight.astype(jnp.bfloat16).astype(jnp.float32)
        parts.append(rounded)
        weight = weight - rounded
    parts.append(jnp.zeros((depth - used, weight.shape[1]), jnp.float32))
    weight = jnp.concatenate(parts, axis=0).T
    for (start, size), out in zip(chunks, outs[4:]):
        out[...] = weight[start : start + size]
    start_lat = lax.axis_index("polar") * rows
    table = filt_ref[...].reshape(bases * lats, width)
    base = lax.broadcasted_iota(jnp.int32, (depth, bases * lats), 0)
    valid = base < used
    for _ in range(TERMS - 1):
        base = jnp.where(base >= bases, base - bases, base)
    column = lax.broadcasted_iota(jnp.int32, (depth, bases * lats), 1)
    for i in range(ext):
        lat = start_lat + (i - REACH)
        inside = (lat >= 0) & (lat < lats)
        lat = jnp.clip(lat, 0, lats - 1)
        pick = jnp.where(valid & (column == base * lats + lat), 1.0, 0.0).astype(jnp.bfloat16)
        row = dot_nn(pick, table)
        real, imag = row[:, :modes], row[:, modes:]
        rest_re, rest_im = real[:, whole:], imag[:, whole:]
        filter_out[i] = jnp.concatenate(
            [real[:, :whole], rest_re, rest_re, imag[:, :whole], rest_im, -rest_im], axis=1
        ).astype(jnp.bfloat16)
        local = jnp.where(inside, offset_ref[pl.ds(lat, 1), :] - start_lat, -1)
        spare = jnp.full((1, depth - used), -1, jnp.int32)
        target_out[i : i + 1, :] = jnp.concatenate([local] * TERMS + [spare], axis=1)


def prepare(basis_weight, filt, offsets, forth, back, rows, count, chunks):
    bases = filt.shape[0]
    width = filt.shape[2]
    ext = rows + 2 * REACH
    depth = round_up(TERMS * bases, 16)
    shapes = [
        jax.ShapeDtypeStruct((ext, depth, width + LANES), jnp.bfloat16),
        jax.ShapeDtypeStruct((ext, depth), jnp.int32),
        jax.ShapeDtypeStruct(forth.shape, forth.dtype),
        jax.ShapeDtypeStruct(back.shape, back.dtype),
    ] + [jax.ShapeDtypeStruct((size, depth), jnp.float32) for _, size in chunks]
    return pl.pallas_call(
        functools.partial(prepare_kernel, count, chunks),
        in_specs=[pl.BlockSpec(memory_space=VMEM)] * 5,
        out_specs=[pl.BlockSpec(memory_space=VMEM)] * len(shapes),
        out_shape=shapes,
        compiler_params=pltpu.CompilerParams(vmem_limit_bytes=16 * 2**20),
        cost_estimate=pl.CostEstimate(flops=10**9, bytes_accessed=6 * 2**20, transcendentals=0),
        name="prepare",
    )(basis_weight, filt, offsets, forth, back)


def halo(upward, downward):
    count = lax.axis_size("polar")
    forward = [(i, i + 1) for i in range(count - 1)]
    backward = [(i + 1, i) for i in range(count - 1)]
    return lax.ppermute(upward, "polar", forward), lax.ppermute(downward, "polar", backward)


def on_device(chunks, conv_out, grad_out, w_in, b_in, w_out, basis_weight, filt, offsets):
    rows, part, channels = conv_out.shape
    count = lax.axis_size("azimuth")
    forth, back = tables(count, part, filt.shape[2] // 2)
    forth, back = jnp.asarray(forth), jnp.asarray(back)
    blocks = mlp(conv_out, grad_out, w_in, b_in, w_out, count, chunks)
    filters, target, forth, back, *weights = prepare(
        basis_weight, filt, offsets, forth, back, rows, count, chunks
    )
    returned = []
    for q, (start, size) in enumerate(chunks):
        pieces = [exchange(blocks[q * count + k], k, count) for k in range(count)]
        own, upward, downward = analyze(pieces, forth, rows)
        low, high = halo(upward, downward)
        own = own_terms(own, weights[q], target, filters)
        grids = finish(own, low, high, weights[q], target, filters, back, count, part)
        returned += [exchange(grids[k], k, count) for k in range(count)]
    return add_back(grad_out, returned, count, chunks)


def solution(mesh):
    grid = P(("member", "polar"), "azimuth", None)

    def run(conv_out, grad_out, *others):
        owned = conv_out.shape[2] // mesh.shape["azimuth"]
        chunks = ((0, owned),) if owned % 32 else ((0, owned * 3 // 5), (owned * 3 // 5, owned - owned * 3 // 5))
        return jax.shard_map(
            functools.partial(on_device, chunks),
            mesh=mesh,
            in_specs=(grid, grid) + (P(),) * 6,
            out_specs=grid,
            check_vma=False,
        )(conv_out, grad_out, *others)

    return run
```

```python
import functools
import math

import jax
import jax.numpy as jnp
import ml_dtypes
import numpy as np
from jax import lax
from jax.experimental import pallas as pl
from jax.experimental.pallas import tpu as pltpu
from jax.sharding import PartitionSpec as P

REACH = 3
LANES = 128
HALF = 64
TERMS = 3
VMEM = pltpu.MemorySpace.VMEM


def round_up(value, unit):
    return -(-value // unit) * unit


def partner(me, step, count, sign):
    if count & (count - 1) == 0:
        return me ^ step
    return lax.rem(me + sign * step + count, count)


def exchange(block, step, count):
    if step == 0:
        return block
    pairs = [(a, int(partner_static(a, step, count))) for a in range(count)]
    return lax.ppermute(block, "azimuth", pairs)


def partner_static(a, step, count, sign=1):
    return a ^ step if count & (count - 1) == 0 else (a + sign * step) % count


def tables(count, part, modes):
    length = count * part
    whole = modes // LANES * LANES
    order = np.concatenate(
        [
            np.arange(whole),
            modes + np.arange(whole),
            np.arange(whole, modes),
            modes + np.arange(whole, modes),
        ]
    )
    positions = np.arange(length)
    waves = np.arange(modes)
    phase = (positions[:, None] * waves[None, :]) % length
    angle = (2.0 * math.pi / length) * phase
    scale = 1.0 / math.sqrt(length)
    factor = np.where(waves == 0, 1.0, 2.0)
    analysis = np.concatenate([np.cos(angle), -np.sin(angle)], axis=1) * scale
    synth = np.concatenate([np.cos(angle) * factor, -np.sin(angle) * factor], axis=1) * scale
    analysis = analysis.astype(np.float32).astype(ml_dtypes.bfloat16)[:, order]
    synth = synth.astype(np.float32).astype(ml_dtypes.bfloat16)[:, order]
    wide = round_up(part, HALF)
    window = round_up(HALF + wide, LANES)
    forth = np.zeros((count, HALF + window, 2 * modes), ml_dtypes.bfloat16)
    back = np.zeros((count, wide, 2 * modes), ml_dtypes.bfloat16)
    for s in range(count):
        forth[s, HALF : HALF + part] = analysis[s * part : (s + 1) * part]
        back[s, :part] = synth[s * part : (s + 1) * part]
    return forth, back


def gelu_slope(values):
    size = jnp.abs(values)
    decay = jnp.exp(-0.5 * (values * values))
    t = pl.reciprocal(1.0 + (0.3275911 * math.sqrt(0.5)) * size)
    tail = 0.5 * 1.061405429
    for factor in (-1.453152027, 1.421413741, -0.284496736, 0.254829592):
        tail = tail * t + 0.5 * factor
    lower = decay * (tail * t - (1.0 / math.sqrt(2.0 * math.pi)) * size)
    return jnp.where(values < 0.0, lower, 1.0 - lower)


def dot_nt(left, right):
    return lax.dot_general(left, right, (((1,), (1,)), ((), ())), preferred_element_type=jnp.float32)


def dot_nn(left, right):
    return jnp.dot(left, right, preferred_element_type=jnp.float32)


def mlp_kernel(count, chunk, conv_ref, grad_ref, win_ref, bias_ref, wout_ref, *rest):
    outs, slope_ref, total_ref = rest[:-2], rest[-2], rest[-1]
    step = pl.program_id(0)
    rows, part, channels = conv_ref.shape
    wide = slope_ref.shape[0] // rows
    owned = channels // count
    start, size = chunk
    me = lax.axis_index("azimuth")

    @pl.when(step == 0)
    def _():
        total_ref[...] = jnp.zeros_like(total_ref)

    block = win_ref.shape[1]
    bias = bias_ref[pl.ds(pl.multiple_of(step * block, block), block)].reshape(1, block)
    spare = jnp.zeros((wide - part, block), jnp.bfloat16)
    for row in range(rows):
        pre = dot_nn(conv_ref[row], win_ref[...]) + bias
        back = dot_nt(grad_ref[row], wout_ref[...])
        slope = (back * gelu_slope(pre)).astype(jnp.bfloat16)
        slope_ref[row * wide : row * wide + part, :] = slope
        slope_ref[row * wide + part : (row + 1) * wide, :] = spare
    for k in range(count):
        target = partner(me, k, count, 1)
        weight = win_ref[pl.ds(pl.multiple_of(target * owned + start, 32), size), :]
        total_ref[k] += dot_nt(weight, slope_ref[...])

    @pl.when(step == pl.num_programs(0) - 1)
    def _():
        for k in range(count):
            outs[k][...] = total_ref[k].astype(jnp.bfloat16)


def mlp(conv_out, grad_out, w_in, b_in, w_out, count, chunk):
    rows, part, channels = conv_out.shape
    hidden = w_in.shape[1]
    block = 256
    wide = round_up(part, HALF)
    whole = lambda shape: pl.BlockSpec(shape, lambda t: (0,) * len(shape))
    piece = jax.ShapeDtypeStruct((chunk[1], rows * wide), jnp.bfloat16)
    return pl.pallas_call(
        functools.partial(mlp_kernel, count, chunk),
        grid=(hidden // block,),
        in_specs=[
            whole(conv_out.shape),
            whole(grad_out.shape),
            pl.BlockSpec((channels, block), lambda t: (0, t)),
            whole(b_in.shape),
            pl.BlockSpec((block, channels), lambda t: (t, 0)),
        ],
        out_specs=[whole(piece.shape)] * count + [pl.BlockSpec((rows * wide, block), lambda t: (0, t))],
        out_shape=[piece] * count + [jax.ShapeDtypeStruct((rows * wide, hidden), jnp.bfloat16)],
        scratch_shapes=[pltpu.VMEM((count, chunk[1], rows * wide), jnp.float32)],
        compiler_params=pltpu.CompilerParams(vmem_limit_bytes=16 * 2**20),
        cost_estimate=pl.CostEstimate(
            flops=6 * rows * part * channels * hidden, bytes_accessed=8 * 2**20, transcendentals=0
        ),
        name="mlp",
    )(conv_out, grad_out, w_in, b_in, w_out)


def rest_kernel(count, chunk, win_ref, slope_ref, *outs):
    owned = win_ref.shape[0] // count
    start, size = chunk
    me = lax.axis_index("azimuth")
    for k in range(count):
        target = partner(me, k, count, 1)
        weight = win_ref[pl.ds(pl.multiple_of(target * owned + start, 32), size), :]
        outs[k][...] = dot_nt(weight, slope_ref[...]).astype(jnp.bfloat16)


def rest_of_mlp(w_in, slope, count, chunk):
    piece = jax.ShapeDtypeStruct((chunk[1], slope.shape[0]), jnp.bfloat16)
    return pl.pallas_call(
        functools.partial(rest_kernel, count, chunk),
        in_specs=[pl.BlockSpec(memory_space=VMEM)] * 2,
        out_specs=[pl.BlockSpec(memory_space=VMEM)] * count,
        out_shape=[piece] * count,
        compiler_params=pltpu.CompilerParams(vmem_limit_bytes=12 * 2**20),
        cost_estimate=pl.CostEstimate(
            flops=2 * count * chunk[1] * slope.size, bytes_accessed=4 * 2**20, transcendentals=0
        ),
        name="rest_of_mlp",
    )(w_in, slope)


def analysis_kernel(count, rows, *refs):
    pieces, table_ref = refs[:count], refs[count]
    own_ref, upward_ref, downward_ref = refs[count + 1 :]
    wide = pieces[0].shape[1] // rows
    window = table_ref.shape[1] - HALF
    me = lax.axis_index("azimuth")
    sources = [partner(me, k, count, -1) for k in range(count)]
    for row in range(rows):
        first = row * wide // LANES * LANES
        shift = row * wide - first
        total = None
        for k in range(count):
            term = dot_nn(
                pieces[k][:, first : first + window],
                table_ref[sources[k], HALF - shift : HALF - shift + window, :],
            )
            total = term if total is None else total + term
        own_ref[row] = total
        sent = total.astype(jnp.bfloat16)
        if row >= rows - REACH:
            upward_ref[row - (rows - REACH)] = sent
        if row < REACH:
            downward_ref[row] = sent


def analyze(pieces, table, rows):
    count = len(pieces)
    size = pieces[0].shape[0]
    width = table.shape[2]
    halo = jax.ShapeDtypeStruct((REACH, size, width), jnp.bfloat16)
    return pl.pallas_call(
        functools.partial(analysis_kernel, count, rows),
        in_specs=[pl.BlockSpec(memory_space=VMEM)] * (count + 1),
        out_specs=[pl.BlockSpec(memory_space=VMEM)] * 3,
        out_shape=[jax.ShapeDtypeStruct((rows, size, width), jnp.float32), halo, halo],
        compiler_params=pltpu.CompilerParams(vmem_limit_bytes=12 * 2**20),
        cost_estimate=pl.CostEstimate(
            flops=8 * rows * size * 256 * width, bytes_accessed=4 * 2**20, transcendentals=0
        ),
        name="analysis",
    )(*pieces, table)


def add_pair(acc, spectrum, weight, target_row, filter_row, target):
    masked = jnp.where(target_row == target, weight, 0.0).astype(jnp.bfloat16)
    gain = dot_nn(masked, filter_row)
    whole = (gain.shape[1] // 2) // LANES * LANES - LANES
    spec_re = spectrum[:, :whole]
    spec_im = spectrum[:, whole : 2 * whole]
    spec_x = spectrum[:, 2 * whole :]
    swapped = pltpu.roll(spec_x, HALF, 1)
    gain_re = gain[:, :whole]
    gain_rx = gain[:, whole : whole + LANES]
    gain_im = gain[:, whole + LANES : 2 * whole + LANES]
    gain_ix = gain[:, 2 * whole + LANES :]
    acc_re, acc_im, acc_x = acc
    acc_re = acc_re + (gain_re * spec_re + gain_im * spec_im)
    acc_im = acc_im + (gain_re * spec_im - gain_im * spec_re)
    acc_x = acc_x + (gain_rx * spec_x + gain_ix * swapped)
    return acc_re, acc_im, acc_x


def split_tiles(value):
    whole = (value.shape[1] - LANES) // 2
    return value[:, :whole], value[:, whole : 2 * whole], value[:, 2 * whole :]


def own_kernel(own_ref, weight_ref, target_ref, filter_ref, out_ref):
    rows, size, width = own_ref.shape
    for target in range(rows):
        acc = split_tiles(jnp.zeros((size, width), jnp.float32))
        for row in range(rows):
            if abs(row - target) <= REACH:
                at = row + REACH
                acc = add_pair(
                    acc, own_ref[row], weight_ref[...], target_ref[at : at + 1, :], filter_ref[at], target
                )
        out_ref[target] = jnp.concatenate(acc, axis=1)


def own_terms(own, weight, target, filters):
    return pl.pallas_call(
        own_kernel,
        in_specs=[pl.BlockSpec(memory_space=VMEM)] * 4,
        out_specs=pl.BlockSpec(memory_space=VMEM),
        out_shape=jax.ShapeDtypeStruct(own.shape, jnp.float32),
        compiler_params=pltpu.CompilerParams(vmem_limit_bytes=12 * 2**20),
        cost_estimate=pl.CostEstimate(flops=2 * 10**9, bytes_accessed=4 * 2**20, transcendentals=0),
        name="own_terms",
    )(own, weight, target, filters)


def finish_kernel(count, part_ref, low_ref, high_ref, weight_ref, target_ref, filter_ref, table_ref, *rest):
    outs, stacked_ref = rest[-count - 1 : -1], rest[-1]
    rows, size, width = part_ref.shape
    part = outs[0].shape[0]
    for target in range(rows):
        acc = split_tiles(part_ref[target])
        for side, base in ((low_ref, -REACH), (high_ref, rows)):
            for h in range(REACH):
                row = base + h
                if abs(row - target) <= REACH:
                    at = row + REACH
                    acc = add_pair(
                        acc,
                        side[h].astype(jnp.float32),
                        weight_ref[...],
                        target_ref[at : at + 1, :],
                        filter_ref[at],
                        target,
                    )
        stacked_ref[target * size : (target + 1) * size, :] = jnp.concatenate(acc, axis=1).astype(
            jnp.bfloat16
        )
    me = lax.axis_index("azimuth")
    for k in range(count):
        grid = dot_nt(table_ref[partner(me, k, count, 1)], stacked_ref[...])
        outs[k][...] = grid[:part].astype(jnp.bfloat16)


def finish(own, low, high, weight, target, filters, table, count, part, after):
    rows, size, width = own.shape
    return pl.pallas_call(
        functools.partial(finish_kernel, count),
        in_specs=[pl.BlockSpec(memory_space=VMEM)] * 7 + [pl.BlockSpec(memory_space=pl.ANY)] * len(after),
        out_specs=[pl.BlockSpec(memory_space=VMEM)] * count,
        out_shape=[jax.ShapeDtypeStruct((part, rows * size), jnp.bfloat16)] * count,
        scratch_shapes=[pltpu.VMEM((rows * size, width), jnp.bfloat16)],
        compiler_params=pltpu.CompilerParams(vmem_limit_bytes=12 * 2**20),
        cost_estimate=pl.CostEstimate(flops=2 * 10**9, bytes_accessed=4 * 2**20, transcendentals=0),
        name="finish",
    )(own, low, high, weight, target, filters, table, *after)


def add_kernel(count, chunks, grad_ref, *refs):
    pieces, out_ref = refs[:-1], refs[-1]
    rows, part, channels = grad_ref.shape
    me = lax.axis_index("azimuth")

    def add(mine):
        order = [[k for k in range(count) if partner_static(mine, k, count, -1) == s][0] for s in range(count)]
        for row in range(rows):
            conv = jnp.concatenate(
                [
                    pieces[q * count + k][:, row * size : (row + 1) * size]
                    for k in order
                    for q, (_, size) in enumerate(chunks)
                ],
                axis=1,
            )
            out_ref[row] = (grad_ref[row].astype(jnp.float32) + conv.astype(jnp.float32)).astype(
                jnp.bfloat16
            )

    for mine in range(count):
        pl.when(me == mine)(functools.partial(add, mine))


def add_back(grad_out, pieces, count, chunks):
    return pl.pallas_call(
        functools.partial(add_kernel, count, chunks),
        in_specs=[pl.BlockSpec(memory_space=VMEM)] * (1 + len(pieces)),
        out_specs=pl.BlockSpec(memory_space=VMEM),
        out_shape=jax.ShapeDtypeStruct(grad_out.shape, jnp.bfloat16),
        compiler_params=pltpu.CompilerParams(vmem_limit_bytes=12 * 2**20),
        cost_estimate=pl.CostEstimate(flops=10**6, bytes_accessed=4 * 2**20, transcendentals=0),
        name="add_back",
    )(grad_out, *pieces)


def prepare_kernel(count, chunks, weight_ref, filt_ref, offset_ref, forth_ref, back_ref, *outs):
    filter_out, target_out, forth_out, back_out = outs[:4]
    forth_out[...] = forth_ref[...]
    back_out[...] = back_ref[...]
    bases, channels = weight_ref.shape
    lats, width = filt_ref.shape[1:]
    ext, depth = target_out.shape
    rows = ext - 2 * REACH
    modes = width // 2
    whole = modes // LANES * LANES
    used = TERMS * bases
    weight = pltpu.roll(
        weight_ref[...], lax.rem(count - lax.axis_index("azimuth"), count) * (channels // count), 1
    )[:, : channels // count]
    parts = []
    for _ in range(TERMS):
        rounded = weight.astype(jnp.bfloat16).astype(jnp.float32)
        parts.append(rounded)
        weight = weight - rounded
    parts.append(jnp.zeros((depth - used, weight.shape[1]), jnp.float32))
    weight = jnp.concatenate(parts, axis=0).T
    for (start, size), out in zip(chunks, outs[4:]):
        out[...] = weight[start : start + size]
    start_lat = lax.axis_index("polar") * rows
    table = filt_ref[...].reshape(bases * lats, width)
    base = lax.broadcasted_iota(jnp.int32, (depth, bases * lats), 0)
    valid = base < used
    for _ in range(TERMS - 1):
        base = jnp.where(base >= bases, base - bases, base)
    column = lax.broadcasted_iota(jnp.int32, (depth, bases * lats), 1)
    for i in range(ext):
        lat = start_lat + (i - REACH)
        inside = (lat >= 0) & (lat < lats)
        lat = jnp.clip(lat, 0, lats - 1)
        pick = jnp.where(valid & (column == base * lats + lat), 1.0, 0.0).astype(jnp.bfloat16)
        row = dot_nn(pick, table)
        real, imag = row[:, :modes], row[:, modes:]
        rest_re, rest_im = real[:, whole:], imag[:, whole:]
        filter_out[i] = jnp.concatenate(
            [real[:, :whole], rest_re, rest_re, imag[:, :whole], rest_im, -rest_im], axis=1
        ).astype(jnp.bfloat16)
        local = jnp.where(inside, offset_ref[pl.ds(lat, 1), :] - start_lat, -1)
        spare = jnp.full((1, depth - used), -1, jnp.int32)
        target_out[i : i + 1, :] = jnp.concatenate([local] * TERMS + [spare], axis=1)


def prepare(basis_weight, filt, offsets, forth, back, rows, count, chunks):
    bases = filt.shape[0]
    width = filt.shape[2]
    ext = rows + 2 * REACH
    depth = round_up(TERMS * bases, 16)
    shapes = [
        jax.ShapeDtypeStruct((ext, depth, width + LANES), jnp.bfloat16),
        jax.ShapeDtypeStruct((ext, depth), jnp.int32),
        jax.ShapeDtypeStruct(forth.shape, forth.dtype),
        jax.ShapeDtypeStruct(back.shape, back.dtype),
    ] + [jax.ShapeDtypeStruct((size, depth), jnp.float32) for _, size in chunks]
    return pl.pallas_call(
        functools.partial(prepare_kernel, count, chunks),
        in_specs=[pl.BlockSpec(memory_space=VMEM)] * 5,
        out_specs=[pl.BlockSpec(memory_space=VMEM)] * len(shapes),
        out_shape=shapes,
        compiler_params=pltpu.CompilerParams(vmem_limit_bytes=16 * 2**20),
        cost_estimate=pl.CostEstimate(flops=10**9, bytes_accessed=6 * 2**20, transcendentals=0),
        name="prepare",
    )(basis_weight, filt, offsets, forth, back)


def halo(upward, downward):
    count = lax.axis_size("polar")
    forward = [(i, i + 1) for i in range(count - 1)]
    backward = [(i + 1, i) for i in range(count - 1)]
    return lax.ppermute(upward, "polar", forward), lax.ppermute(downward, "polar", backward)


def on_device(chunks, conv_out, grad_out, w_in, b_in, w_out, basis_weight, filt, offsets):
    rows, part, channels = conv_out.shape
    count = lax.axis_size("azimuth")
    forth, back = tables(count, part, filt.shape[2] // 2)
    forth, back = jnp.asarray(forth), jnp.asarray(back)
    *blocks, slope = mlp(conv_out, grad_out, w_in, b_in, w_out, count, chunks[0])
    for chunk in chunks[1:]:
        blocks += rest_of_mlp(w_in, slope, count, chunk)
    filters, target, forth, back, *weights = prepare(
        basis_weight, filt, offsets, forth, back, rows, count, chunks
    )
    returned = []
    for q, (start, size) in enumerate(chunks):
        pieces = [exchange(blocks[q * count + k], k, count) for k in range(count)]
        own, upward, downward = analyze(pieces, forth, rows)
        low, high = halo(upward, downward)
        own = own_terms(own, weights[q], target, filters)
        grids = finish(own, low, high, weights[q], target, filters, back, count, part, returned[1 - count :] if q else [])
        returned += [exchange(grids[k], k, count) for k in range(count)]
    return add_back(grad_out, returned, count, chunks)


def solution(mesh):
    grid = P(("member", "polar"), "azimuth", None)

    def run(conv_out, grad_out, *others):
        owned = conv_out.shape[2] // mesh.shape["azimuth"]
        chunks = ((0, owned),) if owned % 32 else ((0, owned * 3 // 5), (owned * 3 // 5, owned - owned * 3 // 5))
        return jax.shard_map(
            functools.partial(on_device, chunks),
            mesh=mesh,
            in_specs=(grid, grid) + (P(),) * 6,
            out_specs=grid,
            check_vma=False,
        )(conv_out, grad_out, *others)

    return run
```

```python
import functools
import math

import jax
import jax.numpy as jnp
import ml_dtypes
import numpy as np
from jax import lax
from jax.experimental import pallas as pl
from jax.experimental.pallas import tpu as pltpu
from jax.sharding import PartitionSpec as P

REACH = 3
LANES = 128
HALF = 64
TERMS = 3
VMEM = pltpu.MemorySpace.VMEM
NO_COST = pl.CostEstimate(flops=0, bytes_accessed=0, transcendentals=0)


def round_up(value, unit):
    return -(-value // unit) * unit


def partner(me, step, count, sign):
    if count & (count - 1) == 0:
        return me ^ step
    return lax.rem(me + sign * step + count, count)


def exchange(block, step, count):
    if step == 0:
        return block
    pairs = [(a, int(partner_static(a, step, count))) for a in range(count)]
    return lax.ppermute(block, "azimuth", pairs)


def partner_static(a, step, count, sign=1):
    return a ^ step if count & (count - 1) == 0 else (a + sign * step) % count


def tables(count, part, modes):
    length = count * part
    whole = modes // LANES * LANES
    order = np.concatenate(
        [
            np.arange(whole),
            modes + np.arange(whole),
            np.arange(whole, modes),
            modes + np.arange(whole, modes),
        ]
    )
    positions = np.arange(length)
    waves = np.arange(modes)
    phase = (positions[:, None] * waves[None, :]) % length
    angle = (2.0 * math.pi / length) * phase
    scale = 1.0 / math.sqrt(length)
    factor = np.where(waves == 0, 1.0, 2.0)
    analysis = np.concatenate([np.cos(angle), -np.sin(angle)], axis=1) * scale
    synth = np.concatenate([np.cos(angle) * factor, -np.sin(angle) * factor], axis=1) * scale
    analysis = analysis.astype(np.float32).astype(ml_dtypes.bfloat16)[:, order]
    synth = synth.astype(np.float32).astype(ml_dtypes.bfloat16)[:, order]
    wide = round_up(part, HALF)
    window = round_up(HALF + wide, LANES)
    forth = np.zeros((count, HALF + window, 2 * modes), ml_dtypes.bfloat16)
    back = np.zeros((count, wide, 2 * modes), ml_dtypes.bfloat16)
    for s in range(count):
        forth[s, HALF : HALF + part] = analysis[s * part : (s + 1) * part]
        back[s, :part] = synth[s * part : (s + 1) * part]
    return forth, back


def gelu_slope(values):
    size = jnp.abs(values)
    decay = jnp.exp(-0.5 * (values * values))
    t = pl.reciprocal(1.0 + (0.3275911 * math.sqrt(0.5)) * size)
    tail = 0.5 * 1.061405429
    for factor in (-1.453152027, 1.421413741, -0.284496736, 0.254829592):
        tail = tail * t + 0.5 * factor
    lower = decay * (tail * t - (1.0 / math.sqrt(2.0 * math.pi)) * size)
    return jnp.where(values < 0.0, lower, 1.0 - lower)


def dot_nt(left, right):
    return lax.dot_general(left, right, (((1,), (1,)), ((), ())), preferred_element_type=jnp.float32)


def dot_nn(left, right):
    return jnp.dot(left, right, preferred_element_type=jnp.float32)


def mlp_kernel(count, chunks, conv_hbm, grad_hbm, win_hbm, bias_ref, wout_hbm, *rest):
    pieces = len(chunks) * count
    outs, grad_ref = rest[:pieces], rest[pieces]
    (conv_in, grad_in, conv_ref, win_ref, wout_ref, pre_ref, back_ref, tall_ref, slope_ref, total_ref, sems) = rest[
        pieces + 1 :
    ]
    part, rows, channels = conv_in.shape
    hidden = win_ref.shape[1]
    block = slope_ref.shape[2]
    steps = hidden // block
    wide = slope_ref.shape[1] // rows
    owned = channels // count
    me = lax.axis_index("azimuth")

    def columns(t):
        return pl.ds(t * block, block)

    conv_copy = pltpu.make_async_copy(conv_hbm, conv_in, sems.at[0])
    grad_copy = pltpu.make_async_copy(grad_hbm, grad_in, sems.at[1])
    win_copies = [
        pltpu.make_async_copy(win_hbm.at[:, columns(t)], win_ref.at[:, columns(t)], sems.at[2 + t])
        for t in range(steps)
    ]
    wout_copies = [
        pltpu.make_async_copy(wout_hbm.at[columns(t)], wout_ref.at[columns(t)], sems.at[2 + steps + t])
        for t in range(steps)
    ]
    conv_copy.start()
    win_copies[0].start()
    grad_copy.start()
    wout_copies[0].start()
    for t in range(1, steps):
        win_copies[t].start()
        wout_copies[t].start()

    spare = jnp.zeros((wide - part, block), jnp.bfloat16)
    for slot in range(2):
        for row in range(rows):
            slope_ref[slot, row * wide + part : (row + 1) * wide, :] = spare

    def project(t):
        slot = t % 2
        if t == 0:
            conv_copy.wait()
            conv_ref[...] = conv_in[...].reshape(conv_ref.shape)
        win_copies[t].wait()
        bias = bias_ref[t * block : (t + 1) * block].reshape(1, block)
        pre_ref[slot] = dot_nn(conv_ref[...], win_ref[:, t * block : (t + 1) * block]) + bias
        if t == 0:
            grad_copy.wait()
            grad_ref[...] = grad_in[...].reshape(grad_ref.shape)
        wout_copies[t].wait()
        back_ref[slot] = dot_nt(grad_ref[...], wout_ref[t * block : (t + 1) * block, :])

    def slope(t):
        slot = t % 2
        group = 24
        for first in range(0, part * rows, group):
            at = slice(first, first + group)
            value = back_ref[slot, at, :] * gelu_slope(pre_ref[slot, at, :])
            for h in range(block // LANES):
                tall_ref[slot * (block // LANES) + h, at, :] = value[:, h * LANES : (h + 1) * LANES]
        for row in range(rows):
            for h in range(block // LANES):
                picked = tall_ref[slot * (block // LANES) + h, pl.ds(row, part, stride=rows), :]
                slope_ref[slot, row * wide : row * wide + part, h * LANES : (h + 1) * LANES] = picked.astype(
                    jnp.bfloat16
                )

    def gather(t):
        term = dot_nt(win_ref[:, t * block : (t + 1) * block], slope_ref[t % 2])
        total_ref[...] = term if t == 0 else total_ref[...] + term

    project(0)
    for t in range(steps):
        if t + 1 < steps:
            project(t + 1)
        if t > 0:
            gather(t - 1)
        slope(t)
    gather(steps - 1)
    for q, (start, size) in enumerate(chunks):
        for k in range(count):
            first = partner(me, k, count, 1) * owned + start
            outs[q * count + k][...] = total_ref[pl.ds(pl.multiple_of(first, 32), size), :].astype(jnp.bfloat16)


def mlp(conv_out, grad_out, w_in, b_in, w_out, count, chunks):
    part, rows, channels = conv_out.shape
    hidden = w_in.shape[1]
    block = 256
    wide = round_up(part, HALF)
    points = part * rows
    out_shape = [
        jax.ShapeDtypeStruct((size, rows * wide), jnp.bfloat16) for _, size in chunks for _ in range(count)
    ] + [jax.ShapeDtypeStruct((points, channels), jnp.bfloat16)]
    hbm = pl.BlockSpec(memory_space=pltpu.MemorySpace.HBM)
    vmem = pl.BlockSpec(memory_space=VMEM)
    return pl.pallas_call(
        functools.partial(mlp_kernel, count, chunks),
        in_specs=[hbm, hbm, hbm, vmem, hbm],
        out_specs=[vmem] * len(out_shape),
        out_shape=out_shape,
        scratch_shapes=[
            pltpu.VMEM(conv_out.shape, jnp.bfloat16),
            pltpu.VMEM(conv_out.shape, jnp.bfloat16),
            pltpu.VMEM((points, channels), jnp.bfloat16),
            pltpu.VMEM(w_in.shape, jnp.bfloat16),
            pltpu.VMEM(w_out.shape, jnp.bfloat16),
            pltpu.VMEM((2, points, block), jnp.float32),
            pltpu.VMEM((2, points, block), jnp.float32),
            pltpu.VMEM((2 * (block // LANES), points, LANES), jnp.float32),
            pltpu.VMEM((2, rows * wide, block), jnp.bfloat16),
            pltpu.VMEM((channels, rows * wide), jnp.float32),
            pltpu.SemaphoreType.DMA((2 + 2 * (hidden // block),)),
        ],
        compiler_params=pltpu.CompilerParams(vmem_limit_bytes=58 * 2**20),
        cost_estimate=NO_COST,
        name="mlp",
    )(conv_out, grad_out, w_in, b_in, w_out)


def gate_kernel(*refs):
    pass


def gate(arrays, after):
    anywhere = pl.BlockSpec(memory_space=pl.ANY)
    return pl.pallas_call(
        gate_kernel,
        in_specs=[anywhere] * (len(arrays) + len(after)),
        out_specs=[anywhere] * len(arrays),
        out_shape=[jax.ShapeDtypeStruct(x.shape, x.dtype) for x in arrays],
        input_output_aliases={i: i for i in range(len(arrays))},
        cost_estimate=NO_COST,
        name="gate",
    )(*arrays, *after)


def analysis_kernel(count, rows, *refs):
    pieces, table_ref = refs[:count], refs[count]
    own_ref, first_ref, second_ref = refs[count + 1 :]
    wide = pieces[0].shape[1] // rows
    window = table_ref.shape[1] - HALF
    me = lax.axis_index("azimuth")
    sources = [partner(me, k, count, -1) for k in range(count)]
    for row in range(rows):
        first = row * wide // LANES * LANES
        shift = row * wide - first
        total = None
        for k in range(count):
            term = dot_nn(
                pieces[k][:, first : first + window],
                table_ref[sources[k], HALF - shift : HALF - shift + window, :],
            )
            total = term if total is None else total + term
        own_ref[row] = total
    first_row = jnp.where(lax.rem(lax.axis_index("polar"), 2) == 0, rows - REACH, 0)
    for h in range(REACH):
        first_ref[h] = own_ref[first_row + h].astype(jnp.bfloat16)
        second_ref[h] = own_ref[rows - REACH - first_row + h].astype(jnp.bfloat16)


def analyze(pieces, table, rows):
    count = len(pieces)
    size = pieces[0].shape[0]
    width = table.shape[2]
    halo = jax.ShapeDtypeStruct((REACH, size, width), jnp.bfloat16)
    return pl.pallas_call(
        functools.partial(analysis_kernel, count, rows),
        in_specs=[pl.BlockSpec(memory_space=VMEM)] * (count + 1),
        out_specs=[pl.BlockSpec(memory_space=VMEM)] * 3,
        out_shape=[jax.ShapeDtypeStruct((rows, size, width), jnp.float32), halo, halo],
        compiler_params=pltpu.CompilerParams(vmem_limit_bytes=12 * 2**20),
        cost_estimate=NO_COST,
        name="analysis",
    )(*pieces, table)


def add_pair(acc, spectrum, weight, target_row, filter_row, target):
    masked = jnp.where(target_row == target, weight, 0.0).astype(jnp.bfloat16)
    gain = dot_nn(masked, filter_row)
    whole = (gain.shape[1] // 2) // LANES * LANES - LANES
    spec_re = spectrum[:, :whole]
    spec_im = spectrum[:, whole : 2 * whole]
    spec_x = spectrum[:, 2 * whole :]
    swapped = pltpu.roll(spec_x, HALF, 1)
    gain_re = gain[:, :whole]
    gain_rx = gain[:, whole : whole + LANES]
    gain_im = gain[:, whole + LANES : 2 * whole + LANES]
    gain_ix = gain[:, 2 * whole + LANES :]
    acc_re, acc_im, acc_x = acc
    acc_re = acc_re + (gain_re * spec_re + gain_im * spec_im)
    acc_im = acc_im + (gain_re * spec_im - gain_im * spec_re)
    acc_x = acc_x + (gain_rx * spec_x + gain_ix * swapped)
    return acc_re, acc_im, acc_x


def split_tiles(value):
    whole = (value.shape[1] - LANES) // 2
    return value[:, :whole], value[:, whole : 2 * whole], value[:, 2 * whole :]


def own_kernel(own_ref, weight_ref, target_ref, filter_ref, out_ref):
    rows, size, width = own_ref.shape
    for target in range(rows):
        acc = split_tiles(jnp.zeros((size, width), jnp.float32))
        for row in range(rows):
            if abs(row - target) <= REACH:
                at = row + REACH
                acc = add_pair(
                    acc, own_ref[row], weight_ref[...], target_ref[at : at + 1, :], filter_ref[at], target
                )
        out_ref[target] = jnp.concatenate(acc, axis=1)


def own_terms(own, weight, target, filters):
    return pl.pallas_call(
        own_kernel,
        in_specs=[pl.BlockSpec(memory_space=VMEM)] * 4,
        out_specs=pl.BlockSpec(memory_space=VMEM),
        out_shape=jax.ShapeDtypeStruct(own.shape, jnp.float32),
        compiler_params=pltpu.CompilerParams(vmem_limit_bytes=12 * 2**20),
        cost_estimate=NO_COST,
        name="own_terms",
    )(own, weight, target, filters)


def finish_kernel(count, part_ref, first_ref, second_ref, weight_ref, target_ref, filter_ref, table_ref, *rest):
    outs, stacked_ref = rest[-count - 1 : -1], rest[-1]
    rows, size, width = part_ref.shape
    part = outs[0].shape[0]
    even = lax.rem(lax.axis_index("polar"), 2) == 0

    def combine(low_ref, high_ref):
        for target in range(rows):
            acc = split_tiles(part_ref[target])
            for side, base in ((low_ref, -REACH), (high_ref, rows)):
                for h in range(REACH):
                    row = base + h
                    if abs(row - target) <= REACH:
                        at = row + REACH
                        acc = add_pair(
                            acc,
                            side[h].astype(jnp.float32),
                            weight_ref[...],
                            target_ref[at : at + 1, :],
                            filter_ref[at],
                            target,
                        )
            stacked_ref[target * size : (target + 1) * size, :] = jnp.concatenate(acc, axis=1).astype(
                jnp.bfloat16
            )

    pl.when(even)(lambda: combine(second_ref, first_ref))
    pl.when(jnp.logical_not(even))(lambda: combine(first_ref, second_ref))
    me = lax.axis_index("azimuth")
    for k in range(count):
        grid = dot_nt(table_ref[partner(me, k, count, 1)], stacked_ref[...])
        outs[k][...] = grid[:part].astype(jnp.bfloat16)


def finish(own, first, second, weight, target, filters, table, count, part, after):
    rows, size, width = own.shape
    return pl.pallas_call(
        functools.partial(finish_kernel, count),
        in_specs=[pl.BlockSpec(memory_space=VMEM)] * 7 + [pl.BlockSpec(memory_space=pl.ANY)] * len(after),
        out_specs=[pl.BlockSpec(memory_space=VMEM)] * count,
        out_shape=[jax.ShapeDtypeStruct((part, rows * size), jnp.bfloat16)] * count,
        scratch_shapes=[pltpu.VMEM((rows * size, width), jnp.bfloat16)],
        compiler_params=pltpu.CompilerParams(vmem_limit_bytes=12 * 2**20),
        cost_estimate=NO_COST,
        name="finish",
    )(own, first, second, weight, target, filters, table, *after)


def add_kernel(count, chunks, grad_ref, *refs):
    pieces, out_ref, tall_ref = refs[:-2], refs[-2], refs[-1]
    part, rows, channels = out_ref.shape
    me = lax.axis_index("azimuth")

    def collect(mine):
        order = [[k for k in range(count) if partner_static(mine, k, count, -1) == s][0] for s in range(count)]
        for row in range(rows):
            conv = jnp.concatenate(
                [
                    pieces[q * count + k][:, row * size : (row + 1) * size]
                    for k in order
                    for q, (_, size) in enumerate(chunks)
                ],
                axis=1,
            ).astype(jnp.float32)
            for h in range(channels // LANES):
                tall_ref[h, pl.ds(row, part, stride=rows), :] = conv[:, h * LANES : (h + 1) * LANES]

    for mine in range(count):
        pl.when(me == mine)(functools.partial(collect, mine))
    for h in range(channels // LANES):
        at = slice(h * LANES, (h + 1) * LANES)
        total = grad_ref[:, at].astype(jnp.float32) + tall_ref[h]
        out_ref[:, :, at] = total.reshape(part, rows, LANES).astype(jnp.bfloat16)


def add_back(grad, pieces, count, chunks, shape):
    return pl.pallas_call(
        functools.partial(add_kernel, count, chunks),
        in_specs=[pl.BlockSpec(memory_space=VMEM)] * (1 + len(pieces)),
        out_specs=pl.BlockSpec(memory_space=VMEM),
        out_shape=jax.ShapeDtypeStruct(shape, jnp.bfloat16),
        scratch_shapes=[pltpu.VMEM((shape[2] // LANES, shape[0] * shape[1], LANES), jnp.float32)],
        compiler_params=pltpu.CompilerParams(vmem_limit_bytes=12 * 2**20),
        cost_estimate=NO_COST,
        name="add_back",
    )(grad, *pieces)


def prepare_kernel(count, chunks, weight_ref, filt_ref, offset_ref, forth_ref, back_ref, *outs):
    filter_out, target_out, forth_out, back_out = outs[:4]
    forth_out[...] = forth_ref[...]
    back_out[...] = back_ref[...]
    bases, channels = weight_ref.shape
    lats, width = filt_ref.shape[1:]
    ext, depth = target_out.shape
    rows = ext - 2 * REACH
    modes = width // 2
    whole = modes // LANES * LANES
    used = TERMS * bases
    weight = pltpu.roll(
        weight_ref[...], lax.rem(count - lax.axis_index("azimuth"), count) * (channels // count), 1
    )[:, : channels // count]
    parts = []
    for _ in range(TERMS):
        rounded = weight.astype(jnp.bfloat16).astype(jnp.float32)
        parts.append(rounded)
        weight = weight - rounded
    parts.append(jnp.zeros((depth - used, weight.shape[1]), jnp.float32))
    weight = jnp.concatenate(parts, axis=0).T
    for (start, size), out in zip(chunks, outs[4:]):
        out[...] = weight[start : start + size]
    start_lat = lax.axis_index("polar") * rows
    table = filt_ref[...].reshape(bases * lats, width)
    base = lax.broadcasted_iota(jnp.int32, (depth, bases * lats), 0)
    valid = base < used
    for _ in range(TERMS - 1):
        base = jnp.where(base >= bases, base - bases, base)
    column = lax.broadcasted_iota(jnp.int32, (depth, bases * lats), 1)
    for i in range(ext):
        lat = start_lat + (i - REACH)
        inside = (lat >= 0) & (lat < lats)
        lat = jnp.clip(lat, 0, lats - 1)
        pick = jnp.where(valid & (column == base * lats + lat), 1.0, 0.0).astype(jnp.bfloat16)
        row = dot_nn(pick, table)
        real, imag = row[:, :modes], row[:, modes:]
        rest_re, rest_im = real[:, whole:], imag[:, whole:]
        filter_out[i] = jnp.concatenate(
            [real[:, :whole], rest_re, rest_re, imag[:, :whole], rest_im, -rest_im], axis=1
        ).astype(jnp.bfloat16)
        local = jnp.where(inside, offset_ref[pl.ds(lat, 1), :] - start_lat, -1)
        spare = jnp.full((1, depth - used), -1, jnp.int32)
        target_out[i : i + 1, :] = jnp.concatenate([local] * TERMS + [spare], axis=1)


def prepare(basis_weight, filt, offsets, forth, back, rows, count, chunks):
    bases = filt.shape[0]
    width = filt.shape[2]
    ext = rows + 2 * REACH
    depth = round_up(TERMS * bases, 16)
    shapes = [
        jax.ShapeDtypeStruct((ext, depth, width + LANES), jnp.bfloat16),
        jax.ShapeDtypeStruct((ext, depth), jnp.int32),
        jax.ShapeDtypeStruct(forth.shape, forth.dtype),
        jax.ShapeDtypeStruct(back.shape, back.dtype),
    ] + [jax.ShapeDtypeStruct((size, depth), jnp.float32) for _, size in chunks]
    return pl.pallas_call(
        functools.partial(prepare_kernel, count, chunks),
        in_specs=[pl.BlockSpec(memory_space=VMEM)] * 5,
        out_specs=[pl.BlockSpec(memory_space=VMEM)] * len(shapes),
        out_shape=shapes,
        compiler_params=pltpu.CompilerParams(vmem_limit_bytes=16 * 2**20),
        cost_estimate=NO_COST,
        name="prepare",
    )(basis_weight, filt, offsets, forth, back)


def halo(first, second):
    count = lax.axis_size("polar")
    pairs = []
    for odd in (0, 1):
        other = [((a + odd) ^ 1) - odd for a in range(count)]
        pairs.append([(a, o if 0 <= o < count else a) for a, o in enumerate(other)])
    return lax.ppermute(first, "polar", pairs[0]), lax.ppermute(second, "polar", pairs[1])


def on_device(chunks, conv_out, grad_out, w_in, b_in, w_out, basis_weight, filt, offsets):
    rows, part, channels = conv_out.shape
    count = lax.axis_size("azimuth")
    forth, back = tables(count, part, filt.shape[2] // 2)
    forth, back = jnp.asarray(forth), jnp.asarray(back)
    conv_out, grad_out = (jnp.transpose(x, (1, 0, 2)) for x in (conv_out, grad_out))
    *blocks, grad = mlp(conv_out, grad_out, w_in, b_in, w_out, count, chunks)
    filters, target, forth, back, *weights = prepare(
        basis_weight, filt, offsets, forth, back, rows, count, chunks
    )
    returned = []
    received = []
    for q, (start, size) in enumerate(chunks):
        pieces = blocks[q * count : (q + 1) * count]
        if q:
            pieces = gate(pieces, [received[-1]])
        pieces = [exchange(pieces[k], k, count) for k in range(count)]
        received.append(pieces[count // 2])
        own, first, second = analyze(pieces, forth, rows)
        first, second = halo(first, second)
        own = own_terms(own, weights[q], target, filters)
        after = [returned[-(count // 2)]] if q else []
        grids = finish(own, first, second, weights[q], target, filters, back, count, part, after)
        returned += [exchange(grids[k], k, count) for k in range(count)]
    return jnp.transpose(add_back(grad, returned, count, chunks, conv_out.shape), (1, 0, 2))


def solution(mesh):
    grid = P(("member", "polar"), "azimuth", None)

    def run(conv_out, grad_out, *others):
        owned = conv_out.shape[2] // mesh.shape["azimuth"]
        chunks = ((0, owned),) if owned % 32 else ((0, owned * 3 // 5), (owned * 3 // 5, owned - owned * 3 // 5))
        return jax.shard_map(
            functools.partial(on_device, chunks),
            mesh=mesh,
            in_specs=(grid, grid) + (P(),) * 6,
            out_specs=grid,
            check_vma=False,
        )(conv_out, grad_out, *others)

    return run
```

```python
import functools
import math

import jax
import jax.numpy as jnp
import ml_dtypes
import numpy as np
from jax import lax
from jax.experimental import pallas as pl
from jax.experimental.pallas import tpu as pltpu
from jax.sharding import PartitionSpec as P

REACH = 3
LANES = 128
HALF = 64
TERMS = 3
VMEM = pltpu.MemorySpace.VMEM


def round_up(value, unit):
    return -(-value // unit) * unit


def partner(me, step, count, sign):
    if count & (count - 1) == 0:
        return me ^ step
    return lax.rem(me + sign * step + count, count)


def exchange(block, step, count):
    if step == 0:
        return block
    pairs = [(a, int(partner_static(a, step, count))) for a in range(count)]
    return lax.ppermute(block, "azimuth", pairs)


def partner_static(a, step, count, sign=1):
    return a ^ step if count & (count - 1) == 0 else (a + sign * step) % count


def tables(count, part, modes):
    length = count * part
    whole = modes // LANES * LANES
    order = np.concatenate(
        [
            np.arange(whole),
            modes + np.arange(whole),
            np.arange(whole, modes),
            modes + np.arange(whole, modes),
        ]
    )
    positions = np.arange(length)
    waves = np.arange(modes)
    phase = (positions[:, None] * waves[None, :]) % length
    angle = (2.0 * math.pi / length) * phase
    scale = 1.0 / math.sqrt(length)
    factor = np.where(waves == 0, 1.0, 2.0)
    analysis = np.concatenate([np.cos(angle), -np.sin(angle)], axis=1) * scale
    synth = np.concatenate([np.cos(angle) * factor, -np.sin(angle) * factor], axis=1) * scale
    analysis = analysis.astype(np.float32).astype(ml_dtypes.bfloat16)[:, order]
    synth = synth.astype(np.float32).astype(ml_dtypes.bfloat16)[:, order]
    wide = round_up(part, HALF)
    window = round_up(HALF + wide, LANES)
    forth = np.zeros((count, HALF + window, 2 * modes), ml_dtypes.bfloat16)
    back = np.zeros((count, wide, 2 * modes), ml_dtypes.bfloat16)
    for s in range(count):
        forth[s, HALF : HALF + part] = analysis[s * part : (s + 1) * part]
        back[s, :part] = synth[s * part : (s + 1) * part]
    return forth, back


def gelu_slope(values):
    size = jnp.abs(values)
    decay = jnp.exp(-0.5 * (values * values))
    t = pl.reciprocal(1.0 + (0.3275911 * math.sqrt(0.5)) * size)
    tail = 0.5 * 1.061405429
    for factor in (-1.453152027, 1.421413741, -0.284496736, 0.254829592):
        tail = tail * t + 0.5 * factor
    lower = decay * (tail * t - (1.0 / math.sqrt(2.0 * math.pi)) * size)
    return jnp.where(values < 0.0, lower, 1.0 - lower)


def dot_nt(left, right):
    return lax.dot_general(left, right, (((1,), (1,)), ((), ())), preferred_element_type=jnp.float32)


def dot_nn(left, right):
    return jnp.dot(left, right, preferred_element_type=jnp.float32)


def mlp_kernel(count, chunks, conv_ref, grad_ref, win_ref, bias_ref, wout_ref, *rest):
    outs, (slope_ref, total_ref) = rest[:-2], rest[-2:]
    step = pl.program_id(0)
    rows, part, channels = conv_ref.shape
    wide = slope_ref.shape[0] // rows
    owned = channels // count
    me = lax.axis_index("azimuth")

    @pl.when(step == 0)
    def _():
        total_ref[...] = jnp.zeros_like(total_ref)

    block = win_ref.shape[1]
    bias = bias_ref[pl.ds(pl.multiple_of(step * block, block), block)].reshape(1, block)
    spare = jnp.zeros((wide - part, block), jnp.bfloat16)
    for row in range(rows):
        pre = dot_nn(conv_ref[row], win_ref[...]) + bias
        back = dot_nt(grad_ref[row], wout_ref[...])
        slope = (back * gelu_slope(pre)).astype(jnp.bfloat16)
        slope_ref[row * wide : row * wide + part, :] = slope
        slope_ref[row * wide + part : (row + 1) * wide, :] = spare
    total_ref[...] += dot_nt(win_ref[...], slope_ref[...])

    @pl.when(step == pl.num_programs(0) - 1)
    def _():
        sent = [(k, 0, owned) for k in range(count - 1)] + [(count - 1,) + chunk for chunk in chunks]
        for out, (k, start, size) in zip(outs, sent):
            first = partner(me, k, count, 1) * owned + start
            out[...] = total_ref[pl.ds(pl.multiple_of(first, 32), size), :].astype(jnp.bfloat16)


def mlp(conv_out, grad_out, w_in, b_in, w_out, count, chunks):
    rows, part, channels = conv_out.shape
    hidden = w_in.shape[1]
    block = 256
    wide = round_up(part, HALF)
    whole = lambda shape: pl.BlockSpec(shape, lambda t: (0,) * len(shape))
    out_shape = [
        jax.ShapeDtypeStruct((size, rows * wide), jnp.bfloat16)
        for size in [channels // count] * (count - 1) + [size for _, size in chunks]
    ]
    return pl.pallas_call(
        functools.partial(mlp_kernel, count, chunks),
        grid=(hidden // block,),
        in_specs=[
            whole(conv_out.shape),
            whole(grad_out.shape),
            pl.BlockSpec((channels, block), lambda t: (0, t)),
            whole(b_in.shape),
            pl.BlockSpec((block, channels), lambda t: (t, 0)),
        ],
        out_specs=[whole(x.shape) for x in out_shape],
        out_shape=out_shape,
        scratch_shapes=[
            pltpu.VMEM((rows * wide, block), jnp.bfloat16),
            pltpu.VMEM((channels, rows * wide), jnp.float32),
        ],
        compiler_params=pltpu.CompilerParams(vmem_limit_bytes=16 * 2**20),
        cost_estimate=pl.CostEstimate(
            flops=6 * rows * part * channels * hidden, bytes_accessed=8 * 2**20, transcendentals=0
        ),
        name="mlp",
    )(conv_out, grad_out, w_in, b_in, w_out)


def analysis_kernel(count, rows, chunk, *refs):
    pieces, table_ref = refs[:count], refs[count]
    own_ref, first_ref, second_ref = refs[count + 1 :]
    wide = pieces[0].shape[1] // rows
    start, size = chunk
    base = [start] * (count - 1) + [0]
    window = table_ref.shape[1] - HALF
    me = lax.axis_index("azimuth")
    sources = [partner(me, k, count, -1) for k in range(count)]
    even = lax.rem(lax.axis_index("polar"), 2) == 0
    for row in range(rows):
        first = row * wide // LANES * LANES
        shift = row * wide - first
        total = None
        for k in range(count):
            term = dot_nn(
                pieces[k][base[k] : base[k] + size, first : first + window],
                table_ref[sources[k], HALF - shift : HALF - shift + window, :],
            )
            total = term if total is None else total + term
        own_ref[row] = total
        sent = total.astype(jnp.bfloat16)
        for above, parity in ((first_ref, even), (second_ref, jnp.logical_not(even))):
            below = second_ref if above is first_ref else first_ref

            @pl.when(parity)
            def _(above=above, below=below, sent=sent, row=row):
                if row >= rows - REACH:
                    above[row - (rows - REACH)] = sent
                if row < REACH:
                    below[row] = sent


def analyze(pieces, table, rows, chunk):
    count = len(pieces)
    size = chunk[1]
    width = table.shape[2]
    halo = jax.ShapeDtypeStruct((REACH, size, width), jnp.bfloat16)
    return pl.pallas_call(
        functools.partial(analysis_kernel, count, rows, chunk),
        in_specs=[pl.BlockSpec(memory_space=VMEM)] * (count + 1),
        out_specs=[pl.BlockSpec(memory_space=VMEM)] * 3,
        out_shape=[jax.ShapeDtypeStruct((rows, size, width), jnp.float32), halo, halo],
        compiler_params=pltpu.CompilerParams(vmem_limit_bytes=12 * 2**20),
        cost_estimate=pl.CostEstimate(
            flops=8 * rows * size * 256 * width, bytes_accessed=4 * 2**20, transcendentals=0
        ),
        name="analysis",
    )(*pieces, table)


def add_pair(acc, spectrum, weight, target_row, filter_row, target):
    masked = jnp.where(target_row == target, weight, 0.0).astype(jnp.bfloat16)
    gain = dot_nn(masked, filter_row)
    whole = (gain.shape[1] // 2) // LANES * LANES - LANES
    spec_re = spectrum[:, :whole]
    spec_im = spectrum[:, whole : 2 * whole]
    spec_x = spectrum[:, 2 * whole :]
    swapped = pltpu.roll(spec_x, HALF, 1)
    gain_re = gain[:, :whole]
    gain_rx = gain[:, whole : whole + LANES]
    gain_im = gain[:, whole + LANES : 2 * whole + LANES]
    gain_ix = gain[:, 2 * whole + LANES :]
    acc_re, acc_im, acc_x = acc
    acc_re = acc_re + (gain_re * spec_re + gain_im * spec_im)
    acc_im = acc_im + (gain_re * spec_im - gain_im * spec_re)
    acc_x = acc_x + (gain_rx * spec_x + gain_ix * swapped)
    return acc_re, acc_im, acc_x


def split_tiles(value):
    whole = (value.shape[1] - LANES) // 2
    return value[:, :whole], value[:, whole : 2 * whole], value[:, 2 * whole :]


def own_kernel(own_ref, weight_ref, target_ref, filter_ref, out_ref):
    rows, size, width = own_ref.shape
    for target in range(rows):
        acc = split_tiles(jnp.zeros((size, width), jnp.float32))
        for row in range(rows):
            if abs(row - target) <= REACH:
                at = row + REACH
                acc = add_pair(
                    acc, own_ref[row], weight_ref[...], target_ref[at : at + 1, :], filter_ref[at], target
                )
        out_ref[target] = jnp.concatenate(acc, axis=1)


def own_terms(own, weight, target, filters):
    return pl.pallas_call(
        own_kernel,
        in_specs=[pl.BlockSpec(memory_space=VMEM)] * 4,
        out_specs=pl.BlockSpec(memory_space=VMEM),
        out_shape=jax.ShapeDtypeStruct(own.shape, jnp.float32),
        compiler_params=pltpu.CompilerParams(vmem_limit_bytes=12 * 2**20),
        cost_estimate=pl.CostEstimate(flops=2 * 10**9, bytes_accessed=4 * 2**20, transcendentals=0),
        name="own_terms",
    )(own, weight, target, filters)


def finish_kernel(count, part_ref, first_ref, second_ref, weight_ref, target_ref, filter_ref, table_ref, *rest):
    outs, stacked_ref = rest[-count - 1 : -1], rest[-1]
    rows, size, width = part_ref.shape
    part = outs[0].shape[0]
    even = lax.rem(lax.axis_index("polar"), 2) == 0

    def combine(low_ref, high_ref):
        for target in range(rows):
            acc = split_tiles(part_ref[target])
            for side, base in ((low_ref, -REACH), (high_ref, rows)):
                for h in range(REACH):
                    row = base + h
                    if abs(row - target) <= REACH:
                        at = row + REACH
                        acc = add_pair(
                            acc,
                            side[h].astype(jnp.float32),
                            weight_ref[...],
                            target_ref[at : at + 1, :],
                            filter_ref[at],
                            target,
                        )
            stacked_ref[target * size : (target + 1) * size, :] = jnp.concatenate(acc, axis=1).astype(
                jnp.bfloat16
            )

    pl.when(even)(lambda: combine(second_ref, first_ref))
    pl.when(jnp.logical_not(even))(lambda: combine(first_ref, second_ref))
    me = lax.axis_index("azimuth")
    for k in range(count):
        grid = dot_nt(table_ref[partner(me, k, count, 1)], stacked_ref[...])
        outs[k][...] = grid[:part].astype(jnp.bfloat16)


def finish(own, first, second, weight, target, filters, table, count, part, after):
    rows, size, width = own.shape
    return pl.pallas_call(
        functools.partial(finish_kernel, count),
        in_specs=[pl.BlockSpec(memory_space=VMEM)] * 7 + [pl.BlockSpec(memory_space=pl.ANY)] * len(after),
        out_specs=[pl.BlockSpec(memory_space=VMEM)] * count,
        out_shape=[jax.ShapeDtypeStruct((part, rows * size), jnp.bfloat16)] * count,
        scratch_shapes=[pltpu.VMEM((rows * size, width), jnp.bfloat16)],
        compiler_params=pltpu.CompilerParams(vmem_limit_bytes=12 * 2**20),
        cost_estimate=pl.CostEstimate(flops=2 * 10**9, bytes_accessed=4 * 2**20, transcendentals=0),
        name="finish",
    )(own, first, second, weight, target, filters, table, *after)


def add_kernel(count, chunks, grad_ref, *refs):
    pieces, out_ref = refs[:-1], refs[-1]
    rows, part, channels = grad_ref.shape
    me = lax.axis_index("azimuth")

    def add(mine):
        order = [[k for k in range(count) if partner_static(mine, k, count, -1) == s][0] for s in range(count)]
        for row in range(rows):
            conv = jnp.concatenate(
                [
                    pieces[q * count + k][:, row * size : (row + 1) * size]
                    for k in order
                    for q, (_, size) in enumerate(chunks)
                ],
                axis=1,
            )
            out_ref[row] = (grad_ref[row].astype(jnp.float32) + conv.astype(jnp.float32)).astype(
                jnp.bfloat16
            )

    for mine in range(count):
        pl.when(me == mine)(functools.partial(add, mine))


def add_back(grad_out, pieces, count, chunks):
    return pl.pallas_call(
        functools.partial(add_kernel, count, chunks),
        in_specs=[pl.BlockSpec(memory_space=VMEM)] * (1 + len(pieces)),
        out_specs=pl.BlockSpec(memory_space=VMEM),
        out_shape=jax.ShapeDtypeStruct(grad_out.shape, jnp.bfloat16),
        compiler_params=pltpu.CompilerParams(vmem_limit_bytes=12 * 2**20),
        cost_estimate=pl.CostEstimate(flops=10**6, bytes_accessed=4 * 2**20, transcendentals=0),
        name="add_back",
    )(grad_out, *pieces)


def prepare_kernel(count, chunks, weight_ref, filt_ref, offset_ref, forth_ref, back_ref, *outs):
    filter_out, target_out, forth_out, back_out = outs[:4]
    forth_out[...] = forth_ref[...]
    back_out[...] = back_ref[...]
    bases, channels = weight_ref.shape
    lats, width = filt_ref.shape[1:]
    ext, depth = target_out.shape
    rows = ext - 2 * REACH
    modes = width // 2
    whole = modes // LANES * LANES
    used = TERMS * bases
    weight = pltpu.roll(
        weight_ref[...], lax.rem(count - lax.axis_index("azimuth"), count) * (channels // count), 1
    )[:, : channels // count]
    parts = []
    for _ in range(TERMS):
        rounded = weight.astype(jnp.bfloat16).astype(jnp.float32)
        parts.append(rounded)
        weight = weight - rounded
    parts.append(jnp.zeros((depth - used, weight.shape[1]), jnp.float32))
    weight = jnp.concatenate(parts, axis=0).T
    for (start, size), out in zip(chunks, outs[4:]):
        out[...] = weight[start : start + size]
    start_lat = lax.axis_index("polar") * rows
    table = filt_ref[...].reshape(bases * lats, width)
    base = lax.broadcasted_iota(jnp.int32, (depth, bases * lats), 0)
    valid = base < used
    for _ in range(TERMS - 1):
        base = jnp.where(base >= bases, base - bases, base)
    column = lax.broadcasted_iota(jnp.int32, (depth, bases * lats), 1)
    for i in range(ext):
        lat = start_lat + (i - REACH)
        inside = (lat >= 0) & (lat < lats)
        lat = jnp.clip(lat, 0, lats - 1)
        pick = jnp.where(valid & (column == base * lats + lat), 1.0, 0.0).astype(jnp.bfloat16)
        row = dot_nn(pick, table)
        real, imag = row[:, :modes], row[:, modes:]
        rest_re, rest_im = real[:, whole:], imag[:, whole:]
        filter_out[i] = jnp.concatenate(
            [real[:, :whole], rest_re, rest_re, imag[:, :whole], rest_im, -rest_im], axis=1
        ).astype(jnp.bfloat16)
        local = jnp.where(inside, offset_ref[pl.ds(lat, 1), :] - start_lat, -1)
        spare = jnp.full((1, depth - used), -1, jnp.int32)
        target_out[i : i + 1, :] = jnp.concatenate([local] * TERMS + [spare], axis=1)


def prepare(basis_weight, filt, offsets, forth, back, rows, count, chunks):
    bases = filt.shape[0]
    width = filt.shape[2]
    ext = rows + 2 * REACH
    depth = round_up(TERMS * bases, 16)
    shapes = [
        jax.ShapeDtypeStruct((ext, depth, width + LANES), jnp.bfloat16),
        jax.ShapeDtypeStruct((ext, depth), jnp.int32),
        jax.ShapeDtypeStruct(forth.shape, forth.dtype),
        jax.ShapeDtypeStruct(back.shape, back.dtype),
    ] + [jax.ShapeDtypeStruct((size, depth), jnp.float32) for _, size in chunks]
    return pl.pallas_call(
        functools.partial(prepare_kernel, count, chunks),
        in_specs=[pl.BlockSpec(memory_space=VMEM)] * 5,
        out_specs=[pl.BlockSpec(memory_space=VMEM)] * len(shapes),
        out_shape=shapes,
        compiler_params=pltpu.CompilerParams(vmem_limit_bytes=16 * 2**20),
        cost_estimate=pl.CostEstimate(flops=10**9, bytes_accessed=6 * 2**20, transcendentals=0),
        name="prepare",
    )(basis_weight, filt, offsets, forth, back)


def halo(first, second):
    bands, count = lax.axis_size("polar"), lax.axis_size("azimuth")
    blocks = []
    for odd, block in ((0, first), (1, second)):
        pairs = []
        for a in range(bands):
            other = ((a + odd) ^ 1) - odd
            for b in range(count):
                paired = 0 <= other < bands
                target = (other, b) if paired else (a, b ^ 1 if b ^ 1 < count else b)
                pairs.append((a * count + b, target[0] * count + target[1]))
        blocks.append(lax.ppermute(block, ("polar", "azimuth"), pairs))
    return blocks


def on_device(chunks, conv_out, grad_out, w_in, b_in, w_out, basis_weight, filt, offsets):
    rows, part, channels = conv_out.shape
    count = lax.axis_size("azimuth")
    forth, back = tables(count, part, filt.shape[2] // 2)
    forth, back = jnp.asarray(forth), jnp.asarray(back)
    blocks = mlp(conv_out, grad_out, w_in, b_in, w_out, count, chunks)
    filters, target, forth, back, *weights = prepare(
        basis_weight, filt, offsets, forth, back, rows, count, chunks
    )
    pieces = [exchange(blocks[k], k, count) for k in range(count - 1)]
    returned = []
    for q, chunk in enumerate(chunks):
        last = exchange(blocks[count - 1 + q], count - 1, count)
        own, first, second = analyze(pieces + [last], forth, rows, chunk)
        first, second = halo(first, second)
        own = own_terms(own, weights[q], target, filters)
        after = [returned[-(count // 2)]] if q else []
        grids = finish(own, first, second, weights[q], target, filters, back, count, part, after)
        returned += [exchange(grids[k], k, count) for k in range(count)]
    return add_back(grad_out, returned, count, chunks)


def solution(mesh):
    grid = P(("member", "polar"), "azimuth", None)

    def run(conv_out, grad_out, *others):
        owned = conv_out.shape[2] // mesh.shape["azimuth"]
        chunks = ((0, owned),) if owned % 32 else ((0, owned * 3 // 5), (owned * 3 // 5, owned - owned * 3 // 5))
        return jax.shard_map(
            functools.partial(on_device, chunks),
            mesh=mesh,
            in_specs=(grid, grid) + (P(),) * 6,
            out_specs=grid,
            check_vma=False,
        )(conv_out, grad_out, *others)

    return run
```

```python
import functools
import math

import jax
import jax.numpy as jnp
import ml_dtypes
import numpy as np
from jax import lax
from jax.experimental import pallas as pl
from jax.experimental.pallas import tpu as pltpu
from jax.sharding import PartitionSpec as P

REACH = 3
LANES = 128
HALF = 64
TERMS = 3
VMEM = pltpu.MemorySpace.VMEM
NO_COST = pl.CostEstimate(flops=0, bytes_accessed=0, transcendentals=0)


def round_up(value, unit):
    return -(-value // unit) * unit


def partner(me, step, count, sign):
    if count & (count - 1) == 0:
        return me ^ step
    return lax.rem(me + sign * step + count, count)


def exchange(block, step, count):
    if step == 0:
        return block
    pairs = [(a, int(partner_static(a, step, count))) for a in range(count)]
    return lax.ppermute(block, "azimuth", pairs)


def partner_static(a, step, count, sign=1):
    return a ^ step if count & (count - 1) == 0 else (a + sign * step) % count


def tables(count, part, modes):
    length = count * part
    whole = modes // LANES * LANES
    order = np.concatenate(
        [
            np.arange(whole),
            modes + np.arange(whole),
            np.arange(whole, modes),
            modes + np.arange(whole, modes),
        ]
    )
    positions = np.arange(length)
    waves = np.arange(modes)
    phase = (positions[:, None] * waves[None, :]) % length
    angle = (2.0 * math.pi / length) * phase
    scale = 1.0 / math.sqrt(length)
    factor = np.where(waves == 0, 1.0, 2.0)
    analysis = np.concatenate([np.cos(angle), -np.sin(angle)], axis=1) * scale
    synth = np.concatenate([np.cos(angle) * factor, -np.sin(angle) * factor], axis=1) * scale
    analysis = analysis.astype(np.float32).astype(ml_dtypes.bfloat16)[:, order]
    synth = synth.astype(np.float32).astype(ml_dtypes.bfloat16)[:, order]
    wide = round_up(part, HALF)
    window = round_up(HALF + wide, LANES)
    forth = np.zeros((count, HALF + window, 2 * modes), ml_dtypes.bfloat16)
    back = np.zeros((count, wide, 2 * modes), ml_dtypes.bfloat16)
    for s in range(count):
        forth[s, HALF : HALF + part] = analysis[s * part : (s + 1) * part]
        back[s, :part] = synth[s * part : (s + 1) * part]
    return forth, back


def gelu_slope(values):
    size = jnp.abs(values)
    decay = jnp.exp(-0.5 * (values * values))
    t = pl.reciprocal(1.0 + (0.3275911 * math.sqrt(0.5)) * size)
    tail = 0.5 * 1.061405429
    for factor in (-1.453152027, 1.421413741, -0.284496736, 0.254829592):
        tail = tail * t + 0.5 * factor
    lower = decay * (tail * t - (1.0 / math.sqrt(2.0 * math.pi)) * size)
    return jnp.where(values < 0.0, lower, 1.0 - lower)


def dot_nt(left, right):
    return lax.dot_general(left, right, (((1,), (1,)), ((), ())), preferred_element_type=jnp.float32)


def dot_nn(left, right):
    return jnp.dot(left, right, preferred_element_type=jnp.float32)


def mlp_kernel(count, chunks, conv_ref, grad_ref, win_ref, bias_ref, wout_ref, *rest):
    outs, (slope_ref, total_ref) = rest[:-2], rest[-2:]
    step = pl.program_id(0)
    rows, part, channels = conv_ref.shape
    wide = slope_ref.shape[0] // rows
    owned = channels // count
    me = lax.axis_index("azimuth")

    @pl.when(step == 0)
    def _():
        total_ref[...] = jnp.zeros_like(total_ref)

    block = win_ref.shape[1]
    bias = bias_ref[pl.ds(pl.multiple_of(step * block, block), block)].reshape(1, block)
    spare = jnp.zeros((wide - part, block), jnp.bfloat16)
    for row in range(rows):
        pre = dot_nn(conv_ref[row], win_ref[...]) + bias
        back = dot_nt(grad_ref[row], wout_ref[...])
        slope = (back * gelu_slope(pre)).astype(jnp.bfloat16)
        slope_ref[row * wide : row * wide + part, :] = slope
        slope_ref[row * wide + part : (row + 1) * wide, :] = spare
    total_ref[...] += dot_nt(win_ref[...], slope_ref[...])

    @pl.when(step == pl.num_programs(0) - 1)
    def _():
        sent = [(k, 0, owned) for k in range(count - 1)] + [(count - 1,) + chunk for chunk in chunks]
        for out, (k, start, size) in zip(outs, sent):
            first = partner(me, k, count, 1) * owned + start
            out[...] = total_ref[pl.ds(pl.multiple_of(first, 32), size), :].astype(jnp.bfloat16)


def mlp(conv_out, grad_out, w_in, b_in, w_out, count, chunks):
    rows, part, channels = conv_out.shape
    hidden = w_in.shape[1]
    block = 256
    wide = round_up(part, HALF)
    whole = lambda shape: pl.BlockSpec(shape, lambda t: (0,) * len(shape))
    out_shape = [
        jax.ShapeDtypeStruct((size, rows * wide), jnp.bfloat16)
        for size in [channels // count] * (count - 1) + [size for _, size in chunks]
    ]
    return pl.pallas_call(
        functools.partial(mlp_kernel, count, chunks),
        grid=(hidden // block,),
        in_specs=[
            whole(conv_out.shape),
            whole(grad_out.shape),
            pl.BlockSpec((channels, block), lambda t: (0, t)),
            whole(b_in.shape),
            pl.BlockSpec((block, channels), lambda t: (t, 0)),
        ],
        out_specs=[whole(x.shape) for x in out_shape],
        out_shape=out_shape,
        scratch_shapes=[
            pltpu.VMEM((rows * wide, block), jnp.bfloat16),
            pltpu.VMEM((channels, rows * wide), jnp.float32),
        ],
        compiler_params=pltpu.CompilerParams(vmem_limit_bytes=16 * 2**20),
        cost_estimate=NO_COST,
        name="mlp",
    )(conv_out, grad_out, w_in, b_in, w_out)


def analysis_kernel(count, rows, chunk, *refs):
    pieces, table_ref = refs[:count], refs[count]
    own_ref, first_ref, second_ref = refs[-3:]
    wide = pieces[0].shape[1] // rows
    start, size = chunk
    base = [start] * (count - 1) + [0]
    window = table_ref.shape[1] - HALF
    me = lax.axis_index("azimuth")
    sources = [partner(me, k, count, -1) for k in range(count)]
    even = lax.rem(lax.axis_index("polar"), 2) == 0
    for row in range(rows):
        first = row * wide // LANES * LANES
        shift = row * wide - first
        total = None
        for k in range(count):
            term = dot_nn(
                pieces[k][base[k] : base[k] + size, first : first + window],
                table_ref[sources[k], HALF - shift : HALF - shift + window, :],
            )
            total = term if total is None else total + term
        own_ref[row] = total
        sent = total.astype(jnp.bfloat16)
        for above, parity in ((first_ref, even), (second_ref, jnp.logical_not(even))):
            below = second_ref if above is first_ref else first_ref

            @pl.when(parity)
            def _(above=above, below=below, sent=sent, row=row):
                if row >= rows - REACH:
                    above[row - (rows - REACH)] = sent
                if row < REACH:
                    below[row] = sent


def analyze(pieces, table, rows, chunk, after):
    count = len(pieces)
    size = chunk[1]
    width = table.shape[2]
    halo = jax.ShapeDtypeStruct((REACH, size, width), jnp.bfloat16)
    return pl.pallas_call(
        functools.partial(analysis_kernel, count, rows, chunk),
        in_specs=[pl.BlockSpec(memory_space=VMEM)] * (count + 1)
        + [pl.BlockSpec(memory_space=pl.ANY)] * len(after),
        out_specs=[pl.BlockSpec(memory_space=VMEM)] * 3,
        out_shape=[jax.ShapeDtypeStruct((rows, size, width), jnp.float32), halo, halo],
        compiler_params=pltpu.CompilerParams(vmem_limit_bytes=12 * 2**20),
        cost_estimate=NO_COST,
        name="analysis",
    )(*pieces, table, *after)


def add_pair(acc, spectrum, weight, target_row, filter_row, target):
    masked = jnp.where(target_row == target, weight, 0.0).astype(jnp.bfloat16)
    gain = dot_nn(masked, filter_row)
    whole = (gain.shape[1] // 2) // LANES * LANES - LANES
    spec_re = spectrum[:, :whole]
    spec_im = spectrum[:, whole : 2 * whole]
    spec_x = spectrum[:, 2 * whole :]
    swapped = pltpu.roll(spec_x, HALF, 1)
    gain_re = gain[:, :whole]
    gain_rx = gain[:, whole : whole + LANES]
    gain_im = gain[:, whole + LANES : 2 * whole + LANES]
    gain_ix = gain[:, 2 * whole + LANES :]
    acc_re, acc_im, acc_x = acc
    acc_re = acc_re + (gain_re * spec_re + gain_im * spec_im)
    acc_im = acc_im + (gain_re * spec_im - gain_im * spec_re)
    acc_x = acc_x + (gain_rx * spec_x + gain_ix * swapped)
    return acc_re, acc_im, acc_x


def split_tiles(value):
    whole = (value.shape[1] - LANES) // 2
    return value[:, :whole], value[:, whole : 2 * whole], value[:, 2 * whole :]


def own_kernel(own_ref, weight_ref, target_ref, filter_ref, out_ref):
    rows, size, width = own_ref.shape
    for target in range(rows):
        acc = split_tiles(jnp.zeros((size, width), jnp.float32))
        for row in range(rows):
            if abs(row - target) <= REACH:
                at = row + REACH
                acc = add_pair(
                    acc, own_ref[row], weight_ref[...], target_ref[at : at + 1, :], filter_ref[at], target
                )
        out_ref[target] = jnp.concatenate(acc, axis=1)


def own_terms(own, weight, target, filters):
    return pl.pallas_call(
        own_kernel,
        in_specs=[pl.BlockSpec(memory_space=VMEM)] * 4,
        out_specs=pl.BlockSpec(memory_space=VMEM),
        out_shape=jax.ShapeDtypeStruct(own.shape, jnp.float32),
        compiler_params=pltpu.CompilerParams(vmem_limit_bytes=12 * 2**20),
        cost_estimate=NO_COST,
        name="own_terms",
    )(own, weight, target, filters)


def finish_kernel(count, part_ref, first_ref, second_ref, weight_ref, target_ref, filter_ref, table_ref, *rest):
    outs, stacked_ref = rest[-count - 1 : -1], rest[-1]
    rows, size, width = part_ref.shape
    part = outs[0].shape[0]
    even = lax.rem(lax.axis_index("polar"), 2) == 0

    def combine(low_ref, high_ref):
        for target in range(rows):
            acc = split_tiles(part_ref[target])
            for side, base in ((low_ref, -REACH), (high_ref, rows)):
                for h in range(REACH):
                    row = base + h
                    if abs(row - target) <= REACH:
                        at = row + REACH
                        acc = add_pair(
                            acc,
                            side[h].astype(jnp.float32),
                            weight_ref[...],
                            target_ref[at : at + 1, :],
                            filter_ref[at],
                            target,
                        )
            stacked_ref[target * size : (target + 1) * size, :] = jnp.concatenate(acc, axis=1).astype(
                jnp.bfloat16
            )

    pl.when(even)(lambda: combine(second_ref, first_ref))
    pl.when(jnp.logical_not(even))(lambda: combine(first_ref, second_ref))
    me = lax.axis_index("azimuth")
    for k in range(count):
        grid = dot_nt(table_ref[partner(me, k, count, 1)], stacked_ref[...])
        outs[k][...] = grid[:part].astype(jnp.bfloat16)


def finish(own, first, second, weight, target, filters, table, count, part, after):
    rows, size, width = own.shape
    return pl.pallas_call(
        functools.partial(finish_kernel, count),
        in_specs=[pl.BlockSpec(memory_space=VMEM)] * 7 + [pl.BlockSpec(memory_space=pl.ANY)] * len(after),
        out_specs=[pl.BlockSpec(memory_space=VMEM)] * count,
        out_shape=[jax.ShapeDtypeStruct((part, rows * size), jnp.bfloat16)] * count,
        scratch_shapes=[pltpu.VMEM((rows * size, width), jnp.bfloat16)],
        compiler_params=pltpu.CompilerParams(vmem_limit_bytes=12 * 2**20),
        cost_estimate=NO_COST,
        name="finish",
    )(own, first, second, weight, target, filters, table, *after)


def add_kernel(count, chunks, grad_ref, *refs):
    pieces, out_ref = refs[:-1], refs[-1]
    rows, part, channels = grad_ref.shape
    me = lax.axis_index("azimuth")

    def add(mine):
        order = [[k for k in range(count) if partner_static(mine, k, count, -1) == s][0] for s in range(count)]
        for row in range(rows):
            conv = jnp.concatenate(
                [
                    pieces[q * count + k][:, row * size : (row + 1) * size]
                    for k in order
                    for q, (_, size) in enumerate(chunks)
                ],
                axis=1,
            )
            out_ref[row] = (grad_ref[row].astype(jnp.float32) + conv.astype(jnp.float32)).astype(
                jnp.bfloat16
            )

    for mine in range(count):
        pl.when(me == mine)(functools.partial(add, mine))


def add_back(grad_out, pieces, count, chunks):
    return pl.pallas_call(
        functools.partial(add_kernel, count, chunks),
        in_specs=[pl.BlockSpec(memory_space=VMEM)] * (1 + len(pieces)),
        out_specs=pl.BlockSpec(memory_space=VMEM),
        out_shape=jax.ShapeDtypeStruct(grad_out.shape, jnp.bfloat16),
        compiler_params=pltpu.CompilerParams(vmem_limit_bytes=12 * 2**20),
        cost_estimate=NO_COST,
        name="add_back",
    )(grad_out, *pieces)


def prepare_kernel(count, chunks, weight_ref, filt_ref, offset_ref, forth_ref, back_ref, *outs):
    filter_out, target_out, forth_out, back_out = outs[:4]
    forth_out[...] = forth_ref[...]
    back_out[...] = back_ref[...]
    bases, channels = weight_ref.shape
    lats, width = filt_ref.shape[1:]
    ext, depth = target_out.shape
    rows = ext - 2 * REACH
    modes = width // 2
    whole = modes // LANES * LANES
    used = TERMS * bases
    weight = pltpu.roll(
        weight_ref[...], lax.rem(count - lax.axis_index("azimuth"), count) * (channels // count), 1
    )[:, : channels // count]
    parts = []
    for _ in range(TERMS):
        rounded = weight.astype(jnp.bfloat16).astype(jnp.float32)
        parts.append(rounded)
        weight = weight - rounded
    parts.append(jnp.zeros((depth - used, weight.shape[1]), jnp.float32))
    weight = jnp.concatenate(parts, axis=0).T
    for (start, size), out in zip(chunks, outs[4:]):
        out[...] = weight[start : start + size]
    start_lat = lax.axis_index("polar") * rows
    table = filt_ref[...].reshape(bases * lats, width)
    base = lax.broadcasted_iota(jnp.int32, (depth, bases * lats), 0)
    valid = base < used
    for _ in range(TERMS - 1):
        base = jnp.where(base >= bases, base - bases, base)
    column = lax.broadcasted_iota(jnp.int32, (depth, bases * lats), 1)
    for i in range(ext):
        lat = start_lat + (i - REACH)
        inside = (lat >= 0) & (lat < lats)
        lat = jnp.clip(lat, 0, lats - 1)
        pick = jnp.where(valid & (column == base * lats + lat), 1.0, 0.0).astype(jnp.bfloat16)
        row = dot_nn(pick, table)
        real, imag = row[:, :modes], row[:, modes:]
        rest_re, rest_im = real[:, whole:], imag[:, whole:]
        filter_out[i] = jnp.concatenate(
            [real[:, :whole], rest_re, rest_re, imag[:, :whole], rest_im, -rest_im], axis=1
        ).astype(jnp.bfloat16)
        local = jnp.where(inside, offset_ref[pl.ds(lat, 1), :] - start_lat, -1)
        spare = jnp.full((1, depth - used), -1, jnp.int32)
        target_out[i : i + 1, :] = jnp.concatenate([local] * TERMS + [spare], axis=1)


def prepare(basis_weight, filt, offsets, forth, back, rows, count, chunks):
    bases = filt.shape[0]
    width = filt.shape[2]
    ext = rows + 2 * REACH
    depth = round_up(TERMS * bases, 16)
    shapes = [
        jax.ShapeDtypeStruct((ext, depth, width + LANES), jnp.bfloat16),
        jax.ShapeDtypeStruct((ext, depth), jnp.int32),
        jax.ShapeDtypeStruct(forth.shape, forth.dtype),
        jax.ShapeDtypeStruct(back.shape, back.dtype),
    ] + [jax.ShapeDtypeStruct((size, depth), jnp.float32) for _, size in chunks]
    return pl.pallas_call(
        functools.partial(prepare_kernel, count, chunks),
        in_specs=[pl.BlockSpec(memory_space=VMEM)] * 5,
        out_specs=[pl.BlockSpec(memory_space=VMEM)] * len(shapes),
        out_shape=shapes,
        compiler_params=pltpu.CompilerParams(vmem_limit_bytes=16 * 2**20),
        cost_estimate=NO_COST,
        name="prepare",
    )(basis_weight, filt, offsets, forth, back)


def halo(first, second):
    bands, count = lax.axis_size("polar"), lax.axis_size("azimuth")
    blocks = []
    for odd, block in ((0, first), (1, second)):
        pairs = []
        for a in range(bands):
            other = ((a + odd) ^ 1) - odd
            for b in range(count):
                paired = 0 <= other < bands
                target = (other, b) if paired else (a, b ^ 1 if b ^ 1 < count else b)
                pairs.append((a * count + b, target[0] * count + target[1]))
        blocks.append(lax.ppermute(block, ("polar", "azimuth"), pairs))
    return blocks


def on_device(chunks, conv_out, grad_out, w_in, b_in, w_out, basis_weight, filt, offsets):
    rows, part, channels = conv_out.shape
    count = lax.axis_size("azimuth")
    forth, back = tables(count, part, filt.shape[2] // 2)
    forth, back = jnp.asarray(forth), jnp.asarray(back)
    blocks = mlp(conv_out, grad_out, w_in, b_in, w_out, count, chunks)
    filters, target, forth, back, *weights = prepare(
        basis_weight, filt, offsets, forth, back, rows, count, chunks
    )
    pieces = [exchange(blocks[k], k, count) for k in range(count - 1)]
    spectra, terms, grids, returned = {}, {}, {}, []

    def open_chunk(q, after):
        last = exchange(blocks[count - 1 + q], count - 1, count)
        own, first, second = analyze(pieces + [last], forth, rows, chunks[q], after)
        spectra[q] = halo(first, second)
        terms[q] = own_terms(own, weights[q], target, filters)

    def close_chunk(q):
        after = [returned[(q - 1) * count + 1]] if q else []
        grids[q] = finish(terms[q], *spectra[q], weights[q], target, filters, back, count, part, after)
        returned.extend(exchange(grids[q][k], k, count) for k in range(count))

    last = len(chunks) - 1
    open_chunk(0, [])
    if last > 0:
        open_chunk(1, [terms[0]])
    for q in range(last + 1):
        close_chunk(q)
        if q + 2 <= last:
            open_chunk(q + 2, [grids[q][0]])
    return add_back(grad_out, returned, count, chunks)


def solution(mesh):
    grid = P(("member", "polar"), "azimuth", None)

    def run(conv_out, grad_out, *others):
        owned = conv_out.shape[2] // mesh.shape["azimuth"]
        sizes = [owned]
        if owned % 32 == 0 and owned >= 96:
            big = owned * 3 // 5 // 32 * 32
            sizes = [big, owned - big]
        chunks = tuple((sum(sizes[:q]), size) for q, size in enumerate(sizes))
        return jax.shard_map(
            functools.partial(on_device, chunks),
            mesh=mesh,
            in_specs=(grid, grid) + (P(),) * 6,
            out_specs=grid,
            check_vma=False,
        )(conv_out, grad_out, *others)

    return run
```

```python
import functools
import math

import jax
import jax.numpy as jnp
import ml_dtypes
import numpy as np
from jax import lax
from jax.experimental import pallas as pl
from jax.experimental.pallas import tpu as pltpu
from jax.sharding import PartitionSpec as P

REACH = 3
LANES = 128
HALF = 64
TERMS = 3
VMEM = pltpu.MemorySpace.VMEM
NO_COST = pl.CostEstimate(flops=0, bytes_accessed=0, transcendentals=0)


def round_up(value, unit):
    return -(-value // unit) * unit


def partner(me, step, count, sign):
    if count & (count - 1) == 0:
        return me ^ step
    return lax.rem(me + sign * step + count, count)


def exchange(block, step, count):
    if step == 0:
        return block
    pairs = [(a, int(partner_static(a, step, count))) for a in range(count)]
    return lax.ppermute(block, "azimuth", pairs)


def partner_static(a, step, count, sign=1):
    return a ^ step if count & (count - 1) == 0 else (a + sign * step) % count


def tables(count, part, modes):
    length = count * part
    whole = modes // LANES * LANES
    order = np.concatenate(
        [
            np.arange(whole),
            modes + np.arange(whole),
            np.arange(whole, modes),
            modes + np.arange(whole, modes),
        ]
    )
    positions = np.arange(length)
    waves = np.arange(modes)
    phase = (positions[:, None] * waves[None, :]) % length
    angle = (2.0 * math.pi / length) * phase
    scale = 1.0 / math.sqrt(length)
    factor = np.where(waves == 0, 1.0, 2.0)
    analysis = np.concatenate([np.cos(angle), -np.sin(angle)], axis=1) * scale
    synth = np.concatenate([np.cos(angle) * factor, -np.sin(angle) * factor], axis=1) * scale
    analysis = analysis.astype(np.float32).astype(ml_dtypes.bfloat16)[:, order]
    synth = synth.astype(np.float32).astype(ml_dtypes.bfloat16)[:, order]
    wide = round_up(part, HALF)
    window = round_up(HALF + wide, LANES)
    forth = np.zeros((count, HALF + window, 2 * modes), ml_dtypes.bfloat16)
    back = np.zeros((count * wide, 2 * modes), ml_dtypes.bfloat16)
    for s in range(count):
        forth[s, HALF : HALF + part] = analysis[s * part : (s + 1) * part]
        back[s * wide : s * wide + part] = synth[s * part : (s + 1) * part]
    return forth, back


def gelu_slope(values):
    size = jnp.abs(values)
    decay = jnp.exp(-0.5 * (values * values))
    t = pl.reciprocal(1.0 + (0.3275911 * math.sqrt(0.5)) * size)
    tail = 0.5 * 1.061405429
    for factor in (-1.453152027, 1.421413741, -0.284496736, 0.254829592):
        tail = tail * t + 0.5 * factor
    lower = decay * (tail * t - (1.0 / math.sqrt(2.0 * math.pi)) * size)
    return jnp.where(values < 0.0, lower, 1.0 - lower)


def dot_nt(left, right):
    return lax.dot_general(left, right, (((1,), (1,)), ((), ())), preferred_element_type=jnp.float32)


def dot_nn(left, right):
    return jnp.dot(left, right, preferred_element_type=jnp.float32)


def mlp_kernel(count, sent, conv_ref, grad_ref, win_ref, bias_ref, wout_ref, *rest):
    outs, (tall_conv, tall_grad, slope_ref, total_ref) = rest[-4 - len(sent) : -4], rest[-4:]
    step = pl.program_id(0)
    rows, part, channels = conv_ref.shape
    wide = slope_ref.shape[0] // rows
    owned = channels // count
    me = lax.axis_index("azimuth")

    @pl.when(step == 0)
    def _():
        total_ref[...] = jnp.zeros_like(total_ref)
        tall_conv[...] = jnp.zeros_like(tall_conv)
        tall_grad[...] = jnp.zeros_like(tall_grad)
        for row in range(rows):
            tall_conv[row * wide : row * wide + part, :] = conv_ref[row]
            tall_grad[row * wide : row * wide + part, :] = grad_ref[row]

    block = win_ref.shape[1]
    bias = bias_ref[pl.ds(pl.multiple_of(step * block, block), block)].reshape(1, block)
    pre = dot_nn(tall_conv[...], win_ref[...])
    back = dot_nt(tall_grad[...], wout_ref[...])
    group = 48
    for first in range(0, rows * wide, group):
        at = slice(first, first + group)
        slope_ref[at, :] = (back[at] * gelu_slope(pre[at] + bias)).astype(jnp.bfloat16)
    total_ref[...] += dot_nt(win_ref[...], slope_ref[...])

    @pl.when(step == pl.num_programs(0) - 1)
    def _():
        for out, (k, start, size) in zip(outs, sent):
            first = partner(me, k, count, 1) * owned + start
            out[...] = total_ref[pl.ds(pl.multiple_of(first, 32), size), :].astype(jnp.bfloat16)


def mlp(conv_out, grad_out, w_in, b_in, w_out, count, half, halves, sent, after):
    rows, part, channels = conv_out.shape
    rows //= halves
    hidden = w_in.shape[1]
    block = 256
    wide = round_up(part, HALF)
    whole = lambda shape: pl.BlockSpec(shape, lambda t: (0,) * len(shape))
    mine = pl.BlockSpec((rows, part, channels), lambda t: (half, 0, 0))
    out_shape = [jax.ShapeDtypeStruct((size, rows * wide), jnp.bfloat16) for _, _, size in sent]
    return pl.pallas_call(
        functools.partial(mlp_kernel, count, sent),
        grid=(hidden // block,),
        in_specs=[
            mine,
            mine,
            pl.BlockSpec((channels, block), lambda t: (0, t)),
            whole(b_in.shape),
            pl.BlockSpec((block, channels), lambda t: (t, 0)),
        ]
        + [pl.BlockSpec(memory_space=pl.ANY)] * len(after),
        out_specs=[whole(x.shape) for x in out_shape],
        out_shape=out_shape,
        scratch_shapes=[
            pltpu.VMEM((rows * wide, channels), jnp.bfloat16),
            pltpu.VMEM((rows * wide, channels), jnp.bfloat16),
            pltpu.VMEM((rows * wide, block), jnp.bfloat16),
            pltpu.VMEM((channels, rows * wide), jnp.float32),
        ],
        compiler_params=pltpu.CompilerParams(vmem_limit_bytes=16 * 2**20),
        cost_estimate=NO_COST,
        name="mlp",
    )(conv_out, grad_out, w_in, b_in, w_out, *after)


def analysis_kernel(count, rows, chunk, *refs):
    own_ref, first_ref, second_ref = refs[-3:]
    start, size = chunk
    halves = next(h for h in range(1, rows + 1) if refs[h * count].ndim == 3)
    table_ref = refs[halves * count]
    rows_each = rows // halves
    wide = refs[0].shape[1] // rows_each
    window = table_ref.shape[1] - HALF
    me = lax.axis_index("azimuth")
    sources = [partner(me, k, count, -1) for k in range(count)]
    even = lax.rem(lax.axis_index("polar"), 2) == 0

    def columns(row, k):
        half, row = divmod(row, rows_each)
        piece = refs[half * count + k]
        base = 0 if half == halves - 1 and k == count - 1 else start
        first = row * wide // LANES * LANES
        return piece[base : base + size, first : first + window]

    shifts = [row % rows_each * wide % LANES for row in range(rows)]
    for shift in sorted(set(shifts)):
        group = [row for row in range(rows) if shifts[row] == shift]
        total = None
        for k in range(count):
            left = jnp.concatenate([columns(row, k) for row in group], axis=0)
            term = dot_nn(left, table_ref[sources[k], HALF - shift : HALF - shift + window, :])
            total = term if total is None else total + term
        for at, row in enumerate(group):
            mine = total[at * size : (at + 1) * size]
            own_ref[row] = mine
            sent = mine.astype(jnp.bfloat16)
            for above, parity in ((first_ref, even), (second_ref, jnp.logical_not(even))):
                below = second_ref if above is first_ref else first_ref

                @pl.when(parity)
                def _(above=above, below=below, sent=sent, row=row):
                    if row >= rows - REACH:
                        above[row - (rows - REACH)] = sent
                    if row < REACH:
                        below[row] = sent


def analyze(pieces, table, rows, chunk, count, after):
    size = chunk[1]
    width = table.shape[2]
    halo = jax.ShapeDtypeStruct((REACH, size, width), jnp.bfloat16)
    return pl.pallas_call(
        functools.partial(analysis_kernel, count, rows, chunk),
        in_specs=[pl.BlockSpec(memory_space=VMEM)] * (len(pieces) + 1)
        + [pl.BlockSpec(memory_space=pl.ANY)] * len(after),
        out_specs=[pl.BlockSpec(memory_space=VMEM)] * 3,
        out_shape=[jax.ShapeDtypeStruct((rows, size, width), jnp.float32), halo, halo],
        compiler_params=pltpu.CompilerParams(vmem_limit_bytes=12 * 2**20),
        cost_estimate=NO_COST,
        name="analysis",
    )(*pieces, table, *after)


def add_pair(acc, spectrum, weight, target_row, filter_row, target):
    masked = jnp.where(target_row == target, weight, 0.0).astype(jnp.bfloat16)
    gain = dot_nn(masked, filter_row)
    whole = (gain.shape[1] // 2) // LANES * LANES - LANES
    spec_re = spectrum[:, :whole]
    spec_im = spectrum[:, whole : 2 * whole]
    spec_x = spectrum[:, 2 * whole :]
    swapped = pltpu.roll(spec_x, HALF, 1)
    gain_re = gain[:, :whole]
    gain_rx = gain[:, whole : whole + LANES]
    gain_im = gain[:, whole + LANES : 2 * whole + LANES]
    gain_ix = gain[:, 2 * whole + LANES :]
    acc_re, acc_im, acc_x = acc
    acc_re = acc_re + (gain_re * spec_re + gain_im * spec_im)
    acc_im = acc_im + (gain_re * spec_im - gain_im * spec_re)
    acc_x = acc_x + (gain_rx * spec_x + gain_ix * swapped)
    return acc_re, acc_im, acc_x


def split_tiles(value):
    whole = (value.shape[1] - LANES) // 2
    return value[:, :whole], value[:, whole : 2 * whole], value[:, 2 * whole :]


def own_kernel(own_ref, weight_ref, target_ref, filter_ref, out_ref):
    rows, size, width = own_ref.shape
    for target in range(rows):
        acc = split_tiles(jnp.zeros((size, width), jnp.float32))
        for row in range(rows):
            if abs(row - target) <= REACH:
                at = row + REACH
                acc = add_pair(
                    acc, own_ref[row], weight_ref[...], target_ref[at : at + 1, :], filter_ref[at], target
                )
        out_ref[target] = jnp.concatenate(acc, axis=1)


def own_terms(own, weight, target, filters):
    return pl.pallas_call(
        own_kernel,
        in_specs=[pl.BlockSpec(memory_space=VMEM)] * 4,
        out_specs=pl.BlockSpec(memory_space=VMEM),
        out_shape=jax.ShapeDtypeStruct(own.shape, jnp.float32),
        compiler_params=pltpu.CompilerParams(vmem_limit_bytes=12 * 2**20),
        cost_estimate=NO_COST,
        name="own_terms",
    )(own, weight, target, filters)


def finish_kernel(count, part_ref, first_ref, second_ref, weight_ref, target_ref, filter_ref, table_ref, *rest):
    outs, stacked_ref, grid_ref = rest[-count - 2 : -2], rest[-2], rest[-1]
    rows, size, width = part_ref.shape
    part = outs[0].shape[0]
    even = lax.rem(lax.axis_index("polar"), 2) == 0

    def combine(low_ref, high_ref):
        for target in range(rows):
            acc = split_tiles(part_ref[target])
            for side, base in ((low_ref, -REACH), (high_ref, rows)):
                for h in range(REACH):
                    row = base + h
                    if abs(row - target) <= REACH:
                        at = row + REACH
                        acc = add_pair(
                            acc,
                            side[h].astype(jnp.float32),
                            weight_ref[...],
                            target_ref[at : at + 1, :],
                            filter_ref[at],
                            target,
                        )
            stacked_ref[target * size : (target + 1) * size, :] = jnp.concatenate(acc, axis=1).astype(
                jnp.bfloat16
            )

    pl.when(even)(lambda: combine(second_ref, first_ref))
    pl.when(jnp.logical_not(even))(lambda: combine(first_ref, second_ref))
    me = lax.axis_index("azimuth")
    grid_ref[...] = dot_nt(table_ref[...], stacked_ref[...])
    wide = grid_ref.shape[0] // count
    for k in range(count):
        first = pl.multiple_of(partner(me, k, count, 1) * wide, HALF)
        outs[k][...] = grid_ref[pl.ds(first, wide), :][:part].astype(jnp.bfloat16)


def finish(own, first, second, weight, target, filters, table, count, part, after):
    rows, size, width = own.shape
    return pl.pallas_call(
        functools.partial(finish_kernel, count),
        in_specs=[pl.BlockSpec(memory_space=VMEM)] * 7 + [pl.BlockSpec(memory_space=pl.ANY)] * len(after),
        out_specs=[pl.BlockSpec(memory_space=VMEM)] * count,
        out_shape=[jax.ShapeDtypeStruct((part, rows * size), jnp.bfloat16)] * count,
        scratch_shapes=[
            pltpu.VMEM((rows * size, width), jnp.bfloat16),
            pltpu.VMEM((table.shape[0], rows * size), jnp.float32),
        ],
        compiler_params=pltpu.CompilerParams(vmem_limit_bytes=12 * 2**20),
        cost_estimate=NO_COST,
        name="finish",
    )(own, first, second, weight, target, filters, table, *after)


def add_kernel(count, chunks, grad_ref, *refs):
    pieces, out_ref = refs[:-1], refs[-1]
    rows, part, channels = grad_ref.shape
    me = lax.axis_index("azimuth")

    def add(mine):
        order = [[k for k in range(count) if partner_static(mine, k, count, -1) == s][0] for s in range(count)]
        for row in range(rows):
            conv = jnp.concatenate(
                [
                    pieces[q * count + k][:, row * size : (row + 1) * size]
                    for k in order
                    for q, (_, size) in enumerate(chunks)
                ],
                axis=1,
            )
            out_ref[row] = (grad_ref[row].astype(jnp.float32) + conv.astype(jnp.float32)).astype(
                jnp.bfloat16
            )

    for mine in range(count):
        pl.when(me == mine)(functools.partial(add, mine))


def add_back(grad_out, pieces, count, chunks):
    return pl.pallas_call(
        functools.partial(add_kernel, count, chunks),
        in_specs=[pl.BlockSpec(memory_space=VMEM)] * (1 + len(pieces)),
        out_specs=pl.BlockSpec(memory_space=VMEM),
        out_shape=jax.ShapeDtypeStruct(grad_out.shape, jnp.bfloat16),
        compiler_params=pltpu.CompilerParams(vmem_limit_bytes=12 * 2**20),
        cost_estimate=NO_COST,
        name="add_back",
    )(grad_out, *pieces)


def prepare_kernel(count, chunks, weight_ref, filt_ref, offset_ref, forth_ref, back_ref, *outs):
    filter_out, target_out, forth_out, back_out = outs[:4]
    forth_out[...] = forth_ref[...]
    back_out[...] = back_ref[...]
    bases, channels = weight_ref.shape
    lats, width = filt_ref.shape[1:]
    ext, depth = target_out.shape
    rows = ext - 2 * REACH
    modes = width // 2
    whole = modes // LANES * LANES
    used = TERMS * bases
    weight = pltpu.roll(
        weight_ref[...], lax.rem(count - lax.axis_index("azimuth"), count) * (channels // count), 1
    )[:, : channels // count]
    parts = []
    for _ in range(TERMS):
        rounded = weight.astype(jnp.bfloat16).astype(jnp.float32)
        parts.append(rounded)
        weight = weight - rounded
    parts.append(jnp.zeros((depth - used, weight.shape[1]), jnp.float32))
    weight = jnp.concatenate(parts, axis=0).T
    for (start, size), out in zip(chunks, outs[4:]):
        out[...] = weight[start : start + size]
    start_lat = lax.axis_index("polar") * rows
    table = filt_ref[...].reshape(bases * lats, width)
    base = lax.broadcasted_iota(jnp.int32, (depth, bases * lats), 0)
    valid = base < used
    for _ in range(TERMS - 1):
        base = jnp.where(base >= bases, base - bases, base)
    column = lax.broadcasted_iota(jnp.int32, (depth, bases * lats), 1)
    for i in range(ext):
        lat = start_lat + (i - REACH)
        inside = (lat >= 0) & (lat < lats)
        lat = jnp.clip(lat, 0, lats - 1)
        pick = jnp.where(valid & (column == base * lats + lat), 1.0, 0.0).astype(jnp.bfloat16)
        row = dot_nn(pick, table)
        real, imag = row[:, :modes], row[:, modes:]
        rest_re, rest_im = real[:, whole:], imag[:, whole:]
        filter_out[i] = jnp.concatenate(
            [real[:, :whole], rest_re, rest_re, imag[:, :whole], rest_im, -rest_im], axis=1
        ).astype(jnp.bfloat16)
        local = jnp.where(inside, offset_ref[pl.ds(lat, 1), :] - start_lat, -1)
        spare = jnp.full((1, depth - used), -1, jnp.int32)
        target_out[i : i + 1, :] = jnp.concatenate([local] * TERMS + [spare], axis=1)


def prepare(basis_weight, filt, offsets, forth, back, rows, count, chunks):
    bases = filt.shape[0]
    width = filt.shape[2]
    ext = rows + 2 * REACH
    depth = round_up(TERMS * bases, 16)
    shapes = [
        jax.ShapeDtypeStruct((ext, depth, width + LANES), jnp.bfloat16),
        jax.ShapeDtypeStruct((ext, depth), jnp.int32),
        jax.ShapeDtypeStruct(forth.shape, forth.dtype),
        jax.ShapeDtypeStruct(back.shape, back.dtype),
    ] + [jax.ShapeDtypeStruct((size, depth), jnp.float32) for _, size in chunks]
    return pl.pallas_call(
        functools.partial(prepare_kernel, count, chunks),
        in_specs=[pl.BlockSpec(memory_space=VMEM)] * 5,
        out_specs=[pl.BlockSpec(memory_space=VMEM)] * len(shapes),
        out_shape=shapes,
        compiler_params=pltpu.CompilerParams(vmem_limit_bytes=16 * 2**20),
        cost_estimate=NO_COST,
        name="prepare",
    )(basis_weight, filt, offsets, forth, back)


def halo(first, second):
    bands, count = lax.axis_size("polar"), lax.axis_size("azimuth")
    blocks = []
    for odd, block in ((0, first), (1, second)):
        pairs = []
        for a in range(bands):
            other = ((a + odd) ^ 1) - odd
            for b in range(count):
                paired = 0 <= other < bands
                target = (other, b) if paired else (a, b ^ 1 if b ^ 1 < count else b)
                pairs.append((a * count + b, target[0] * count + target[1]))
        blocks.append(lax.ppermute(block, ("polar", "azimuth"), pairs))
    return blocks


def on_device(chunks, conv_out, grad_out, w_in, b_in, w_out, basis_weight, filt, offsets):
    rows, part, channels = conv_out.shape
    count = lax.axis_size("azimuth")
    forth, back = tables(count, part, filt.shape[2] // 2)
    forth, back = jnp.asarray(forth), jnp.asarray(back)
    owned = channels // count
    halves = 2 if rows % 2 == 0 else 1
    pieces = []
    for half in range(halves):
        sent = [(k, 0, owned) for k in range(count)]
        if half == halves - 1:
            sent[-1:] = [(count - 1,) + chunk for chunk in chunks]
        blocks = mlp(conv_out, grad_out, w_in, b_in, w_out, count, half, halves, sent, pieces[1:2])
        whole = count if half < halves - 1 else count - 1
        pieces += [exchange(blocks[k], k, count) for k in range(whole)]
    filters, target, forth, back, *weights = prepare(
        basis_weight, filt, offsets, forth, back, rows, count, chunks
    )
    spectra, terms, grids, returned = {}, {}, {}, []

    def open_chunk(q, after):
        last = exchange(blocks[count - 1 + q], count - 1, count)
        own, first, second = analyze(pieces + [last], forth, rows, chunks[q], count, after)
        spectra[q] = halo(first, second)
        terms[q] = own_terms(own, weights[q], target, filters)

    def close_chunk(q):
        after = [returned[(q - 1) * count + 1]] if q else []
        grids[q] = finish(terms[q], *spectra[q], weights[q], target, filters, back, count, part, after)
        returned.extend(exchange(grids[q][k], k, count) for k in range(count))

    last = len(chunks) - 1
    open_chunk(0, [])
    if last > 0:
        open_chunk(1, [terms[0]])
    for q in range(last + 1):
        close_chunk(q)
        if q + 2 <= last:
            open_chunk(q + 2, [grids[q][0]])
    return add_back(grad_out, returned, count, chunks)


def solution(mesh):
    grid = P(("member", "polar"), "azimuth", None)

    def run(conv_out, grad_out, *others):
        owned = conv_out.shape[2] // mesh.shape["azimuth"]
        sizes = [owned]
        if owned % 32 == 0 and owned >= 96:
            big = owned * 3 // 5 // 32 * 32
            sizes = [big, owned - big]
        chunks = tuple((sum(sizes[:q]), size) for q, size in enumerate(sizes))
        return jax.shard_map(
            functools.partial(on_device, chunks),
            mesh=mesh,
            in_specs=(grid, grid) + (P(),) * 6,
            out_specs=grid,
            check_vma=False,
        )(conv_out, grad_out, *others)

    return run
```

```python
import functools
import math

import jax
import jax.numpy as jnp
import ml_dtypes
import numpy as np
from jax import lax
from jax.experimental import pallas as pl
from jax.experimental.pallas import tpu as pltpu
from jax.sharding import PartitionSpec as P

REACH = 3
LANES = 128
HALF = 64
TERMS = 3
VMEM = pltpu.MemorySpace.VMEM
NO_COST = pl.CostEstimate(flops=0, bytes_accessed=0, transcendentals=0)


def round_up(value, unit):
    return -(-value // unit) * unit


def partner(me, step, count, sign):
    if count & (count - 1) == 0:
        return me ^ step
    return lax.rem(me + sign * step + count, count)


def exchange(block, step, count):
    if step == 0:
        return block
    pairs = [(a, int(partner_static(a, step, count))) for a in range(count)]
    return lax.ppermute(block, "azimuth", pairs)


def partner_static(a, step, count, sign=1):
    return a ^ step if count & (count - 1) == 0 else (a + sign * step) % count


def tables(count, part, modes):
    length = count * part
    whole = modes // LANES * LANES
    order = np.concatenate(
        [
            np.arange(whole),
            modes + np.arange(whole),
            np.arange(whole, modes),
            modes + np.arange(whole, modes),
        ]
    )
    positions = np.arange(length)
    waves = np.arange(modes)
    phase = (positions[:, None] * waves[None, :]) % length
    angle = (2.0 * math.pi / length) * phase
    scale = 1.0 / math.sqrt(length)
    factor = np.where(waves == 0, 1.0, 2.0)
    analysis = np.concatenate([np.cos(angle), -np.sin(angle)], axis=1) * scale
    synth = np.concatenate([np.cos(angle) * factor, -np.sin(angle) * factor], axis=1) * scale
    analysis = analysis.astype(np.float32).astype(ml_dtypes.bfloat16)[:, order]
    synth = synth.astype(np.float32).astype(ml_dtypes.bfloat16)[:, order]
    wide = round_up(part, HALF)
    window = round_up(HALF + wide, LANES)
    forth = np.zeros((count, HALF + window, 2 * modes), ml_dtypes.bfloat16)
    back = np.zeros((count * wide, 2 * modes), ml_dtypes.bfloat16)
    for s in range(count):
        forth[s, HALF : HALF + part] = analysis[s * part : (s + 1) * part]
        back[s * wide : s * wide + part] = synth[s * part : (s + 1) * part]
    return forth, back


def gelu_slope(values):
    size = jnp.abs(values)
    decay = jnp.exp(-0.5 * (values * values))
    t = pl.reciprocal(1.0 + (0.3275911 * math.sqrt(0.5)) * size)
    tail = 0.5 * 1.061405429
    for factor in (-1.453152027, 1.421413741, -0.284496736, 0.254829592):
        tail = tail * t + 0.5 * factor
    lower = decay * (tail * t - (1.0 / math.sqrt(2.0 * math.pi)) * size)
    return jnp.where(values < 0.0, lower, 1.0 - lower)


def dot_nt(left, right):
    return lax.dot_general(left, right, (((1,), (1,)), ((), ())), preferred_element_type=jnp.float32)


def dot_nn(left, right):
    return jnp.dot(left, right, preferred_element_type=jnp.float32)


def mlp_kernel(count, half, sent, conv_ref, grad_ref, win_ref, bias_ref, wout_ref, *rest):
    outs, (tall_conv, tall_grad, slope_ref, total_ref) = rest[-4 - len(sent) : -4], rest[-4:]
    part, channels = conv_ref.shape[1:]
    wide = round_up(part, HALF)
    rows = tall_conv.shape[0] // wide
    owned = channels // count
    block = slope_ref.shape[2]
    steps = win_ref.shape[1] // block
    me = lax.axis_index("azimuth")
    for tall, source in ((tall_conv, conv_ref), (tall_grad, grad_ref)):
        for row in range(rows):
            whole = part // 16 * 16
            tall[row * wide + whole : (row + 1) * wide, :] = jnp.zeros((wide - whole, channels), jnp.bfloat16)
            tall[row * wide : row * wide + part, :] = source[half * rows + row]
    for step in range(steps):
        at = slice(step * block, (step + 1) * block)
        bias = bias_ref[at].reshape(1, block)
        pre = dot_nn(tall_conv[...], win_ref[:, at])
        back = dot_nt(tall_grad[...], wout_ref[at, :])
        group = 48
        for first in range(0, rows * wide, group):
            some = slice(first, first + group)
            slope_ref[step % 2, some, :] = (back[some] * gelu_slope(pre[some] + bias)).astype(jnp.bfloat16)
        term = dot_nt(win_ref[:, at], slope_ref[step % 2])
        total_ref[...] = term if step == 0 else total_ref[...] + term
    for out, (k, start, size) in zip(outs, sent):
        first = partner(me, k, count, 1) * owned + start
        out[...] = total_ref[pl.ds(pl.multiple_of(first, 32), size), :].astype(jnp.bfloat16)


def mlp(conv_out, grad_out, w_in, b_in, w_out, count, half, halves, sent, after):
    rows, part, channels = conv_out.shape
    rows //= halves
    block = 256
    wide = round_up(part, HALF)
    vmem = pl.BlockSpec(memory_space=VMEM)
    out_shape = [jax.ShapeDtypeStruct((size, rows * wide), jnp.bfloat16) for _, _, size in sent]
    return pl.pallas_call(
        functools.partial(mlp_kernel, count, half, sent),
        in_specs=[vmem] * 5 + [pl.BlockSpec(memory_space=pl.ANY)] * len(after),
        out_specs=[vmem] * len(out_shape),
        out_shape=out_shape,
        scratch_shapes=[
            pltpu.VMEM((rows * wide, channels), jnp.bfloat16),
            pltpu.VMEM((rows * wide, channels), jnp.bfloat16),
            pltpu.VMEM((2, rows * wide, block), jnp.bfloat16),
            pltpu.VMEM((channels, rows * wide), jnp.float32),
        ],
        compiler_params=pltpu.CompilerParams(vmem_limit_bytes=16 * 2**20),
        cost_estimate=NO_COST,
        name="mlp",
    )(conv_out, grad_out, w_in, b_in, w_out, *after)


def analysis_kernel(count, rows, chunk, *refs):
    own_ref, first_ref, second_ref = refs[-3:]
    start, size = chunk
    halves = next(h for h in range(1, rows + 1) if refs[h * count].ndim == 3)
    table_ref = refs[halves * count]
    rows_each = rows // halves
    wide = refs[0].shape[1] // rows_each
    window = table_ref.shape[1] - HALF
    me = lax.axis_index("azimuth")
    sources = [partner(me, k, count, -1) for k in range(count)]
    even = lax.rem(lax.axis_index("polar"), 2) == 0

    def columns(row, k):
        half, row = divmod(row, rows_each)
        piece = refs[half * count + k]
        base = 0 if half == halves - 1 and k == count - 1 else start
        first = row * wide // LANES * LANES
        return piece[base : base + size, first : first + window]

    shifts = [row % rows_each * wide % LANES for row in range(rows)]
    for shift in sorted(set(shifts)):
        group = [row for row in range(rows) if shifts[row] == shift]
        total = None
        for k in range(count):
            left = jnp.concatenate([columns(row, k) for row in group], axis=0)
            term = dot_nn(left, table_ref[sources[k], HALF - shift : HALF - shift + window, :])
            total = term if total is None else total + term
        for at, row in enumerate(group):
            mine = total[at * size : (at + 1) * size]
            own_ref[row] = mine
            sent = mine.astype(jnp.bfloat16)
            for above, parity in ((first_ref, even), (second_ref, jnp.logical_not(even))):
                below = second_ref if above is first_ref else first_ref

                @pl.when(parity)
                def _(above=above, below=below, sent=sent, row=row):
                    if row >= rows - REACH:
                        above[row - (rows - REACH)] = sent
                    if row < REACH:
                        below[row] = sent


def analyze(pieces, table, rows, chunk, count, after):
    size = chunk[1]
    width = table.shape[2]
    halo = jax.ShapeDtypeStruct((REACH, size, width), jnp.bfloat16)
    return pl.pallas_call(
        functools.partial(analysis_kernel, count, rows, chunk),
        in_specs=[pl.BlockSpec(memory_space=VMEM)] * (len(pieces) + 1)
        + [pl.BlockSpec(memory_space=pl.ANY)] * len(after),
        out_specs=[pl.BlockSpec(memory_space=VMEM)] * 3,
        out_shape=[jax.ShapeDtypeStruct((rows, size, width), jnp.float32), halo, halo],
        compiler_params=pltpu.CompilerParams(vmem_limit_bytes=12 * 2**20),
        cost_estimate=NO_COST,
        name="analysis",
    )(*pieces, table, *after)


def add_row(accs, spectrum, weight, target_row, filter_row, targets):
    size = spectrum.shape[0]
    masked = jnp.concatenate([jnp.where(target_row == t, weight, 0.0) for t in targets], axis=0)
    gains = dot_nn(masked.astype(jnp.bfloat16), filter_row)
    whole = (gains.shape[1] // 2) // LANES * LANES - LANES
    spec_re = spectrum[:, :whole]
    spec_im = spectrum[:, whole : 2 * whole]
    spec_x = spectrum[:, 2 * whole :]
    swapped = pltpu.roll(spec_x, HALF, 1)
    for at, target in enumerate(targets):
        gain = gains[at * size : (at + 1) * size]
        gain_re = gain[:, :whole]
        gain_rx = gain[:, whole : whole + LANES]
        gain_im = gain[:, whole + LANES : 2 * whole + LANES]
        gain_ix = gain[:, 2 * whole + LANES :]
        acc_re, acc_im, acc_x = accs[target]
        acc_re = acc_re + (gain_re * spec_re + gain_im * spec_im)
        acc_im = acc_im + (gain_re * spec_im - gain_im * spec_re)
        acc_x = acc_x + (gain_rx * spec_x + gain_ix * swapped)
        accs[target] = acc_re, acc_im, acc_x


def split_tiles(value):
    whole = (value.shape[1] - LANES) // 2
    return value[:, :whole], value[:, whole : 2 * whole], value[:, 2 * whole :]


def own_kernel(own_ref, weight_ref, target_ref, filter_ref, out_ref):
    rows, size, width = own_ref.shape
    accs = {t: split_tiles(jnp.zeros((size, width), jnp.float32)) for t in range(rows)}
    for row in range(rows):
        at = row + REACH
        targets = [t for t in range(rows) if abs(row - t) <= REACH]
        add_row(accs, own_ref[row], weight_ref[...], target_ref[at : at + 1, :], filter_ref[at], targets)
    for t in range(rows):
        out_ref[t] = jnp.concatenate(accs[t], axis=1)


def own_terms(own, weight, target, filters):
    return pl.pallas_call(
        own_kernel,
        in_specs=[pl.BlockSpec(memory_space=VMEM)] * 4,
        out_specs=pl.BlockSpec(memory_space=VMEM),
        out_shape=jax.ShapeDtypeStruct(own.shape, jnp.float32),
        compiler_params=pltpu.CompilerParams(vmem_limit_bytes=12 * 2**20),
        cost_estimate=NO_COST,
        name="own_terms",
    )(own, weight, target, filters)


def finish_kernel(count, part_ref, first_ref, second_ref, weight_ref, target_ref, filter_ref, table_ref, *rest):
    outs, stacked_ref, grid_ref = rest[-count - 2 : -2], rest[-2], rest[-1]
    rows, size, width = part_ref.shape
    part = outs[0].shape[0]
    even = lax.rem(lax.axis_index("polar"), 2) == 0

    def combine(low_ref, high_ref):
        accs = {t: split_tiles(part_ref[t]) for t in range(rows)}
        for side, base in ((low_ref, -REACH), (high_ref, rows)):
            for h in range(REACH):
                at = base + h + REACH
                targets = [t for t in range(rows) if abs(base + h - t) <= REACH]
                add_row(
                    accs,
                    side[h].astype(jnp.float32),
                    weight_ref[...],
                    target_ref[at : at + 1, :],
                    filter_ref[at],
                    targets,
                )
        for t in range(rows):
            stacked_ref[t * size : (t + 1) * size, :] = jnp.concatenate(accs[t], axis=1).astype(jnp.bfloat16)

    pl.when(even)(lambda: combine(second_ref, first_ref))
    pl.when(jnp.logical_not(even))(lambda: combine(first_ref, second_ref))
    me = lax.axis_index("azimuth")
    grid_ref[...] = dot_nt(table_ref[...], stacked_ref[...])
    wide = grid_ref.shape[0] // count
    for k in range(count):
        first = pl.multiple_of(partner(me, k, count, 1) * wide, HALF)
        outs[k][...] = grid_ref[pl.ds(first, wide), :][:part].astype(jnp.bfloat16)


def finish(own, first, second, weight, target, filters, table, count, part, after):
    rows, size, width = own.shape
    return pl.pallas_call(
        functools.partial(finish_kernel, count),
        in_specs=[pl.BlockSpec(memory_space=VMEM)] * 7 + [pl.BlockSpec(memory_space=pl.ANY)] * len(after),
        out_specs=[pl.BlockSpec(memory_space=VMEM)] * count,
        out_shape=[jax.ShapeDtypeStruct((part, rows * size), jnp.bfloat16)] * count,
        scratch_shapes=[
            pltpu.VMEM((rows * size, width), jnp.bfloat16),
            pltpu.VMEM((table.shape[0], rows * size), jnp.float32),
        ],
        compiler_params=pltpu.CompilerParams(vmem_limit_bytes=12 * 2**20),
        cost_estimate=NO_COST,
        name="finish",
    )(own, first, second, weight, target, filters, table, *after)


def add_kernel(count, chunks, grad_ref, *refs):
    pieces, out_ref = refs[:-1], refs[-1]
    rows, part, channels = grad_ref.shape
    me = lax.axis_index("azimuth")

    def add(mine):
        order = [[k for k in range(count) if partner_static(mine, k, count, -1) == s][0] for s in range(count)]
        for row in range(rows):
            conv = jnp.concatenate(
                [
                    pieces[q * count + k][:, row * size : (row + 1) * size]
                    for k in order
                    for q, (_, size) in enumerate(chunks)
                ],
                axis=1,
            )
            out_ref[row] = (grad_ref[row].astype(jnp.float32) + conv.astype(jnp.float32)).astype(
                jnp.bfloat16
            )

    for mine in range(count):
        pl.when(me == mine)(functools.partial(add, mine))


def add_back(grad_out, pieces, count, chunks):
    return pl.pallas_call(
        functools.partial(add_kernel, count, chunks),
        in_specs=[pl.BlockSpec(memory_space=VMEM)] * (1 + len(pieces)),
        out_specs=pl.BlockSpec(memory_space=VMEM),
        out_shape=jax.ShapeDtypeStruct(grad_out.shape, jnp.bfloat16),
        compiler_params=pltpu.CompilerParams(vmem_limit_bytes=12 * 2**20),
        cost_estimate=NO_COST,
        name="add_back",
    )(grad_out, *pieces)


def prepare_kernel(count, chunks, weight_ref, filt_ref, offset_ref, forth_ref, back_ref, *outs):
    filter_out, target_out, forth_out, back_out = outs[:4]
    forth_out[...] = forth_ref[...]
    back_out[...] = back_ref[...]
    bases, channels = weight_ref.shape
    lats, width = filt_ref.shape[1:]
    ext, depth = target_out.shape
    rows = ext - 2 * REACH
    modes = width // 2
    whole = modes // LANES * LANES
    used = TERMS * bases
    weight = pltpu.roll(
        weight_ref[...], lax.rem(count - lax.axis_index("azimuth"), count) * (channels // count), 1
    )[:, : channels // count]
    parts = []
    for _ in range(TERMS):
        rounded = weight.astype(jnp.bfloat16).astype(jnp.float32)
        parts.append(rounded)
        weight = weight - rounded
    parts.append(jnp.zeros((depth - used, weight.shape[1]), jnp.float32))
    weight = jnp.concatenate(parts, axis=0).T
    for (start, size), out in zip(chunks, outs[4:]):
        out[...] = weight[start : start + size]
    start_lat = lax.axis_index("polar") * rows
    table = filt_ref[...].reshape(bases * lats, width)
    base = lax.broadcasted_iota(jnp.int32, (depth, bases * lats), 0)
    valid = base < used
    for _ in range(TERMS - 1):
        base = jnp.where(base >= bases, base - bases, base)
    column = lax.broadcasted_iota(jnp.int32, (depth, bases * lats), 1)
    for i in range(ext):
        lat = start_lat + (i - REACH)
        inside = (lat >= 0) & (lat < lats)
        lat = jnp.clip(lat, 0, lats - 1)
        pick = jnp.where(valid & (column == base * lats + lat), 1.0, 0.0).astype(jnp.bfloat16)
        row = dot_nn(pick, table)
        real, imag = row[:, :modes], row[:, modes:]
        rest_re, rest_im = real[:, whole:], imag[:, whole:]
        filter_out[i] = jnp.concatenate(
            [real[:, :whole], rest_re, rest_re, imag[:, :whole], rest_im, -rest_im], axis=1
        ).astype(jnp.bfloat16)
        local = jnp.where(inside, offset_ref[pl.ds(lat, 1), :] - start_lat, -1)
        spare = jnp.full((1, depth - used), -1, jnp.int32)
        target_out[i : i + 1, :] = jnp.concatenate([local] * TERMS + [spare], axis=1)


def prepare(basis_weight, filt, offsets, forth, back, rows, count, chunks):
    bases = filt.shape[0]
    width = filt.shape[2]
    ext = rows + 2 * REACH
    depth = round_up(TERMS * bases, 16)
    shapes = [
        jax.ShapeDtypeStruct((ext, depth, width + LANES), jnp.bfloat16),
        jax.ShapeDtypeStruct((ext, depth), jnp.int32),
        jax.ShapeDtypeStruct(forth.shape, forth.dtype),
        jax.ShapeDtypeStruct(back.shape, back.dtype),
    ] + [jax.ShapeDtypeStruct((size, depth), jnp.float32) for _, size in chunks]
    return pl.pallas_call(
        functools.partial(prepare_kernel, count, chunks),
        in_specs=[pl.BlockSpec(memory_space=VMEM)] * 5,
        out_specs=[pl.BlockSpec(memory_space=VMEM)] * len(shapes),
        out_shape=shapes,
        compiler_params=pltpu.CompilerParams(vmem_limit_bytes=16 * 2**20),
        cost_estimate=NO_COST,
        name="prepare",
    )(basis_weight, filt, offsets, forth, back)


def halo(first, second):
    bands, count = lax.axis_size("polar"), lax.axis_size("azimuth")
    blocks = []
    for odd, block in ((0, first), (1, second)):
        pairs = []
        for a in range(bands):
            other = ((a + odd) ^ 1) - odd
            for b in range(count):
                paired = 0 <= other < bands
                target = (other, b) if paired else (a, b ^ 1 if b ^ 1 < count else b)
                pairs.append((a * count + b, target[0] * count + target[1]))
        blocks.append(lax.ppermute(block, ("polar", "azimuth"), pairs))
    return blocks


def on_device(chunks, conv_out, grad_out, w_in, b_in, w_out, basis_weight, filt, offsets):
    rows, part, channels = conv_out.shape
    count = lax.axis_size("azimuth")
    forth, back = tables(count, part, filt.shape[2] // 2)
    forth, back = jnp.asarray(forth), jnp.asarray(back)
    owned = channels // count
    halves = 2 if rows % 2 == 0 else 1
    pieces = []
    for half in range(halves):
        sent = [(k, 0, owned) for k in range(count)]
        if half == halves - 1:
            sent[-1:] = [(count - 1,) + chunk for chunk in chunks]
        blocks = mlp(conv_out, grad_out, w_in, b_in, w_out, count, half, halves, sent, pieces[1:2])
        whole = count if half < halves - 1 else count - 1
        pieces += [exchange(blocks[k], k, count) for k in range(whole)]
    filters, target, forth, back, *weights = prepare(
        basis_weight, filt, offsets, forth, back, rows, count, chunks
    )
    spectra, terms, grids, returned = {}, {}, {}, []

    def open_chunk(q, after):
        last = exchange(blocks[count - 1 + q], count - 1, count)
        own, first, second = analyze(pieces + [last], forth, rows, chunks[q], count, after)
        spectra[q] = halo(first, second)
        terms[q] = own_terms(own, weights[q], target, filters)

    def close_chunk(q):
        after = [returned[(q - 1) * count + 1]] if q else []
        grids[q] = finish(terms[q], *spectra[q], weights[q], target, filters, back, count, part, after)
        returned.extend(exchange(grids[q][k], k, count) for k in range(count))

    last = len(chunks) - 1
    open_chunk(0, [])
    if last > 0:
        open_chunk(1, [terms[0]])
    for q in range(last + 1):
        close_chunk(q)
        if q + 2 <= last:
            open_chunk(q + 2, [grids[q][0]])
    return add_back(grad_out, returned, count, chunks)


def solution(mesh):
    grid = P(("member", "polar"), "azimuth", None)

    def run(conv_out, grad_out, *others):
        owned = conv_out.shape[2] // mesh.shape["azimuth"]
        sizes = [owned]
        if owned % 32 == 0 and owned >= 96:
            big = owned * 3 // 5 // 32 * 32
            sizes = [big, owned - big]
        chunks = tuple((sum(sizes[:q]), size) for q, size in enumerate(sizes))
        return jax.shard_map(
            functools.partial(on_device, chunks),
            mesh=mesh,
            in_specs=(grid, grid) + (P(),) * 6,
            out_specs=grid,
            check_vma=False,
        )(conv_out, grad_out, *others)

    return run
```

```python
import functools
import math

import jax
import jax.numpy as jnp
import ml_dtypes
import numpy as np
from jax import lax
from jax.experimental import pallas as pl
from jax.experimental.pallas import tpu as pltpu
from jax.sharding import PartitionSpec as P

REACH = 3
LANES = 128
HALF = 64
TERMS = 3
VMEM = pltpu.MemorySpace.VMEM
NO_COST = pl.CostEstimate(flops=0, bytes_accessed=0, transcendentals=0)


def round_up(value, unit):
    return -(-value // unit) * unit


def partner(me, step, count, sign):
    if count & (count - 1) == 0:
        return me ^ step
    return lax.rem(me + sign * step + count, count)


def exchange(block, step, count):
    if step == 0:
        return block
    pairs = [(a, int(partner_static(a, step, count))) for a in range(count)]
    return lax.ppermute(block, "azimuth", pairs)


def partner_static(a, step, count, sign=1):
    return a ^ step if count & (count - 1) == 0 else (a + sign * step) % count


def tables(count, part, modes):
    length = count * part
    whole = modes // LANES * LANES
    order = np.concatenate(
        [
            np.arange(whole),
            modes + np.arange(whole),
            np.arange(whole, modes),
            modes + np.arange(whole, modes),
        ]
    )
    positions = np.arange(length)
    waves = np.arange(modes)
    phase = (positions[:, None] * waves[None, :]) % length
    angle = (2.0 * math.pi / length) * phase
    scale = 1.0 / math.sqrt(length)
    factor = np.where(waves == 0, 1.0, 2.0)
    analysis = np.concatenate([np.cos(angle), -np.sin(angle)], axis=1) * scale
    synth = np.concatenate([np.cos(angle) * factor, -np.sin(angle) * factor], axis=1) * scale
    analysis = analysis.astype(np.float32).astype(ml_dtypes.bfloat16)[:, order]
    synth = synth.astype(np.float32).astype(ml_dtypes.bfloat16)[:, order]
    wide = round_up(part, HALF)
    window = round_up(HALF + wide, LANES)
    forth = np.zeros((count, HALF + window, 2 * modes), ml_dtypes.bfloat16)
    back = np.zeros((count * wide, 2 * modes), ml_dtypes.bfloat16)
    for s in range(count):
        forth[s, HALF : HALF + part] = analysis[s * part : (s + 1) * part]
        back[s * wide : s * wide + part] = synth[s * part : (s + 1) * part]
    return forth, back


def gelu_slope(values):
    size = jnp.abs(values)
    decay = jnp.exp(-0.5 * (values * values))
    t = pl.reciprocal(1.0 + (0.3275911 * math.sqrt(0.5)) * size)
    tail = 0.5 * 1.061405429
    for factor in (-1.453152027, 1.421413741, -0.284496736, 0.254829592):
        tail = tail * t + 0.5 * factor
    lower = decay * (tail * t - (1.0 / math.sqrt(2.0 * math.pi)) * size)
    return jnp.where(values < 0.0, lower, 1.0 - lower)


def dot_nt(left, right):
    return lax.dot_general(left, right, (((1,), (1,)), ((), ())), preferred_element_type=jnp.float32)


def dot_nn(left, right):
    return jnp.dot(left, right, preferred_element_type=jnp.float32)


def mlp_kernel(count, half, sent, conv_ref, grad_ref, win_ref, bias_ref, wout_ref, *rest):
    outs, (tall_conv, tall_grad, slope_ref, total_ref) = rest[-4 - len(sent) : -4], rest[-4:]
    part, channels = conv_ref.shape[1:]
    wide = round_up(part, HALF)
    rows = tall_conv.shape[0] // wide
    owned = channels // count
    block = slope_ref.shape[2]
    steps = win_ref.shape[1] // block
    me = lax.axis_index("azimuth")
    for tall, source in ((tall_conv, conv_ref), (tall_grad, grad_ref)):
        for row in range(rows):
            whole = part // 16 * 16
            tall[row * wide + whole : (row + 1) * wide, :] = jnp.zeros((wide - whole, channels), jnp.bfloat16)
            tall[row * wide : row * wide + part, :] = source[half * rows + row]
    for step in range(steps):
        at = slice(step * block, (step + 1) * block)
        bias = bias_ref[at].reshape(1, block)
        pre = dot_nn(tall_conv[...], win_ref[:, at])
        back = dot_nt(tall_grad[...], wout_ref[at, :])
        group = 48
        for first in range(0, rows * wide, group):
            some = slice(first, first + group)
            slope_ref[step % 2, some, :] = (back[some] * gelu_slope(pre[some] + bias)).astype(jnp.bfloat16)
        term = dot_nt(win_ref[:, at], slope_ref[step % 2])
        total_ref[...] = term if step == 0 else total_ref[...] + term
    for out, (k, start, size) in zip(outs, sent):
        first = partner(me, k, count, 1) * owned + start
        out[...] = total_ref[pl.ds(pl.multiple_of(first, 32), size), :].astype(jnp.bfloat16)


def mlp(conv_out, grad_out, w_in, b_in, w_out, count, half, halves, sent, after):
    rows, part, channels = conv_out.shape
    rows //= halves
    block = 256
    wide = round_up(part, HALF)
    vmem = pl.BlockSpec(memory_space=VMEM)
    out_shape = [jax.ShapeDtypeStruct((size, rows * wide), jnp.bfloat16) for _, _, size in sent]
    return pl.pallas_call(
        functools.partial(mlp_kernel, count, half, sent),
        in_specs=[vmem] * 5 + [pl.BlockSpec(memory_space=pl.ANY)] * len(after),
        out_specs=[vmem] * len(out_shape),
        out_shape=out_shape,
        scratch_shapes=[
            pltpu.VMEM((rows * wide, channels), jnp.bfloat16),
            pltpu.VMEM((rows * wide, channels), jnp.bfloat16),
            pltpu.VMEM((2, rows * wide, block), jnp.bfloat16),
            pltpu.VMEM((channels, rows * wide), jnp.float32),
        ],
        compiler_params=pltpu.CompilerParams(vmem_limit_bytes=16 * 2**20),
        cost_estimate=NO_COST,
        name="mlp",
    )(conv_out, grad_out, w_in, b_in, w_out, *after)


def gate_kernel(*refs):
    pass


def gate(arrays):
    anywhere = pl.BlockSpec(memory_space=pl.ANY)
    return pl.pallas_call(
        gate_kernel,
        in_specs=[anywhere] * len(arrays),
        out_specs=[anywhere] * len(arrays),
        out_shape=[jax.ShapeDtypeStruct(x.shape, x.dtype) for x in arrays],
        input_output_aliases={i: i for i in range(len(arrays))},
        cost_estimate=NO_COST,
        name="gate",
    )(*arrays)


def analysis_kernel(count, rows, chunk, last_start, *refs):
    own_ref, first_ref, second_ref = refs[-3:]
    start, size = chunk
    halves = next(h for h in range(1, rows + 1) if refs[h * count].ndim == 3)
    table_ref = refs[halves * count]
    rows_each = rows // halves
    wide = refs[0].shape[1] // rows_each
    window = table_ref.shape[1] - HALF
    me = lax.axis_index("azimuth")
    sources = [partner(me, k, count, -1) for k in range(count)]
    even = lax.rem(lax.axis_index("polar"), 2) == 0

    def columns(row, k):
        half, row = divmod(row, rows_each)
        piece = refs[half * count + k]
        base = start - last_start if half == halves - 1 and k == count - 1 else start
        first = row * wide // LANES * LANES
        return piece[base : base + size, first : first + window]

    shifts = [row % rows_each * wide % LANES for row in range(rows)]
    for shift in sorted(set(shifts)):
        group = [row for row in range(rows) if shifts[row] == shift]
        total = None
        for k in range(count):
            left = jnp.concatenate([columns(row, k) for row in group], axis=0)
            term = dot_nn(left, table_ref[sources[k], HALF - shift : HALF - shift + window, :])
            total = term if total is None else total + term
        for at, row in enumerate(group):
            mine = total[at * size : (at + 1) * size]
            own_ref[row] = mine
            sent = mine.astype(jnp.bfloat16)
            for above, parity in ((first_ref, even), (second_ref, jnp.logical_not(even))):
                below = second_ref if above is first_ref else first_ref

                @pl.when(parity)
                def _(above=above, below=below, sent=sent, row=row):
                    if row >= rows - REACH:
                        above[row - (rows - REACH)] = sent
                    if row < REACH:
                        below[row] = sent


def analyze(pieces, table, rows, chunk, last_start, count, after):
    size = chunk[1]
    width = table.shape[2]
    halo = jax.ShapeDtypeStruct((REACH, size, width), jnp.bfloat16)
    return pl.pallas_call(
        functools.partial(analysis_kernel, count, rows, chunk, last_start),
        in_specs=[pl.BlockSpec(memory_space=VMEM)] * (len(pieces) + 1)
        + [pl.BlockSpec(memory_space=pl.ANY)] * len(after),
        out_specs=[pl.BlockSpec(memory_space=VMEM)] * 3,
        out_shape=[jax.ShapeDtypeStruct((rows, size, width), jnp.float32), halo, halo],
        compiler_params=pltpu.CompilerParams(vmem_limit_bytes=12 * 2**20),
        cost_estimate=NO_COST,
        name="analysis",
    )(*pieces, table, *after)


def add_row(accs, spectrum, weight, target_row, filter_row, targets):
    size = spectrum.shape[0]
    masked = jnp.concatenate([jnp.where(target_row == t, weight, 0.0) for t in targets], axis=0)
    gains = dot_nn(masked.astype(jnp.bfloat16), filter_row)
    whole = (gains.shape[1] // 2) // LANES * LANES - LANES
    spec_re = spectrum[:, :whole]
    spec_im = spectrum[:, whole : 2 * whole]
    spec_x = spectrum[:, 2 * whole :]
    swapped = pltpu.roll(spec_x, HALF, 1)
    for at, target in enumerate(targets):
        gain = gains[at * size : (at + 1) * size]
        gain_re = gain[:, :whole]
        gain_rx = gain[:, whole : whole + LANES]
        gain_im = gain[:, whole + LANES : 2 * whole + LANES]
        gain_ix = gain[:, 2 * whole + LANES :]
        acc_re, acc_im, acc_x = accs[target]
        acc_re = acc_re + (gain_re * spec_re + gain_im * spec_im)
        acc_im = acc_im + (gain_re * spec_im - gain_im * spec_re)
        acc_x = acc_x + (gain_rx * spec_x + gain_ix * swapped)
        accs[target] = acc_re, acc_im, acc_x


def split_tiles(value):
    whole = (value.shape[1] - LANES) // 2
    return value[:, :whole], value[:, whole : 2 * whole], value[:, 2 * whole :]


def own_kernel(own_ref, weight_ref, target_ref, filter_ref, out_ref):
    rows, size, width = own_ref.shape
    accs = {t: split_tiles(jnp.zeros((size, width), jnp.float32)) for t in range(rows)}
    for row in range(rows):
        at = row + REACH
        targets = [t for t in range(rows) if abs(row - t) <= REACH]
        add_row(accs, own_ref[row], weight_ref[...], target_ref[at : at + 1, :], filter_ref[at], targets)
    for t in range(rows):
        out_ref[t] = jnp.concatenate(accs[t], axis=1)


def own_terms(own, weight, target, filters):
    return pl.pallas_call(
        own_kernel,
        in_specs=[pl.BlockSpec(memory_space=VMEM)] * 4,
        out_specs=pl.BlockSpec(memory_space=VMEM),
        out_shape=jax.ShapeDtypeStruct(own.shape, jnp.float32),
        compiler_params=pltpu.CompilerParams(vmem_limit_bytes=12 * 2**20),
        cost_estimate=NO_COST,
        name="own_terms",
    )(own, weight, target, filters)


def finish_kernel(count, part_ref, first_ref, second_ref, weight_ref, target_ref, filter_ref, table_ref, *rest):
    outs, stacked_ref, grid_ref = rest[-count - 2 : -2], rest[-2], rest[-1]
    rows, size, width = part_ref.shape
    part = outs[0].shape[0]
    even = lax.rem(lax.axis_index("polar"), 2) == 0

    def combine(low_ref, high_ref):
        accs = {t: split_tiles(part_ref[t]) for t in range(rows)}
        for side, base in ((low_ref, -REACH), (high_ref, rows)):
            for h in range(REACH):
                at = base + h + REACH
                targets = [t for t in range(rows) if abs(base + h - t) <= REACH]
                add_row(
                    accs,
                    side[h].astype(jnp.float32),
                    weight_ref[...],
                    target_ref[at : at + 1, :],
                    filter_ref[at],
                    targets,
                )
        for t in range(rows):
            stacked_ref[t * size : (t + 1) * size, :] = jnp.concatenate(accs[t], axis=1).astype(jnp.bfloat16)

    pl.when(even)(lambda: combine(second_ref, first_ref))
    pl.when(jnp.logical_not(even))(lambda: combine(first_ref, second_ref))
    me = lax.axis_index("azimuth")
    grid_ref[...] = dot_nt(table_ref[...], stacked_ref[...])
    wide = grid_ref.shape[0] // count
    for k in range(count):
        first = pl.multiple_of(partner(me, k, count, 1) * wide, HALF)
        outs[k][...] = grid_ref[pl.ds(first, wide), :][:part].astype(jnp.bfloat16)


def finish(own, first, second, weight, target, filters, table, count, part, after):
    rows, size, width = own.shape
    return pl.pallas_call(
        functools.partial(finish_kernel, count),
        in_specs=[pl.BlockSpec(memory_space=VMEM)] * 7 + [pl.BlockSpec(memory_space=pl.ANY)] * len(after),
        out_specs=[pl.BlockSpec(memory_space=VMEM)] * count,
        out_shape=[jax.ShapeDtypeStruct((part, rows * size), jnp.bfloat16)] * count,
        scratch_shapes=[
            pltpu.VMEM((rows * size, width), jnp.bfloat16),
            pltpu.VMEM((table.shape[0], rows * size), jnp.float32),
        ],
        compiler_params=pltpu.CompilerParams(vmem_limit_bytes=12 * 2**20),
        cost_estimate=NO_COST,
        name="finish",
    )(own, first, second, weight, target, filters, table, *after)


def add_kernel(count, chunks, grad_ref, *refs):
    pieces, out_ref = refs[:-1], refs[-1]
    rows, part, channels = grad_ref.shape
    me = lax.axis_index("azimuth")

    def add(mine):
        order = [[k for k in range(count) if partner_static(mine, k, count, -1) == s][0] for s in range(count)]
        for row in range(rows):
            conv = jnp.concatenate(
                [
                    pieces[q * count + k][:, row * size : (row + 1) * size]
                    for k in order
                    for q, (_, size) in enumerate(chunks)
                ],
                axis=1,
            )
            out_ref[row] = (grad_ref[row].astype(jnp.float32) + conv.astype(jnp.float32)).astype(
                jnp.bfloat16
            )

    for mine in range(count):
        pl.when(me == mine)(functools.partial(add, mine))


def add_back(grad_out, pieces, count, chunks):
    return pl.pallas_call(
        functools.partial(add_kernel, count, chunks),
        in_specs=[pl.BlockSpec(memory_space=VMEM)] * (1 + len(pieces)),
        out_specs=pl.BlockSpec(memory_space=VMEM),
        out_shape=jax.ShapeDtypeStruct(grad_out.shape, jnp.bfloat16),
        compiler_params=pltpu.CompilerParams(vmem_limit_bytes=12 * 2**20),
        cost_estimate=NO_COST,
        name="add_back",
    )(grad_out, *pieces)


def prepare_kernel(count, chunks, weight_ref, filt_ref, offset_ref, forth_ref, back_ref, *outs):
    filter_out, target_out, forth_out, back_out = outs[:4]
    forth_out[...] = forth_ref[...]
    back_out[...] = back_ref[...]
    bases, channels = weight_ref.shape
    lats, width = filt_ref.shape[1:]
    ext, depth = target_out.shape
    rows = ext - 2 * REACH
    modes = width // 2
    whole = modes // LANES * LANES
    used = TERMS * bases
    weight = pltpu.roll(
        weight_ref[...], lax.rem(count - lax.axis_index("azimuth"), count) * (channels // count), 1
    )[:, : channels // count]
    parts = []
    for _ in range(TERMS):
        rounded = weight.astype(jnp.bfloat16).astype(jnp.float32)
        parts.append(rounded)
        weight = weight - rounded
    parts.append(jnp.zeros((depth - used, weight.shape[1]), jnp.float32))
    weight = jnp.concatenate(parts, axis=0).T
    for (start, size), out in zip(chunks, outs[4:]):
        out[...] = weight[start : start + size]
    start_lat = lax.axis_index("polar") * rows
    table = filt_ref[...].reshape(bases * lats, width)
    base = lax.broadcasted_iota(jnp.int32, (depth, bases * lats), 0)
    valid = base < used
    for _ in range(TERMS - 1):
        base = jnp.where(base >= bases, base - bases, base)
    column = lax.broadcasted_iota(jnp.int32, (depth, bases * lats), 1)
    for i in range(ext):
        lat = start_lat + (i - REACH)
        inside = (lat >= 0) & (lat < lats)
        lat = jnp.clip(lat, 0, lats - 1)
        pick = jnp.where(valid & (column == base * lats + lat), 1.0, 0.0).astype(jnp.bfloat16)
        row = dot_nn(pick, table)
        real, imag = row[:, :modes], row[:, modes:]
        rest_re, rest_im = real[:, whole:], imag[:, whole:]
        filter_out[i] = jnp.concatenate(
            [real[:, :whole], rest_re, rest_re, imag[:, :whole], rest_im, -rest_im], axis=1
        ).astype(jnp.bfloat16)
        local = jnp.where(inside, offset_ref[pl.ds(lat, 1), :] - start_lat, -1)
        spare = jnp.full((1, depth - used), -1, jnp.int32)
        target_out[i : i + 1, :] = jnp.concatenate([local] * TERMS + [spare], axis=1)


def prepare(basis_weight, filt, offsets, forth, back, rows, count, chunks):
    bases = filt.shape[0]
    width = filt.shape[2]
    ext = rows + 2 * REACH
    depth = round_up(TERMS * bases, 16)
    shapes = [
        jax.ShapeDtypeStruct((ext, depth, width + LANES), jnp.bfloat16),
        jax.ShapeDtypeStruct((ext, depth), jnp.int32),
        jax.ShapeDtypeStruct(forth.shape, forth.dtype),
        jax.ShapeDtypeStruct(back.shape, back.dtype),
    ] + [jax.ShapeDtypeStruct((size, depth), jnp.float32) for _, size in chunks]
    return pl.pallas_call(
        functools.partial(prepare_kernel, count, chunks),
        in_specs=[pl.BlockSpec(memory_space=VMEM)] * 5,
        out_specs=[pl.BlockSpec(memory_space=VMEM)] * len(shapes),
        out_shape=shapes,
        compiler_params=pltpu.CompilerParams(vmem_limit_bytes=16 * 2**20),
        cost_estimate=NO_COST,
        name="prepare",
    )(basis_weight, filt, offsets, forth, back)


def halo(first, second):
    bands, count = lax.axis_size("polar"), lax.axis_size("azimuth")
    blocks = []
    for odd, block in ((0, first), (1, second)):
        pairs = []
        for a in range(bands):
            other = ((a + odd) ^ 1) - odd
            for b in range(count):
                paired = 0 <= other < bands
                target = (other, b) if paired else (a, b ^ 1 if b ^ 1 < count else b)
                pairs.append((a * count + b, target[0] * count + target[1]))
        blocks.append(lax.ppermute(block, ("polar", "azimuth"), pairs))
    return blocks


def on_device(chunks, conv_out, grad_out, w_in, b_in, w_out, basis_weight, filt, offsets):
    rows, part, channels = conv_out.shape
    count = lax.axis_size("azimuth")
    forth, back = tables(count, part, filt.shape[2] // 2)
    forth, back = jnp.asarray(forth), jnp.asarray(back)
    owned = channels // count
    parts = chunks[:1] + (((chunks[1][0], owned - chunks[1][0]),) if len(chunks) > 1 else ())
    halves = 2 if rows % 2 == 0 else 1
    pieces = []
    for half in range(halves):
        sent = [(k, 0, owned) for k in range(count)]
        if half == halves - 1:
            sent[-1:] = [(count - 1,) + chunk for chunk in parts]
        blocks = mlp(conv_out, grad_out, w_in, b_in, w_out, count, half, halves, sent, pieces[1:2])
        whole = count if half < halves - 1 else count - 1
        pieces += [exchange(blocks[k], k, count) for k in range(whole)]
    filters, target, forth, back, *weights = prepare(
        basis_weight, filt, offsets, forth, back, rows, count, chunks
    )
    tails = [exchange(blocks[count - 1 + p], count - 1, count) for p in range(len(parts))]
    spectra, terms, grids, returned = {}, {}, {}, []

    def open_chunk(q, after):
        p = min(q, 1)
        own, first, second = analyze(
            pieces + [tails[p]], forth, rows, chunks[q], parts[p][0], count, after
        )
        spectra[q] = halo(first, second)
        terms[q] = own_terms(own, weights[q], target, filters)

    def close_chunk(q):
        after = [returned[(q - 1) * count + 1]] if q else []
        if q > 1:
            older = slice((q - 2) * count + 2, (q - 1) * count)
            returned[older] = gate(returned[older])
            after.append(returned[older][0])
        grids[q] = finish(terms[q], *spectra[q], weights[q], target, filters, back, count, part, after)
        returned.extend(exchange(grids[q][k], k, count) for k in range(count))

    last = len(chunks) - 1
    open_chunk(0, [])
    if last > 0:
        open_chunk(1, [terms[0]])
    for q in range(last + 1):
        close_chunk(q)
        if q + 2 <= last:
            open_chunk(q + 2, [returned[q * count + 1]])
    return add_back(grad_out, returned, count, chunks)


def solution(mesh):
    grid = P(("member", "polar"), "azimuth", None)

    def run(conv_out, grad_out, *others):
        owned = conv_out.shape[2] // mesh.shape["azimuth"]
        sizes = [owned]
        if owned % 32 == 0 and owned >= 96:
            big = owned * 2 // 5 // 32 * 32
            sizes = [big, big, owned - 2 * big]
        chunks = tuple((sum(sizes[:q]), size) for q, size in enumerate(sizes))
        return jax.shard_map(
            functools.partial(on_device, chunks),
            mesh=mesh,
            in_specs=(grid, grid) + (P(),) * 6,
            out_specs=grid,
            check_vma=False,
        )(conv_out, grad_out, *others)

    return run
```

```python
import functools
import math

import jax
import jax.numpy as jnp
import ml_dtypes
import numpy as np
from jax import lax
from jax.experimental import pallas as pl
from jax.experimental.pallas import tpu as pltpu
from jax.sharding import PartitionSpec as P

REACH = 3
LANES = 128
HALF = 64
TERMS = 3
VMEM = pltpu.MemorySpace.VMEM
NO_COST = pl.CostEstimate(flops=0, bytes_accessed=0, transcendentals=0)


def round_up(value, unit):
    return -(-value // unit) * unit


def partner(me, step, count, sign):
    if count & (count - 1) == 0:
        return me ^ step
    return lax.rem(me + sign * step + count, count)


def exchange(block, step, count):
    if step == 0:
        return block
    pairs = [(a, int(partner_static(a, step, count))) for a in range(count)]
    return lax.ppermute(block, "azimuth", pairs)


def partner_static(a, step, count, sign=1):
    return a ^ step if count & (count - 1) == 0 else (a + sign * step) % count


def tables(count, part, modes):
    length = count * part
    whole = modes // LANES * LANES
    order = np.concatenate(
        [
            np.arange(whole),
            modes + np.arange(whole),
            np.arange(whole, modes),
            modes + np.arange(whole, modes),
        ]
    )
    positions = np.arange(length)
    waves = np.arange(modes)
    phase = (positions[:, None] * waves[None, :]) % length
    angle = (2.0 * math.pi / length) * phase
    scale = 1.0 / math.sqrt(length)
    factor = np.where(waves == 0, 1.0, 2.0)
    analysis = np.concatenate([np.cos(angle), -np.sin(angle)], axis=1) * scale
    synth = np.concatenate([np.cos(angle) * factor, -np.sin(angle) * factor], axis=1) * scale
    analysis = analysis.astype(np.float32).astype(ml_dtypes.bfloat16)[:, order]
    synth = synth.astype(np.float32).astype(ml_dtypes.bfloat16)[:, order]
    wide = round_up(part, HALF)
    window = round_up(HALF + wide, LANES)
    forth = np.zeros((count, HALF + window, 2 * modes), ml_dtypes.bfloat16)
    back = np.zeros((count * wide, 2 * modes), ml_dtypes.bfloat16)
    for s in range(count):
        forth[s, HALF : HALF + part] = analysis[s * part : (s + 1) * part]
        back[s * wide : s * wide + part] = synth[s * part : (s + 1) * part]
    return forth, back


def gelu_slope(values):
    size = jnp.abs(values)
    decay = jnp.exp2((-0.5 / math.log(2.0)) * (values * values))
    shifted = 1.0 + (0.3275911 * math.sqrt(0.5)) * size
    t = pl.reciprocal(shifted, approx=True)
    t = t * (2.0 - shifted * t)
    tail = 0.5 * 1.061405429
    for factor in (-1.453152027, 1.421413741, -0.284496736, 0.254829592):
        tail = tail * t + 0.5 * factor
    lower = decay * (tail * t - (1.0 / math.sqrt(2.0 * math.pi)) * size)
    return jnp.where(values < 0.0, lower, 1.0 - lower)


def dot_nt(left, right):
    return lax.dot_general(left, right, (((1,), (1,)), ((), ())), preferred_element_type=jnp.float32)


def dot_nn(left, right):
    return jnp.dot(left, right, preferred_element_type=jnp.float32)


def mlp_kernel(count, half, sent, conv_ref, grad_ref, win_ref, bias_ref, wout_ref, *rest):
    outs, (tall_conv, tall_grad, pre_ref, back_ref, slope_ref, total_ref) = rest[-6 - len(sent) : -6], rest[-6:]
    part, channels = conv_ref.shape[1:]
    wide = round_up(part, HALF)
    rows = tall_conv.shape[0] // wide
    owned = channels // count
    block = slope_ref.shape[2]
    steps = win_ref.shape[1] // block
    me = lax.axis_index("azimuth")
    for tall, source in ((tall_conv, conv_ref), (tall_grad, grad_ref)):
        for row in range(rows):
            whole = part // 16 * 16
            tall[row * wide + whole : (row + 1) * wide, :] = jnp.zeros((wide - whole, channels), jnp.bfloat16)
            tall[row * wide : row * wide + part, :] = source[half * rows + row]
    group = 48
    groups = rows * wide // group

    def span(step):
        return slice(step * block, (step + 1) * block)

    def project_pre(step):
        pre_ref[step % 2] = dot_nn(tall_conv[...], win_ref[:, span(step)])

    def project_back(step):
        back_ref[step % 2] = dot_nt(tall_grad[...], wout_ref[span(step), :])

    def slope(step, first, last):
        bias = bias_ref[span(step)].reshape(1, block)
        for g in range(first, last):
            some = slice(g * group, (g + 1) * group)
            value = back_ref[step % 2, some, :] * gelu_slope(pre_ref[step % 2, some, :] + bias)
            slope_ref[step % 2, some, :] = value.astype(jnp.bfloat16)

    def gather(step):
        term = dot_nt(win_ref[:, span(step)], slope_ref[step % 2])
        total_ref[...] = term if step == 0 else total_ref[...] + term

    project_pre(0)
    project_back(0)
    thirds = [groups * n // 3 for n in range(4)]
    for step in range(steps):
        if step + 1 < steps:
            project_pre(step + 1)
        slope(step, thirds[0], thirds[1])
        if step:
            gather(step - 1)
        slope(step, thirds[1], thirds[2])
        if step + 1 < steps:
            project_back(step + 1)
        slope(step, thirds[2], thirds[3])
    gather(steps - 1)
    for out, (k, start, size) in zip(outs, sent):
        first = partner(me, k, count, 1) * owned + start
        out[...] = total_ref[pl.ds(pl.multiple_of(first, 32), size), :].astype(jnp.bfloat16)


def mlp(conv_out, grad_out, w_in, b_in, w_out, count, half, halves, sent, after):
    rows, part, channels = conv_out.shape
    rows //= halves
    block = 256
    wide = round_up(part, HALF)
    vmem = pl.BlockSpec(memory_space=VMEM)
    out_shape = [jax.ShapeDtypeStruct((size, rows * wide), jnp.bfloat16) for _, _, size in sent]
    return pl.pallas_call(
        functools.partial(mlp_kernel, count, half, sent),
        in_specs=[vmem] * 5 + [pl.BlockSpec(memory_space=pl.ANY)] * len(after),
        out_specs=[vmem] * len(out_shape),
        out_shape=out_shape,
        scratch_shapes=[
            pltpu.VMEM((rows * wide, channels), jnp.bfloat16),
            pltpu.VMEM((rows * wide, channels), jnp.bfloat16),
            pltpu.VMEM((2, rows * wide, block), jnp.float32),
            pltpu.VMEM((2, rows * wide, block), jnp.float32),
            pltpu.VMEM((2, rows * wide, block), jnp.bfloat16),
            pltpu.VMEM((channels, rows * wide), jnp.float32),
        ],
        compiler_params=pltpu.CompilerParams(vmem_limit_bytes=16 * 2**20),
        cost_estimate=NO_COST,
        name="mlp",
    )(conv_out, grad_out, w_in, b_in, w_out, *after)


def analysis_kernel(count, rows, chunk, *refs):
    own_ref, first_ref, second_ref = refs[-3:]
    start, size = chunk
    halves = next(h for h in range(1, rows + 1) if refs[h * count].ndim == 3)
    table_ref = refs[halves * count]
    rows_each = rows // halves
    wide = refs[0].shape[1] // rows_each
    window = table_ref.shape[1] - HALF
    me = lax.axis_index("azimuth")
    sources = [partner(me, k, count, -1) for k in range(count)]
    even = lax.rem(lax.axis_index("polar"), 2) == 0

    def columns(row, k):
        half, row = divmod(row, rows_each)
        piece = refs[half * count + k]
        base = 0 if half == halves - 1 and k == count - 1 else start
        first = row * wide // LANES * LANES
        return piece[base : base + size, first : first + window]

    shifts = [row % rows_each * wide % LANES for row in range(rows)]
    for shift in sorted(set(shifts)):
        group = [row for row in range(rows) if shifts[row] == shift]
        total = None
        for k in range(count):
            left = jnp.concatenate([columns(row, k) for row in group], axis=0)
            term = dot_nn(left, table_ref[sources[k], HALF - shift : HALF - shift + window, :])
            total = term if total is None else total + term
        for at, row in enumerate(group):
            mine = total[at * size : (at + 1) * size]
            own_ref[row] = mine
            sent = mine.astype(jnp.bfloat16)
            for above, parity in ((first_ref, even), (second_ref, jnp.logical_not(even))):
                below = second_ref if above is first_ref else first_ref

                @pl.when(parity)
                def _(above=above, below=below, sent=sent, row=row):
                    if row >= rows - REACH:
                        above[row - (rows - REACH)] = sent
                    if row < REACH:
                        below[row] = sent


def analyze(pieces, table, rows, chunk, count, after):
    size = chunk[1]
    width = table.shape[2]
    halo = jax.ShapeDtypeStruct((REACH, size, width), jnp.bfloat16)
    return pl.pallas_call(
        functools.partial(analysis_kernel, count, rows, chunk),
        in_specs=[pl.BlockSpec(memory_space=VMEM)] * (len(pieces) + 1)
        + [pl.BlockSpec(memory_space=pl.ANY)] * len(after),
        out_specs=[pl.BlockSpec(memory_space=VMEM)] * 3,
        out_shape=[jax.ShapeDtypeStruct((rows, size, width), jnp.float32), halo, halo],
        compiler_params=pltpu.CompilerParams(vmem_limit_bytes=12 * 2**20),
        cost_estimate=NO_COST,
        name="analysis",
    )(*pieces, table, *after)


def add_row(accs, spectrum, weight, target_row, filter_row, targets):
    size = spectrum.shape[0]
    masked = jnp.concatenate([jnp.where(target_row == t, weight, 0.0) for t in targets], axis=0)
    gains = dot_nn(masked.astype(jnp.bfloat16), filter_row)
    whole = (gains.shape[1] // 2) // LANES * LANES - LANES
    spec_re = spectrum[:, :whole]
    spec_im = spectrum[:, whole : 2 * whole]
    spec_x = spectrum[:, 2 * whole :]
    swapped = pltpu.roll(spec_x, HALF, 1)
    for at, target in enumerate(targets):
        gain = gains[at * size : (at + 1) * size]
        gain_re = gain[:, :whole]
        gain_rx = gain[:, whole : whole + LANES]
        gain_im = gain[:, whole + LANES : 2 * whole + LANES]
        gain_ix = gain[:, 2 * whole + LANES :]
        acc_re, acc_im, acc_x = accs[target]
        acc_re = acc_re + (gain_re * spec_re + gain_im * spec_im)
        acc_im = acc_im + (gain_re * spec_im - gain_im * spec_re)
        acc_x = acc_x + (gain_rx * spec_x + gain_ix * swapped)
        accs[target] = acc_re, acc_im, acc_x


def split_tiles(value):
    whole = (value.shape[1] - LANES) // 2
    return value[:, :whole], value[:, whole : 2 * whole], value[:, 2 * whole :]


def own_kernel(own_ref, weight_ref, target_ref, filter_ref, out_ref):
    rows, size, width = own_ref.shape
    accs = {t: split_tiles(jnp.zeros((size, width), jnp.float32)) for t in range(rows)}
    for row in range(rows):
        at = row + REACH
        targets = [t for t in range(rows) if abs(row - t) <= REACH]
        add_row(accs, own_ref[row], weight_ref[...], target_ref[at : at + 1, :], filter_ref[at], targets)
    for t in range(rows):
        out_ref[t] = jnp.concatenate(accs[t], axis=1)


def own_terms(own, weight, target, filters):
    return pl.pallas_call(
        own_kernel,
        in_specs=[pl.BlockSpec(memory_space=VMEM)] * 4,
        out_specs=pl.BlockSpec(memory_space=VMEM),
        out_shape=jax.ShapeDtypeStruct(own.shape, jnp.float32),
        compiler_params=pltpu.CompilerParams(vmem_limit_bytes=12 * 2**20),
        cost_estimate=NO_COST,
        name="own_terms",
    )(own, weight, target, filters)


def finish_kernel(count, part_ref, first_ref, second_ref, weight_ref, target_ref, filter_ref, table_ref, *rest):
    outs, stacked_ref, grid_ref = rest[-count - 2 : -2], rest[-2], rest[-1]
    rows, size, width = part_ref.shape
    part = outs[0].shape[0]
    even = lax.rem(lax.axis_index("polar"), 2) == 0

    def combine(low_ref, high_ref):
        accs = {t: split_tiles(part_ref[t]) for t in range(rows)}
        for side, base in ((low_ref, -REACH), (high_ref, rows)):
            for h in range(REACH):
                at = base + h + REACH
                targets = [t for t in range(rows) if abs(base + h - t) <= REACH]
                add_row(
                    accs,
                    side[h].astype(jnp.float32),
                    weight_ref[...],
                    target_ref[at : at + 1, :],
                    filter_ref[at],
                    targets,
                )
        for t in range(rows):
            stacked_ref[t * size : (t + 1) * size, :] = jnp.concatenate(accs[t], axis=1).astype(jnp.bfloat16)

    pl.when(even)(lambda: combine(second_ref, first_ref))
    pl.when(jnp.logical_not(even))(lambda: combine(first_ref, second_ref))
    me = lax.axis_index("azimuth")
    grid_ref[...] = dot_nt(table_ref[...], stacked_ref[...])
    wide = grid_ref.shape[0] // count
    for k in range(count):
        first = pl.multiple_of(partner(me, k, count, 1) * wide, HALF)
        outs[k][...] = grid_ref[pl.ds(first, wide), :][:part].astype(jnp.bfloat16)


def finish(own, first, second, weight, target, filters, table, count, part, after):
    rows, size, width = own.shape
    return pl.pallas_call(
        functools.partial(finish_kernel, count),
        in_specs=[pl.BlockSpec(memory_space=VMEM)] * 7 + [pl.BlockSpec(memory_space=pl.ANY)] * len(after),
        out_specs=[pl.BlockSpec(memory_space=VMEM)] * count,
        out_shape=[jax.ShapeDtypeStruct((part, rows * size), jnp.bfloat16)] * count,
        scratch_shapes=[
            pltpu.VMEM((rows * size, width), jnp.bfloat16),
            pltpu.VMEM((table.shape[0], rows * size), jnp.float32),
        ],
        compiler_params=pltpu.CompilerParams(vmem_limit_bytes=12 * 2**20),
        cost_estimate=NO_COST,
        name="finish",
    )(own, first, second, weight, target, filters, table, *after)


def add_kernel(count, chunks, grad_ref, *refs):
    pieces, out_ref = refs[:-1], refs[-1]
    rows, part, channels = grad_ref.shape
    me = lax.axis_index("azimuth")

    def add(mine):
        order = [[k for k in range(count) if partner_static(mine, k, count, -1) == s][0] for s in range(count)]
        for row in range(rows):
            conv = jnp.concatenate(
                [
                    pieces[q * count + k][:, row * size : (row + 1) * size]
                    for k in order
                    for q, (_, size) in enumerate(chunks)
                ],
                axis=1,
            )
            out_ref[row] = (grad_ref[row].astype(jnp.float32) + conv.astype(jnp.float32)).astype(
                jnp.bfloat16
            )

    for mine in range(count):
        pl.when(me == mine)(functools.partial(add, mine))


def add_back(grad_out, pieces, count, chunks):
    return pl.pallas_call(
        functools.partial(add_kernel, count, chunks),
        in_specs=[pl.BlockSpec(memory_space=VMEM)] * (1 + len(pieces)),
        out_specs=pl.BlockSpec(memory_space=VMEM),
        out_shape=jax.ShapeDtypeStruct(grad_out.shape, jnp.bfloat16),
        compiler_params=pltpu.CompilerParams(vmem_limit_bytes=12 * 2**20),
        cost_estimate=NO_COST,
        name="add_back",
    )(grad_out, *pieces)


def prepare_kernel(count, chunks, weight_ref, filt_ref, offset_ref, forth_ref, back_ref, *outs):
    filter_out, target_out, forth_out, back_out = outs[:4]
    forth_out[...] = forth_ref[...]
    back_out[...] = back_ref[...]
    bases, channels = weight_ref.shape
    lats, width = filt_ref.shape[1:]
    ext, depth = target_out.shape
    rows = ext - 2 * REACH
    modes = width // 2
    whole = modes // LANES * LANES
    used = TERMS * bases
    weight = pltpu.roll(
        weight_ref[...], lax.rem(count - lax.axis_index("azimuth"), count) * (channels // count), 1
    )[:, : channels // count]
    parts = []
    for _ in range(TERMS):
        rounded = weight.astype(jnp.bfloat16).astype(jnp.float32)
        parts.append(rounded)
        weight = weight - rounded
    parts.append(jnp.zeros((depth - used, weight.shape[1]), jnp.float32))
    weight = jnp.concatenate(parts, axis=0).T
    for (start, size), out in zip(chunks, outs[4:]):
        out[...] = weight[start : start + size]
    start_lat = lax.axis_index("polar") * rows
    table = filt_ref[...].reshape(bases * lats, width)
    base = lax.broadcasted_iota(jnp.int32, (depth, bases * lats), 0)
    valid = base < used
    for _ in range(TERMS - 1):
        base = jnp.where(base >= bases, base - bases, base)
    column = lax.broadcasted_iota(jnp.int32, (depth, bases * lats), 1)
    for i in range(ext):
        lat = start_lat + (i - REACH)
        inside = (lat >= 0) & (lat < lats)
        lat = jnp.clip(lat, 0, lats - 1)
        pick = jnp.where(valid & (column == base * lats + lat), 1.0, 0.0).astype(jnp.bfloat16)
        row = dot_nn(pick, table)
        real, imag = row[:, :modes], row[:, modes:]
        rest_re, rest_im = real[:, whole:], imag[:, whole:]
        filter_out[i] = jnp.concatenate(
            [real[:, :whole], rest_re, rest_re, imag[:, :whole], rest_im, -rest_im], axis=1
        ).astype(jnp.bfloat16)
        local = jnp.where(inside, offset_ref[pl.ds(lat, 1), :] - start_lat, -1)
        spare = jnp.full((1, depth - used), -1, jnp.int32)
        target_out[i : i + 1, :] = jnp.concatenate([local] * TERMS + [spare], axis=1)


def prepare(basis_weight, filt, offsets, forth, back, rows, count, chunks):
    bases = filt.shape[0]
    width = filt.shape[2]
    ext = rows + 2 * REACH
    depth = round_up(TERMS * bases, 16)
    shapes = [
        jax.ShapeDtypeStruct((ext, depth, width + LANES), jnp.bfloat16),
        jax.ShapeDtypeStruct((ext, depth), jnp.int32),
        jax.ShapeDtypeStruct(forth.shape, forth.dtype),
        jax.ShapeDtypeStruct(back.shape, back.dtype),
    ] + [jax.ShapeDtypeStruct((size, depth), jnp.float32) for _, size in chunks]
    return pl.pallas_call(
        functools.partial(prepare_kernel, count, chunks),
        in_specs=[pl.BlockSpec(memory_space=VMEM)] * 5,
        out_specs=[pl.BlockSpec(memory_space=VMEM)] * len(shapes),
        out_shape=shapes,
        compiler_params=pltpu.CompilerParams(vmem_limit_bytes=16 * 2**20),
        cost_estimate=NO_COST,
        name="prepare",
    )(basis_weight, filt, offsets, forth, back)


def halo(first, second):
    bands, count = lax.axis_size("polar"), lax.axis_size("azimuth")
    blocks = []
    for odd, block in ((0, first), (1, second)):
        pairs = []
        for a in range(bands):
            other = ((a + odd) ^ 1) - odd
            for b in range(count):
                paired = 0 <= other < bands
                target = (other, b) if paired else (a, b ^ 1 if b ^ 1 < count else b)
                pairs.append((a * count + b, target[0] * count + target[1]))
        blocks.append(lax.ppermute(block, ("polar", "azimuth"), pairs))
    return blocks


def on_device(chunks, conv_out, grad_out, w_in, b_in, w_out, basis_weight, filt, offsets):
    rows, part, channels = conv_out.shape
    count = lax.axis_size("azimuth")
    forth, back = tables(count, part, filt.shape[2] // 2)
    forth, back = jnp.asarray(forth), jnp.asarray(back)
    owned = channels // count
    halves = 2 if rows % 2 == 0 else 1
    pieces = []
    for half in range(halves):
        sent = [(k, 0, owned) for k in range(count)]
        if half == halves - 1:
            sent[-1:] = [(count - 1,) + chunk for chunk in chunks]
        blocks = mlp(conv_out, grad_out, w_in, b_in, w_out, count, half, halves, sent, pieces[1:2])
        whole = count if half < halves - 1 else count - 1
        pieces += [exchange(blocks[k], k, count) for k in range(whole)]
    filters, target, forth, back, *weights = prepare(
        basis_weight, filt, offsets, forth, back, rows, count, chunks
    )
    spectra, terms, grids, returned = {}, {}, {}, []

    def open_chunk(q, after):
        last = exchange(blocks[count - 1 + q], count - 1, count)
        own, first, second = analyze(pieces + [last], forth, rows, chunks[q], count, after)
        spectra[q] = halo(first, second)
        terms[q] = own_terms(own, weights[q], target, filters)

    def close_chunk(q):
        after = [returned[(q - 1) * count + 1]] if q else []
        grids[q] = finish(terms[q], *spectra[q], weights[q], target, filters, back, count, part, after)
        returned.extend(exchange(grids[q][k], k, count) for k in range(count))

    last = len(chunks) - 1
    open_chunk(0, [])
    if last > 0:
        open_chunk(1, [terms[0]])
    for q in range(last + 1):
        close_chunk(q)
        if q + 2 <= last:
            open_chunk(q + 2, [grids[q][0]])
    return add_back(grad_out, returned, count, chunks)


def solution(mesh):
    grid = P(("member", "polar"), "azimuth", None)

    def run(conv_out, grad_out, *others):
        owned = conv_out.shape[2] // mesh.shape["azimuth"]
        sizes = [owned]
        if owned % 32 == 0 and owned >= 96:
            big = owned * 3 // 5 // 32 * 32
            sizes = [big, owned - big]
        chunks = tuple((sum(sizes[:q]), size) for q, size in enumerate(sizes))
        return jax.shard_map(
            functools.partial(on_device, chunks),
            mesh=mesh,
            in_specs=(grid, grid) + (P(),) * 6,
            out_specs=grid,
            check_vma=False,
        )(conv_out, grad_out, *others)

    return run
```

```python
import functools
import math

import jax
import jax.numpy as jnp
import ml_dtypes
import numpy as np
from jax import lax
from jax.experimental import pallas as pl
from jax.experimental.pallas import tpu as pltpu
from jax.sharding import PartitionSpec as P

REACH = 3
LANES = 128
HALF = 64
TERMS = 3
NEAR = 1
VMEM = pltpu.MemorySpace.VMEM
NO_COST = pl.CostEstimate(flops=0, bytes_accessed=0, transcendentals=0)


def round_up(value, unit):
    return -(-value // unit) * unit


def partner(me, step, count, sign):
    if count & (count - 1) == 0:
        return me ^ step
    return lax.rem(me + sign * step + count, count)


def exchange(block, step, count):
    if step == 0:
        return block
    pairs = [(a, int(partner_static(a, step, count))) for a in range(count)]
    return lax.ppermute(block, "azimuth", pairs)


def partner_static(a, step, count, sign=1):
    return a ^ step if count & (count - 1) == 0 else (a + sign * step) % count


def tables(count, part, modes):
    length = count * part
    whole = modes // LANES * LANES
    order = np.concatenate(
        [
            np.arange(whole),
            modes + np.arange(whole),
            np.arange(whole, modes),
            modes + np.arange(whole, modes),
        ]
    )
    positions = np.arange(length)
    waves = np.arange(modes)
    phase = (positions[:, None] * waves[None, :]) % length
    angle = (2.0 * math.pi / length) * phase
    scale = 1.0 / math.sqrt(length)
    factor = np.where(waves == 0, 1.0, 2.0)
    analysis = np.concatenate([np.cos(angle), -np.sin(angle)], axis=1) * scale
    synth = np.concatenate([np.cos(angle) * factor, -np.sin(angle) * factor], axis=1) * scale
    analysis = analysis.astype(np.float32).astype(ml_dtypes.bfloat16)[:, order]
    synth = synth.astype(np.float32).astype(ml_dtypes.bfloat16)[:, order]
    wide = round_up(part, HALF)
    window = round_up(HALF + wide, LANES)
    forth = np.zeros((count, HALF + window, 2 * modes), ml_dtypes.bfloat16)
    back = np.zeros((count * wide, 2 * modes), ml_dtypes.bfloat16)
    for s in range(count):
        forth[s, HALF : HALF + part] = analysis[s * part : (s + 1) * part]
        back[s * wide : s * wide + part] = synth[s * part : (s + 1) * part]
    return forth, back


def gelu_slope(values):
    normal_cdf = 0.5 + 0.5 * lax.erf(values * math.sqrt(0.5))
    density = jnp.exp2((-0.5 / math.log(2.0)) * (values * values)) * (1.0 / math.sqrt(2.0 * math.pi))
    return normal_cdf + values * density


def dot_nt(left, right):
    return lax.dot_general(left, right, (((1,), (1,)), ((), ())), preferred_element_type=jnp.float32)


def dot_nn(left, right):
    return jnp.dot(left, right, preferred_element_type=jnp.float32)


def mlp_kernel(count, half, sent, conv_ref, grad_ref, win_ref, bias_ref, wout_ref, *rest):
    outs, (tall_conv, tall_grad, pre_ref, back_ref, slope_ref, total_ref) = rest[-6 - len(sent) : -6], rest[-6:]
    part, channels = conv_ref.shape[1:]
    wide = round_up(part, HALF)
    rows = tall_conv.shape[0] // wide
    owned = channels // count
    block = slope_ref.shape[2]
    steps = win_ref.shape[1] // block
    me = lax.axis_index("azimuth")
    for tall, source in ((tall_conv, conv_ref), (tall_grad, grad_ref)):
        for row in range(rows):
            whole = part // 16 * 16
            tall[row * wide + whole : (row + 1) * wide, :] = jnp.zeros((wide - whole, channels), jnp.bfloat16)
            tall[row * wide : row * wide + part, :] = source[half * rows + row]
    group = 48
    groups = rows * wide // group

    def span(step):
        return slice(step * block, (step + 1) * block)

    def project_pre(step):
        pre_ref[step % 2] = dot_nn(tall_conv[...], win_ref[:, span(step)])

    def project_back(step):
        back_ref[step % 2] = dot_nt(tall_grad[...], wout_ref[span(step), :])

    def slope(step, first, last):
        bias = bias_ref[span(step)].reshape(1, block)
        for g in range(first, last):
            some = slice(g * group, (g + 1) * group)
            value = back_ref[step % 2, some, :] * gelu_slope(pre_ref[step % 2, some, :] + bias)
            slope_ref[step % 2, some, :] = value.astype(jnp.bfloat16)

    def gather(step):
        term = dot_nt(win_ref[:, span(step)], slope_ref[step % 2])
        total_ref[...] = term if step == 0 else total_ref[...] + term

    project_pre(0)
    project_back(0)
    thirds = [groups * n // 3 for n in range(4)]
    for step in range(steps):
        if step + 1 < steps:
            project_pre(step + 1)
        slope(step, thirds[0], thirds[1])
        if step:
            gather(step - 1)
        slope(step, thirds[1], thirds[2])
        if step + 1 < steps:
            project_back(step + 1)
        slope(step, thirds[2], thirds[3])
    gather(steps - 1)
    for out, (k, start, size) in zip(outs, sent):
        first = partner(me, k, count, 1) * owned + start
        out[...] = total_ref[pl.ds(pl.multiple_of(first, 32), size), :].astype(jnp.bfloat16)


def mlp(conv_out, grad_out, w_in, b_in, w_out, count, half, halves, sent, after):
    rows, part, channels = conv_out.shape
    rows //= halves
    block = 256
    wide = round_up(part, HALF)
    vmem = pl.BlockSpec(memory_space=VMEM)
    out_shape = [jax.ShapeDtypeStruct((size, rows * wide), jnp.bfloat16) for _, _, size in sent]
    return pl.pallas_call(
        functools.partial(mlp_kernel, count, half, sent),
        in_specs=[vmem] * 5 + [pl.BlockSpec(memory_space=pl.ANY)] * len(after),
        out_specs=[vmem] * len(out_shape),
        out_shape=out_shape,
        scratch_shapes=[
            pltpu.VMEM((rows * wide, channels), jnp.bfloat16),
            pltpu.VMEM((rows * wide, channels), jnp.bfloat16),
            pltpu.VMEM((2, rows * wide, block), jnp.float32),
            pltpu.VMEM((2, rows * wide, block), jnp.float32),
            pltpu.VMEM((2, rows * wide, block), jnp.bfloat16),
            pltpu.VMEM((channels, rows * wide), jnp.float32),
        ],
        compiler_params=pltpu.CompilerParams(vmem_limit_bytes=16 * 2**20),
        cost_estimate=NO_COST,
        name="mlp",
    )(conv_out, grad_out, w_in, b_in, w_out, *after)


def analysis_kernel(count, rows, chunk, *refs):
    own_ref, first_ref, second_ref = refs[-3:]
    start, size = chunk
    halves = next(h for h in range(1, rows + 1) if refs[h * count].ndim == 3)
    table_ref = refs[halves * count]
    rows_each = rows // halves
    wide = refs[0].shape[1] // rows_each
    window = table_ref.shape[1] - HALF
    me = lax.axis_index("azimuth")
    sources = [partner(me, k, count, -1) for k in range(count)]
    even = lax.rem(lax.axis_index("polar"), 2) == 0

    def columns(row, k):
        half, row = divmod(row, rows_each)
        piece = refs[half * count + k]
        base = 0 if half == halves - 1 and k > NEAR else start
        first = row * wide // LANES * LANES
        return piece[base : base + size, first : first + window]

    shifts = [row % rows_each * wide % LANES for row in range(rows)]
    for shift in sorted(set(shifts)):
        group = [row for row in range(rows) if shifts[row] == shift]
        total = None
        for k in range(count):
            left = jnp.concatenate([columns(row, k) for row in group], axis=0)
            term = dot_nn(left, table_ref[sources[k], HALF - shift : HALF - shift + window, :])
            total = term if total is None else total + term
        for at, row in enumerate(group):
            mine = total[at * size : (at + 1) * size]
            own_ref[row] = mine
            sent = mine.astype(jnp.bfloat16)
            for above, parity in ((first_ref, even), (second_ref, jnp.logical_not(even))):
                below = second_ref if above is first_ref else first_ref

                @pl.when(parity)
                def _(above=above, below=below, sent=sent, row=row):
                    if row >= rows - REACH:
                        above[row - (rows - REACH)] = sent
                    if row < REACH:
                        below[row] = sent


def analyze(pieces, table, rows, chunk, count, after):
    size = chunk[1]
    width = table.shape[2]
    halo = jax.ShapeDtypeStruct((REACH, size, width), jnp.bfloat16)
    return pl.pallas_call(
        functools.partial(analysis_kernel, count, rows, chunk),
        in_specs=[pl.BlockSpec(memory_space=VMEM)] * (len(pieces) + 1)
        + [pl.BlockSpec(memory_space=pl.ANY)] * len(after),
        out_specs=[pl.BlockSpec(memory_space=VMEM)] * 3,
        out_shape=[jax.ShapeDtypeStruct((rows, size, width), jnp.float32), halo, halo],
        compiler_params=pltpu.CompilerParams(vmem_limit_bytes=12 * 2**20),
        cost_estimate=NO_COST,
        name="analysis",
    )(*pieces, table, *after)


def add_row(accs, spectrum, weight, target_row, filter_row, targets):
    size = spectrum.shape[0]
    masked = jnp.concatenate([jnp.where(target_row == t, weight, 0.0) for t in targets], axis=0)
    gains = dot_nn(masked.astype(jnp.bfloat16), filter_row)
    whole = (gains.shape[1] // 2) // LANES * LANES - LANES
    spec_re = spectrum[:, :whole]
    spec_im = spectrum[:, whole : 2 * whole]
    spec_x = spectrum[:, 2 * whole :]
    swapped = pltpu.roll(spec_x, HALF, 1)
    for at, target in enumerate(targets):
        gain = gains[at * size : (at + 1) * size]
        gain_re = gain[:, :whole]
        gain_rx = gain[:, whole : whole + LANES]
        gain_im = gain[:, whole + LANES : 2 * whole + LANES]
        gain_ix = gain[:, 2 * whole + LANES :]
        acc_re, acc_im, acc_x = accs[target]
        acc_re = acc_re + (gain_re * spec_re + gain_im * spec_im)
        acc_im = acc_im + (gain_re * spec_im - gain_im * spec_re)
        acc_x = acc_x + (gain_rx * spec_x + gain_ix * swapped)
        accs[target] = acc_re, acc_im, acc_x


def split_tiles(value):
    whole = (value.shape[1] - LANES) // 2
    return value[:, :whole], value[:, whole : 2 * whole], value[:, 2 * whole :]


def own_kernel(own_ref, weight_ref, target_ref, filter_ref, out_ref):
    rows, size, width = own_ref.shape
    accs = {t: split_tiles(jnp.zeros((size, width), jnp.float32)) for t in range(rows)}
    for row in range(rows):
        at = row + REACH
        targets = [t for t in range(rows) if abs(row - t) <= REACH]
        add_row(accs, own_ref[row], weight_ref[...], target_ref[at : at + 1, :], filter_ref[at], targets)
    for t in range(rows):
        out_ref[t] = jnp.concatenate(accs[t], axis=1)


def own_terms(own, weight, target, filters):
    return pl.pallas_call(
        own_kernel,
        in_specs=[pl.BlockSpec(memory_space=VMEM)] * 4,
        out_specs=pl.BlockSpec(memory_space=VMEM),
        out_shape=jax.ShapeDtypeStruct(own.shape, jnp.float32),
        compiler_params=pltpu.CompilerParams(vmem_limit_bytes=12 * 2**20),
        cost_estimate=NO_COST,
        name="own_terms",
    )(own, weight, target, filters)


def finish_kernel(count, part_ref, first_ref, second_ref, weight_ref, target_ref, filter_ref, table_ref, *rest):
    outs, stacked_ref, grid_ref = rest[-count - 2 : -2], rest[-2], rest[-1]
    rows, size, width = part_ref.shape
    part = outs[0].shape[0]
    even = lax.rem(lax.axis_index("polar"), 2) == 0

    def combine(low_ref, high_ref):
        accs = {t: split_tiles(part_ref[t]) for t in range(rows)}
        for side, base in ((low_ref, -REACH), (high_ref, rows)):
            for h in range(REACH):
                at = base + h + REACH
                targets = [t for t in range(rows) if abs(base + h - t) <= REACH]
                add_row(
                    accs,
                    side[h].astype(jnp.float32),
                    weight_ref[...],
                    target_ref[at : at + 1, :],
                    filter_ref[at],
                    targets,
                )
        for t in range(rows):
            stacked_ref[t * size : (t + 1) * size, :] = jnp.concatenate(accs[t], axis=1).astype(jnp.bfloat16)

    pl.when(even)(lambda: combine(second_ref, first_ref))
    pl.when(jnp.logical_not(even))(lambda: combine(first_ref, second_ref))
    me = lax.axis_index("azimuth")
    grid_ref[...] = dot_nt(table_ref[...], stacked_ref[...])
    wide = grid_ref.shape[0] // count
    for k in range(count):
        first = pl.multiple_of(partner(me, k, count, 1) * wide, HALF)
        outs[k][...] = grid_ref[pl.ds(first, wide), :][:part].astype(jnp.bfloat16)


def finish(own, first, second, weight, target, filters, table, count, part, after):
    rows, size, width = own.shape
    return pl.pallas_call(
        functools.partial(finish_kernel, count),
        in_specs=[pl.BlockSpec(memory_space=VMEM)] * 7 + [pl.BlockSpec(memory_space=pl.ANY)] * len(after),
        out_specs=[pl.BlockSpec(memory_space=VMEM)] * count,
        out_shape=[jax.ShapeDtypeStruct((part, rows * size), jnp.bfloat16)] * count,
        scratch_shapes=[
            pltpu.VMEM((rows * size, width), jnp.bfloat16),
            pltpu.VMEM((table.shape[0], rows * size), jnp.float32),
        ],
        compiler_params=pltpu.CompilerParams(vmem_limit_bytes=12 * 2**20),
        cost_estimate=NO_COST,
        name="finish",
    )(own, first, second, weight, target, filters, table, *after)


def add_kernel(count, chunks, grad_ref, *refs):
    pieces, out_ref = refs[:-1], refs[-1]
    rows, part, channels = grad_ref.shape
    me = lax.axis_index("azimuth")

    def add(mine):
        order = [[k for k in range(count) if partner_static(mine, k, count, -1) == s][0] for s in range(count)]
        for row in range(rows):
            conv = jnp.concatenate(
                [
                    pieces[q * count + k][:, row * size : (row + 1) * size]
                    for k in order
                    for q, (_, size) in enumerate(chunks)
                ],
                axis=1,
            )
            out_ref[row] = (grad_ref[row].astype(jnp.float32) + conv.astype(jnp.float32)).astype(
                jnp.bfloat16
            )

    for mine in range(count):
        pl.when(me == mine)(functools.partial(add, mine))


def add_back(grad_out, pieces, count, chunks):
    return pl.pallas_call(
        functools.partial(add_kernel, count, chunks),
        in_specs=[pl.BlockSpec(memory_space=VMEM)] * (1 + len(pieces)),
        out_specs=pl.BlockSpec(memory_space=VMEM),
        out_shape=jax.ShapeDtypeStruct(grad_out.shape, jnp.bfloat16),
        compiler_params=pltpu.CompilerParams(vmem_limit_bytes=12 * 2**20),
        cost_estimate=NO_COST,
        name="add_back",
    )(grad_out, *pieces)


def prepare_kernel(count, chunks, weight_ref, filt_ref, offset_ref, forth_ref, back_ref, *outs):
    filter_out, target_out, forth_out, back_out = outs[:4]
    forth_out[...] = forth_ref[...]
    back_out[...] = back_ref[...]
    bases, channels = weight_ref.shape
    lats, width = filt_ref.shape[1:]
    ext, depth = target_out.shape
    rows = ext - 2 * REACH
    modes = width // 2
    whole = modes // LANES * LANES
    used = TERMS * bases
    weight = pltpu.roll(
        weight_ref[...], lax.rem(count - lax.axis_index("azimuth"), count) * (channels // count), 1
    )[:, : channels // count]
    parts = []
    for _ in range(TERMS):
        rounded = weight.astype(jnp.bfloat16).astype(jnp.float32)
        parts.append(rounded)
        weight = weight - rounded
    parts.append(jnp.zeros((depth - used, weight.shape[1]), jnp.float32))
    weight = jnp.concatenate(parts, axis=0).T
    for (start, size), out in zip(chunks, outs[4:]):
        out[...] = weight[start : start + size]
    start_lat = lax.axis_index("polar") * rows
    table = filt_ref[...].reshape(bases * lats, width)
    base = lax.broadcasted_iota(jnp.int32, (depth, bases * lats), 0)
    valid = base < used
    for _ in range(TERMS - 1):
        base = jnp.where(base >= bases, base - bases, base)
    column = lax.broadcasted_iota(jnp.int32, (depth, bases * lats), 1)
    for i in range(ext):
        lat = start_lat + (i - REACH)
        inside = (lat >= 0) & (lat < lats)
        lat = jnp.clip(lat, 0, lats - 1)
        pick = jnp.where(valid & (column == base * lats + lat), 1.0, 0.0).astype(jnp.bfloat16)
        row = dot_nn(pick, table)
        real, imag = row[:, :modes], row[:, modes:]
        rest_re, rest_im = real[:, whole:], imag[:, whole:]
        filter_out[i] = jnp.concatenate(
            [real[:, :whole], rest_re, rest_re, imag[:, :whole], rest_im, -rest_im], axis=1
        ).astype(jnp.bfloat16)
        local = jnp.where(inside, offset_ref[pl.ds(lat, 1), :] - start_lat, -1)
        spare = jnp.full((1, depth - used), -1, jnp.int32)
        target_out[i : i + 1, :] = jnp.concatenate([local] * TERMS + [spare], axis=1)


def prepare(basis_weight, filt, offsets, forth, back, rows, count, chunks):
    bases = filt.shape[0]
    width = filt.shape[2]
    ext = rows + 2 * REACH
    depth = round_up(TERMS * bases, 16)
    shapes = [
        jax.ShapeDtypeStruct((ext, depth, width + LANES), jnp.bfloat16),
        jax.ShapeDtypeStruct((ext, depth), jnp.int32),
        jax.ShapeDtypeStruct(forth.shape, forth.dtype),
        jax.ShapeDtypeStruct(back.shape, back.dtype),
    ] + [jax.ShapeDtypeStruct((size, depth), jnp.float32) for _, size in chunks]
    return pl.pallas_call(
        functools.partial(prepare_kernel, count, chunks),
        in_specs=[pl.BlockSpec(memory_space=VMEM)] * 5,
        out_specs=[pl.BlockSpec(memory_space=VMEM)] * len(shapes),
        out_shape=shapes,
        compiler_params=pltpu.CompilerParams(vmem_limit_bytes=16 * 2**20),
        cost_estimate=NO_COST,
        name="prepare",
    )(basis_weight, filt, offsets, forth, back)


def halo(first, second):
    bands, count = lax.axis_size("polar"), lax.axis_size("azimuth")
    blocks = []
    for odd, block in ((0, first), (1, second)):
        pairs = []
        for a in range(bands):
            other = ((a + odd) ^ 1) - odd
            for b in range(count):
                paired = 0 <= other < bands
                target = (other, b) if paired else (a, b ^ 1 if b ^ 1 < count else b)
                pairs.append((a * count + b, target[0] * count + target[1]))
        blocks.append(lax.ppermute(block, ("polar", "azimuth"), pairs))
    return blocks


def on_device(chunks, conv_out, grad_out, w_in, b_in, w_out, basis_weight, filt, offsets):
    rows, part, channels = conv_out.shape
    count = lax.axis_size("azimuth")
    forth, back = tables(count, part, filt.shape[2] // 2)
    forth, back = jnp.asarray(forth), jnp.asarray(back)
    owned = channels // count
    halves = 2 if rows % 2 == 0 else 1
    pieces = []
    for half in range(halves):
        final = half == halves - 1
        far = range(NEAR + 1, count)
        sent = [(k, 0, owned) for k in range(count)]
        if final:
            sent[NEAR + 1 :] = [(k,) + chunk for chunk in chunks for k in far]
        blocks = mlp(conv_out, grad_out, w_in, b_in, w_out, count, half, halves, sent, pieces[1:2])
        pieces += [exchange(blocks[k], k, count) for k in range(NEAR + 1 if final else count)]
    filters, target, forth, back, *weights = prepare(
        basis_weight, filt, offsets, forth, back, rows, count, chunks
    )
    spectra, terms, grids, returned = {}, {}, {}, []

    def open_chunk(q, after):
        tail = [exchange(blocks[NEAR + 1 + q * len(far) + i], k, count) for i, k in enumerate(far)]
        own, first, second = analyze(pieces + tail, forth, rows, chunks[q], count, after)
        spectra[q] = halo(first, second)
        terms[q] = own_terms(own, weights[q], target, filters)

    def close_chunk(q):
        after = [returned[(q - 1) * count + 1]] if q else []
        grids[q] = finish(terms[q], *spectra[q], weights[q], target, filters, back, count, part, after)
        returned.extend(exchange(grids[q][k], k, count) for k in range(count))

    last = len(chunks) - 1
    open_chunk(0, [])
    if last > 0:
        open_chunk(1, [terms[0]])
    for q in range(last + 1):
        close_chunk(q)
        if q + 2 <= last:
            open_chunk(q + 2, [grids[q][0]])
    return add_back(grad_out, returned, count, chunks)


def solution(mesh):
    grid = P(("member", "polar"), "azimuth", None)

    def run(conv_out, grad_out, *others):
        owned = conv_out.shape[2] // mesh.shape["azimuth"]
        sizes = [owned]
        if owned % 32 == 0 and owned >= 96:
            big = owned * 3 // 5 // 32 * 32
            sizes = [big, owned - big]
        chunks = tuple((sum(sizes[:q]), size) for q, size in enumerate(sizes))
        return jax.shard_map(
            functools.partial(on_device, chunks),
            mesh=mesh,
            in_specs=(grid, grid) + (P(),) * 6,
            out_specs=grid,
            check_vma=False,
        )(conv_out, grad_out, *others)

    return run
```

```python
import functools
import math

import jax
import jax.numpy as jnp
import ml_dtypes
import numpy as np
from jax import lax
from jax.experimental import pallas as pl
from jax.experimental.pallas import tpu as pltpu
from jax.sharding import PartitionSpec as P

REACH = 3
LANES = 128
HALF = 64
TERMS = 3
NEAR = 1
VMEM = pltpu.MemorySpace.VMEM
NO_COST = pl.CostEstimate(flops=0, bytes_accessed=0, transcendentals=0)


def round_up(value, unit):
    return -(-value // unit) * unit


def partner(me, step, count, sign):
    if count & (count - 1) == 0:
        return me ^ step
    return lax.rem(me + sign * step + count, count)


def exchange(block, step, count):
    if step == 0:
        return block
    pairs = [(a, int(partner_static(a, step, count))) for a in range(count)]
    return lax.ppermute(block, "azimuth", pairs)


def partner_static(a, step, count, sign=1):
    return a ^ step if count & (count - 1) == 0 else (a + sign * step) % count


def tables(count, part, modes):
    length = count * part
    whole = modes // LANES * LANES
    order = np.concatenate(
        [
            np.arange(whole),
            modes + np.arange(whole),
            np.arange(whole, modes),
            modes + np.arange(whole, modes),
        ]
    )
    positions = np.arange(length)
    waves = np.arange(modes)
    phase = (positions[:, None] * waves[None, :]) % length
    angle = (2.0 * math.pi / length) * phase
    scale = 1.0 / math.sqrt(length)
    factor = np.where(waves == 0, 1.0, 2.0)
    analysis = np.concatenate([np.cos(angle), -np.sin(angle)], axis=1) * scale
    synth = np.concatenate([np.cos(angle) * factor, -np.sin(angle) * factor], axis=1) * scale
    analysis = analysis.astype(np.float32).astype(ml_dtypes.bfloat16)[:, order]
    synth = synth.astype(np.float32).astype(ml_dtypes.bfloat16)[:, order]
    wide = round_up(part, HALF)
    window = round_up(HALF + wide, LANES)
    forth = np.zeros((count, HALF + window, 2 * modes), ml_dtypes.bfloat16)
    back = np.zeros((count * wide, 2 * modes), ml_dtypes.bfloat16)
    for s in range(count):
        forth[s, HALF : HALF + part] = analysis[s * part : (s + 1) * part]
        back[s * wide : s * wide + part] = synth[s * part : (s + 1) * part]
    return forth, back


def twice_gelu_slope(scaled):
    power = math.log2(2.0 / math.sqrt(math.pi)) - (1.0 / math.log(2.0)) * (scaled * scaled)
    return (1.0 + lax.erf(scaled)) + scaled * jnp.exp2(power)


def dot_nt(left, right):
    return lax.dot_general(left, right, (((1,), (1,)), ((), ())), preferred_element_type=jnp.float32)


def dot_nn(left, right):
    return jnp.dot(left, right, preferred_element_type=jnp.float32)


def mlp_kernel(count, half, sent, conv_ref, grad_ref, win_ref, bias_ref, wout_ref, *rest):
    outs, (tall_conv, tall_grad, pre_ref, back_ref, slope_ref, total_ref) = rest[-6 - len(sent) : -6], rest[-6:]
    part, channels = conv_ref.shape[1:]
    wide = round_up(part, HALF)
    rows = tall_conv.shape[0] // wide
    owned = channels // count
    block = slope_ref.shape[2]
    steps = win_ref.shape[1] // block
    me = lax.axis_index("azimuth")
    for tall, source in ((tall_conv, conv_ref), (tall_grad, grad_ref)):
        for row in range(rows):
            whole = part // 16 * 16
            tall[row * wide + whole : (row + 1) * wide, :] = jnp.zeros((wide - whole, channels), jnp.bfloat16)
            tall[row * wide : row * wide + part, :] = source[half * rows + row]
    group = 48
    groups = rows * wide // group

    def span(step):
        return slice(step * block, (step + 1) * block)

    def project_pre(step):
        pre_ref[step % 2] = dot_nn(tall_conv[...], win_ref[:, span(step)])

    def project_back(step):
        back_ref[step % 2] = dot_nt(tall_grad[...], wout_ref[span(step), :])

    def slope(step, first, last):
        root = math.sqrt(0.5)
        bias = bias_ref[span(step)].reshape(1, block) * root
        for g in range(first, last):
            some = slice(g * group, (g + 1) * group)
            value = back_ref[step % 2, some, :] * twice_gelu_slope(pre_ref[step % 2, some, :] * root + bias)
            slope_ref[step % 2, some, :] = value.astype(jnp.bfloat16)

    def gather(step):
        term = dot_nt(win_ref[:, span(step)], slope_ref[step % 2])
        total_ref[...] = term if step == 0 else total_ref[...] + term

    project_pre(0)
    project_back(0)
    thirds = [groups * n // 3 for n in range(4)]
    for step in range(steps):
        if step + 1 < steps:
            project_pre(step + 1)
        slope(step, thirds[0], thirds[1])
        if step:
            gather(step - 1)
        slope(step, thirds[1], thirds[2])
        if step + 1 < steps:
            project_back(step + 1)
        slope(step, thirds[2], thirds[3])
    gather(steps - 1)
    for out, (k, start, size) in zip(outs, sent):
        first = partner(me, k, count, 1) * owned + start
        out[...] = (0.5 * total_ref[pl.ds(pl.multiple_of(first, 16), size), :]).astype(jnp.bfloat16)


def mlp(conv_out, grad_out, w_in, b_in, w_out, count, half, halves, sent, after):
    rows, part, channels = conv_out.shape
    rows //= halves
    block = 256
    wide = round_up(part, HALF)
    vmem = pl.BlockSpec(memory_space=VMEM)
    out_shape = [jax.ShapeDtypeStruct((size, rows * wide), jnp.bfloat16) for _, _, size in sent]
    return pl.pallas_call(
        functools.partial(mlp_kernel, count, half, sent),
        in_specs=[vmem] * 5 + [pl.BlockSpec(memory_space=pl.ANY)] * len(after),
        out_specs=[vmem] * len(out_shape),
        out_shape=out_shape,
        scratch_shapes=[
            pltpu.VMEM((rows * wide, channels), jnp.bfloat16),
            pltpu.VMEM((rows * wide, channels), jnp.bfloat16),
            pltpu.VMEM((2, rows * wide, block), jnp.float32),
            pltpu.VMEM((2, rows * wide, block), jnp.float32),
            pltpu.VMEM((2, rows * wide, block), jnp.bfloat16),
            pltpu.VMEM((channels, rows * wide), jnp.float32),
        ],
        compiler_params=pltpu.CompilerParams(vmem_limit_bytes=16 * 2**20),
        cost_estimate=NO_COST,
        name="mlp",
    )(conv_out, grad_out, w_in, b_in, w_out, *after)


def analysis_kernel(count, rows, chunk, *refs):
    own_ref, first_ref, second_ref = refs[-3:]
    start, size = chunk
    halves = next(h for h in range(1, rows + 1) if refs[h * count].ndim == 3)
    table_ref = refs[halves * count]
    rows_each = rows // halves
    wide = refs[0].shape[1] // rows_each
    window = table_ref.shape[1] - HALF
    me = lax.axis_index("azimuth")
    sources = [partner(me, k, count, -1) for k in range(count)]
    even = lax.rem(lax.axis_index("polar"), 2) == 0

    def columns(row, k):
        half, row = divmod(row, rows_each)
        piece = refs[half * count + k]
        base = 0 if half == halves - 1 and k > NEAR else start
        first = row * wide // LANES * LANES
        return piece[base : base + size, first : first + window]

    shifts = [row % rows_each * wide % LANES for row in range(rows)]
    for shift in sorted(set(shifts)):
        group = [row for row in range(rows) if shifts[row] == shift]
        total = None
        for k in range(count):
            left = jnp.concatenate([columns(row, k) for row in group], axis=0)
            term = dot_nn(left, table_ref[sources[k], HALF - shift : HALF - shift + window, :])
            total = term if total is None else total + term
        for at, row in enumerate(group):
            mine = total[at * size : (at + 1) * size]
            own_ref[row] = mine
            sent = mine.astype(jnp.bfloat16)
            for above, parity in ((first_ref, even), (second_ref, jnp.logical_not(even))):
                below = second_ref if above is first_ref else first_ref

                @pl.when(parity)
                def _(above=above, below=below, sent=sent, row=row):
                    if row >= rows - REACH:
                        above[row - (rows - REACH)] = sent
                    if row < REACH:
                        below[row] = sent


def analyze(pieces, table, rows, chunk, count, after):
    size = chunk[1]
    width = table.shape[2]
    halo = jax.ShapeDtypeStruct((REACH, size, width), jnp.bfloat16)
    return pl.pallas_call(
        functools.partial(analysis_kernel, count, rows, chunk),
        in_specs=[pl.BlockSpec(memory_space=VMEM)] * (len(pieces) + 1)
        + [pl.BlockSpec(memory_space=pl.ANY)] * len(after),
        out_specs=[pl.BlockSpec(memory_space=VMEM)] * 3,
        out_shape=[jax.ShapeDtypeStruct((rows, size, width), jnp.float32), halo, halo],
        compiler_params=pltpu.CompilerParams(vmem_limit_bytes=12 * 2**20),
        cost_estimate=NO_COST,
        name="analysis",
    )(*pieces, table, *after)


def add_row(accs, spectrum, weight, target_row, filter_row, targets):
    size = spectrum.shape[0]
    masked = jnp.concatenate([jnp.where(target_row == t, weight, 0.0) for t in targets], axis=0)
    gains = dot_nn(masked.astype(jnp.bfloat16), filter_row)
    whole = (gains.shape[1] // 2) // LANES * LANES - LANES
    spec_re = spectrum[:, :whole]
    spec_im = spectrum[:, whole : 2 * whole]
    spec_x = spectrum[:, 2 * whole :]
    swapped = pltpu.roll(spec_x, HALF, 1)
    for at, target in enumerate(targets):
        gain = gains[at * size : (at + 1) * size]
        gain_re = gain[:, :whole]
        gain_rx = gain[:, whole : whole + LANES]
        gain_im = gain[:, whole + LANES : 2 * whole + LANES]
        gain_ix = gain[:, 2 * whole + LANES :]
        acc_re, acc_im, acc_x = accs[target]
        acc_re = acc_re + (gain_re * spec_re + gain_im * spec_im)
        acc_im = acc_im + (gain_re * spec_im - gain_im * spec_re)
        acc_x = acc_x + (gain_rx * spec_x + gain_ix * swapped)
        accs[target] = acc_re, acc_im, acc_x


def split_tiles(value):
    whole = (value.shape[1] - LANES) // 2
    return value[:, :whole], value[:, whole : 2 * whole], value[:, 2 * whole :]


def own_kernel(own_ref, weight_ref, target_ref, filter_ref, out_ref):
    rows, size, width = own_ref.shape
    accs = {t: split_tiles(jnp.zeros((size, width), jnp.float32)) for t in range(rows)}
    for row in range(rows):
        at = row + REACH
        targets = [t for t in range(rows) if abs(row - t) <= REACH]
        add_row(accs, own_ref[row], weight_ref[...], target_ref[at : at + 1, :], filter_ref[at], targets)
    for t in range(rows):
        out_ref[t] = jnp.concatenate(accs[t], axis=1)


def own_terms(own, weight, target, filters):
    return pl.pallas_call(
        own_kernel,
        in_specs=[pl.BlockSpec(memory_space=VMEM)] * 4,
        out_specs=pl.BlockSpec(memory_space=VMEM),
        out_shape=jax.ShapeDtypeStruct(own.shape, jnp.float32),
        compiler_params=pltpu.CompilerParams(vmem_limit_bytes=12 * 2**20),
        cost_estimate=NO_COST,
        name="own_terms",
    )(own, weight, target, filters)


def folded(part, lanes):
    if lanes % LANES == HALF:
        return round_up(part, HALF) // 2, 2 * lanes
    return part, lanes


def finish_kernel(count, part_ref, first_ref, second_ref, weight_ref, target_ref, filter_ref, table_ref, *rest):
    outs, stacked_ref, grid_ref = rest[-count - 2 : -2], rest[-2], rest[-1]
    rows, size, width = part_ref.shape
    even = lax.rem(lax.axis_index("polar"), 2) == 0

    def combine(low_ref, high_ref):
        accs = {t: split_tiles(part_ref[t]) for t in range(rows)}
        for side, base in ((low_ref, -REACH), (high_ref, rows)):
            for h in range(REACH):
                at = base + h + REACH
                targets = [t for t in range(rows) if abs(base + h - t) <= REACH]
                add_row(
                    accs,
                    side[h].astype(jnp.float32),
                    weight_ref[...],
                    target_ref[at : at + 1, :],
                    filter_ref[at],
                    targets,
                )
        for t in range(rows):
            stacked_ref[t * size : (t + 1) * size, :] = jnp.concatenate(accs[t], axis=1).astype(jnp.bfloat16)

    pl.when(even)(lambda: combine(second_ref, first_ref))
    pl.when(jnp.logical_not(even))(lambda: combine(first_ref, second_ref))
    me = lax.axis_index("azimuth")
    grid_ref[...] = dot_nt(table_ref[...], stacked_ref[...])
    wide = grid_ref.shape[0] // count
    for k in range(count):
        first = pl.multiple_of(partner(me, k, count, 1) * wide, HALF)
        value = grid_ref[pl.ds(first, wide), :].astype(jnp.bfloat16)
        height, fold = outs[k].shape[0], outs[k].shape[1] // (rows * size)
        if fold == 1:
            outs[k][...] = value[:height]
        else:
            parts = [value[f * height : (f + 1) * height] for f in range(fold)]
            outs[k][...] = jnp.concatenate(parts, axis=1)


def finish(own, first, second, weight, target, filters, table, count, part, after):
    rows, size, width = own.shape
    return pl.pallas_call(
        functools.partial(finish_kernel, count),
        in_specs=[pl.BlockSpec(memory_space=VMEM)] * 7 + [pl.BlockSpec(memory_space=pl.ANY)] * len(after),
        out_specs=[pl.BlockSpec(memory_space=VMEM)] * count,
        out_shape=[jax.ShapeDtypeStruct(folded(part, rows * size), jnp.bfloat16)] * count,
        scratch_shapes=[
            pltpu.VMEM((rows * size, width), jnp.bfloat16),
            pltpu.VMEM((table.shape[0], rows * size), jnp.float32),
        ],
        compiler_params=pltpu.CompilerParams(vmem_limit_bytes=12 * 2**20),
        cost_estimate=NO_COST,
        name="finish",
    )(own, first, second, weight, target, filters, table, *after)


def add_kernel(count, chunks, grad_ref, *refs):
    pieces, out_ref = refs[:-1], refs[-1]
    rows, part, channels = grad_ref.shape
    me = lax.axis_index("azimuth")

    def unfold(piece, base, size, lanes):
        height = piece.shape[0]
        parts = [
            piece[: min(height, part - first), at + base : at + base + size]
            for first, at in zip(range(0, part, height), range(0, piece.shape[1], lanes))
        ]
        return jnp.concatenate(parts, axis=0)

    def add(mine):
        order = [[k for k in range(count) if partner_static(mine, k, count, -1) == s][0] for s in range(count)]
        for row in range(rows):
            conv = jnp.concatenate(
                [
                    unfold(pieces[q * count + k], row * size, size, rows * size)
                    for k in order
                    for q, (_, size) in enumerate(chunks)
                ],
                axis=1,
            )
            out_ref[row] = (grad_ref[row].astype(jnp.float32) + conv.astype(jnp.float32)).astype(
                jnp.bfloat16
            )

    for mine in range(count):
        pl.when(me == mine)(functools.partial(add, mine))


def add_back(grad_out, pieces, count, chunks):
    return pl.pallas_call(
        functools.partial(add_kernel, count, chunks),
        in_specs=[pl.BlockSpec(memory_space=VMEM)] * (1 + len(pieces)),
        out_specs=pl.BlockSpec(memory_space=VMEM),
        out_shape=jax.ShapeDtypeStruct(grad_out.shape, jnp.bfloat16),
        compiler_params=pltpu.CompilerParams(vmem_limit_bytes=12 * 2**20),
        cost_estimate=NO_COST,
        name="add_back",
    )(grad_out, *pieces)


def prepare_kernel(count, chunks, weight_ref, filt_ref, offset_ref, forth_ref, back_ref, *outs):
    filter_out, target_out, forth_out, back_out = outs[:4]
    forth_out[...] = forth_ref[...]
    back_out[...] = back_ref[...]
    bases, channels = weight_ref.shape
    lats, width = filt_ref.shape[1:]
    ext, depth = target_out.shape
    rows = ext - 2 * REACH
    modes = width // 2
    whole = modes // LANES * LANES
    used = TERMS * bases
    weight = pltpu.roll(
        weight_ref[...], lax.rem(count - lax.axis_index("azimuth"), count) * (channels // count), 1
    )[:, : channels // count]
    parts = []
    for _ in range(TERMS):
        rounded = weight.astype(jnp.bfloat16).astype(jnp.float32)
        parts.append(rounded)
        weight = weight - rounded
    parts.append(jnp.zeros((depth - used, weight.shape[1]), jnp.float32))
    weight = jnp.concatenate(parts, axis=0).T
    for (start, size), out in zip(chunks, outs[4:]):
        out[...] = weight[start : start + size]
    start_lat = lax.axis_index("polar") * rows
    table = filt_ref[...].reshape(bases * lats, width)
    base = lax.broadcasted_iota(jnp.int32, (depth, bases * lats), 0)
    valid = base < used
    for _ in range(TERMS - 1):
        base = jnp.where(base >= bases, base - bases, base)
    column = lax.broadcasted_iota(jnp.int32, (depth, bases * lats), 1)
    for i in range(ext):
        lat = start_lat + (i - REACH)
        inside = (lat >= 0) & (lat < lats)
        lat = jnp.clip(lat, 0, lats - 1)
        pick = jnp.where(valid & (column == base * lats + lat), 1.0, 0.0).astype(jnp.bfloat16)
        row = dot_nn(pick, table)
        real, imag = row[:, :modes], row[:, modes:]
        rest_re, rest_im = real[:, whole:], imag[:, whole:]
        filter_out[i] = jnp.concatenate(
            [real[:, :whole], rest_re, rest_re, imag[:, :whole], rest_im, -rest_im], axis=1
        ).astype(jnp.bfloat16)
        local = jnp.where(inside, offset_ref[pl.ds(lat, 1), :] - start_lat, -1)
        spare = jnp.full((1, depth - used), -1, jnp.int32)
        target_out[i : i + 1, :] = jnp.concatenate([local] * TERMS + [spare], axis=1)


def prepare(basis_weight, filt, offsets, forth, back, rows, count, chunks):
    bases = filt.shape[0]
    width = filt.shape[2]
    ext = rows + 2 * REACH
    depth = round_up(TERMS * bases, 16)
    shapes = [
        jax.ShapeDtypeStruct((ext, depth, width + LANES), jnp.bfloat16),
        jax.ShapeDtypeStruct((ext, depth), jnp.int32),
        jax.ShapeDtypeStruct(forth.shape, forth.dtype),
        jax.ShapeDtypeStruct(back.shape, back.dtype),
    ] + [jax.ShapeDtypeStruct((size, depth), jnp.float32) for _, size in chunks]
    return pl.pallas_call(
        functools.partial(prepare_kernel, count, chunks),
        in_specs=[pl.BlockSpec(memory_space=VMEM)] * 5,
        out_specs=[pl.BlockSpec(memory_space=VMEM)] * len(shapes),
        out_shape=shapes,
        compiler_params=pltpu.CompilerParams(vmem_limit_bytes=16 * 2**20),
        cost_estimate=NO_COST,
        name="prepare",
    )(basis_weight, filt, offsets, forth, back)


def halo(first, second):
    bands, count = lax.axis_size("polar"), lax.axis_size("azimuth")
    blocks = []
    for odd, block in ((0, first), (1, second)):
        pairs = []
        for a in range(bands):
            other = ((a + odd) ^ 1) - odd
            for b in range(count):
                paired = 0 <= other < bands
                target = (other, b) if paired else (a, b ^ 1 if b ^ 1 < count else b)
                pairs.append((a * count + b, target[0] * count + target[1]))
        blocks.append(lax.ppermute(block, ("polar", "azimuth"), pairs))
    return blocks


def on_device(chunks, conv_out, grad_out, w_in, b_in, w_out, basis_weight, filt, offsets):
    rows, part, channels = conv_out.shape
    count = lax.axis_size("azimuth")
    forth, back = tables(count, part, filt.shape[2] // 2)
    forth, back = jnp.asarray(forth), jnp.asarray(back)
    owned = channels // count
    halves = 2 if rows % 2 == 0 else 1
    pieces = []
    for half in range(halves):
        final = half == halves - 1
        far = range(NEAR + 1, count)
        sent = [(k, 0, owned) for k in range(count)]
        if final:
            sent[NEAR + 1 :] = [(k,) + chunk for chunk in chunks for k in far]
        blocks = mlp(conv_out, grad_out, w_in, b_in, w_out, count, half, halves, sent, pieces[1:2])
        pieces += [exchange(blocks[k], k, count) for k in range(NEAR + 1 if final else count)]
    filters, target, forth, back, *weights = prepare(
        basis_weight, filt, offsets, forth, back, rows, count, chunks
    )
    spectra, terms, grids, returned = {}, {}, {}, []

    def open_chunk(q, after):
        tail = [exchange(blocks[NEAR + 1 + q * len(far) + i], k, count) for i, k in enumerate(far)]
        own, first, second = analyze(pieces + tail, forth, rows, chunks[q], count, after)
        spectra[q] = halo(first, second)
        terms[q] = own_terms(own, weights[q], target, filters)

    def close_chunk(q):
        after = [returned[(q - 1) * count + 1]] if q else []
        grids[q] = finish(terms[q], *spectra[q], weights[q], target, filters, back, count, part, after)
        returned.extend(exchange(grids[q][k], k, count) for k in range(count))

    last = len(chunks) - 1
    open_chunk(0, [])
    if last > 0:
        open_chunk(1, [terms[0]])
    for q in range(last + 1):
        close_chunk(q)
        if q + 2 <= last:
            open_chunk(q + 2, [grids[q][0]])
    return add_back(grad_out, returned, count, chunks)


def solution(mesh):
    grid = P(("member", "polar"), "azimuth", None)

    def run(conv_out, grad_out, *others):
        owned = conv_out.shape[2] // mesh.shape["azimuth"]
        half = owned // 32 * 16
        sizes = [half, owned - half] if half else [owned]
        chunks = tuple((sum(sizes[:q]), size) for q, size in enumerate(sizes))
        return jax.shard_map(
            functools.partial(on_device, chunks),
            mesh=mesh,
            in_specs=(grid, grid) + (P(),) * 6,
            out_specs=grid,
            check_vma=False,
        )(conv_out, grad_out, *others)

    return run
```

```python
import functools
import math

import jax
import jax.numpy as jnp
import ml_dtypes
import numpy as np
from jax import lax
from jax.experimental import pallas as pl
from jax.experimental.pallas import tpu as pltpu
from jax.sharding import PartitionSpec as P

REACH = 3
LANES = 128
HALF = 64
TERMS = 3
NEAR = 1
VMEM = pltpu.MemorySpace.VMEM
NO_COST = pl.CostEstimate(flops=0, bytes_accessed=0, transcendentals=0)


def round_up(value, unit):
    return -(-value // unit) * unit


def partner(me, step, count, sign):
    if count & (count - 1) == 0:
        return me ^ step
    return lax.rem(me + sign * step + count, count)


def far_first(number, count):
    return sorted(range(number), key=lambda i: (i // count, i % count <= NEAR))


def exchange(block, step, count):
    if step == 0:
        return block
    pairs = [(a, int(partner_static(a, step, count))) for a in range(count)]
    return lax.ppermute(block, "azimuth", pairs)


def partner_static(a, step, count, sign=1):
    return a ^ step if count & (count - 1) == 0 else (a + sign * step) % count


def tables(count, part, modes):
    length = count * part
    whole = modes // LANES * LANES
    order = np.concatenate(
        [
            np.arange(whole),
            modes + np.arange(whole),
            np.arange(whole, modes),
            modes + np.arange(whole, modes),
        ]
    )
    positions = np.arange(length)
    waves = np.arange(modes)
    phase = (positions[:, None] * waves[None, :]) % length
    angle = (2.0 * math.pi / length) * phase
    scale = 1.0 / math.sqrt(length)
    factor = np.where(waves == 0, 1.0, 2.0)
    analysis = np.concatenate([np.cos(angle), -np.sin(angle)], axis=1) * scale
    synth = np.concatenate([np.cos(angle) * factor, -np.sin(angle) * factor], axis=1) * scale
    analysis = analysis.astype(np.float32).astype(ml_dtypes.bfloat16)[:, order]
    synth = synth.astype(np.float32).astype(ml_dtypes.bfloat16)[:, order]
    wide = round_up(part, HALF)
    window = round_up(HALF + wide, LANES)
    forth = np.zeros((count, HALF + window, 2 * modes), ml_dtypes.bfloat16)
    back = np.zeros((count * wide, 2 * modes), ml_dtypes.bfloat16)
    for s in range(count):
        forth[s, HALF : HALF + part] = analysis[s * part : (s + 1) * part]
        back[s * wide : s * wide + part] = synth[s * part : (s + 1) * part]
    return forth, back


def gelu_slope(values):
    normal_cdf = 0.5 + 0.5 * lax.erf(values * math.sqrt(0.5))
    density = jnp.exp2((-0.5 / math.log(2.0)) * (values * values)) * (1.0 / math.sqrt(2.0 * math.pi))
    return normal_cdf + values * density


def dot_nt(left, right):
    return lax.dot_general(left, right, (((1,), (1,)), ((), ())), preferred_element_type=jnp.float32)


def dot_nn(left, right):
    return jnp.dot(left, right, preferred_element_type=jnp.float32)


def mlp_kernel(count, half, sent, chunks, conv_ref, grad_ref, win_ref, bias_ref, wout_ref, *rest):
    outs, (tall_conv, tall_grad, pre_ref, back_ref, slope_ref, total_ref) = rest[-6 - len(sent) : -6], rest[-6:]
    part, channels = conv_ref.shape[1:]
    wide = round_up(part, HALF)
    rows = tall_conv.shape[0] // wide
    owned = channels // count
    block = slope_ref.shape[2]
    steps = win_ref.shape[1] // block
    me = lax.axis_index("azimuth")
    for tall, source in ((tall_conv, conv_ref), (tall_grad, grad_ref)):
        for row in range(rows):
            whole = part // 16 * 16
            tall[row * wide + whole : (row + 1) * wide, :] = jnp.zeros((wide - whole, channels), jnp.bfloat16)
            tall[row * wide : row * wide + part, :] = source[half * rows + row]
    group = 48
    groups = rows * wide // group

    def span(step):
        return slice(step * block, (step + 1) * block)

    def project_pre(step):
        pre_ref[step % 2] = dot_nn(tall_conv[...], win_ref[:, span(step)])

    def project_back(step):
        back_ref[step % 2] = dot_nt(tall_grad[...], wout_ref[span(step), :])

    def slope(step, first, last):
        bias = bias_ref[span(step)].reshape(1, block)
        for g in range(first, last):
            some = slice(g * group, (g + 1) * group)
            value = back_ref[step % 2, some, :] * gelu_slope(pre_ref[step % 2, some, :] + bias)
            slope_ref[step % 2, some, :] = value.astype(jnp.bfloat16)

    def gather(step):
        term = dot_nt(win_ref[:, span(step)], slope_ref[step % 2])
        total_ref[...] = term if step == 0 else total_ref[...] + term

    project_pre(0)
    project_back(0)
    thirds = [groups * n // 3 for n in range(4)]
    for step in range(steps):
        if step + 1 < steps:
            project_pre(step + 1)
        slope(step, thirds[0], thirds[1])
        if step:
            gather(step - 1)
        slope(step, thirds[1], thirds[2])
        if step + 1 < steps:
            project_back(step + 1)
        slope(step, thirds[2], thirds[3])
    gather(steps - 1)
    for out, (k, start, size) in zip(outs, sent):
        target = partner(me, k, count, 1)
        for begin, width in chunks:
            if start <= begin < start + size:
                first = pl.multiple_of(count * begin + target * width, 32)
                out[begin - start : begin - start + width, :] = total_ref[pl.ds(first, width), :].astype(
                    jnp.bfloat16
                )


def mlp(conv_out, grad_out, w_in, b_in, w_out, count, half, halves, sent, chunks, after):
    rows, part, channels = conv_out.shape
    rows //= halves
    block = 256
    wide = round_up(part, HALF)
    vmem = pl.BlockSpec(memory_space=VMEM)
    out_shape = [jax.ShapeDtypeStruct((size, rows * wide), jnp.bfloat16) for _, _, size in sent]
    return pl.pallas_call(
        functools.partial(mlp_kernel, count, half, sent, chunks),
        in_specs=[vmem] * 5 + [pl.BlockSpec(memory_space=pl.ANY)] * len(after),
        out_specs=[vmem] * len(out_shape),
        out_shape=out_shape,
        scratch_shapes=[
            pltpu.VMEM((rows * wide, channels), jnp.bfloat16),
            pltpu.VMEM((rows * wide, channels), jnp.bfloat16),
            pltpu.VMEM((2, rows * wide, block), jnp.float32),
            pltpu.VMEM((2, rows * wide, block), jnp.float32),
            pltpu.VMEM((2, rows * wide, block), jnp.bfloat16),
            pltpu.VMEM((channels, rows * wide), jnp.float32),
        ],
        compiler_params=pltpu.CompilerParams(vmem_limit_bytes=16 * 2**20),
        cost_estimate=NO_COST,
        name="mlp",
    )(conv_out, grad_out, w_in, b_in, w_out, *after)


def analysis_kernel(count, rows, chunk, *refs):
    own_ref, first_ref, second_ref = refs[-3:]
    start, size = chunk
    halves = next(h for h in range(1, rows + 1) if refs[h * count].ndim == 3)
    table_ref = refs[halves * count]
    ranks = far_first(halves * count, count)
    pieces = [refs[ranks.index(i)] for i in range(halves * count)]
    rows_each = rows // halves
    wide = refs[0].shape[1] // rows_each
    window = table_ref.shape[1] - HALF
    me = lax.axis_index("azimuth")
    sources = [partner(me, k, count, -1) for k in range(count)]
    even = lax.rem(lax.axis_index("polar"), 2) == 0

    def columns(row, k):
        half, row = divmod(row, rows_each)
        piece = pieces[half * count + k]
        base = 0 if half == halves - 1 and k > NEAR else start
        first = row * wide // LANES * LANES
        return piece[base : base + size, first : first + window]

    shifts = [row % rows_each * wide % LANES for row in range(rows)]
    for shift in sorted(set(shifts)):
        group = [row for row in range(rows) if shifts[row] == shift]
        total = None
        for k in range(count):
            left = jnp.concatenate([columns(row, k) for row in group], axis=0)
            term = dot_nn(left, table_ref[sources[k], HALF - shift : HALF - shift + window, :])
            total = term if total is None else total + term
        for at, row in enumerate(group):
            mine = total[at * size : (at + 1) * size]
            own_ref[row] = mine
            sent = mine.astype(jnp.bfloat16)
            for above, parity in ((first_ref, even), (second_ref, jnp.logical_not(even))):
                below = second_ref if above is first_ref else first_ref

                @pl.when(parity)
                def _(above=above, below=below, sent=sent, row=row):
                    if row >= rows - REACH:
                        above[row - (rows - REACH)] = sent
                    if row < REACH:
                        below[row] = sent


def analyze(pieces, table, rows, chunk, count, after):
    size = chunk[1]
    width = table.shape[2]
    halo = jax.ShapeDtypeStruct((REACH, size, width), jnp.bfloat16)
    return pl.pallas_call(
        functools.partial(analysis_kernel, count, rows, chunk),
        in_specs=[pl.BlockSpec(memory_space=VMEM)] * (len(pieces) + 1)
        + [pl.BlockSpec(memory_space=pl.ANY)] * len(after),
        out_specs=[pl.BlockSpec(memory_space=VMEM)] * 3,
        out_shape=[jax.ShapeDtypeStruct((rows, size, width), jnp.float32), halo, halo],
        compiler_params=pltpu.CompilerParams(vmem_limit_bytes=12 * 2**20),
        cost_estimate=NO_COST,
        name="analysis",
    )(*(pieces[i] for i in far_first(len(pieces), count)), table, *after)


def add_row(accs, spectrum, weight, target_row, filter_row, targets):
    size = spectrum.shape[0]
    masked = jnp.concatenate([jnp.where(target_row == t, weight, 0.0) for t in targets], axis=0)
    gains = dot_nn(masked.astype(jnp.bfloat16), filter_row)
    whole = (gains.shape[1] // 2) // LANES * LANES - LANES
    spec_re = spectrum[:, :whole]
    spec_im = spectrum[:, whole : 2 * whole]
    spec_x = spectrum[:, 2 * whole :]
    swapped = pltpu.roll(spec_x, HALF, 1)
    for at, target in enumerate(targets):
        gain = gains[at * size : (at + 1) * size]
        gain_re = gain[:, :whole]
        gain_rx = gain[:, whole : whole + LANES]
        gain_im = gain[:, whole + LANES : 2 * whole + LANES]
        gain_ix = gain[:, 2 * whole + LANES :]
        acc_re, acc_im, acc_x = accs[target]
        acc_re = acc_re + (gain_re * spec_re + gain_im * spec_im)
        acc_im = acc_im + (gain_re * spec_im - gain_im * spec_re)
        acc_x = acc_x + (gain_rx * spec_x + gain_ix * swapped)
        accs[target] = acc_re, acc_im, acc_x


def split_tiles(value):
    whole = (value.shape[1] - LANES) // 2
    return value[:, :whole], value[:, whole : 2 * whole], value[:, 2 * whole :]


def own_kernel(own_ref, weight_ref, target_ref, filter_ref, out_ref):
    rows, size, width = own_ref.shape
    accs = {t: split_tiles(jnp.zeros((size, width), jnp.float32)) for t in range(rows)}
    for row in range(rows):
        at = row + REACH
        targets = [t for t in range(rows) if abs(row - t) <= REACH]
        add_row(accs, own_ref[row], weight_ref[...], target_ref[at : at + 1, :], filter_ref[at], targets)
    for t in range(rows):
        out_ref[t] = jnp.concatenate(accs[t], axis=1)


def own_terms(own, weight, target, filters):
    return pl.pallas_call(
        own_kernel,
        in_specs=[pl.BlockSpec(memory_space=VMEM)] * 4,
        out_specs=pl.BlockSpec(memory_space=VMEM),
        out_shape=jax.ShapeDtypeStruct(own.shape, jnp.float32),
        compiler_params=pltpu.CompilerParams(vmem_limit_bytes=12 * 2**20),
        cost_estimate=NO_COST,
        name="own_terms",
    )(own, weight, target, filters)


def finish_kernel(count, part_ref, first_ref, second_ref, weight_ref, target_ref, filter_ref, table_ref, *rest):
    outs, stacked_ref, grid_ref = rest[-count - 2 : -2], rest[-2], rest[-1]
    rows, size, width = part_ref.shape
    part = outs[0].shape[0]
    even = lax.rem(lax.axis_index("polar"), 2) == 0

    def combine(low_ref, high_ref):
        accs = {t: split_tiles(part_ref[t]) for t in range(rows)}
        for side, base in ((low_ref, -REACH), (high_ref, rows)):
            for h in range(REACH):
                at = base + h + REACH
                targets = [t for t in range(rows) if abs(base + h - t) <= REACH]
                add_row(
                    accs,
                    side[h].astype(jnp.float32),
                    weight_ref[...],
                    target_ref[at : at + 1, :],
                    filter_ref[at],
                    targets,
                )
        for t in range(rows):
            stacked_ref[t * size : (t + 1) * size, :] = jnp.concatenate(accs[t], axis=1).astype(jnp.bfloat16)

    pl.when(even)(lambda: combine(second_ref, first_ref))
    pl.when(jnp.logical_not(even))(lambda: combine(first_ref, second_ref))
    me = lax.axis_index("azimuth")
    grid_ref[...] = dot_nt(table_ref[...], stacked_ref[...])
    wide = grid_ref.shape[0] // count
    for k in range(count):
        first = pl.multiple_of(partner(me, k, count, 1) * wide, HALF)
        outs[k][...] = grid_ref[pl.ds(first, wide), :][:part].astype(jnp.bfloat16)


def finish(own, first, second, weight, target, filters, table, count, part, after):
    rows, size, width = own.shape
    return pl.pallas_call(
        functools.partial(finish_kernel, count),
        in_specs=[pl.BlockSpec(memory_space=VMEM)] * 7 + [pl.BlockSpec(memory_space=pl.ANY)] * len(after),
        out_specs=[pl.BlockSpec(memory_space=VMEM)] * count,
        out_shape=[jax.ShapeDtypeStruct((part, rows * size), jnp.bfloat16)] * count,
        scratch_shapes=[
            pltpu.VMEM((rows * size, width), jnp.bfloat16),
            pltpu.VMEM((table.shape[0], rows * size), jnp.float32),
        ],
        compiler_params=pltpu.CompilerParams(vmem_limit_bytes=12 * 2**20),
        cost_estimate=NO_COST,
        name="finish",
    )(own, first, second, weight, target, filters, table, *after)


def add_kernel(count, chunk, grad_ref, *refs):
    out_ref, tall_ref = refs[-2:]
    ranks = far_first(count, count)
    pieces = [refs[ranks.index(k)] for k in range(count)]
    part, rows, _ = out_ref.shape
    start, size = chunk
    me = lax.axis_index("azimuth")

    def add(tile, mine):
        order = [[k for k in range(count) if partner_static(mine, k, count, -1) == s][0] for s in range(count)]
        lanes = range(tile * LANES, (tile + 1) * LANES)
        for row in range(rows):
            parts = []
            for s in range(lanes[0] // size, lanes[-1] // size + 1):
                low, high = max(lanes[0], s * size) - s * size, min(lanes[-1] + 1, (s + 1) * size) - s * size
                parts.append(pieces[order[s]][:, row * size + low : row * size + high])
            conv = jnp.concatenate(parts, axis=1).astype(jnp.float32)
            first = count * start + tile * LANES
            total = grad_ref[row, :, first : first + LANES].astype(jnp.float32) + conv
            tall_ref[0, pl.ds(row, part, stride=rows), :] = total
        out_ref[...] = tall_ref[0].reshape(part, rows, LANES).astype(jnp.bfloat16)

    for tile in range(count * size // LANES):
        for mine in range(count):
            here = jnp.logical_and(pl.program_id(0) == tile, me == mine)
            pl.when(here)(functools.partial(add, tile, mine))


def add_chunk(grad_out, pieces, chunk, count, before):
    rows, part, channels = grad_out.shape
    start, size = chunk
    vmem = pl.BlockSpec(memory_space=VMEM)
    return pl.pallas_call(
        functools.partial(add_kernel, count, chunk),
        grid=(count * size // LANES,),
        in_specs=[vmem] * (1 + count) + [pl.BlockSpec(memory_space=pl.ANY)] * len(before),
        out_specs=pl.BlockSpec((part, rows, LANES), lambda t: (0, 0, count * start // LANES + t)),
        out_shape=jax.ShapeDtypeStruct((part, rows, channels), jnp.bfloat16),
        scratch_shapes=[pltpu.VMEM((1, rows * part, LANES), jnp.float32)],
        input_output_aliases={1 + count: 0} if before else {},
        compiler_params=pltpu.CompilerParams(vmem_limit_bytes=12 * 2**20),
        cost_estimate=NO_COST,
        name="add_chunk",
    )(grad_out, *(pieces[i] for i in far_first(count, count)), *before)


def prepare_kernel(count, chunks, weight_ref, filt_ref, offset_ref, forth_ref, back_ref, *outs):
    filter_out, target_out, forth_out, back_out = outs[:4]
    forth_out[...] = forth_ref[...]
    back_out[...] = back_ref[...]
    bases, channels = weight_ref.shape
    lats, width = filt_ref.shape[1:]
    ext, depth = target_out.shape
    rows = ext - 2 * REACH
    modes = width // 2
    whole = modes // LANES * LANES
    used = TERMS * bases
    for (start, size), out in zip(chunks, outs[4:]):
        first = count * start + lax.axis_index("azimuth") * size
        weight = pltpu.roll(weight_ref[...], lax.rem(channels - first, channels), 1)[:, :size]
        parts = []
        for _ in range(TERMS):
            rounded = weight.astype(jnp.bfloat16).astype(jnp.float32)
            parts.append(rounded)
            weight = weight - rounded
        parts.append(jnp.zeros((depth - used, size), jnp.float32))
        out[...] = jnp.concatenate(parts, axis=0).T
    start_lat = lax.axis_index("polar") * rows
    table = filt_ref[...].reshape(bases * lats, width)
    base = lax.broadcasted_iota(jnp.int32, (depth, bases * lats), 0)
    valid = base < used
    for _ in range(TERMS - 1):
        base = jnp.where(base >= bases, base - bases, base)
    column = lax.broadcasted_iota(jnp.int32, (depth, bases * lats), 1)
    for i in range(ext):
        lat = start_lat + (i - REACH)
        inside = (lat >= 0) & (lat < lats)
        lat = jnp.clip(lat, 0, lats - 1)
        pick = jnp.where(valid & (column == base * lats + lat), 1.0, 0.0).astype(jnp.bfloat16)
        row = dot_nn(pick, table)
        real, imag = row[:, :modes], row[:, modes:]
        rest_re, rest_im = real[:, whole:], imag[:, whole:]
        filter_out[i] = jnp.concatenate(
            [real[:, :whole], rest_re, rest_re, imag[:, :whole], rest_im, -rest_im], axis=1
        ).astype(jnp.bfloat16)
        local = jnp.where(inside, offset_ref[pl.ds(lat, 1), :] - start_lat, -1)
        spare = jnp.full((1, depth - used), -1, jnp.int32)
        target_out[i : i + 1, :] = jnp.concatenate([local] * TERMS + [spare], axis=1)


def prepare(basis_weight, filt, offsets, forth, back, rows, count, chunks):
    bases = filt.shape[0]
    width = filt.shape[2]
    ext = rows + 2 * REACH
    depth = round_up(TERMS * bases, 16)
    shapes = [
        jax.ShapeDtypeStruct((ext, depth, width + LANES), jnp.bfloat16),
        jax.ShapeDtypeStruct((ext, depth), jnp.int32),
        jax.ShapeDtypeStruct(forth.shape, forth.dtype),
        jax.ShapeDtypeStruct(back.shape, back.dtype),
    ] + [jax.ShapeDtypeStruct((size, depth), jnp.float32) for _, size in chunks]
    return pl.pallas_call(
        functools.partial(prepare_kernel, count, chunks),
        in_specs=[pl.BlockSpec(memory_space=VMEM)] * 5,
        out_specs=[pl.BlockSpec(memory_space=VMEM)] * len(shapes),
        out_shape=shapes,
        compiler_params=pltpu.CompilerParams(vmem_limit_bytes=16 * 2**20),
        cost_estimate=NO_COST,
        name="prepare",
    )(basis_weight, filt, offsets, forth, back)


def halo(first, second):
    bands, count = lax.axis_size("polar"), lax.axis_size("azimuth")
    blocks = []
    for odd, block in ((0, first), (1, second)):
        pairs = []
        for a in range(bands):
            other = ((a + odd) ^ 1) - odd
            for b in range(count):
                paired = 0 <= other < bands
                target = (other, b) if paired else (a, b ^ 1 if b ^ 1 < count else b)
                pairs.append((a * count + b, target[0] * count + target[1]))
        blocks.append(lax.ppermute(block, ("polar", "azimuth"), pairs))
    return blocks


def on_device(chunks, conv_out, grad_out, w_in, b_in, w_out, basis_weight, filt, offsets):
    rows, part, channels = conv_out.shape
    count = lax.axis_size("azimuth")
    forth, back = tables(count, part, filt.shape[2] // 2)
    forth, back = jnp.asarray(forth), jnp.asarray(back)
    owned = channels // count
    halves = 2 if rows % 2 == 0 else 1
    pieces = []
    for half in range(halves):
        final = half == halves - 1
        far = range(NEAR + 1, count)
        sent = [(k, 0, owned) for k in range(count)]
        if final:
            sent[NEAR + 1 :] = [(k,) + chunk for chunk in chunks for k in far]
        blocks = mlp(conv_out, grad_out, w_in, b_in, w_out, count, half, halves, sent, chunks, pieces[1:2])
        steps = [] if final else list(far)
        moved = {k: exchange(blocks[k], k, count) for k in steps + list(range(NEAR + 1))}
        pieces += [moved[k] for k in sorted(moved)]
    filters, target, forth, back, *weights = prepare(
        basis_weight, filt, offsets, forth, back, rows, count, chunks
    )
    spectra, terms, grids, returned = {}, {}, {}, []

    def open_chunk(q, after):
        tail = [exchange(blocks[NEAR + 1 + q * len(far) + i], k, count) for i, k in enumerate(far)]
        own, first, second = analyze(pieces + tail, forth, rows, chunks[q], count, after)
        spectra[q] = halo(first, second)
        terms[q] = own_terms(own, weights[q], target, filters)

    def close_chunk(q):
        after = [returned[(q - 1) * count + 1]] if q else []
        grids[q] = finish(terms[q], *spectra[q], weights[q], target, filters, back, count, part, after)
        blocks = {k: exchange(grids[q][k], k, count) for k in [*far, *range(NEAR + 1)]}
        returned.extend(blocks[k] for k in range(count))

    last = len(chunks) - 1
    open_chunk(0, [])
    if last > 0:
        open_chunk(1, [terms[0]])
    for q in range(last + 1):
        close_chunk(q)
        if q + 2 <= last:
            open_chunk(q + 2, [grids[q][0]])
    total = []
    for q, chunk in enumerate(chunks):
        total = [add_chunk(grad_out, returned[q * count : (q + 1) * count], chunk, count, total)]
    return jnp.transpose(total[0], (1, 0, 2))


def solution(mesh):
    grid = P(("member", "polar"), "azimuth", None)

    def run(conv_out, grad_out, *others):
        owned = conv_out.shape[2] // mesh.shape["azimuth"]
        sizes = [owned]
        if owned % 32 == 0 and owned >= 96:
            big = owned * 3 // 5 // 32 * 32
            sizes = [big, owned - big]
        chunks = tuple((sum(sizes[:q]), size) for q, size in enumerate(sizes))
        return jax.shard_map(
            functools.partial(on_device, chunks),
            mesh=mesh,
            in_specs=(grid, grid) + (P(),) * 6,
            out_specs=grid,
            check_vma=False,
        )(conv_out, grad_out, *others)

    return run
```

```python
import functools
import math

import jax
import jax.numpy as jnp
import ml_dtypes
import numpy as np
from jax import lax
from jax.experimental import pallas as pl
from jax.experimental.pallas import tpu as pltpu
from jax.sharding import PartitionSpec as P

REACH = 3
LANES = 128
HALF = 64
TERMS = 3
NEAR = 1
VMEM = pltpu.MemorySpace.VMEM
NO_COST = pl.CostEstimate(flops=0, bytes_accessed=0, transcendentals=0)


def round_up(value, unit):
    return -(-value // unit) * unit


def partner(me, step, count, sign):
    if count & (count - 1) == 0:
        return me ^ step
    return lax.rem(me + sign * step + count, count)


def far_first(number, count):
    return sorted(range(number), key=lambda i: (i // count, i % count <= NEAR))


def exchange(block, step, count):
    if step == 0:
        return block
    pairs = [(a, int(partner_static(a, step, count))) for a in range(count)]
    return lax.ppermute(block, "azimuth", pairs)


def partner_static(a, step, count, sign=1):
    return a ^ step if count & (count - 1) == 0 else (a + sign * step) % count


def tables(count, part, modes):
    length = count * part
    whole = modes // LANES * LANES
    order = np.concatenate(
        [
            np.arange(whole),
            modes + np.arange(whole),
            np.arange(whole, modes),
            modes + np.arange(whole, modes),
        ]
    )
    positions = np.arange(length)
    waves = np.arange(modes)
    phase = (positions[:, None] * waves[None, :]) % length
    angle = (2.0 * math.pi / length) * phase
    scale = 1.0 / math.sqrt(length)
    factor = np.where(waves == 0, 1.0, 2.0)
    analysis = np.concatenate([np.cos(angle), -np.sin(angle)], axis=1) * scale
    synth = np.concatenate([np.cos(angle) * factor, -np.sin(angle) * factor], axis=1) * scale
    analysis = analysis.astype(np.float32).astype(ml_dtypes.bfloat16)[:, order]
    synth = synth.astype(np.float32).astype(ml_dtypes.bfloat16)[:, order]
    wide = round_up(part, HALF)
    window = round_up(HALF + wide, LANES)
    forth = np.zeros((count, HALF + window, 2 * modes), ml_dtypes.bfloat16)
    back = np.zeros((count * wide, 2 * modes), ml_dtypes.bfloat16)
    for s in range(count):
        forth[s, HALF : HALF + part] = analysis[s * part : (s + 1) * part]
        back[s * wide : s * wide + part] = synth[s * part : (s + 1) * part]
    return forth, back


def gelu_slope(values):
    normal_cdf = 0.5 + 0.5 * lax.erf(values * math.sqrt(0.5))
    density = jnp.exp2((-0.5 / math.log(2.0)) * (values * values)) * (1.0 / math.sqrt(2.0 * math.pi))
    return normal_cdf + values * density


def dot_nt(left, right):
    return lax.dot_general(left, right, (((1,), (1,)), ((), ())), preferred_element_type=jnp.float32)


def dot_nn(left, right):
    return jnp.dot(left, right, preferred_element_type=jnp.float32)


def mlp_kernel(count, half, sent, chunks, conv_ref, grad_ref, win_ref, bias_ref, wout_ref, *rest):
    outs, (tall_conv, tall_grad, pre_ref, back_ref, slope_ref, total_ref) = rest[-6 - len(sent) : -6], rest[-6:]
    part, channels = conv_ref.shape[1:]
    wide = round_up(part, HALF)
    rows = tall_conv.shape[0] // wide
    owned = channels // count
    block = slope_ref.shape[2]
    steps = win_ref.shape[1] // block
    me = lax.axis_index("azimuth")
    for tall, source in ((tall_conv, conv_ref), (tall_grad, grad_ref)):
        for row in range(rows):
            whole = part // 16 * 16
            tall[row * wide + whole : (row + 1) * wide, :] = jnp.zeros((wide - whole, channels), jnp.bfloat16)
            tall[row * wide : row * wide + part, :] = source[half * rows + row]
    group = 48
    groups = rows * wide // group

    def span(step):
        return slice(step * block, (step + 1) * block)

    def project_pre(step):
        pre_ref[step % 2] = dot_nn(tall_conv[...], win_ref[:, span(step)])

    def project_back(step):
        back_ref[step % 2] = dot_nt(tall_grad[...], wout_ref[span(step), :])

    def slope(step, first, last):
        bias = bias_ref[span(step)].reshape(1, block)
        for g in range(first, last):
            some = slice(g * group, (g + 1) * group)
            value = back_ref[step % 2, some, :] * gelu_slope(pre_ref[step % 2, some, :] + bias)
            slope_ref[step % 2, some, :] = value.astype(jnp.bfloat16)

    def gather(step):
        term = dot_nt(win_ref[:, span(step)], slope_ref[step % 2])
        total_ref[...] = term if step == 0 else total_ref[...] + term

    project_pre(0)
    project_back(0)
    thirds = [groups * n // 3 for n in range(4)]
    for step in range(steps):
        if step + 1 < steps:
            project_pre(step + 1)
        slope(step, thirds[0], thirds[1])
        if step:
            gather(step - 1)
        slope(step, thirds[1], thirds[2])
        if step + 1 < steps:
            project_back(step + 1)
        slope(step, thirds[2], thirds[3])
    gather(steps - 1)
    for out, (k, start, size) in zip(outs, sent):
        target = partner(me, k, count, 1)
        for begin, width in chunks:
            if start <= begin < start + size:
                first = pl.multiple_of(count * begin + target * width, 32)
                out[begin - start : begin - start + width, :] = total_ref[pl.ds(first, width), :].astype(
                    jnp.bfloat16
                )


def mlp(conv_out, grad_out, w_in, b_in, w_out, count, half, halves, sent, chunks, after):
    rows, part, channels = conv_out.shape
    rows //= halves
    block = 256
    wide = round_up(part, HALF)
    vmem = pl.BlockSpec(memory_space=VMEM)
    out_shape = [jax.ShapeDtypeStruct((size, rows * wide), jnp.bfloat16) for _, _, size in sent]
    return pl.pallas_call(
        functools.partial(mlp_kernel, count, half, sent, chunks),
        in_specs=[vmem] * 5 + [pl.BlockSpec(memory_space=pl.ANY)] * len(after),
        out_specs=[vmem] * len(out_shape),
        out_shape=out_shape,
        scratch_shapes=[
            pltpu.VMEM((rows * wide, channels), jnp.bfloat16),
            pltpu.VMEM((rows * wide, channels), jnp.bfloat16),
            pltpu.VMEM((2, rows * wide, block), jnp.float32),
            pltpu.VMEM((2, rows * wide, block), jnp.float32),
            pltpu.VMEM((2, rows * wide, block), jnp.bfloat16),
            pltpu.VMEM((channels, rows * wide), jnp.float32),
        ],
        compiler_params=pltpu.CompilerParams(vmem_limit_bytes=16 * 2**20),
        cost_estimate=NO_COST,
        name="mlp",
    )(conv_out, grad_out, w_in, b_in, w_out, *after)


def analysis_kernel(count, rows, chunk, *refs):
    own_ref, first_ref, second_ref = refs[-3:]
    start, size = chunk
    halves = next(h for h in range(1, rows + 1) if refs[h * count].ndim == 3)
    table_ref = refs[halves * count]
    ranks = far_first(halves * count, count)
    pieces = [refs[ranks.index(i)] for i in range(halves * count)]
    rows_each = rows // halves
    wide = refs[0].shape[1] // rows_each
    window = table_ref.shape[1] - HALF
    me = lax.axis_index("azimuth")
    sources = [partner(me, k, count, -1) for k in range(count)]
    even = lax.rem(lax.axis_index("polar"), 2) == 0

    def columns(row, k):
        half, row = divmod(row, rows_each)
        piece = pieces[half * count + k]
        base = 0 if half == halves - 1 and k > NEAR else start
        first = row * wide // LANES * LANES
        return piece[base : base + size, first : first + window]

    shifts = [row % rows_each * wide % LANES for row in range(rows)]
    for shift in sorted(set(shifts)):
        group = [row for row in range(rows) if shifts[row] == shift]
        total = None
        for k in range(count):
            left = jnp.concatenate([columns(row, k) for row in group], axis=0)
            term = dot_nn(left, table_ref[sources[k], HALF - shift : HALF - shift + window, :])
            total = term if total is None else total + term
        for at, row in enumerate(group):
            mine = total[at * size : (at + 1) * size]
            own_ref[row] = mine

    def share(above, below):
        for h in range(REACH):
            above[h] = own_ref[rows - REACH + h].astype(jnp.bfloat16)
            below[h] = own_ref[h].astype(jnp.bfloat16)

    pl.when(even)(lambda: share(first_ref, second_ref))
    pl.when(jnp.logical_not(even))(lambda: share(second_ref, first_ref))


def analyze(pieces, table, rows, chunk, count, after):
    size = chunk[1]
    width = table.shape[2]
    halo = jax.ShapeDtypeStruct((REACH, size, width), jnp.bfloat16)
    return pl.pallas_call(
        functools.partial(analysis_kernel, count, rows, chunk),
        in_specs=[pl.BlockSpec(memory_space=VMEM)] * (len(pieces) + 1)
        + [pl.BlockSpec(memory_space=pl.ANY)] * len(after),
        out_specs=[pl.BlockSpec(memory_space=VMEM)] * 3,
        out_shape=[jax.ShapeDtypeStruct((rows, size, width), jnp.float32), halo, halo],
        compiler_params=pltpu.CompilerParams(vmem_limit_bytes=12 * 2**20),
        cost_estimate=NO_COST,
        name="analysis",
    )(*(pieces[i] for i in far_first(len(pieces), count)), table, *after)


def add_row(accs, spectrum, weight, target_row, filter_row, targets):
    size = spectrum.shape[0]
    masked = jnp.concatenate([jnp.where(target_row == t, weight, 0.0) for t in targets], axis=0)
    gains = dot_nn(masked.astype(jnp.bfloat16), filter_row)
    whole = (gains.shape[1] // 2) // LANES * LANES - LANES
    spec_re = spectrum[:, :whole]
    spec_im = spectrum[:, whole : 2 * whole]
    spec_x = spectrum[:, 2 * whole :]
    swapped = pltpu.roll(spec_x, HALF, 1)
    for at, target in enumerate(targets):
        gain = gains[at * size : (at + 1) * size]
        gain_re = gain[:, :whole]
        gain_rx = gain[:, whole : whole + LANES]
        gain_im = gain[:, whole + LANES : 2 * whole + LANES]
        gain_ix = gain[:, 2 * whole + LANES :]
        acc_re, acc_im, acc_x = accs[target]
        acc_re = acc_re + (gain_re * spec_re + gain_im * spec_im)
        acc_im = acc_im + (gain_re * spec_im - gain_im * spec_re)
        acc_x = acc_x + (gain_rx * spec_x + gain_ix * swapped)
        accs[target] = acc_re, acc_im, acc_x


def split_tiles(value):
    whole = (value.shape[1] - LANES) // 2
    return value[:, :whole], value[:, whole : 2 * whole], value[:, 2 * whole :]


def own_kernel(own_ref, weight_ref, target_ref, filter_ref, out_ref):
    rows, size, width = own_ref.shape
    accs = {t: split_tiles(jnp.zeros((size, width), jnp.float32)) for t in range(rows)}
    for row in range(rows):
        at = row + REACH
        targets = [t for t in range(rows) if abs(row - t) <= REACH]
        add_row(accs, own_ref[row], weight_ref[...], target_ref[at : at + 1, :], filter_ref[at], targets)
    for t in range(rows):
        out_ref[t] = jnp.concatenate(accs[t], axis=1)


def own_terms(own, weight, target, filters):
    return pl.pallas_call(
        own_kernel,
        in_specs=[pl.BlockSpec(memory_space=VMEM)] * 4,
        out_specs=pl.BlockSpec(memory_space=VMEM),
        out_shape=jax.ShapeDtypeStruct(own.shape, jnp.float32),
        compiler_params=pltpu.CompilerParams(vmem_limit_bytes=12 * 2**20),
        cost_estimate=NO_COST,
        name="own_terms",
    )(own, weight, target, filters)


def add_halo(accs, sides, rows, weight_ref, target_ref, filter_ref):
    for side, base in sides:
        for h in range(REACH):
            at = base + h + REACH
            targets = [t for t in range(rows) if abs(base + h - t) <= REACH]
            add_row(
                accs,
                side[h].astype(jnp.float32),
                weight_ref[...],
                target_ref[at : at + 1, :],
                filter_ref[at],
                targets,
            )


def side_kernel(part_ref, first_ref, weight_ref, target_ref, filter_ref, out_ref):
    rows = part_ref.shape[0]
    even = lax.rem(lax.axis_index("polar"), 2) == 0

    def combine(base):
        accs = {t: split_tiles(part_ref[t]) for t in range(rows)}
        add_halo(accs, [(first_ref, base)], rows, weight_ref, target_ref, filter_ref)
        for t in range(rows):
            out_ref[t] = jnp.concatenate(accs[t], axis=1)

    pl.when(even)(lambda: combine(rows))
    pl.when(jnp.logical_not(even))(lambda: combine(-REACH))


def side_terms(own, first, weight, target, filters):
    return pl.pallas_call(
        side_kernel,
        in_specs=[pl.BlockSpec(memory_space=VMEM)] * 5,
        out_specs=pl.BlockSpec(memory_space=VMEM),
        out_shape=jax.ShapeDtypeStruct(own.shape, jnp.float32),
        compiler_params=pltpu.CompilerParams(vmem_limit_bytes=12 * 2**20),
        cost_estimate=NO_COST,
        name="side_terms",
    )(own, first, weight, target, filters)


def finish_kernel(count, swaps, part_ref, *refs):
    halos, (weight_ref, target_ref, filter_ref, table_ref) = refs[:swaps], refs[swaps : swaps + 4]
    outs, stacked_ref, grid_ref = refs[-count - 2 : -2], refs[-2], refs[-1]
    rows, size, width = part_ref.shape
    part = outs[0].shape[0]
    even = lax.rem(lax.axis_index("polar"), 2) == 0

    def combine(bases):
        accs = {t: split_tiles(part_ref[t]) for t in range(rows)}
        sides = list(zip(halos, bases[-swaps:]))
        add_halo(accs, sides, rows, weight_ref, target_ref, filter_ref)
        for t in range(rows):
            stacked_ref[t * size : (t + 1) * size, :] = jnp.concatenate(accs[t], axis=1).astype(jnp.bfloat16)

    pl.when(even)(lambda: combine((rows, -REACH)))
    pl.when(jnp.logical_not(even))(lambda: combine((-REACH, rows)))
    me = lax.axis_index("azimuth")
    grid_ref[...] = dot_nt(table_ref[...], stacked_ref[...])
    wide = grid_ref.shape[0] // count
    for k in range(count):
        first = pl.multiple_of(partner(me, k, count, 1) * wide, HALF)
        outs[k][...] = grid_ref[pl.ds(first, wide), :][:part].astype(jnp.bfloat16)


def finish(own, halos, weight, target, filters, table, count, part, after):
    rows, size, width = own.shape
    return pl.pallas_call(
        functools.partial(finish_kernel, count, len(halos)),
        in_specs=[pl.BlockSpec(memory_space=VMEM)] * (5 + len(halos)) + [pl.BlockSpec(memory_space=pl.ANY)] * len(after),
        out_specs=[pl.BlockSpec(memory_space=VMEM)] * count,
        out_shape=[jax.ShapeDtypeStruct((part, rows * size), jnp.bfloat16)] * count,
        scratch_shapes=[
            pltpu.VMEM((rows * size, width), jnp.bfloat16),
            pltpu.VMEM((table.shape[0], rows * size), jnp.float32),
        ],
        compiler_params=pltpu.CompilerParams(vmem_limit_bytes=12 * 2**20),
        cost_estimate=NO_COST,
        name="finish",
    )(own, *halos, weight, target, filters, table, *after)


def add_kernel(count, chunk, grad_ref, *refs):
    out_ref, tall_ref, done_ref, sems = refs[-4:]
    ranks = far_first(count, count)
    pieces = [refs[ranks.index(k)] for k in range(count)]
    tiles, part, rows, _ = done_ref.shape
    start, size = chunk
    me = lax.axis_index("azimuth")

    def add(tile, mine):
        order = [[k for k in range(count) if partner_static(mine, k, count, -1) == s][0] for s in range(count)]
        lanes = range(tile * LANES, (tile + 1) * LANES)
        for row in range(rows):
            parts = []
            for s in range(lanes[0] // size, lanes[-1] // size + 1):
                low, high = max(lanes[0], s * size) - s * size, min(lanes[-1] + 1, (s + 1) * size) - s * size
                parts.append(pieces[order[s]][:, row * size + low : row * size + high])
            conv = jnp.concatenate(parts, axis=1).astype(jnp.float32)
            first = count * start + tile * LANES
            total = grad_ref[row, :, first : first + LANES].astype(jnp.float32) + conv
            tall_ref[tile, pl.ds(row, part, stride=rows), :] = total
        done_ref[tile] = tall_ref[tile].reshape(part, rows, LANES).astype(jnp.bfloat16)

    copies = []
    for tile in range(tiles):
        for mine in range(count):
            pl.when(me == mine)(functools.partial(add, tile, mine))
        lanes = pl.ds(count * start + tile * LANES, LANES)
        copies.append(pltpu.make_async_copy(done_ref.at[tile], out_ref.at[:, :, lanes], sems.at[tile]))
        copies[-1].start()
    for copy in copies:
        copy.wait()


def add_chunk(grad_out, pieces, chunk, count, before):
    rows, part, channels = grad_out.shape
    start, size = chunk
    tiles = count * size // LANES
    vmem = pl.BlockSpec(memory_space=VMEM)
    anywhere = pl.BlockSpec(memory_space=pl.ANY)
    return pl.pallas_call(
        functools.partial(add_kernel, count, chunk),
        in_specs=[vmem] * (1 + count) + [anywhere] * len(before),
        out_specs=anywhere,
        out_shape=jax.ShapeDtypeStruct((part, rows, channels), jnp.bfloat16),
        scratch_shapes=[
            pltpu.VMEM((tiles, rows * part, LANES), jnp.float32),
            pltpu.VMEM((tiles, part, rows, LANES), jnp.bfloat16),
            pltpu.SemaphoreType.DMA((tiles,)),
        ],
        input_output_aliases={1 + count: 0} if before else {},
        compiler_params=pltpu.CompilerParams(vmem_limit_bytes=12 * 2**20),
        cost_estimate=NO_COST,
        name="add_chunk",
    )(grad_out, *(pieces[i] for i in far_first(count, count)), *before)


def prepare_kernel(count, chunks, weight_ref, filt_ref, offset_ref, forth_ref, back_ref, *outs):
    filter_out, target_out, forth_out, back_out = outs[:4]
    forth_out[...] = forth_ref[...]
    back_out[...] = back_ref[...]
    bases, channels = weight_ref.shape
    lats, width = filt_ref.shape[1:]
    ext, depth = target_out.shape
    rows = ext - 2 * REACH
    modes = width // 2
    whole = modes // LANES * LANES
    used = TERMS * bases
    for (start, size), out in zip(chunks, outs[4:]):
        first = count * start + lax.axis_index("azimuth") * size
        weight = pltpu.roll(weight_ref[...], lax.rem(channels - first, channels), 1)[:, :size]
        parts = []
        for _ in range(TERMS):
            rounded = weight.astype(jnp.bfloat16).astype(jnp.float32)
            parts.append(rounded)
            weight = weight - rounded
        parts.append(jnp.zeros((depth - used, size), jnp.float32))
        out[...] = jnp.concatenate(parts, axis=0).T
    start_lat = lax.axis_index("polar") * rows
    table = filt_ref[...].reshape(bases * lats, width)
    base = lax.broadcasted_iota(jnp.int32, (depth, bases * lats), 0)
    valid = base < used
    for _ in range(TERMS - 1):
        base = jnp.where(base >= bases, base - bases, base)
    column = lax.broadcasted_iota(jnp.int32, (depth, bases * lats), 1)
    for i in range(ext):
        lat = start_lat + (i - REACH)
        inside = (lat >= 0) & (lat < lats)
        lat = jnp.clip(lat, 0, lats - 1)
        pick = jnp.where(valid & (column == base * lats + lat), 1.0, 0.0).astype(jnp.bfloat16)
        row = dot_nn(pick, table)
        real, imag = row[:, :modes], row[:, modes:]
        rest_re, rest_im = real[:, whole:], imag[:, whole:]
        filter_out[i] = jnp.concatenate(
            [real[:, :whole], rest_re, rest_re, imag[:, :whole], rest_im, -rest_im], axis=1
        ).astype(jnp.bfloat16)
        local = jnp.where(inside, offset_ref[pl.ds(lat, 1), :] - start_lat, -1)
        spare = jnp.full((1, depth - used), -1, jnp.int32)
        target_out[i : i + 1, :] = jnp.concatenate([local] * TERMS + [spare], axis=1)


def prepare(basis_weight, filt, offsets, forth, back, rows, count, chunks):
    bases = filt.shape[0]
    width = filt.shape[2]
    ext = rows + 2 * REACH
    depth = round_up(TERMS * bases, 16)
    shapes = [
        jax.ShapeDtypeStruct((ext, depth, width + LANES), jnp.bfloat16),
        jax.ShapeDtypeStruct((ext, depth), jnp.int32),
        jax.ShapeDtypeStruct(forth.shape, forth.dtype),
        jax.ShapeDtypeStruct(back.shape, back.dtype),
    ] + [jax.ShapeDtypeStruct((size, depth), jnp.float32) for _, size in chunks]
    return pl.pallas_call(
        functools.partial(prepare_kernel, count, chunks),
        in_specs=[pl.BlockSpec(memory_space=VMEM)] * 5,
        out_specs=[pl.BlockSpec(memory_space=VMEM)] * len(shapes),
        out_shape=shapes,
        compiler_params=pltpu.CompilerParams(vmem_limit_bytes=16 * 2**20),
        cost_estimate=NO_COST,
        name="prepare",
    )(basis_weight, filt, offsets, forth, back)


def halo(first, second):
    bands, count = lax.axis_size("polar"), lax.axis_size("azimuth")
    blocks = []
    for odd, block in ((0, first), (1, second)):
        pairs = []
        for a in range(bands):
            other = ((a + odd) ^ 1) - odd
            for b in range(count):
                paired = 0 <= other < bands
                target = (other, b) if paired else (a, b ^ 1 if b ^ 1 < count else b)
                pairs.append((a * count + b, target[0] * count + target[1]))
        blocks.append(lax.ppermute(block, ("polar", "azimuth"), pairs))
    return blocks


def on_device(chunks, conv_out, grad_out, w_in, b_in, w_out, basis_weight, filt, offsets):
    rows, part, channels = conv_out.shape
    count = lax.axis_size("azimuth")
    forth, back = tables(count, part, filt.shape[2] // 2)
    forth, back = jnp.asarray(forth), jnp.asarray(back)
    owned = channels // count
    halves = 2 if rows % 2 == 0 else 1
    pieces = []
    for half in range(halves):
        final = half == halves - 1
        far = range(NEAR + 1, count)
        sent = [(k, 0, owned) for k in range(count)]
        if final:
            sent[NEAR + 1 :] = [(k,) + chunk for chunk in chunks for k in far]
        blocks = mlp(conv_out, grad_out, w_in, b_in, w_out, count, half, halves, sent, chunks, pieces[1:2])
        steps = [] if final else list(far)
        moved = {k: exchange(blocks[k], k, count) for k in steps + list(range(NEAR + 1))}
        pieces += [moved[k] for k in sorted(moved)]
    filters, target, forth, back, *weights = prepare(
        basis_weight, filt, offsets, forth, back, rows, count, chunks
    )
    spectra, terms, grids, returned = {}, {}, {}, []

    def open_chunk(q, after):
        tail = [exchange(blocks[NEAR + 1 + q * len(far) + i], k, count) for i, k in enumerate(far)]
        own, first, second = analyze(pieces + tail, forth, rows, chunks[q], count, after)
        spectra[q] = halo(first, second)
        terms[q] = own_terms(own, weights[q], target, filters)

    def close_chunk(q):
        after = [returned[(q - 1) * count + 1]] if q else []
        halos = spectra[q]
        if q == 0:
            terms[q] = side_terms(terms[q], halos[0], weights[q], target, filters)
            halos = halos[1:]
        grids[q] = finish(terms[q], halos, weights[q], target, filters, back, count, part, after)
        blocks = {k: exchange(grids[q][k], k, count) for k in [*far, *range(NEAR + 1)]}
        returned.extend(blocks[k] for k in range(count))

    last = len(chunks) - 1
    open_chunk(0, [])
    if last > 0:
        open_chunk(1, [terms[0]])
    for q in range(last + 1):
        close_chunk(q)
        if q + 2 <= last:
            open_chunk(q + 2, [grids[q][0]])
    total = []
    for q, chunk in enumerate(chunks):
        total = [add_chunk(grad_out, returned[q * count : (q + 1) * count], chunk, count, total)]
    return jnp.transpose(total[0], (1, 0, 2))


def solution(mesh):
    grid = P(("member", "polar"), "azimuth", None)

    def run(conv_out, grad_out, *others):
        owned = conv_out.shape[2] // mesh.shape["azimuth"]
        sizes = [owned]
        if owned % 32 == 0 and owned >= 96:
            big = owned * 3 // 5 // 32 * 32
            sizes = [big, owned - big]
        chunks = tuple((sum(sizes[:q]), size) for q, size in enumerate(sizes))
        return jax.shard_map(
            functools.partial(on_device, chunks),
            mesh=mesh,
            in_specs=(grid, grid) + (P(),) * 6,
            out_specs=grid,
            check_vma=False,
        )(conv_out, grad_out, *others)

    return run
```

```python
import functools
import math

import jax
import jax.numpy as jnp
import ml_dtypes
import numpy as np
from jax import lax
from jax.experimental import pallas as pl
from jax.experimental.pallas import tpu as pltpu
from jax.sharding import PartitionSpec as P

REACH = 3
LANES = 128
HALF = 64
TERMS = 3
NEAR = 1
VMEM = pltpu.MemorySpace.VMEM
NO_COST = pl.CostEstimate(flops=0, bytes_accessed=0, transcendentals=0)


def round_up(value, unit):
    return -(-value // unit) * unit


def partner(me, step, count, sign):
    if count & (count - 1) == 0:
        return me ^ step
    return lax.rem(me + sign * step + count, count)


def far_first(number, count):
    return sorted(range(number), key=lambda i: (i // count, i % count <= NEAR))


def exchange(block, step, count):
    if step == 0:
        return block
    pairs = [(a, int(partner_static(a, step, count))) for a in range(count)]
    return lax.ppermute(block, "azimuth", pairs)


def partner_static(a, step, count, sign=1):
    return a ^ step if count & (count - 1) == 0 else (a + sign * step) % count


def tables(count, part, modes):
    length = count * part
    whole = modes // LANES * LANES
    order = np.concatenate(
        [
            np.arange(whole),
            modes + np.arange(whole),
            np.arange(whole, modes),
            modes + np.arange(whole, modes),
        ]
    )
    positions = np.arange(length)
    waves = np.arange(modes)
    phase = (positions[:, None] * waves[None, :]) % length
    angle = (2.0 * math.pi / length) * phase
    scale = 1.0 / math.sqrt(length)
    factor = np.where(waves == 0, 1.0, 2.0)
    analysis = np.concatenate([np.cos(angle), -np.sin(angle)], axis=1) * scale
    synth = np.concatenate([np.cos(angle) * factor, -np.sin(angle) * factor], axis=1) * scale
    analysis = analysis.astype(np.float32).astype(ml_dtypes.bfloat16)[:, order]
    synth = synth.astype(np.float32).astype(ml_dtypes.bfloat16)[:, order]
    wide = round_up(part, HALF)
    window = round_up(HALF + wide, LANES)
    forth = np.zeros((count, HALF + window, 2 * modes), ml_dtypes.bfloat16)
    back = np.zeros((count * wide, 2 * modes), ml_dtypes.bfloat16)
    for s in range(count):
        forth[s, HALF : HALF + part] = analysis[s * part : (s + 1) * part]
        back[s * wide : s * wide + part] = synth[s * part : (s + 1) * part]
    return forth, back


def gelu_slope(values):
    normal_cdf = 0.5 + 0.5 * lax.erf(values * math.sqrt(0.5))
    density = jnp.exp2((-0.5 / math.log(2.0)) * (values * values)) * (1.0 / math.sqrt(2.0 * math.pi))
    return normal_cdf + values * density


def dot_nt(left, right):
    return lax.dot_general(left, right, (((1,), (1,)), ((), ())), preferred_element_type=jnp.float32)


def dot_nn(left, right):
    return jnp.dot(left, right, preferred_element_type=jnp.float32)


def mlp_kernel(count, half, sent, chunks, conv_ref, grad_ref, win_ref, bias_ref, wout_ref, *rest):
    outs, (tall_conv, tall_grad, pre_ref, back_ref, slope_ref, total_ref) = rest[-6 - len(sent) : -6], rest[-6:]
    part, channels = conv_ref.shape[1:]
    wide = round_up(part, HALF)
    rows = tall_conv.shape[0] // wide
    owned = channels // count
    block = pre_ref.shape[2]
    steps = win_ref.shape[1] // block
    me = lax.axis_index("azimuth")
    def stack(tall, source):
        for row in range(rows):
            whole = part // 16 * 16
            tall[row * wide + whole : (row + 1) * wide, :] = jnp.zeros((wide - whole, channels), jnp.bfloat16)
            tall[row * wide : row * wide + part, :] = source[half * rows + row]

    group = 48
    groups = rows * wide // group

    def span(step):
        return slice(step * block, (step + 1) * block)

    def project_pre(step):
        pre_ref[step % 2] = dot_nn(tall_conv[...], win_ref[:, span(step)])

    def project_back(step):
        back_ref[step % 2] = dot_nt(tall_grad[...], wout_ref[span(step), :])

    def slope(step, first, last):
        bias = bias_ref[span(step)].reshape(1, block)
        for g in range(first, last):
            some = slice(g * group, (g + 1) * group)
            value = back_ref[step % 2, some, :] * gelu_slope(pre_ref[step % 2, some, :] + bias)
            slope_ref[some, span(step)] = value.astype(jnp.bfloat16)

    def gather(first, last):
        at = slice(first * block, last * block)
        term = dot_nt(win_ref[:, at], slope_ref[:, at])
        total_ref[...] = term if first == 0 else total_ref[...] + term

    stack(tall_conv, conv_ref)
    project_pre(0)
    stack(tall_grad, grad_ref)
    project_back(0)
    gathered = 0
    thirds = [groups * n // 3 for n in range(4)]
    for step in range(steps):
        if step + 1 < steps:
            project_pre(step + 1)
        slope(step, thirds[0], thirds[1])
        if step - gathered == 2:
            gather(gathered, step)
            gathered = step
        slope(step, thirds[1], thirds[2])
        if step + 1 < steps:
            project_back(step + 1)
        slope(step, thirds[2], thirds[3])
    gather(gathered, steps)
    for out, (k, start, size) in zip(outs, sent):
        target = partner(me, k, count, 1)
        for begin, width in chunks:
            if start <= begin < start + size:
                first = pl.multiple_of(count * begin + target * width, 32)
                out[begin - start : begin - start + width, :] = total_ref[pl.ds(first, width), :].astype(
                    jnp.bfloat16
                )


def mlp(conv_out, grad_out, w_in, b_in, w_out, count, half, halves, sent, chunks, after):
    rows, part, channels = conv_out.shape
    rows //= halves
    block = 256
    wide = round_up(part, HALF)
    vmem = pl.BlockSpec(memory_space=VMEM)
    out_shape = [jax.ShapeDtypeStruct((size, rows * wide), jnp.bfloat16) for _, _, size in sent]
    return pl.pallas_call(
        functools.partial(mlp_kernel, count, half, sent, chunks),
        in_specs=[vmem] * 5 + [pl.BlockSpec(memory_space=pl.ANY)] * len(after),
        out_specs=[vmem] * len(out_shape),
        out_shape=out_shape,
        scratch_shapes=[
            pltpu.VMEM((rows * wide, channels), jnp.bfloat16),
            pltpu.VMEM((rows * wide, channels), jnp.bfloat16),
            pltpu.VMEM((2, rows * wide, block), jnp.float32),
            pltpu.VMEM((2, rows * wide, block), jnp.float32),
            pltpu.VMEM((rows * wide, w_in.shape[1]), jnp.bfloat16),
            pltpu.VMEM((channels, rows * wide), jnp.float32),
        ],
        compiler_params=pltpu.CompilerParams(vmem_limit_bytes=16 * 2**20),
        cost_estimate=NO_COST,
        name="mlp",
    )(conv_out, grad_out, w_in, b_in, w_out, *after)


def analysis_kernel(count, rows, chunk, *refs):
    own_ref, first_ref, second_ref = refs[-3:]
    start, size = chunk
    halves = next(h for h in range(1, rows + 1) if refs[h * count].ndim == 3)
    table_ref = refs[halves * count]
    ranks = far_first(halves * count, count)
    pieces = [refs[ranks.index(i)] for i in range(halves * count)]
    rows_each = rows // halves
    wide = refs[0].shape[1] // rows_each
    window = table_ref.shape[1] - HALF
    me = lax.axis_index("azimuth")
    sources = [partner(me, k, count, -1) for k in range(count)]
    even = lax.rem(lax.axis_index("polar"), 2) == 0

    def columns(row, k):
        half, row = divmod(row, rows_each)
        piece = pieces[half * count + k]
        base = 0 if half == halves - 1 and k > NEAR else start
        first = row * wide // LANES * LANES
        return piece[base : base + size, first : first + window]

    shifts = [row % rows_each * wide % LANES for row in range(rows)]
    for shift in sorted(set(shifts)):
        group = [row for row in range(rows) if shifts[row] == shift]
        total = None
        for k in range(count):
            left = jnp.concatenate([columns(row, k) for row in group], axis=0)
            term = dot_nn(left, table_ref[sources[k], HALF - shift : HALF - shift + window, :])
            total = term if total is None else total + term
        for at, row in enumerate(group):
            mine = total[at * size : (at + 1) * size]
            own_ref[row] = mine

    def share(above, below):
        for h in range(REACH):
            above[h] = own_ref[rows - REACH + h].astype(jnp.bfloat16)
            below[h] = own_ref[h].astype(jnp.bfloat16)

    pl.when(even)(lambda: share(first_ref, second_ref))
    pl.when(jnp.logical_not(even))(lambda: share(second_ref, first_ref))


def analyze(pieces, table, rows, chunk, count, after):
    size = chunk[1]
    width = table.shape[2]
    halo = jax.ShapeDtypeStruct((REACH, size, width), jnp.bfloat16)
    return pl.pallas_call(
        functools.partial(analysis_kernel, count, rows, chunk),
        in_specs=[pl.BlockSpec(memory_space=VMEM)] * (len(pieces) + 1)
        + [pl.BlockSpec(memory_space=pl.ANY)] * len(after),
        out_specs=[pl.BlockSpec(memory_space=VMEM)] * 3,
        out_shape=[jax.ShapeDtypeStruct((rows, size, width), jnp.float32), halo, halo],
        compiler_params=pltpu.CompilerParams(vmem_limit_bytes=12 * 2**20),
        cost_estimate=NO_COST,
        name="analysis",
    )(*(pieces[i] for i in far_first(len(pieces), count)), table, *after)


def add_row(accs, spectrum, weight, target_row, filter_row, targets):
    size = spectrum.shape[0]
    masked = jnp.concatenate([jnp.where(target_row == t, weight, 0.0) for t in targets], axis=0)
    gains = dot_nn(masked.astype(jnp.bfloat16), filter_row)
    whole = (gains.shape[1] // 2) // LANES * LANES - LANES
    spec_re = spectrum[:, :whole]
    spec_im = spectrum[:, whole : 2 * whole]
    spec_x = spectrum[:, 2 * whole :]
    swapped = pltpu.roll(spec_x, HALF, 1)
    for at, target in enumerate(targets):
        gain = gains[at * size : (at + 1) * size]
        gain_re = gain[:, :whole]
        gain_rx = gain[:, whole : whole + LANES]
        gain_im = gain[:, whole + LANES : 2 * whole + LANES]
        gain_ix = gain[:, 2 * whole + LANES :]
        acc_re, acc_im, acc_x = accs[target]
        acc_re = acc_re + (gain_re * spec_re + gain_im * spec_im)
        acc_im = acc_im + (gain_re * spec_im - gain_im * spec_re)
        acc_x = acc_x + (gain_rx * spec_x + gain_ix * swapped)
        accs[target] = acc_re, acc_im, acc_x


def split_tiles(value):
    whole = (value.shape[1] - LANES) // 2
    return value[:, :whole], value[:, whole : 2 * whole], value[:, 2 * whole :]


def own_kernel(own_ref, weight_ref, target_ref, filter_ref, out_ref):
    rows, size, width = own_ref.shape
    accs = {t: split_tiles(jnp.zeros((size, width), jnp.float32)) for t in range(rows)}
    for row in range(rows):
        at = row + REACH
        targets = [t for t in range(rows) if abs(row - t) <= REACH]
        add_row(accs, own_ref[row], weight_ref[...], target_ref[at : at + 1, :], filter_ref[at], targets)
    for t in range(rows):
        out_ref[t] = jnp.concatenate(accs[t], axis=1)


def own_terms(own, weight, target, filters):
    return pl.pallas_call(
        own_kernel,
        in_specs=[pl.BlockSpec(memory_space=VMEM)] * 4,
        out_specs=pl.BlockSpec(memory_space=VMEM),
        out_shape=jax.ShapeDtypeStruct(own.shape, jnp.float32),
        compiler_params=pltpu.CompilerParams(vmem_limit_bytes=12 * 2**20),
        cost_estimate=NO_COST,
        name="own_terms",
    )(own, weight, target, filters)


def add_halo(accs, sides, rows, weight_ref, target_ref, filter_ref):
    for side, base in sides:
        for h in range(REACH):
            at = base + h + REACH
            targets = [t for t in range(rows) if abs(base + h - t) <= REACH]
            add_row(
                accs,
                side[h].astype(jnp.float32),
                weight_ref[...],
                target_ref[at : at + 1, :],
                filter_ref[at],
                targets,
            )


def side_kernel(part_ref, first_ref, weight_ref, target_ref, filter_ref, out_ref):
    rows = part_ref.shape[0]
    even = lax.rem(lax.axis_index("polar"), 2) == 0

    def combine(base):
        accs = {t: split_tiles(part_ref[t]) for t in range(rows)}
        add_halo(accs, [(first_ref, base)], rows, weight_ref, target_ref, filter_ref)
        for t in range(rows):
            out_ref[t] = jnp.concatenate(accs[t], axis=1)

    pl.when(even)(lambda: combine(rows))
    pl.when(jnp.logical_not(even))(lambda: combine(-REACH))


def side_terms(own, first, weight, target, filters):
    return pl.pallas_call(
        side_kernel,
        in_specs=[pl.BlockSpec(memory_space=VMEM)] * 5,
        out_specs=pl.BlockSpec(memory_space=VMEM),
        out_shape=jax.ShapeDtypeStruct(own.shape, jnp.float32),
        compiler_params=pltpu.CompilerParams(vmem_limit_bytes=12 * 2**20),
        cost_estimate=NO_COST,
        name="side_terms",
    )(own, first, weight, target, filters)


def finish_kernel(count, swaps, part_ref, *refs):
    halos, (weight_ref, target_ref, filter_ref, table_ref) = refs[:swaps], refs[swaps : swaps + 4]
    outs, stacked_ref, grid_ref = refs[-count - 2 : -2], refs[-2], refs[-1]
    rows, size, width = part_ref.shape
    part = outs[0].shape[0]
    even = lax.rem(lax.axis_index("polar"), 2) == 0

    def combine(bases):
        accs = {t: split_tiles(part_ref[t]) for t in range(rows)}
        sides = list(zip(halos, bases[-swaps:]))
        add_halo(accs, sides, rows, weight_ref, target_ref, filter_ref)
        for t in range(rows):
            stacked_ref[t * size : (t + 1) * size, :] = jnp.concatenate(accs[t], axis=1).astype(jnp.bfloat16)

    pl.when(even)(lambda: combine((rows, -REACH)))
    pl.when(jnp.logical_not(even))(lambda: combine((-REACH, rows)))
    me = lax.axis_index("azimuth")
    grid_ref[...] = dot_nt(table_ref[...], stacked_ref[...])
    wide = grid_ref.shape[0] // count
    for k in range(count):
        first = pl.multiple_of(partner(me, k, count, 1) * wide, HALF)
        outs[k][...] = grid_ref[pl.ds(first, wide), :][:part].astype(jnp.bfloat16)


def finish(own, halos, weight, target, filters, table, count, part, after):
    rows, size, width = own.shape
    return pl.pallas_call(
        functools.partial(finish_kernel, count, len(halos)),
        in_specs=[pl.BlockSpec(memory_space=VMEM)] * (5 + len(halos)) + [pl.BlockSpec(memory_space=pl.ANY)] * len(after),
        out_specs=[pl.BlockSpec(memory_space=VMEM)] * count,
        out_shape=[jax.ShapeDtypeStruct((part, rows * size), jnp.bfloat16)] * count,
        scratch_shapes=[
            pltpu.VMEM((rows * size, width), jnp.bfloat16),
            pltpu.VMEM((table.shape[0], rows * size), jnp.float32),
        ],
        compiler_params=pltpu.CompilerParams(vmem_limit_bytes=12 * 2**20),
        cost_estimate=NO_COST,
        name="finish",
    )(own, *halos, weight, target, filters, table, *after)


def add_kernel(count, chunk, grad_ref, *refs):
    out_ref, tall_ref, done_ref, sems = refs[-4:]
    ranks = far_first(count, count)
    pieces = [refs[ranks.index(k)] for k in range(count)]
    tiles, part, rows, _ = done_ref.shape
    start, size = chunk
    me = lax.axis_index("azimuth")

    def add(tile, mine):
        order = [[k for k in range(count) if partner_static(mine, k, count, -1) == s][0] for s in range(count)]
        lanes = range(tile * LANES, (tile + 1) * LANES)
        for row in range(rows):
            parts = []
            for s in range(lanes[0] // size, lanes[-1] // size + 1):
                low, high = max(lanes[0], s * size) - s * size, min(lanes[-1] + 1, (s + 1) * size) - s * size
                parts.append(pieces[order[s]][:, row * size + low : row * size + high])
            conv = jnp.concatenate(parts, axis=1).astype(jnp.float32)
            first = count * start + tile * LANES
            total = grad_ref[row, :, first : first + LANES].astype(jnp.float32) + conv
            tall_ref[tile, pl.ds(row, part, stride=rows), :] = total
        done_ref[tile] = tall_ref[tile].reshape(part, rows, LANES).astype(jnp.bfloat16)

    copies = []
    for tile in range(tiles):
        for mine in range(count):
            pl.when(me == mine)(functools.partial(add, tile, mine))
        lanes = pl.ds(count * start + tile * LANES, LANES)
        copies.append(pltpu.make_async_copy(done_ref.at[tile], out_ref.at[:, :, lanes], sems.at[tile]))
        copies[-1].start()
    for copy in copies:
        copy.wait()


def add_chunk(grad_out, pieces, chunk, count, before):
    rows, part, channels = grad_out.shape
    start, size = chunk
    tiles = count * size // LANES
    vmem = pl.BlockSpec(memory_space=VMEM)
    anywhere = pl.BlockSpec(memory_space=pl.ANY)
    return pl.pallas_call(
        functools.partial(add_kernel, count, chunk),
        in_specs=[vmem] * (1 + count) + [anywhere] * len(before),
        out_specs=anywhere,
        out_shape=jax.ShapeDtypeStruct((part, rows, channels), jnp.bfloat16),
        scratch_shapes=[
            pltpu.VMEM((tiles, rows * part, LANES), jnp.float32),
            pltpu.VMEM((tiles, part, rows, LANES), jnp.bfloat16),
            pltpu.SemaphoreType.DMA((tiles,)),
        ],
        input_output_aliases={1 + count: 0} if before else {},
        compiler_params=pltpu.CompilerParams(vmem_limit_bytes=12 * 2**20),
        cost_estimate=NO_COST,
        name="add_chunk",
    )(grad_out, *(pieces[i] for i in far_first(count, count)), *before)


def prepare_kernel(count, chunks, weight_ref, filt_ref, offset_ref, forth_ref, back_ref, *outs):
    filter_out, target_out, forth_out, back_out = outs[:4]
    forth_out[...] = forth_ref[...]
    back_out[...] = back_ref[...]
    bases, channels = weight_ref.shape
    lats, width = filt_ref.shape[1:]
    ext, depth = target_out.shape
    rows = ext - 2 * REACH
    modes = width // 2
    whole = modes // LANES * LANES
    used = TERMS * bases
    for (start, size), out in zip(chunks, outs[4:]):
        first = count * start + lax.axis_index("azimuth") * size
        weight = pltpu.roll(weight_ref[...], lax.rem(channels - first, channels), 1)[:, :size]
        parts = []
        for _ in range(TERMS):
            rounded = weight.astype(jnp.bfloat16).astype(jnp.float32)
            parts.append(rounded)
            weight = weight - rounded
        parts.append(jnp.zeros((depth - used, size), jnp.float32))
        out[...] = jnp.concatenate(parts, axis=0).T
    start_lat = lax.axis_index("polar") * rows
    table = filt_ref[...].reshape(bases * lats, width)
    base = lax.broadcasted_iota(jnp.int32, (depth, bases * lats), 0)
    valid = base < used
    for _ in range(TERMS - 1):
        base = jnp.where(base >= bases, base - bases, base)
    column = lax.broadcasted_iota(jnp.int32, (depth, bases * lats), 1)
    for i in range(ext):
        lat = start_lat + (i - REACH)
        inside = (lat >= 0) & (lat < lats)
        lat = jnp.clip(lat, 0, lats - 1)
        pick = jnp.where(valid & (column == base * lats + lat), 1.0, 0.0).astype(jnp.bfloat16)
        row = dot_nn(pick, table)
        real, imag = row[:, :modes], row[:, modes:]
        rest_re, rest_im = real[:, whole:], imag[:, whole:]
        filter_out[i] = jnp.concatenate(
            [real[:, :whole], rest_re, rest_re, imag[:, :whole], rest_im, -rest_im], axis=1
        ).astype(jnp.bfloat16)
        local = jnp.where(inside, offset_ref[pl.ds(lat, 1), :] - start_lat, -1)
        spare = jnp.full((1, depth - used), -1, jnp.int32)
        target_out[i : i + 1, :] = jnp.concatenate([local] * TERMS + [spare], axis=1)


def prepare(basis_weight, filt, offsets, forth, back, rows, count, chunks):
    bases = filt.shape[0]
    width = filt.shape[2]
    ext = rows + 2 * REACH
    depth = round_up(TERMS * bases, 16)
    shapes = [
        jax.ShapeDtypeStruct((ext, depth, width + LANES), jnp.bfloat16),
        jax.ShapeDtypeStruct((ext, depth), jnp.int32),
        jax.ShapeDtypeStruct(forth.shape, forth.dtype),
        jax.ShapeDtypeStruct(back.shape, back.dtype),
    ] + [jax.ShapeDtypeStruct((size, depth), jnp.float32) for _, size in chunks]
    return pl.pallas_call(
        functools.partial(prepare_kernel, count, chunks),
        in_specs=[pl.BlockSpec(memory_space=VMEM)] * 5,
        out_specs=[pl.BlockSpec(memory_space=VMEM)] * len(shapes),
        out_shape=shapes,
        compiler_params=pltpu.CompilerParams(vmem_limit_bytes=16 * 2**20),
        cost_estimate=NO_COST,
        name="prepare",
    )(basis_weight, filt, offsets, forth, back)


def halo(first, second):
    bands, count = lax.axis_size("polar"), lax.axis_size("azimuth")
    blocks = []
    for odd, block in ((0, first), (1, second)):
        pairs = []
        for a in range(bands):
            other = ((a + odd) ^ 1) - odd
            for b in range(count):
                paired = 0 <= other < bands
                target = (other, b) if paired else (a, b ^ 1 if b ^ 1 < count else b)
                pairs.append((a * count + b, target[0] * count + target[1]))
        blocks.append(lax.ppermute(block, ("polar", "azimuth"), pairs))
    return blocks


def on_device(chunks, conv_out, grad_out, w_in, b_in, w_out, basis_weight, filt, offsets):
    rows, part, channels = conv_out.shape
    count = lax.axis_size("azimuth")
    forth, back = tables(count, part, filt.shape[2] // 2)
    forth, back = jnp.asarray(forth), jnp.asarray(back)
    owned = channels // count
    halves = 2 if rows % 2 == 0 else 1
    pieces = []
    for half in range(halves):
        final = half == halves - 1
        far = range(NEAR + 1, count)
        sent = [(k, 0, owned) for k in range(count)]
        if final:
            sent[NEAR + 1 :] = [(k,) + chunk for chunk in chunks for k in far]
        blocks = mlp(conv_out, grad_out, w_in, b_in, w_out, count, half, halves, sent, chunks, pieces[1:2])
        steps = [] if final else list(far)
        moved = {k: exchange(blocks[k], k, count) for k in steps + list(range(NEAR + 1))}
        pieces += [moved[k] for k in sorted(moved)]
    filters, target, forth, back, *weights = prepare(
        basis_weight, filt, offsets, forth, back, rows, count, chunks
    )
    spectra, terms, grids, returned = {}, {}, {}, []

    def open_chunk(q, after):
        tail = [exchange(blocks[NEAR + 1 + q * len(far) + i], k, count) for i, k in enumerate(far)]
        own, first, second = analyze(pieces + tail, forth, rows, chunks[q], count, after)
        spectra[q] = halo(first, second)
        terms[q] = own_terms(own, weights[q], target, filters)

    def close_chunk(q):
        after = [returned[(q - 1) * count + 1]] if q else []
        halos = spectra[q]
        if q == 0:
            terms[q] = side_terms(terms[q], halos[0], weights[q], target, filters)
            halos = halos[1:]
        grids[q] = finish(terms[q], halos, weights[q], target, filters, back, count, part, after)
        blocks = {k: exchange(grids[q][k], k, count) for k in [*far, *range(NEAR + 1)]}
        returned.extend(blocks[k] for k in range(count))

    last = len(chunks) - 1
    open_chunk(0, [])
    if last > 0:
        open_chunk(1, [terms[0]])
    for q in range(last + 1):
        close_chunk(q)
        if q + 2 <= last:
            open_chunk(q + 2, [grids[q][0]])
    total = []
    for q, chunk in enumerate(chunks):
        total = [add_chunk(grad_out, returned[q * count : (q + 1) * count], chunk, count, total)]
    return jnp.transpose(total[0], (1, 0, 2))


def solution(mesh):
    grid = P(("member", "polar"), "azimuth", None)

    def run(conv_out, grad_out, *others):
        owned = conv_out.shape[2] // mesh.shape["azimuth"]
        sizes = [owned]
        if owned % 32 == 0 and owned >= 96:
            big = owned * 3 // 5 // 32 * 32
            sizes = [big, owned - big]
        chunks = tuple((sum(sizes[:q]), size) for q, size in enumerate(sizes))
        return jax.shard_map(
            functools.partial(on_device, chunks),
            mesh=mesh,
            in_specs=(grid, grid) + (P(),) * 6,
            out_specs=grid,
            check_vma=False,
        )(conv_out, grad_out, *others)

    return run
```

```python
import functools
import math

import jax
import jax.numpy as jnp
import ml_dtypes
import numpy as np
from jax import lax
from jax.experimental import pallas as pl
from jax.experimental.pallas import tpu as pltpu
from jax.sharding import PartitionSpec as P

REACH = 3
LANES = 128
HALF = 64
TERMS = 3
NEAR = 1
VMEM = pltpu.MemorySpace.VMEM
NO_COST = pl.CostEstimate(flops=0, bytes_accessed=0, transcendentals=0)


def round_up(value, unit):
    return -(-value // unit) * unit


def partner(me, step, count, sign):
    if count & (count - 1) == 0:
        return me ^ step
    return lax.rem(me + sign * step + count, count)


def far_first(number, count):
    return sorted(range(number), key=lambda i: (i // count, i % count <= NEAR))


def exchange(block, step, count):
    if step == 0:
        return block
    pairs = [(a, int(partner_static(a, step, count))) for a in range(count)]
    return lax.ppermute(block, "azimuth", pairs)


def partner_static(a, step, count, sign=1):
    return a ^ step if count & (count - 1) == 0 else (a + sign * step) % count


def tables(count, part, modes):
    length = count * part
    whole = modes // LANES * LANES
    order = np.concatenate(
        [
            np.arange(whole),
            modes + np.arange(whole),
            np.arange(whole, modes),
            modes + np.arange(whole, modes),
        ]
    )
    positions = np.arange(length)
    waves = np.arange(modes)
    phase = (positions[:, None] * waves[None, :]) % length
    angle = (2.0 * math.pi / length) * phase
    scale = 1.0 / math.sqrt(length)
    factor = np.where(waves == 0, 1.0, 2.0)
    analysis = np.concatenate([np.cos(angle), -np.sin(angle)], axis=1) * scale
    synth = np.concatenate([np.cos(angle) * factor, -np.sin(angle) * factor], axis=1) * scale
    analysis = analysis.astype(np.float32).astype(ml_dtypes.bfloat16)[:, order]
    synth = synth.astype(np.float32).astype(ml_dtypes.bfloat16)[:, order]
    wide = round_up(part, HALF)
    window = round_up(HALF + wide, LANES)
    forth = np.zeros((count, HALF + window, 2 * modes), ml_dtypes.bfloat16)
    back = np.zeros((count * wide, 2 * modes), ml_dtypes.bfloat16)
    for s in range(count):
        forth[s, HALF : HALF + part] = analysis[s * part : (s + 1) * part]
        back[s * wide : s * wide + part] = synth[s * part : (s + 1) * part]
    return forth, back


def twice_gelu_slope(scaled):
    power = math.log2(2.0 / math.sqrt(math.pi)) - (1.0 / math.log(2.0)) * (scaled * scaled)
    return (1.0 + lax.erf(scaled)) + scaled * jnp.exp2(power)


def dot_nt(left, right):
    return lax.dot_general(left, right, (((1,), (1,)), ((), ())), preferred_element_type=jnp.float32)


def dot_nn(left, right):
    return jnp.dot(left, right, preferred_element_type=jnp.float32)


def mlp_kernel(count, half, sent, chunks, conv_ref, grad_ref, win_ref, bias_ref, wout_ref, *rest):
    outs, (tall_conv, tall_grad, pre_ref, back_ref, slope_ref, total_ref) = rest[-6 - len(sent) : -6], rest[-6:]
    part, channels = conv_ref.shape[1:]
    wide = round_up(part, HALF)
    rows = tall_conv.shape[0] // wide
    owned = channels // count
    block = pre_ref.shape[2]
    steps = win_ref.shape[1] // block
    me = lax.axis_index("azimuth")
    def stack(tall, source):
        for row in range(rows):
            whole = part // 16 * 16
            tall[row * wide + whole : (row + 1) * wide, :] = jnp.zeros((wide - whole, channels), jnp.bfloat16)
            tall[row * wide : row * wide + part, :] = source[half * rows + row]

    group = 48
    groups = rows * wide // group

    def span(step):
        return slice(step * block, (step + 1) * block)

    def project_pre(step):
        pre_ref[step % 2] = dot_nn(tall_conv[...], win_ref[:, span(step)])

    def project_back(step):
        back_ref[step % 2] = dot_nt(tall_grad[...], wout_ref[span(step), :])

    def slope(step, first, last):
        root = math.sqrt(0.5)
        bias = bias_ref[span(step)].reshape(1, block) * root
        for g in range(first, last):
            some = slice(g * group, (g + 1) * group)
            value = back_ref[step % 2, some, :] * twice_gelu_slope(pre_ref[step % 2, some, :] * root + bias)
            slope_ref[some, span(step)] = value.astype(jnp.bfloat16)

    def gather(first, last):
        at = slice(first * block, last * block)
        term = dot_nt(win_ref[:, at], slope_ref[:, at])
        total_ref[...] = term if first == 0 else total_ref[...] + term

    stack(tall_conv, conv_ref)
    project_pre(0)
    stack(tall_grad, grad_ref)
    project_back(0)
    gathered = 0
    thirds = [groups * n // 3 for n in range(4)]
    for step in range(steps):
        if step + 1 < steps:
            project_pre(step + 1)
        slope(step, thirds[0], thirds[1])
        if step - gathered == 2:
            gather(gathered, step)
            gathered = step
        slope(step, thirds[1], thirds[2])
        if step + 1 < steps:
            project_back(step + 1)
        slope(step, thirds[2], thirds[3])
    gather(gathered, steps)
    for out, (k, start, size) in zip(outs, sent):
        target = partner(me, k, count, 1)
        for begin, width in chunks:
            if start <= begin < start + size:
                first = pl.multiple_of(count * begin + target * width, 32)
                value = 0.5 * total_ref[pl.ds(first, width), :]
                out[begin - start : begin - start + width, :] = value.astype(jnp.bfloat16)


def mlp(conv_out, grad_out, w_in, b_in, w_out, count, half, halves, sent, chunks, after):
    rows, part, channels = conv_out.shape
    rows //= halves
    block = 256
    wide = round_up(part, HALF)
    vmem = pl.BlockSpec(memory_space=VMEM)
    out_shape = [jax.ShapeDtypeStruct((size, rows * wide), jnp.bfloat16) for _, _, size in sent]
    return pl.pallas_call(
        functools.partial(mlp_kernel, count, half, sent, chunks),
        in_specs=[vmem] * 5 + [pl.BlockSpec(memory_space=pl.ANY)] * len(after),
        out_specs=[vmem] * len(out_shape),
        out_shape=out_shape,
        scratch_shapes=[
            pltpu.VMEM((rows * wide, channels), jnp.bfloat16),
            pltpu.VMEM((rows * wide, channels), jnp.bfloat16),
            pltpu.VMEM((2, rows * wide, block), jnp.float32),
            pltpu.VMEM((2, rows * wide, block), jnp.float32),
            pltpu.VMEM((rows * wide, w_in.shape[1]), jnp.bfloat16),
            pltpu.VMEM((channels, rows * wide), jnp.float32),
        ],
        compiler_params=pltpu.CompilerParams(vmem_limit_bytes=16 * 2**20),
        cost_estimate=NO_COST,
        name="mlp",
    )(conv_out, grad_out, w_in, b_in, w_out, *after)


def analysis_kernel(count, rows, chunk, *refs):
    own_ref, first_ref, second_ref = refs[-3:]
    start, size = chunk
    halves = next(h for h in range(1, rows + 1) if refs[h * count].ndim == 3)
    table_ref = refs[halves * count]
    ranks = far_first(halves * count, count)
    pieces = [refs[ranks.index(i)] for i in range(halves * count)]
    rows_each = rows // halves
    wide = refs[0].shape[1] // rows_each
    window = table_ref.shape[1] - HALF
    even = lax.rem(lax.axis_index("polar"), 2) == 0

    def columns(row, k):
        half, row = divmod(row, rows_each)
        piece = pieces[half * count + k]
        base = 0 if half == halves - 1 and k > NEAR else start
        first = row * wide // LANES * LANES
        return piece[base : base + size, first : first + window]

    shifts = [row % rows_each * wide % LANES for row in range(rows)]
    for shift in sorted(set(shifts)):
        group = [row for row in range(rows) if shifts[row] == shift]
        total = None
        for k in range(count):
            left = jnp.concatenate([columns(row, k) for row in group], axis=0)
            term = dot_nn(left, table_ref[k, HALF - shift : HALF - shift + window, :])
            total = term if total is None else total + term
        for at, row in enumerate(group):
            mine = total[at * size : (at + 1) * size]
            own_ref[row] = mine

    def share(above, below):
        for h in range(REACH):
            above[h] = own_ref[rows - REACH + h].astype(jnp.bfloat16)
            below[h] = own_ref[h].astype(jnp.bfloat16)

    pl.when(even)(lambda: share(first_ref, second_ref))
    pl.when(jnp.logical_not(even))(lambda: share(second_ref, first_ref))


def analyze(pieces, table, rows, chunk, count, after):
    size = chunk[1]
    width = table.shape[2]
    halo = jax.ShapeDtypeStruct((REACH, size, width), jnp.bfloat16)
    return pl.pallas_call(
        functools.partial(analysis_kernel, count, rows, chunk),
        in_specs=[pl.BlockSpec(memory_space=VMEM)] * (len(pieces) + 1)
        + [pl.BlockSpec(memory_space=pl.ANY)] * len(after),
        out_specs=[pl.BlockSpec(memory_space=VMEM)] * 3,
        out_shape=[jax.ShapeDtypeStruct((rows, size, width), jnp.float32), halo, halo],
        compiler_params=pltpu.CompilerParams(vmem_limit_bytes=12 * 2**20),
        cost_estimate=NO_COST,
        name="analysis",
    )(*(pieces[i] for i in far_first(len(pieces), count)), table, *after)


def add_row(accs, spectrum, weight, target_row, filter_row, targets):
    size = spectrum.shape[0]
    masked = jnp.concatenate([jnp.where(target_row == t, weight, 0.0) for t in targets], axis=0)
    gains = dot_nn(masked.astype(jnp.bfloat16), filter_row)
    whole = (gains.shape[1] // 2) // LANES * LANES - LANES
    spec_re = spectrum[:, :whole]
    spec_im = spectrum[:, whole : 2 * whole]
    spec_x = spectrum[:, 2 * whole :]
    swapped = pltpu.roll(spec_x, HALF, 1)
    for at, target in enumerate(targets):
        gain = gains[at * size : (at + 1) * size]
        gain_re = gain[:, :whole]
        gain_rx = gain[:, whole : whole + LANES]
        gain_im = gain[:, whole + LANES : 2 * whole + LANES]
        gain_ix = gain[:, 2 * whole + LANES :]
        acc_re, acc_im, acc_x = accs[target]
        acc_re = acc_re + (gain_re * spec_re + gain_im * spec_im)
        acc_im = acc_im + (gain_re * spec_im - gain_im * spec_re)
        acc_x = acc_x + (gain_rx * spec_x + gain_ix * swapped)
        accs[target] = acc_re, acc_im, acc_x


def split_tiles(value):
    whole = (value.shape[1] - LANES) // 2
    return value[:, :whole], value[:, whole : 2 * whole], value[:, 2 * whole :]


def own_kernel(own_ref, weight_ref, target_ref, filter_ref, out_ref):
    rows, size, width = own_ref.shape
    accs = {t: split_tiles(jnp.zeros((size, width), jnp.float32)) for t in range(rows)}
    for row in range(rows):
        at = row + REACH
        targets = [t for t in range(rows) if abs(row - t) <= REACH]
        add_row(accs, own_ref[row], weight_ref[...], target_ref[at : at + 1, :], filter_ref[at], targets)
    for t in range(rows):
        out_ref[t] = jnp.concatenate(accs[t], axis=1)


def own_terms(own, weight, target, filters):
    return pl.pallas_call(
        own_kernel,
        in_specs=[pl.BlockSpec(memory_space=VMEM)] * 4,
        out_specs=pl.BlockSpec(memory_space=VMEM),
        out_shape=jax.ShapeDtypeStruct(own.shape, jnp.float32),
        compiler_params=pltpu.CompilerParams(vmem_limit_bytes=12 * 2**20),
        cost_estimate=NO_COST,
        name="own_terms",
    )(own, weight, target, filters)


def add_halo(accs, sides, rows, weight_ref, target_ref, filter_ref):
    for side, base in sides:
        for h in range(REACH):
            at = base + h + REACH
            targets = [t for t in range(rows) if abs(base + h - t) <= REACH]
            add_row(
                accs,
                side[h].astype(jnp.float32),
                weight_ref[...],
                target_ref[at : at + 1, :],
                filter_ref[at],
                targets,
            )


def side_kernel(part_ref, first_ref, weight_ref, target_ref, filter_ref, out_ref):
    rows = part_ref.shape[0]
    even = lax.rem(lax.axis_index("polar"), 2) == 0

    def combine(base):
        accs = {t: split_tiles(part_ref[t]) for t in range(rows)}
        add_halo(accs, [(first_ref, base)], rows, weight_ref, target_ref, filter_ref)
        for t in range(rows):
            out_ref[t] = jnp.concatenate(accs[t], axis=1)

    pl.when(even)(lambda: combine(rows))
    pl.when(jnp.logical_not(even))(lambda: combine(-REACH))


def side_terms(own, first, weight, target, filters):
    return pl.pallas_call(
        side_kernel,
        in_specs=[pl.BlockSpec(memory_space=VMEM)] * 5,
        out_specs=pl.BlockSpec(memory_space=VMEM),
        out_shape=jax.ShapeDtypeStruct(own.shape, jnp.float32),
        compiler_params=pltpu.CompilerParams(vmem_limit_bytes=12 * 2**20),
        cost_estimate=NO_COST,
        name="side_terms",
    )(own, first, weight, target, filters)


def finish_kernel(count, swaps, part_ref, *refs):
    halos, (weight_ref, target_ref, filter_ref, table_ref) = refs[:swaps], refs[swaps : swaps + 4]
    outs, stacked_ref = refs[-count - 1 : -1], refs[-1]
    rows, size, width = part_ref.shape
    part = outs[0].shape[0]
    even = lax.rem(lax.axis_index("polar"), 2) == 0

    def combine(bases):
        accs = {t: split_tiles(part_ref[t]) for t in range(rows)}
        sides = list(zip(halos, bases[-swaps:]))
        add_halo(accs, sides, rows, weight_ref, target_ref, filter_ref)
        for t in range(rows):
            stacked_ref[t * size : (t + 1) * size, :] = jnp.concatenate(accs[t], axis=1).astype(jnp.bfloat16)

    pl.when(even)(lambda: combine((rows, -REACH)))
    pl.when(jnp.logical_not(even))(lambda: combine((-REACH, rows)))
    grid = dot_nt(table_ref[...], stacked_ref[...])
    wide = grid.shape[0] // count
    for k in range(count):
        outs[k][...] = grid[k * wide : k * wide + part].astype(jnp.bfloat16)


def finish(own, halos, weight, target, filters, table, count, part, after):
    rows, size, width = own.shape
    return pl.pallas_call(
        functools.partial(finish_kernel, count, len(halos)),
        in_specs=[pl.BlockSpec(memory_space=VMEM)] * (5 + len(halos)) + [pl.BlockSpec(memory_space=pl.ANY)] * len(after),
        out_specs=[pl.BlockSpec(memory_space=VMEM)] * count,
        out_shape=[jax.ShapeDtypeStruct((part, rows * size), jnp.bfloat16)] * count,
        scratch_shapes=[pltpu.VMEM((rows * size, width), jnp.bfloat16)],
        compiler_params=pltpu.CompilerParams(vmem_limit_bytes=12 * 2**20),
        cost_estimate=NO_COST,
        name="finish",
    )(own, *halos, weight, target, filters, table, *after)


def add_kernel(count, chunk, grad_ref, *refs):
    out_ref, tall_ref, done_ref, sems = refs[-4:]
    ranks = far_first(count, count)
    pieces = [refs[ranks.index(k)] for k in range(count)]
    tiles, part, rows, _ = done_ref.shape
    start, size = chunk
    me = lax.axis_index("azimuth")

    def add(tile, mine):
        order = [[k for k in range(count) if partner_static(mine, k, count, -1) == s][0] for s in range(count)]
        lanes = range(tile * LANES, (tile + 1) * LANES)
        for row in range(rows):
            parts = []
            for s in range(lanes[0] // size, lanes[-1] // size + 1):
                low, high = max(lanes[0], s * size) - s * size, min(lanes[-1] + 1, (s + 1) * size) - s * size
                parts.append(pieces[order[s]][:, row * size + low : row * size + high])
            conv = jnp.concatenate(parts, axis=1).astype(jnp.float32)
            first = count * start + tile * LANES
            total = grad_ref[row, :, first : first + LANES].astype(jnp.float32) + conv
            tall_ref[tile, pl.ds(row, part, stride=rows), :] = total
        done_ref[tile] = tall_ref[tile].reshape(part, rows, LANES).astype(jnp.bfloat16)

    copies = []
    for tile in range(tiles):
        for mine in range(count):
            pl.when(me == mine)(functools.partial(add, tile, mine))
        lanes = pl.ds(count * start + tile * LANES, LANES)
        copies.append(pltpu.make_async_copy(done_ref.at[tile], out_ref.at[:, :, lanes], sems.at[tile]))
        copies[-1].start()
    for copy in copies:
        copy.wait()


def add_chunk(grad_out, pieces, chunk, count, before):
    rows, part, channels = grad_out.shape
    start, size = chunk
    tiles = count * size // LANES
    vmem = pl.BlockSpec(memory_space=VMEM)
    anywhere = pl.BlockSpec(memory_space=pl.ANY)
    return pl.pallas_call(
        functools.partial(add_kernel, count, chunk),
        in_specs=[vmem] * (1 + count) + [anywhere] * len(before),
        out_specs=anywhere,
        out_shape=jax.ShapeDtypeStruct((part, rows, channels), jnp.bfloat16),
        scratch_shapes=[
            pltpu.VMEM((tiles, rows * part, LANES), jnp.float32),
            pltpu.VMEM((tiles, part, rows, LANES), jnp.bfloat16),
            pltpu.SemaphoreType.DMA((tiles,)),
        ],
        input_output_aliases={1 + count: 0} if before else {},
        compiler_params=pltpu.CompilerParams(vmem_limit_bytes=12 * 2**20),
        cost_estimate=NO_COST,
        name="add_chunk",
    )(grad_out, *(pieces[i] for i in far_first(count, count)), *before)


def prepare_kernel(count, chunks, weight_ref, filt_ref, offset_ref, forth_ref, back_ref, *outs):
    filter_out, target_out, forth_out, back_out = outs[:4]
    me = lax.axis_index("azimuth")
    wide = back_ref.shape[0] // count
    for k in range(count):
        forth_out[k] = forth_ref[partner(me, k, count, -1)]
        first = pl.multiple_of(partner(me, k, count, 1) * wide, HALF)
        back_out[k * wide : (k + 1) * wide, :] = back_ref[pl.ds(first, wide), :]
    bases, channels = weight_ref.shape
    lats, width = filt_ref.shape[1:]
    ext, depth = target_out.shape
    rows = ext - 2 * REACH
    modes = width // 2
    whole = modes // LANES * LANES
    used = TERMS * bases
    for (start, size), out in zip(chunks, outs[4:]):
        first = count * start + lax.axis_index("azimuth") * size
        weight = pltpu.roll(weight_ref[...], lax.rem(channels - first, channels), 1)[:, :size]
        parts = []
        for _ in range(TERMS):
            rounded = weight.astype(jnp.bfloat16).astype(jnp.float32)
            parts.append(rounded)
            weight = weight - rounded
        parts.append(jnp.zeros((depth - used, size), jnp.float32))
        out[...] = jnp.concatenate(parts, axis=0).T
    start_lat = lax.axis_index("polar") * rows
    table = filt_ref[...].reshape(bases * lats, width)
    base = lax.broadcasted_iota(jnp.int32, (depth, bases * lats), 0)
    valid = base < used
    for _ in range(TERMS - 1):
        base = jnp.where(base >= bases, base - bases, base)
    column = lax.broadcasted_iota(jnp.int32, (depth, bases * lats), 1)
    for i in range(ext):
        lat = start_lat + (i - REACH)
        inside = (lat >= 0) & (lat < lats)
        lat = jnp.clip(lat, 0, lats - 1)
        pick = jnp.where(valid & (column == base * lats + lat), 1.0, 0.0).astype(jnp.bfloat16)
        row = dot_nn(pick, table)
        real, imag = row[:, :modes], row[:, modes:]
        rest_re, rest_im = real[:, whole:], imag[:, whole:]
        filter_out[i] = jnp.concatenate(
            [real[:, :whole], rest_re, rest_re, imag[:, :whole], rest_im, -rest_im], axis=1
        ).astype(jnp.bfloat16)
        local = jnp.where(inside, offset_ref[pl.ds(lat, 1), :] - start_lat, -1)
        spare = jnp.full((1, depth - used), -1, jnp.int32)
        target_out[i : i + 1, :] = jnp.concatenate([local] * TERMS + [spare], axis=1)


def prepare(basis_weight, filt, offsets, forth, back, rows, count, chunks):
    bases = filt.shape[0]
    width = filt.shape[2]
    ext = rows + 2 * REACH
    depth = round_up(TERMS * bases, 16)
    shapes = [
        jax.ShapeDtypeStruct((ext, depth, width + LANES), jnp.bfloat16),
        jax.ShapeDtypeStruct((ext, depth), jnp.int32),
        jax.ShapeDtypeStruct(forth.shape, forth.dtype),
        jax.ShapeDtypeStruct(back.shape, back.dtype),
    ] + [jax.ShapeDtypeStruct((size, depth), jnp.float32) for _, size in chunks]
    return pl.pallas_call(
        functools.partial(prepare_kernel, count, chunks),
        in_specs=[pl.BlockSpec(memory_space=VMEM)] * 5,
        out_specs=[pl.BlockSpec(memory_space=VMEM)] * len(shapes),
        out_shape=shapes,
        compiler_params=pltpu.CompilerParams(vmem_limit_bytes=16 * 2**20),
        cost_estimate=NO_COST,
        name="prepare",
    )(basis_weight, filt, offsets, forth, back)


def halo(first, second):
    bands, count = lax.axis_size("polar"), lax.axis_size("azimuth")
    blocks = []
    for odd, block in ((0, first), (1, second)):
        pairs = []
        for a in range(bands):
            other = ((a + odd) ^ 1) - odd
            for b in range(count):
                paired = 0 <= other < bands
                target = (other, b) if paired else (a, b ^ 1 if b ^ 1 < count else b)
                pairs.append((a * count + b, target[0] * count + target[1]))
        blocks.append(lax.ppermute(block, ("polar", "azimuth"), pairs))
    return blocks


def on_device(chunks, conv_out, grad_out, w_in, b_in, w_out, basis_weight, filt, offsets):
    rows, part, channels = conv_out.shape
    count = lax.axis_size("azimuth")
    forth, back = tables(count, part, filt.shape[2] // 2)
    forth, back = jnp.asarray(forth), jnp.asarray(back)
    owned = channels // count
    halves = 2 if rows % 2 == 0 else 1
    pieces = []
    for half in range(halves):
        final = half == halves - 1
        far = range(NEAR + 1, count)
        sent = [(k, 0, owned) for k in range(count)]
        if final:
            sent[NEAR + 1 :] = [(k,) + chunk for chunk in chunks for k in far]
        blocks = mlp(conv_out, grad_out, w_in, b_in, w_out, count, half, halves, sent, chunks, pieces[1:2])
        steps = [] if final else list(far)
        moved = {k: exchange(blocks[k], k, count) for k in steps + list(range(NEAR + 1))}
        pieces += [moved[k] for k in sorted(moved)]
    filters, target, forth, back, *weights = prepare(
        basis_weight, filt, offsets, forth, back, rows, count, chunks
    )
    spectra, terms, grids, returned = {}, {}, {}, []

    def open_chunk(q, after):
        tail = [exchange(blocks[NEAR + 1 + q * len(far) + i], k, count) for i, k in enumerate(far)]
        own, first, second = analyze(pieces + tail, forth, rows, chunks[q], count, after)
        spectra[q] = halo(first, second)
        terms[q] = own_terms(own, weights[q], target, filters)

    def close_chunk(q):
        after = [returned[(q - 1) * count + 1]] if q else []
        halos = spectra[q]
        if q == 0:
            terms[q] = side_terms(terms[q], halos[0], weights[q], target, filters)
            halos = halos[1:]
        grids[q] = finish(terms[q], halos, weights[q], target, filters, back, count, part, after)
        blocks = {k: exchange(grids[q][k], k, count) for k in [*far, *range(NEAR + 1)]}
        returned.extend(blocks[k] for k in range(count))

    last = len(chunks) - 1
    open_chunk(0, [])
    if last > 0:
        open_chunk(1, [terms[0]])
    for q in range(last + 1):
        close_chunk(q)
        if q + 2 <= last:
            open_chunk(q + 2, [grids[q][0]])
    total = []
    for q, chunk in enumerate(chunks):
        total = [add_chunk(grad_out, returned[q * count : (q + 1) * count], chunk, count, total)]
    return jnp.transpose(total[0], (1, 0, 2))


def solution(mesh):
    grid = P(("member", "polar"), "azimuth", None)

    def run(conv_out, grad_out, *others):
        owned = conv_out.shape[2] // mesh.shape["azimuth"]
        sizes = [owned]
        if owned % 32 == 0 and owned >= 96:
            big = owned * 3 // 5 // 32 * 32
            sizes = [big, owned - big]
        chunks = tuple((sum(sizes[:q]), size) for q, size in enumerate(sizes))
        return jax.shard_map(
            functools.partial(on_device, chunks),
            mesh=mesh,
            in_specs=(grid, grid) + (P(),) * 6,
            out_specs=grid,
            check_vma=False,
        )(conv_out, grad_out, *others)

    return run
```

```python
import functools
import math

import jax
import jax.numpy as jnp
import ml_dtypes
import numpy as np
from jax import lax
from jax.experimental import pallas as pl
from jax.experimental.pallas import tpu as pltpu
from jax.sharding import PartitionSpec as P

REACH = 3
LANES = 128
HALF = 64
TERMS = 3
NEAR = 1
TOKEN = -1
VMEM = pltpu.MemorySpace.VMEM
NO_COST = pl.CostEstimate(flops=0, bytes_accessed=0, transcendentals=0)


def round_up(value, unit):
    return -(-value // unit) * unit


def partner(me, step, count, sign):
    if count & (count - 1) == 0:
        return me ^ step
    return lax.rem(me + sign * step + count, count)


def far_first(number, count):
    return sorted(range(number), key=lambda i: (i // count, i % count <= NEAR))


def exchange(block, step, count):
    if step == 0:
        return block
    pairs = [(a, int(partner_static(a, step, count))) for a in range(count)]
    return lax.ppermute(block, "azimuth", pairs)


def partner_static(a, step, count, sign=1):
    return a ^ step if count & (count - 1) == 0 else (a + sign * step) % count


def tables(count, part, modes):
    length = count * part
    whole = modes // LANES * LANES
    order = np.concatenate(
        [
            np.arange(whole),
            modes + np.arange(whole),
            np.arange(whole, modes),
            modes + np.arange(whole, modes),
        ]
    )
    positions = np.arange(length)
    waves = np.arange(modes)
    phase = (positions[:, None] * waves[None, :]) % length
    angle = (2.0 * math.pi / length) * phase
    scale = 1.0 / math.sqrt(length)
    factor = np.where(waves == 0, 1.0, 2.0)
    analysis = np.concatenate([np.cos(angle), -np.sin(angle)], axis=1) * scale
    synth = np.concatenate([np.cos(angle) * factor, -np.sin(angle) * factor], axis=1) * scale
    analysis = analysis.astype(np.float32).astype(ml_dtypes.bfloat16)[:, order]
    synth = synth.astype(np.float32).astype(ml_dtypes.bfloat16)[:, order]
    wide = round_up(part, HALF)
    window = round_up(HALF + wide, LANES)
    forth = np.zeros((count, HALF + window, 2 * modes), ml_dtypes.bfloat16)
    back = np.zeros((count * wide, 2 * modes), ml_dtypes.bfloat16)
    for s in range(count):
        forth[s, HALF : HALF + part] = analysis[s * part : (s + 1) * part]
        back[s * wide : s * wide + part] = synth[s * part : (s + 1) * part]
    return forth, back


def twice_gelu_slope(scaled):
    power = math.log2(2.0 / math.sqrt(math.pi)) - (1.0 / math.log(2.0)) * (scaled * scaled)
    return (1.0 + lax.erf(scaled)) + scaled * jnp.exp2(power)


def dot_nt(left, right):
    return lax.dot_general(left, right, (((1,), (1,)), ((), ())), preferred_element_type=jnp.float32)


def dot_nn(left, right):
    return jnp.dot(left, right, preferred_element_type=jnp.float32)


def mlp_kernel(count, half, sent, chunks, conv_ref, grad_ref, win_ref, bias_ref, wout_ref, *rest):
    outs, (tall_conv, tall_grad, pre_ref, back_ref, slope_ref, total_ref) = rest[-6 - len(sent) : -6], rest[-6:]
    part, channels = conv_ref.shape[1:]
    wide = round_up(part, HALF)
    rows = tall_conv.shape[0] // wide
    owned = channels // count
    block = pre_ref.shape[2]
    steps = win_ref.shape[1] // block
    me = lax.axis_index("azimuth")
    def stack(tall, source):
        for row in range(rows):
            whole = part // 16 * 16
            tall[row * wide + whole : (row + 1) * wide, :] = jnp.zeros((wide - whole, channels), jnp.bfloat16)
            tall[row * wide : row * wide + part, :] = source[half * rows + row]

    group = 48
    groups = rows * wide // group

    def span(step):
        return slice(step * block, (step + 1) * block)

    def project_pre(step):
        pre_ref[step % 2] = dot_nn(tall_conv[...], win_ref[:, span(step)])

    def project_back(step):
        back_ref[step % 2] = dot_nt(tall_grad[...], wout_ref[span(step), :])

    def slope(step, first, last):
        root = math.sqrt(0.5)
        bias = bias_ref[span(step)].reshape(1, block) * root
        for g in range(first, last):
            some = slice(g * group, (g + 1) * group)
            value = back_ref[step % 2, some, :] * twice_gelu_slope(pre_ref[step % 2, some, :] * root + bias)
            slope_ref[some, span(step)] = value.astype(jnp.bfloat16)

    def gather(first, last):
        at = slice(first * block, last * block)
        term = dot_nt(win_ref[:, at], slope_ref[:, at])
        total_ref[...] = term if first == 0 else total_ref[...] + term

    stack(tall_conv, conv_ref)
    project_pre(0)
    stack(tall_grad, grad_ref)
    project_back(0)
    gathered = 0
    thirds = [groups * n // 3 for n in range(4)]
    for step in range(steps):
        if step + 1 < steps:
            project_pre(step + 1)
        slope(step, thirds[0], thirds[1])
        if step - gathered == 2:
            gather(gathered, step)
            gathered = step
        slope(step, thirds[1], thirds[2])
        if step + 1 < steps:
            project_back(step + 1)
        slope(step, thirds[2], thirds[3])
    gather(gathered, steps)
    for out, (k, start, size) in zip(outs, sent):
        target = partner(me, k, count, 1)
        for begin, width in chunks:
            if start <= begin < start + size:
                first = pl.multiple_of(count * begin + target * width, 32)
                value = 0.5 * total_ref[pl.ds(first, width), :]
                out[begin - start : begin - start + width, :] = value.astype(jnp.bfloat16)


def mlp(conv_out, grad_out, w_in, b_in, w_out, count, half, halves, sent, chunks, after):
    rows, part, channels = conv_out.shape
    rows //= halves
    block = 256
    wide = round_up(part, HALF)
    vmem = pl.BlockSpec(memory_space=VMEM)
    out_shape = [jax.ShapeDtypeStruct((size, rows * wide), jnp.bfloat16) for _, _, size in sent]
    return pl.pallas_call(
        functools.partial(mlp_kernel, count, half, sent, chunks),
        in_specs=[vmem] * 5 + [pl.BlockSpec(memory_space=pl.ANY)] * len(after),
        out_specs=[vmem] * len(out_shape),
        out_shape=out_shape,
        scratch_shapes=[
            pltpu.VMEM((rows * wide, channels), jnp.bfloat16),
            pltpu.VMEM((rows * wide, channels), jnp.bfloat16),
            pltpu.VMEM((2, rows * wide, block), jnp.float32),
            pltpu.VMEM((2, rows * wide, block), jnp.float32),
            pltpu.VMEM((rows * wide, w_in.shape[1]), jnp.bfloat16),
            pltpu.VMEM((channels, rows * wide), jnp.float32),
        ],
        compiler_params=pltpu.CompilerParams(vmem_limit_bytes=16 * 2**20),
        cost_estimate=NO_COST,
        name="mlp",
    )(conv_out, grad_out, w_in, b_in, w_out, *after)


def analysis_kernel(count, rows, chunk, *refs):
    own_ref, first_ref, second_ref = refs[-3:]
    start, size = chunk
    halves = next(h for h in range(1, rows + 1) if refs[h * count].ndim == 3)
    table_ref = refs[halves * count]
    ranks = far_first(halves * count, count)
    pieces = [refs[ranks.index(i)] for i in range(halves * count)]
    rows_each = rows // halves
    wide = refs[0].shape[1] // rows_each
    window = table_ref.shape[1] - HALF
    even = lax.rem(lax.axis_index("polar"), 2) == 0

    def columns(row, k):
        half, row = divmod(row, rows_each)
        piece = pieces[half * count + k]
        base = 0 if half == halves - 1 and k > NEAR else start
        first = row * wide // LANES * LANES
        return piece[base : base + size, first : first + window]

    shifts = [row % rows_each * wide % LANES for row in range(rows)]
    for shift in sorted(set(shifts)):
        group = [row for row in range(rows) if shifts[row] == shift]
        total = None
        for k in range(count):
            left = jnp.concatenate([columns(row, k) for row in group], axis=0)
            term = dot_nn(left, table_ref[k, HALF - shift : HALF - shift + window, :])
            total = term if total is None else total + term
        for at, row in enumerate(group):
            mine = total[at * size : (at + 1) * size]
            own_ref[row] = mine

    def share(above, below):
        for h in range(REACH):
            above[h] = own_ref[rows - REACH + h].astype(jnp.bfloat16)
            below[h] = own_ref[h].astype(jnp.bfloat16)

    pl.when(even)(lambda: share(first_ref, second_ref))
    pl.when(jnp.logical_not(even))(lambda: share(second_ref, first_ref))


def analyze(pieces, table, rows, chunk, count, after):
    size = chunk[1]
    width = table.shape[2]
    halo = jax.ShapeDtypeStruct((REACH, size, width), jnp.bfloat16)
    return pl.pallas_call(
        functools.partial(analysis_kernel, count, rows, chunk),
        in_specs=[pl.BlockSpec(memory_space=VMEM)] * (len(pieces) + 1)
        + [pl.BlockSpec(memory_space=pl.ANY)] * len(after),
        out_specs=[pl.BlockSpec(memory_space=VMEM)] * 3,
        out_shape=[jax.ShapeDtypeStruct((rows, size, width), jnp.float32), halo, halo],
        compiler_params=pltpu.CompilerParams(vmem_limit_bytes=12 * 2**20),
        cost_estimate=NO_COST,
        name="analysis",
    )(*(pieces[i] for i in far_first(len(pieces), count)), table, *after)


def add_row(accs, spectrum, weight, target_row, filter_row, targets):
    size = spectrum.shape[0]
    masked = jnp.concatenate([jnp.where(target_row == t, weight, 0.0) for t in targets], axis=0)
    gains = dot_nn(masked.astype(jnp.bfloat16), filter_row)
    whole = (gains.shape[1] // 2) // LANES * LANES - LANES
    spec_re = spectrum[:, :whole]
    spec_im = spectrum[:, whole : 2 * whole]
    spec_x = spectrum[:, 2 * whole :]
    swapped = pltpu.roll(spec_x, HALF, 1)
    for at, target in enumerate(targets):
        gain = gains[at * size : (at + 1) * size]
        gain_re = gain[:, :whole]
        gain_rx = gain[:, whole : whole + LANES]
        gain_im = gain[:, whole + LANES : 2 * whole + LANES]
        gain_ix = gain[:, 2 * whole + LANES :]
        acc_re, acc_im, acc_x = accs[target]
        acc_re = acc_re + (gain_re * spec_re + gain_im * spec_im)
        acc_im = acc_im + (gain_re * spec_im - gain_im * spec_re)
        acc_x = acc_x + (gain_rx * spec_x + gain_ix * swapped)
        accs[target] = acc_re, acc_im, acc_x


def split_tiles(value):
    whole = (value.shape[1] - LANES) // 2
    return value[:, :whole], value[:, whole : 2 * whole], value[:, 2 * whole :]


def own_kernel(own_ref, weight_ref, target_ref, filter_ref, out_ref):
    rows, size, width = own_ref.shape
    accs = {t: split_tiles(jnp.zeros((size, width), jnp.float32)) for t in range(rows)}
    for row in range(rows):
        at = row + REACH
        targets = [t for t in range(rows) if abs(row - t) <= REACH]
        add_row(accs, own_ref[row], weight_ref[...], target_ref[at : at + 1, :], filter_ref[at], targets)
    for t in range(rows):
        out_ref[t] = jnp.concatenate(accs[t], axis=1)


def own_terms(own, weight, target, filters):
    return pl.pallas_call(
        own_kernel,
        in_specs=[pl.BlockSpec(memory_space=VMEM)] * 4,
        out_specs=pl.BlockSpec(memory_space=VMEM),
        out_shape=jax.ShapeDtypeStruct(own.shape, jnp.float32),
        compiler_params=pltpu.CompilerParams(vmem_limit_bytes=12 * 2**20),
        cost_estimate=NO_COST,
        name="own_terms",
    )(own, weight, target, filters)


def add_halo(accs, sides, rows, weight_ref, target_ref, filter_ref):
    for side, base in sides:
        for h in range(REACH):
            at = base + h + REACH
            targets = [t for t in range(rows) if abs(base + h - t) <= REACH]
            add_row(
                accs,
                side[h].astype(jnp.float32),
                weight_ref[...],
                target_ref[at : at + 1, :],
                filter_ref[at],
                targets,
            )


def side_kernel(part_ref, first_ref, weight_ref, target_ref, filter_ref, out_ref):
    rows = part_ref.shape[0]
    even = lax.rem(lax.axis_index("polar"), 2) == 0

    def combine(base):
        accs = {t: split_tiles(part_ref[t]) for t in range(rows)}
        add_halo(accs, [(first_ref, base)], rows, weight_ref, target_ref, filter_ref)
        for t in range(rows):
            out_ref[t] = jnp.concatenate(accs[t], axis=1)

    pl.when(even)(lambda: combine(rows))
    pl.when(jnp.logical_not(even))(lambda: combine(-REACH))


def side_terms(own, first, weight, target, filters):
    return pl.pallas_call(
        side_kernel,
        in_specs=[pl.BlockSpec(memory_space=VMEM)] * 5,
        out_specs=pl.BlockSpec(memory_space=VMEM),
        out_shape=jax.ShapeDtypeStruct(own.shape, jnp.float32),
        compiler_params=pltpu.CompilerParams(vmem_limit_bytes=12 * 2**20),
        cost_estimate=NO_COST,
        name="side_terms",
    )(own, first, weight, target, filters)


def finish_kernel(count, swaps, steps, part_ref, *refs):
    halos, (weight_ref, target_ref, filter_ref, table_ref) = refs[:swaps], refs[swaps : swaps + 4]
    outs, stacked_ref = refs[-len(steps) - 1 : -1], refs[-1]
    rows, size, width = part_ref.shape
    even = lax.rem(lax.axis_index("polar"), 2) == 0

    def combine(bases):
        accs = {t: split_tiles(part_ref[t]) for t in range(rows)}
        sides = list(zip(halos, bases[-swaps:]))
        add_halo(accs, sides, rows, weight_ref, target_ref, filter_ref)
        for t in range(rows):
            stacked_ref[t * size : (t + 1) * size, :] = jnp.concatenate(accs[t], axis=1).astype(jnp.bfloat16)

    pl.when(even)(lambda: combine((rows, -REACH)))
    pl.when(jnp.logical_not(even))(lambda: combine((-REACH, rows)))
    grid = dot_nt(table_ref[...], stacked_ref[...])
    wide = grid.shape[0] // count
    for k, out in zip(steps, outs):
        out[...] = grid[k * wide : k * wide + out.shape[0]].astype(jnp.bfloat16)


def finish(own, halos, weight, target, filters, table, count, part, cut, after):
    rows, size, width = own.shape
    wide = table.shape[0] // count
    ends = {k: wide if cut and k == NEAR else part for k in range(count)}
    if cut:
        ends[TOKEN] = cut
    steps = [NEAR if k == TOKEN else k for k in ends]
    blocks = pl.pallas_call(
        functools.partial(finish_kernel, count, len(halos), steps),
        in_specs=[pl.BlockSpec(memory_space=VMEM)] * (5 + len(halos)) + [pl.BlockSpec(memory_space=pl.ANY)] * len(after),
        out_specs=[pl.BlockSpec(memory_space=VMEM)] * len(ends),
        out_shape=[
            jax.ShapeDtypeStruct((end, rows * size), jnp.bfloat16) for end in ends.values()
        ],
        scratch_shapes=[pltpu.VMEM((rows * size, width), jnp.bfloat16)],
        compiler_params=pltpu.CompilerParams(vmem_limit_bytes=12 * 2**20),
        cost_estimate=NO_COST,
        name="finish",
    )(own, *halos, weight, target, filters, table, *after)
    return dict(zip(ends, blocks))


def add_kernel(count, chunk, steps, grad_ref, *refs):
    out_ref, tall_ref, done_ref, sems = refs[-4:]
    pieces = dict(zip(steps, refs))
    tiles, part, rows, _ = done_ref.shape
    start, size = chunk
    me = lax.axis_index("azimuth")

    def add(tile, mine):
        order = [[k for k in range(count) if partner_static(mine, k, count, -1) == s][0] for s in range(count)]
        lanes = range(tile * LANES, (tile + 1) * LANES)
        for row in range(rows):
            parts = []
            for s in range(lanes[0] // size, lanes[-1] // size + 1):
                low, high = max(lanes[0], s * size) - s * size, min(lanes[-1] + 1, (s + 1) * size) - s * size
                parts.append(pieces[order[s]][:part, row * size + low : row * size + high])
            conv = jnp.concatenate(parts, axis=1).astype(jnp.float32)
            first = count * start + tile * LANES
            total = grad_ref[row, :, first : first + LANES].astype(jnp.float32) + conv
            tall_ref[tile, pl.ds(row, part, stride=rows), :] = total
        done_ref[tile] = tall_ref[tile].reshape(part, rows, LANES).astype(jnp.bfloat16)

    copies = []
    for tile in range(tiles):
        for mine in range(count):
            pl.when(me == mine)(functools.partial(add, tile, mine))
        lanes = pl.ds(count * start + tile * LANES, LANES)
        copies.append(pltpu.make_async_copy(done_ref.at[tile], out_ref.at[:, :, lanes], sems.at[tile]))
        copies[-1].start()
    for copy in copies:
        copy.wait()


def add_chunk(grad_out, pieces, chunk, count, before):
    rows, part, channels = grad_out.shape
    start, size = chunk
    tiles = count * size // LANES
    pieces = sorted(pieces.items(), key=lambda item: item[0] <= NEAR)
    vmem = pl.BlockSpec(memory_space=VMEM)
    anywhere = pl.BlockSpec(memory_space=pl.ANY)
    return pl.pallas_call(
        functools.partial(add_kernel, count, chunk, [k for k, _ in pieces]),
        in_specs=[vmem] * (1 + len(pieces)) + [anywhere] * len(before),
        out_specs=anywhere,
        out_shape=jax.ShapeDtypeStruct((part, rows, channels), jnp.bfloat16),
        scratch_shapes=[
            pltpu.VMEM((tiles, rows * part, LANES), jnp.float32),
            pltpu.VMEM((tiles, part, rows, LANES), jnp.bfloat16),
            pltpu.SemaphoreType.DMA((tiles,)),
        ],
        input_output_aliases={1 + len(pieces): 0} if before else {},
        compiler_params=pltpu.CompilerParams(vmem_limit_bytes=12 * 2**20),
        cost_estimate=NO_COST,
        name="add_chunk",
    )(grad_out, *(block for _, block in pieces), *before)


def prepare_kernel(count, chunks, weight_ref, filt_ref, offset_ref, forth_ref, back_ref, *outs):
    filter_out, target_out, forth_out, back_out = outs[:4]
    me = lax.axis_index("azimuth")
    wide = back_ref.shape[0] // count
    for k in range(count):
        forth_out[k] = forth_ref[partner(me, k, count, -1)]
        first = pl.multiple_of(partner(me, k, count, 1) * wide, HALF)
        back_out[k * wide : (k + 1) * wide, :] = back_ref[pl.ds(first, wide), :]
    bases, channels = weight_ref.shape
    lats, width = filt_ref.shape[1:]
    ext, depth = target_out.shape
    rows = ext - 2 * REACH
    modes = width // 2
    whole = modes // LANES * LANES
    used = TERMS * bases
    for (start, size), out in zip(chunks, outs[4:]):
        first = count * start + lax.axis_index("azimuth") * size
        weight = pltpu.roll(weight_ref[...], lax.rem(channels - first, channels), 1)[:, :size]
        parts = []
        for _ in range(TERMS):
            rounded = weight.astype(jnp.bfloat16).astype(jnp.float32)
            parts.append(rounded)
            weight = weight - rounded
        parts.append(jnp.zeros((depth - used, size), jnp.float32))
        out[...] = jnp.concatenate(parts, axis=0).T
    start_lat = lax.axis_index("polar") * rows
    table = filt_ref[...].reshape(bases * lats, width)
    base = lax.broadcasted_iota(jnp.int32, (depth, bases * lats), 0)
    valid = base < used
    for _ in range(TERMS - 1):
        base = jnp.where(base >= bases, base - bases, base)
    column = lax.broadcasted_iota(jnp.int32, (depth, bases * lats), 1)
    for i in range(ext):
        lat = start_lat + (i - REACH)
        inside = (lat >= 0) & (lat < lats)
        lat = jnp.clip(lat, 0, lats - 1)
        pick = jnp.where(valid & (column == base * lats + lat), 1.0, 0.0).astype(jnp.bfloat16)
        row = dot_nn(pick, table)
        real, imag = row[:, :modes], row[:, modes:]
        rest_re, rest_im = real[:, whole:], imag[:, whole:]
        filter_out[i] = jnp.concatenate(
            [real[:, :whole], rest_re, rest_re, imag[:, :whole], rest_im, -rest_im], axis=1
        ).astype(jnp.bfloat16)
        local = jnp.where(inside, offset_ref[pl.ds(lat, 1), :] - start_lat, -1)
        spare = jnp.full((1, depth - used), -1, jnp.int32)
        target_out[i : i + 1, :] = jnp.concatenate([local] * TERMS + [spare], axis=1)


def prepare(basis_weight, filt, offsets, forth, back, rows, count, chunks):
    bases = filt.shape[0]
    width = filt.shape[2]
    ext = rows + 2 * REACH
    depth = round_up(TERMS * bases, 16)
    shapes = [
        jax.ShapeDtypeStruct((ext, depth, width + LANES), jnp.bfloat16),
        jax.ShapeDtypeStruct((ext, depth), jnp.int32),
        jax.ShapeDtypeStruct(forth.shape, forth.dtype),
        jax.ShapeDtypeStruct(back.shape, back.dtype),
    ] + [jax.ShapeDtypeStruct((size, depth), jnp.float32) for _, size in chunks]
    return pl.pallas_call(
        functools.partial(prepare_kernel, count, chunks),
        in_specs=[pl.BlockSpec(memory_space=VMEM)] * 5,
        out_specs=[pl.BlockSpec(memory_space=VMEM)] * len(shapes),
        out_shape=shapes,
        compiler_params=pltpu.CompilerParams(vmem_limit_bytes=16 * 2**20),
        cost_estimate=NO_COST,
        name="prepare",
    )(basis_weight, filt, offsets, forth, back)


def halo(first, second):
    bands, count = lax.axis_size("polar"), lax.axis_size("azimuth")
    blocks = []
    for odd, block in ((0, first), (1, second)):
        pairs = []
        for a in range(bands):
            other = ((a + odd) ^ 1) - odd
            for b in range(count):
                paired = 0 <= other < bands
                target = (other, b) if paired else (a, b ^ 1 if b ^ 1 < count else b)
                pairs.append((a * count + b, target[0] * count + target[1]))
        blocks.append(lax.ppermute(block, ("polar", "azimuth"), pairs))
    return blocks


def on_device(chunks, conv_out, grad_out, w_in, b_in, w_out, basis_weight, filt, offsets):
    rows, part, channels = conv_out.shape
    count = lax.axis_size("azimuth")
    forth, back = tables(count, part, filt.shape[2] // 2)
    forth, back = jnp.asarray(forth), jnp.asarray(back)
    owned = channels // count
    halves = 2 if rows % 2 == 0 else 1
    pieces = []
    for half in range(halves):
        final = half == halves - 1
        far = range(NEAR + 1, count)
        sent = [(k, 0, owned) for k in range(count)]
        if final:
            sent[NEAR + 1 :] = [(k,) + chunk for chunk in chunks for k in far]
        blocks = mlp(conv_out, grad_out, w_in, b_in, w_out, count, half, halves, sent, chunks, pieces[1:2])
        steps = [] if final else list(far)
        moved = {k: exchange(blocks[k], k, count) for k in steps + list(range(NEAR + 1))}
        pieces += [moved[k] for k in sorted(moved)]
    filters, target, forth, back, *weights = prepare(
        basis_weight, filt, offsets, forth, back, rows, count, chunks
    )
    spectra, terms, grids, returned = {}, {}, {}, {}

    def open_chunk(q, after):
        tail = [exchange(blocks[NEAR + 1 + q * len(far) + i], k, count) for i, k in enumerate(far)]
        own, first, second = analyze(pieces + tail, forth, rows, chunks[q], count, after)
        spectra[q] = halo(first, second)
        terms[q] = own_terms(own, weights[q], target, filters)

    def close_chunk(q):
        after = [returned[q - 1].pop(TOKEN)] if q else []
        cut = 0 if q == last else 16
        halos = spectra[q]
        if q == 0:
            terms[q] = side_terms(terms[q], halos[0], weights[q], target, filters)
            halos = halos[1:]
        grids[q] = finish(terms[q], halos, weights[q], target, filters, back, count, part, cut, after)
        returned[q] = {k: exchange(block, NEAR if k == TOKEN else k, count) for k, block in grids[q].items()}

    last = len(chunks) - 1
    open_chunk(0, [])
    if last > 0:
        open_chunk(1, [terms[0]])
    for q in range(last + 1):
        close_chunk(q)
        if q + 2 <= last:
            open_chunk(q + 2, [grids[q][0]])
    total = []
    for q, chunk in enumerate(chunks):
        total = [add_chunk(grad_out, returned[q], chunk, count, total)]
    return jnp.transpose(total[0], (1, 0, 2))


def solution(mesh):
    grid = P(("member", "polar"), "azimuth", None)

    def run(conv_out, grad_out, *others):
        owned = conv_out.shape[2] // mesh.shape["azimuth"]
        sizes = [owned]
        if owned % 32 == 0 and owned >= 96:
            big = owned * 3 // 5 // 32 * 32
            sizes = [big, owned - big]
        chunks = tuple((sum(sizes[:q]), size) for q, size in enumerate(sizes))
        return jax.shard_map(
            functools.partial(on_device, chunks),
            mesh=mesh,
            in_specs=(grid, grid) + (P(),) * 6,
            out_specs=grid,
            check_vma=False,
        )(conv_out, grad_out, *others)

    return run
```

```python
import functools
import math

import jax
import jax.numpy as jnp
import ml_dtypes
import numpy as np
from jax import lax
from jax.experimental import pallas as pl
from jax.experimental.pallas import tpu as pltpu
from jax.sharding import PartitionSpec as P

REACH = 3
LANES = 128
HALF = 64
TERMS = 3
NEAR = 1
TOKEN = -1
VMEM = pltpu.MemorySpace.VMEM
NO_COST = pl.CostEstimate(flops=0, bytes_accessed=0, transcendentals=0)


def round_up(value, unit):
    return -(-value // unit) * unit


def partner(me, step, count, sign):
    if count & (count - 1) == 0:
        return me ^ step
    return lax.rem(me + sign * step + count, count)


def far_first(number, count):
    return sorted(range(number), key=lambda i: (i // count, i % count <= NEAR))


def exchange(block, step, count):
    if step == 0:
        return block
    pairs = [(a, int(partner_static(a, step, count))) for a in range(count)]
    return lax.ppermute(block, "azimuth", pairs)


def partner_static(a, step, count, sign=1):
    return a ^ step if count & (count - 1) == 0 else (a + sign * step) % count


def tables(count, part, modes):
    length = count * part
    whole = modes // LANES * LANES
    order = np.concatenate(
        [
            np.arange(whole),
            modes + np.arange(whole),
            np.arange(whole, modes),
            modes + np.arange(whole, modes),
        ]
    )
    positions = np.arange(length)
    waves = np.arange(modes)
    phase = (positions[:, None] * waves[None, :]) % length
    angle = (2.0 * math.pi / length) * phase
    scale = 1.0 / math.sqrt(length)
    factor = np.where(waves == 0, 1.0, 2.0)
    analysis = np.concatenate([np.cos(angle), -np.sin(angle)], axis=1) * scale
    synth = np.concatenate([np.cos(angle) * factor, -np.sin(angle) * factor], axis=1) * scale
    analysis = analysis.astype(np.float32).astype(ml_dtypes.bfloat16)[:, order]
    synth = synth.astype(np.float32).astype(ml_dtypes.bfloat16)[:, order]
    wide = round_up(part, HALF)
    window = round_up(HALF + wide, LANES)
    forth = np.zeros((count, HALF + window, 2 * modes), ml_dtypes.bfloat16)
    back = np.zeros((count * wide, 2 * modes), ml_dtypes.bfloat16)
    for s in range(count):
        forth[s, HALF : HALF + part] = analysis[s * part : (s + 1) * part]
        back[s * wide : s * wide + part] = synth[s * part : (s + 1) * part]
    return forth, back


def twice_gelu_slope(scaled):
    power = math.log2(2.0 / math.sqrt(math.pi)) - (1.0 / math.log(2.0)) * (scaled * scaled)
    return (1.0 + lax.erf(scaled)) + scaled * jnp.exp2(power)


def dot_nt(left, right):
    return lax.dot_general(left, right, (((1,), (1,)), ((), ())), preferred_element_type=jnp.float32)


def dot_nn(left, right):
    return jnp.dot(left, right, preferred_element_type=jnp.float32)


def mlp_kernel(count, half, sent, chunks, conv_ref, grad_ref, win_ref, bias_ref, wout_ref, *rest):
    outs, (tall_conv, tall_grad, pre_ref, back_ref, slope_ref, total_ref) = rest[-6 - len(sent) : -6], rest[-6:]
    part, channels = conv_ref.shape[1:]
    wide = round_up(part, HALF)
    rows = tall_conv.shape[0] // wide
    owned = channels // count
    block = pre_ref.shape[2]
    steps = win_ref.shape[1] // block
    me = lax.axis_index("azimuth")
    def stack(tall, source):
        for row in range(rows):
            whole = part // 16 * 16
            tall[row * wide + whole : (row + 1) * wide, :] = jnp.zeros((wide - whole, channels), jnp.bfloat16)
            tall[row * wide : row * wide + part, :] = source[half * rows + row]

    group = 48
    groups = rows * wide // group

    def span(step):
        return slice(step * block, (step + 1) * block)

    def project_pre(step):
        pre_ref[step % 2] = dot_nn(tall_conv[...], win_ref[:, span(step)])

    def project_back(step):
        back_ref[step % 2] = dot_nt(tall_grad[...], wout_ref[span(step), :])

    def slope(step, first, last):
        root = math.sqrt(0.5)
        bias = bias_ref[span(step)].reshape(1, block) * root
        for g in range(first, last):
            some = slice(g * group, (g + 1) * group)
            value = back_ref[step % 2, some, :] * twice_gelu_slope(pre_ref[step % 2, some, :] * root + bias)
            slope_ref[some, span(step)] = value.astype(jnp.bfloat16)

    def gather(first, last):
        at = slice(first * block, last * block)
        term = dot_nt(win_ref[:, at], slope_ref[:, at])
        total_ref[...] = term if first == 0 else total_ref[...] + term

    stack(tall_conv, conv_ref)
    project_pre(0)
    stack(tall_grad, grad_ref)
    project_back(0)
    gathered = 0
    thirds = [groups * n // 3 for n in range(4)]
    for step in range(steps):
        if step + 1 < steps:
            project_pre(step + 1)
        slope(step, thirds[0], thirds[1])
        if step - gathered == 2:
            gather(gathered, step)
            gathered = step
        slope(step, thirds[1], thirds[2])
        if step + 1 < steps:
            project_back(step + 1)
        slope(step, thirds[2], thirds[3])
    gather(gathered, steps)
    for out, (k, start, size) in zip(outs, sent):
        target = partner(me, k, count, 1)
        for begin, width in chunks:
            if start <= begin < start + size:
                first = pl.multiple_of(count * begin + target * width, 32)
                value = 0.5 * total_ref[pl.ds(first, width), :]
                out[begin - start : begin - start + width, :] = value.astype(jnp.bfloat16)


def mlp(conv_out, grad_out, w_in, b_in, w_out, count, half, halves, sent, chunks, after):
    rows, part, channels = conv_out.shape
    rows //= halves
    block = 256
    wide = round_up(part, HALF)
    vmem = pl.BlockSpec(memory_space=VMEM)
    out_shape = [jax.ShapeDtypeStruct((size, rows * wide), jnp.bfloat16) for _, _, size in sent]
    return pl.pallas_call(
        functools.partial(mlp_kernel, count, half, sent, chunks),
        in_specs=[vmem] * 5 + [pl.BlockSpec(memory_space=pl.ANY)] * len(after),
        out_specs=[vmem] * len(out_shape),
        out_shape=out_shape,
        scratch_shapes=[
            pltpu.VMEM((rows * wide, channels), jnp.bfloat16),
            pltpu.VMEM((rows * wide, channels), jnp.bfloat16),
            pltpu.VMEM((2, rows * wide, block), jnp.float32),
            pltpu.VMEM((2, rows * wide, block), jnp.float32),
            pltpu.VMEM((rows * wide, w_in.shape[1]), jnp.bfloat16),
            pltpu.VMEM((channels, rows * wide), jnp.float32),
        ],
        compiler_params=pltpu.CompilerParams(vmem_limit_bytes=16 * 2**20),
        cost_estimate=NO_COST,
        name="mlp",
    )(conv_out, grad_out, w_in, b_in, w_out, *after)


def analysis_kernel(count, rows, chunk, *refs):
    own_ref, first_ref, second_ref = refs[-3:]
    start, size = chunk
    halves = next(h for h in range(1, rows + 1) if refs[h * count].ndim == 3)
    table_ref = refs[halves * count]
    ranks = far_first(halves * count, count)
    pieces = [refs[ranks.index(i)] for i in range(halves * count)]
    rows_each = rows // halves
    wide = refs[0].shape[1] // rows_each
    window = table_ref.shape[1] - HALF
    even = lax.rem(lax.axis_index("polar"), 2) == 0

    def columns(row, k):
        half, row = divmod(row, rows_each)
        piece = pieces[half * count + k]
        base = 0 if half == halves - 1 and k > NEAR else start
        first = row * wide // LANES * LANES
        return piece[base : base + size, first : first + window]

    shifts = [row % rows_each * wide % LANES for row in range(rows)]
    for shift in sorted(set(shifts)):
        group = [row for row in range(rows) if shifts[row] == shift]
        total = None
        for k in range(count):
            left = jnp.concatenate([columns(row, k) for row in group], axis=0)
            term = dot_nn(left, table_ref[k, HALF - shift : HALF - shift + window, :])
            total = term if total is None else total + term
        for at, row in enumerate(group):
            mine = total[at * size : (at + 1) * size]
            own_ref[row] = mine

    def share(above, below):
        for h in range(REACH):
            above[h] = own_ref[rows - REACH + h].astype(jnp.bfloat16)
            below[h] = own_ref[h].astype(jnp.bfloat16)

    pl.when(even)(lambda: share(first_ref, second_ref))
    pl.when(jnp.logical_not(even))(lambda: share(second_ref, first_ref))


def analyze(pieces, table, rows, chunk, count, after):
    size = chunk[1]
    width = table.shape[2]
    halo = jax.ShapeDtypeStruct((REACH, size, width), jnp.bfloat16)
    return pl.pallas_call(
        functools.partial(analysis_kernel, count, rows, chunk),
        in_specs=[pl.BlockSpec(memory_space=VMEM)] * (len(pieces) + 1)
        + [pl.BlockSpec(memory_space=pl.ANY)] * len(after),
        out_specs=[pl.BlockSpec(memory_space=VMEM)] * 3,
        out_shape=[jax.ShapeDtypeStruct((rows, size, width), jnp.float32), halo, halo],
        compiler_params=pltpu.CompilerParams(vmem_limit_bytes=12 * 2**20),
        cost_estimate=NO_COST,
        name="analysis",
    )(*(pieces[i] for i in far_first(len(pieces), count)), table, *after)


def add_row(accs, spectrum, weight, target_row, filter_row, targets):
    size = spectrum.shape[0]
    masked = jnp.concatenate([jnp.where(target_row == t, weight, 0.0) for t in targets], axis=0)
    gains = dot_nn(masked.astype(jnp.bfloat16), filter_row)
    whole = (gains.shape[1] // 2) // LANES * LANES - LANES
    spec_re = spectrum[:, :whole]
    spec_im = spectrum[:, whole : 2 * whole]
    spec_x = spectrum[:, 2 * whole :]
    swapped = pltpu.roll(spec_x, HALF, 1)
    for at, target in enumerate(targets):
        gain = gains[at * size : (at + 1) * size]
        gain_re = gain[:, :whole]
        gain_rx = gain[:, whole : whole + LANES]
        gain_im = gain[:, whole + LANES : 2 * whole + LANES]
        gain_ix = gain[:, 2 * whole + LANES :]
        acc_re, acc_im, acc_x = accs[target]
        acc_re = acc_re + (gain_re * spec_re + gain_im * spec_im)
        acc_im = acc_im + (gain_re * spec_im - gain_im * spec_re)
        acc_x = acc_x + (gain_rx * spec_x + gain_ix * swapped)
        accs[target] = acc_re, acc_im, acc_x


def split_tiles(value):
    whole = (value.shape[1] - LANES) // 2
    return value[:, :whole], value[:, whole : 2 * whole], value[:, 2 * whole :]


def own_kernel(own_ref, weight_ref, target_ref, filter_ref, out_ref):
    rows, size, width = own_ref.shape
    accs = {t: split_tiles(jnp.zeros((size, width), jnp.float32)) for t in range(rows)}
    for row in range(rows):
        at = row + REACH
        targets = [t for t in range(rows) if abs(row - t) <= REACH]
        add_row(accs, own_ref[row], weight_ref[...], target_ref[at : at + 1, :], filter_ref[at], targets)
    for t in range(rows):
        out_ref[t] = jnp.concatenate(accs[t], axis=1)


def own_terms(own, weight, target, filters):
    return pl.pallas_call(
        own_kernel,
        in_specs=[pl.BlockSpec(memory_space=VMEM)] * 4,
        out_specs=pl.BlockSpec(memory_space=VMEM),
        out_shape=jax.ShapeDtypeStruct(own.shape, jnp.float32),
        compiler_params=pltpu.CompilerParams(vmem_limit_bytes=12 * 2**20),
        cost_estimate=NO_COST,
        name="own_terms",
    )(own, weight, target, filters)


def add_halo(accs, sides, rows, weight_ref, target_ref, filter_ref):
    for side, base in sides:
        for h in range(REACH):
            at = base + h + REACH
            targets = [t for t in range(rows) if abs(base + h - t) <= REACH]
            add_row(
                accs,
                side[h].astype(jnp.float32),
                weight_ref[...],
                target_ref[at : at + 1, :],
                filter_ref[at],
                targets,
            )


def side_kernel(part_ref, first_ref, weight_ref, target_ref, filter_ref, *rest):
    out_ref = rest[-1]
    rows = part_ref.shape[0]
    even = lax.rem(lax.axis_index("polar"), 2) == 0

    def combine(base):
        accs = {t: split_tiles(part_ref[t]) for t in range(rows)}
        add_halo(accs, [(first_ref, base)], rows, weight_ref, target_ref, filter_ref)
        for t in range(rows):
            out_ref[t] = jnp.concatenate(accs[t], axis=1)

    pl.when(even)(lambda: combine(rows))
    pl.when(jnp.logical_not(even))(lambda: combine(-REACH))


def side_terms(own, first, weight, target, filters, after):
    return pl.pallas_call(
        side_kernel,
        in_specs=[pl.BlockSpec(memory_space=VMEM)] * 5 + [pl.BlockSpec(memory_space=pl.ANY)] * len(after),
        out_specs=pl.BlockSpec(memory_space=VMEM),
        out_shape=jax.ShapeDtypeStruct(own.shape, jnp.float32),
        compiler_params=pltpu.CompilerParams(vmem_limit_bytes=12 * 2**20),
        cost_estimate=NO_COST,
        name="side_terms",
    )(own, first, weight, target, filters, *after)


def finish_kernel(count, swaps, steps, part_ref, *refs):
    halos, (weight_ref, target_ref, filter_ref, table_ref) = refs[:swaps], refs[swaps : swaps + 4]
    outs, stacked_ref = refs[-len(steps) - 1 : -1], refs[-1]
    rows, size, width = part_ref.shape
    even = lax.rem(lax.axis_index("polar"), 2) == 0

    def combine(bases):
        accs = {t: split_tiles(part_ref[t]) for t in range(rows)}
        sides = list(zip(halos, bases[-swaps:]))
        add_halo(accs, sides, rows, weight_ref, target_ref, filter_ref)
        for t in range(rows):
            stacked_ref[t * size : (t + 1) * size, :] = jnp.concatenate(accs[t], axis=1).astype(jnp.bfloat16)

    pl.when(even)(lambda: combine((rows, -REACH)))
    pl.when(jnp.logical_not(even))(lambda: combine((-REACH, rows)))
    grid = dot_nt(table_ref[...], stacked_ref[...])
    wide = grid.shape[0] // count
    for k, out in zip(steps, outs):
        out[...] = grid[k * wide : k * wide + out.shape[0]].astype(jnp.bfloat16)


def finish(own, halos, weight, target, filters, table, count, part, cut, after):
    rows, size, width = own.shape
    wide = table.shape[0] // count
    ends = {k: wide if cut and k == NEAR else part for k in range(count)}
    if cut:
        ends[TOKEN] = cut
    steps = [NEAR if k == TOKEN else k for k in ends]
    blocks = pl.pallas_call(
        functools.partial(finish_kernel, count, len(halos), steps),
        in_specs=[pl.BlockSpec(memory_space=VMEM)] * (5 + len(halos)) + [pl.BlockSpec(memory_space=pl.ANY)] * len(after),
        out_specs=[pl.BlockSpec(memory_space=VMEM)] * len(ends),
        out_shape=[
            jax.ShapeDtypeStruct((end, rows * size), jnp.bfloat16) for end in ends.values()
        ],
        scratch_shapes=[pltpu.VMEM((rows * size, width), jnp.bfloat16)],
        compiler_params=pltpu.CompilerParams(vmem_limit_bytes=12 * 2**20),
        cost_estimate=NO_COST,
        name="finish",
    )(own, *halos, weight, target, filters, table, *after)
    return dict(zip(ends, blocks))


def add_kernel(count, chunk, steps, grad_ref, *refs):
    out_ref, tall_ref, done_ref, sems = refs[-4:]
    pieces = dict(zip(steps, refs))
    tiles, part, rows, _ = done_ref.shape
    start, size = chunk
    me = lax.axis_index("azimuth")

    def add(tile, mine):
        order = [[k for k in range(count) if partner_static(mine, k, count, -1) == s][0] for s in range(count)]
        lanes = range(tile * LANES, (tile + 1) * LANES)
        for row in range(rows):
            parts = []
            for s in range(lanes[0] // size, lanes[-1] // size + 1):
                low, high = max(lanes[0], s * size) - s * size, min(lanes[-1] + 1, (s + 1) * size) - s * size
                parts.append(pieces[order[s]][:part, row * size + low : row * size + high])
            conv = jnp.concatenate(parts, axis=1).astype(jnp.float32)
            first = count * start + tile * LANES
            total = grad_ref[row, :, first : first + LANES].astype(jnp.float32) + conv
            tall_ref[tile, pl.ds(row, part, stride=rows), :] = total
        done_ref[tile] = tall_ref[tile].reshape(part, rows, LANES).astype(jnp.bfloat16)

    copies = []
    for tile in range(tiles):
        for mine in range(count):
            pl.when(me == mine)(functools.partial(add, tile, mine))
        lanes = pl.ds(count * start + tile * LANES, LANES)
        copies.append(pltpu.make_async_copy(done_ref.at[tile], out_ref.at[:, :, lanes], sems.at[tile]))
        copies[-1].start()
    for copy in copies:
        copy.wait()


def add_chunk(grad_out, pieces, chunk, count, before):
    rows, part, channels = grad_out.shape
    start, size = chunk
    tiles = count * size // LANES
    pieces = sorted(pieces.items(), key=lambda item: item[0] <= NEAR)
    vmem = pl.BlockSpec(memory_space=VMEM)
    anywhere = pl.BlockSpec(memory_space=pl.ANY)
    return pl.pallas_call(
        functools.partial(add_kernel, count, chunk, [k for k, _ in pieces]),
        in_specs=[vmem] * (1 + len(pieces)) + [anywhere] * len(before),
        out_specs=anywhere,
        out_shape=jax.ShapeDtypeStruct((part, rows, channels), jnp.bfloat16),
        scratch_shapes=[
            pltpu.VMEM((tiles, rows * part, LANES), jnp.float32),
            pltpu.VMEM((tiles, part, rows, LANES), jnp.bfloat16),
            pltpu.SemaphoreType.DMA((tiles,)),
        ],
        input_output_aliases={1 + len(pieces): 0} if before else {},
        compiler_params=pltpu.CompilerParams(vmem_limit_bytes=12 * 2**20),
        cost_estimate=NO_COST,
        name="add_chunk",
    )(grad_out, *(block for _, block in pieces), *before)


def prepare_kernel(count, chunks, weight_ref, filt_ref, offset_ref, forth_ref, back_ref, *outs):
    filter_out, target_out, forth_out, back_out = outs[:4]
    me = lax.axis_index("azimuth")
    wide = back_ref.shape[0] // count
    for k in range(count):
        forth_out[k] = forth_ref[partner(me, k, count, -1)]
        first = pl.multiple_of(partner(me, k, count, 1) * wide, HALF)
        back_out[k * wide : (k + 1) * wide, :] = back_ref[pl.ds(first, wide), :]
    bases, channels = weight_ref.shape
    lats, width = filt_ref.shape[1:]
    ext, depth = target_out.shape
    rows = ext - 2 * REACH
    modes = width // 2
    whole = modes // LANES * LANES
    used = TERMS * bases
    for (start, size), out in zip(chunks, outs[4:]):
        first = count * start + lax.axis_index("azimuth") * size
        weight = pltpu.roll(weight_ref[...], lax.rem(channels - first, channels), 1)[:, :size]
        parts = []
        for _ in range(TERMS):
            rounded = weight.astype(jnp.bfloat16).astype(jnp.float32)
            parts.append(rounded)
            weight = weight - rounded
        parts.append(jnp.zeros((depth - used, size), jnp.float32))
        out[...] = jnp.concatenate(parts, axis=0).T
    start_lat = lax.axis_index("polar") * rows
    table = filt_ref[...].reshape(bases * lats, width)
    base = lax.broadcasted_iota(jnp.int32, (depth, bases * lats), 0)
    valid = base < used
    for _ in range(TERMS - 1):
        base = jnp.where(base >= bases, base - bases, base)
    column = lax.broadcasted_iota(jnp.int32, (depth, bases * lats), 1)
    for i in range(ext):
        lat = start_lat + (i - REACH)
        inside = (lat >= 0) & (lat < lats)
        lat = jnp.clip(lat, 0, lats - 1)
        pick = jnp.where(valid & (column == base * lats + lat), 1.0, 0.0).astype(jnp.bfloat16)
        row = dot_nn(pick, table)
        real, imag = row[:, :modes], row[:, modes:]
        rest_re, rest_im = real[:, whole:], imag[:, whole:]
        filter_out[i] = jnp.concatenate(
            [real[:, :whole], rest_re, rest_re, imag[:, :whole], rest_im, -rest_im], axis=1
        ).astype(jnp.bfloat16)
        local = jnp.where(inside, offset_ref[pl.ds(lat, 1), :] - start_lat, -1)
        spare = jnp.full((1, depth - used), -1, jnp.int32)
        target_out[i : i + 1, :] = jnp.concatenate([local] * TERMS + [spare], axis=1)


def prepare(basis_weight, filt, offsets, forth, back, rows, count, chunks):
    bases = filt.shape[0]
    width = filt.shape[2]
    ext = rows + 2 * REACH
    depth = round_up(TERMS * bases, 16)
    shapes = [
        jax.ShapeDtypeStruct((ext, depth, width + LANES), jnp.bfloat16),
        jax.ShapeDtypeStruct((ext, depth), jnp.int32),
        jax.ShapeDtypeStruct(forth.shape, forth.dtype),
        jax.ShapeDtypeStruct(back.shape, back.dtype),
    ] + [jax.ShapeDtypeStruct((size, depth), jnp.float32) for _, size in chunks]
    return pl.pallas_call(
        functools.partial(prepare_kernel, count, chunks),
        in_specs=[pl.BlockSpec(memory_space=VMEM)] * 5,
        out_specs=[pl.BlockSpec(memory_space=VMEM)] * len(shapes),
        out_shape=shapes,
        compiler_params=pltpu.CompilerParams(vmem_limit_bytes=16 * 2**20),
        cost_estimate=NO_COST,
        name="prepare",
    )(basis_weight, filt, offsets, forth, back)


def halo(first, second):
    bands, count = lax.axis_size("polar"), lax.axis_size("azimuth")
    blocks = []
    for odd, block in ((0, first), (1, second)):
        pairs = []
        for a in range(bands):
            other = ((a + odd) ^ 1) - odd
            for b in range(count):
                paired = 0 <= other < bands
                target = (other, b) if paired else (a, b ^ 1 if b ^ 1 < count else b)
                pairs.append((a * count + b, target[0] * count + target[1]))
        blocks.append(lax.ppermute(block, ("polar", "azimuth"), pairs))
    return blocks


def on_device(chunks, conv_out, grad_out, w_in, b_in, w_out, basis_weight, filt, offsets):
    rows, part, channels = conv_out.shape
    count = lax.axis_size("azimuth")
    forth, back = tables(count, part, filt.shape[2] // 2)
    forth, back = jnp.asarray(forth), jnp.asarray(back)
    owned = channels // count
    halves = 2 if rows % 2 == 0 else 1
    pieces = []
    for half in range(halves):
        final = half == halves - 1
        far = range(NEAR + 1, count)
        sent = [(k, 0, owned) for k in range(count)]
        if final:
            sent[NEAR + 1 :] = [(k,) + chunk for chunk in chunks for k in far]
        blocks = mlp(conv_out, grad_out, w_in, b_in, w_out, count, half, halves, sent, chunks, pieces[1:2])
        steps = [] if final else list(far)
        moved = {k: exchange(blocks[k], k, count) for k in steps + list(range(NEAR + 1))}
        pieces += [moved[k] for k in sorted(moved)]
    filters, target, forth, back, *weights = prepare(
        basis_weight, filt, offsets, forth, back, rows, count, chunks
    )
    spectra, terms, grids, returned = {}, {}, {}, {}

    def open_chunk(q, after):
        tail = [exchange(blocks[NEAR + 1 + q * len(far) + i], k, count) for i, k in enumerate(far)]
        own, first, second = analyze(pieces + tail, forth, rows, chunks[q], count, after)
        spectra[q] = halo(first, second)
        terms[q] = own_terms(own, weights[q], target, filters)

    def close_chunk(q):
        after = []
        cut = 0
        halos = spectra[q]
        if q == 0:
            others = [terms[other] for other in terms if other > q]
            terms[q] = side_terms(terms[q], halos[0], weights[q], target, filters, others)
            halos = halos[1:]
        grids[q] = finish(terms[q], halos, weights[q], target, filters, back, count, part, cut, after)
        returned[q] = {k: exchange(block, NEAR if k == TOKEN else k, count) for k, block in grids[q].items()}

    last = len(chunks) - 1
    open_chunk(0, [])
    if last > 0:
        open_chunk(1, [terms[0]])
    for q in range(last + 1):
        close_chunk(q)
        if q + 2 <= last:
            open_chunk(q + 2, [grids[q][0]])
    total = []
    for q, chunk in enumerate(chunks):
        total = [add_chunk(grad_out, returned[q], chunk, count, total)]
    return jnp.transpose(total[0], (1, 0, 2))


def solution(mesh):
    grid = P(("member", "polar"), "azimuth", None)

    def run(conv_out, grad_out, *others):
        owned = conv_out.shape[2] // mesh.shape["azimuth"]
        sizes = [owned]
        if owned % 32 == 0 and owned >= 96:
            big = owned * 3 // 5 // 32 * 32
            sizes = [big, owned - big]
        chunks = tuple((sum(sizes[:q]), size) for q, size in enumerate(sizes))
        return jax.shard_map(
            functools.partial(on_device, chunks),
            mesh=mesh,
            in_specs=(grid, grid) + (P(),) * 6,
            out_specs=grid,
            check_vma=False,
        )(conv_out, grad_out, *others)

    return run
```

```python
import functools
import math

import jax
import jax.numpy as jnp
import ml_dtypes
import numpy as np
from jax import lax
from jax.experimental import pallas as pl
from jax.experimental.pallas import tpu as pltpu
from jax.sharding import PartitionSpec as P

REACH = 3
LANES = 128
HALF = 64
TERMS = 3
NEAR = 1
VMEM = pltpu.MemorySpace.VMEM
NO_COST = pl.CostEstimate(flops=0, bytes_accessed=0, transcendentals=0)


def round_up(value, unit):
    return -(-value // unit) * unit


def partner(me, step, count, sign):
    if count & (count - 1) == 0:
        return me ^ step
    return lax.rem(me + sign * step + count, count)


def far_first(number, count):
    return sorted(range(number), key=lambda i: (i // count, i % count <= NEAR))


def exchange(block, step, count):
    if step == 0:
        return block
    pairs = [(a, int(partner_static(a, step, count))) for a in range(count)]
    return lax.ppermute(block, "azimuth", pairs)


def partner_static(a, step, count, sign=1):
    return a ^ step if count & (count - 1) == 0 else (a + sign * step) % count


def tables(count, part, modes):
    length = count * part
    whole = modes // LANES * LANES
    order = np.concatenate(
        [
            np.arange(whole),
            modes + np.arange(whole),
            np.arange(whole, modes),
            modes + np.arange(whole, modes),
        ]
    )
    positions = np.arange(length)
    waves = np.arange(modes)
    phase = (positions[:, None] * waves[None, :]) % length
    angle = (2.0 * math.pi / length) * phase
    scale = 1.0 / math.sqrt(length)
    factor = np.where(waves == 0, 1.0, 2.0)
    analysis = np.concatenate([np.cos(angle), -np.sin(angle)], axis=1) * scale
    synth = np.concatenate([np.cos(angle) * factor, -np.sin(angle) * factor], axis=1) * scale
    analysis = analysis.astype(np.float32).astype(ml_dtypes.bfloat16)[:, order]
    synth = synth.astype(np.float32).astype(ml_dtypes.bfloat16)[:, order]
    wide = round_up(part, HALF)
    window = round_up(HALF + wide, LANES)
    forth = np.zeros((count, HALF + window, 2 * modes), ml_dtypes.bfloat16)
    back = np.zeros((count * wide, 2 * modes), ml_dtypes.bfloat16)
    for s in range(count):
        forth[s, HALF : HALF + part] = analysis[s * part : (s + 1) * part]
        back[s * wide : s * wide + part] = synth[s * part : (s + 1) * part]
    return forth, back


def twice_gelu_slope(scaled):
    power = math.log2(2.0 / math.sqrt(math.pi)) - (1.0 / math.log(2.0)) * (scaled * scaled)
    return (1.0 + lax.erf(scaled)) + scaled * jnp.exp2(power)


def dot_nt(left, right):
    return lax.dot_general(left, right, (((1,), (1,)), ((), ())), preferred_element_type=jnp.float32)


def dot_nn(left, right):
    return jnp.dot(left, right, preferred_element_type=jnp.float32)


def mlp_kernel(count, half, sent, chunks, conv_ref, grad_ref, win_ref, bias_ref, wout_ref, *rest):
    outs, (tall_conv, tall_grad, pre_ref, back_ref, slope_ref, total_ref) = rest[-6 - len(sent) : -6], rest[-6:]
    part, channels = conv_ref.shape[1:]
    wide = round_up(part, HALF)
    rows = tall_conv.shape[0] // wide
    owned = channels // count
    block = pre_ref.shape[2]
    steps = win_ref.shape[1] // block
    me = lax.axis_index("azimuth")
    def stack(tall, source):
        for row in range(rows):
            whole = part // 16 * 16
            tall[row * wide + whole : (row + 1) * wide, :] = jnp.zeros((wide - whole, channels), jnp.bfloat16)
            tall[row * wide : row * wide + part, :] = source[half * rows + row]

    group = 48
    groups = rows * wide // group

    def span(step):
        return slice(step * block, (step + 1) * block)

    def project_pre(step):
        pre_ref[step % 2] = dot_nn(tall_conv[...], win_ref[:, span(step)])

    def project_back(step):
        back_ref[step % 2] = dot_nt(tall_grad[...], wout_ref[span(step), :])

    def slope(step, first, last):
        root = math.sqrt(0.5)
        bias = bias_ref[span(step)].reshape(1, block) * root
        for g in range(first, last):
            some = slice(g * group, (g + 1) * group)
            value = back_ref[step % 2, some, :] * twice_gelu_slope(pre_ref[step % 2, some, :] * root + bias)
            slope_ref[some, span(step)] = value.astype(jnp.bfloat16)

    def gather(first, last):
        at = slice(first * block, last * block)
        term = dot_nt(win_ref[:, at], slope_ref[:, at])
        total_ref[...] = term if first == 0 else total_ref[...] + term

    stack(tall_conv, conv_ref)
    project_pre(0)
    stack(tall_grad, grad_ref)
    project_back(0)
    gathered = 0
    thirds = [groups * n // 3 for n in range(4)]
    for step in range(steps):
        if step + 1 < steps:
            project_pre(step + 1)
        slope(step, thirds[0], thirds[1])
        if step - gathered == 2:
            gather(gathered, step)
            gathered = step
        slope(step, thirds[1], thirds[2])
        if step + 1 < steps:
            project_back(step + 1)
        slope(step, thirds[2], thirds[3])
    gather(gathered, steps)
    for out, (k, start, size) in zip(outs, sent):
        target = partner(me, k, count, 1)
        for begin, width in chunks:
            if start <= begin < start + size:
                first = pl.multiple_of(count * begin + target * width, 32)
                value = 0.5 * total_ref[pl.ds(first, width), :]
                out[begin - start : begin - start + width, :] = value.astype(jnp.bfloat16)


def mlp(conv_out, grad_out, w_in, b_in, w_out, count, half, halves, sent, chunks, after):
    rows, part, channels = conv_out.shape
    rows //= halves
    block = 256
    wide = round_up(part, HALF)
    vmem = pl.BlockSpec(memory_space=VMEM)
    out_shape = [jax.ShapeDtypeStruct((size, rows * wide), jnp.bfloat16) for _, _, size in sent]
    return pl.pallas_call(
        functools.partial(mlp_kernel, count, half, sent, chunks),
        in_specs=[vmem] * 5 + [pl.BlockSpec(memory_space=pl.ANY)] * len(after),
        out_specs=[vmem] * len(out_shape),
        out_shape=out_shape,
        scratch_shapes=[
            pltpu.VMEM((rows * wide, channels), jnp.bfloat16),
            pltpu.VMEM((rows * wide, channels), jnp.bfloat16),
            pltpu.VMEM((2, rows * wide, block), jnp.float32),
            pltpu.VMEM((2, rows * wide, block), jnp.float32),
            pltpu.VMEM((rows * wide, w_in.shape[1]), jnp.bfloat16),
            pltpu.VMEM((channels, rows * wide), jnp.float32),
        ],
        compiler_params=pltpu.CompilerParams(vmem_limit_bytes=16 * 2**20),
        cost_estimate=NO_COST,
        name="mlp",
    )(conv_out, grad_out, w_in, b_in, w_out, *after)


def spectra_of(pieces, channels, table_ref, wide):
    size = channels[1]
    rows = pieces[0][0].shape[1] // wide
    window = table_ref.shape[1] - HALF
    shifts = [row * wide % LANES for row in range(rows)]
    spectra = [None] * rows
    for shift in sorted(set(shifts)):
        group = [row for row in range(rows) if shifts[row] == shift]
        total = None
        for k, (piece, base) in enumerate(pieces):
            windows = [row * wide // LANES * LANES for row in group]
            left = jnp.concatenate([piece[base : base + size, at : at + window] for at in windows], axis=0)
            term = dot_nn(left, table_ref[k, HALF - shift : HALF - shift + window, :])
            total = term if total is None else total + term
        for at, row in enumerate(group):
            spectra[row] = total[at * size : (at + 1) * size]
    return spectra


def early_kernel(count, wide, *refs):
    ranks = far_first(count, count)
    pieces = [(refs[ranks.index(k)], 0) for k in range(count)]
    table_ref, out_ref = refs[count], refs[-1]
    for row, spectrum in enumerate(spectra_of(pieces, (0, pieces[0][0].shape[0]), table_ref, wide)):
        out_ref[row] = spectrum


def analyze_early(pieces, table, wide):
    count = len(pieces)
    size, across = pieces[0].shape
    return pl.pallas_call(
        functools.partial(early_kernel, count, wide),
        in_specs=[pl.BlockSpec(memory_space=VMEM)] * (count + 1),
        out_specs=pl.BlockSpec(memory_space=VMEM),
        out_shape=jax.ShapeDtypeStruct((across // wide, size, table.shape[2]), jnp.float32),
        compiler_params=pltpu.CompilerParams(vmem_limit_bytes=12 * 2**20),
        cost_estimate=NO_COST,
        name="analysis_early",
    )(*(pieces[k] for k in far_first(count, count)), table)


def analysis_kernel(count, rows, wide, chunk, halves, *refs):
    own_ref, first_ref, second_ref = refs[-3:]
    start, size = chunk
    ranks = far_first(count, count)
    pieces = [(refs[ranks.index(k)], 0 if k > NEAR else start) for k in range(count)]
    table_ref, early = refs[count], refs[count + 1 : count + halves]
    per = rows // halves
    even = lax.rem(lax.axis_index("polar"), 2) == 0
    for row, spectrum in enumerate(spectra_of(pieces, chunk, table_ref, wide)):
        own_ref[row] = spectrum

    def row_of(row):
        half, row = divmod(row, per)
        return own_ref[row] if half == halves - 1 else early[half][row, start : start + size, :]

    def share(above, below):
        for h in range(REACH):
            above[h] = row_of(rows - REACH + h).astype(jnp.bfloat16)
            below[h] = row_of(h).astype(jnp.bfloat16)

    pl.when(even)(lambda: share(first_ref, second_ref))
    pl.when(jnp.logical_not(even))(lambda: share(second_ref, first_ref))


def analyze(pieces, table, early, rows, wide, chunk, after):
    count = len(pieces)
    size = chunk[1]
    width = table.shape[2]
    halves = len(early) + 1
    halo = jax.ShapeDtypeStruct((REACH, size, width), jnp.bfloat16)
    return pl.pallas_call(
        functools.partial(analysis_kernel, count, rows, wide, chunk, halves),
        in_specs=[pl.BlockSpec(memory_space=VMEM)] * (count + halves)
        + [pl.BlockSpec(memory_space=pl.ANY)] * len(after),
        out_specs=[pl.BlockSpec(memory_space=VMEM)] * 3,
        out_shape=[jax.ShapeDtypeStruct((rows // halves, size, width), jnp.float32), halo, halo],
        compiler_params=pltpu.CompilerParams(vmem_limit_bytes=12 * 2**20),
        cost_estimate=NO_COST,
        name="analysis",
    )(*(pieces[k] for k in far_first(count, count)), table, *early, *after)


def add_row(accs, spectrum, weight, target_row, filter_row, targets):
    size = spectrum.shape[0]
    masked = jnp.concatenate([jnp.where(target_row == t, weight, 0.0) for t in targets], axis=0)
    gains = dot_nn(masked.astype(jnp.bfloat16), filter_row)
    whole = (gains.shape[1] // 2) // LANES * LANES - LANES
    spec_re = spectrum[:, :whole]
    spec_im = spectrum[:, whole : 2 * whole]
    spec_x = spectrum[:, 2 * whole :]
    swapped = pltpu.roll(spec_x, HALF, 1)
    for at, target in enumerate(targets):
        gain = gains[at * size : (at + 1) * size]
        gain_re = gain[:, :whole]
        gain_rx = gain[:, whole : whole + LANES]
        gain_im = gain[:, whole + LANES : 2 * whole + LANES]
        gain_ix = gain[:, 2 * whole + LANES :]
        acc_re, acc_im, acc_x = accs[target]
        acc_re = acc_re + (gain_re * spec_re + gain_im * spec_im)
        acc_im = acc_im + (gain_re * spec_im - gain_im * spec_re)
        acc_x = acc_x + (gain_rx * spec_x + gain_ix * swapped)
        accs[target] = acc_re, acc_im, acc_x


def split_tiles(value):
    whole = (value.shape[1] - LANES) // 2
    return value[:, :whole], value[:, whole : 2 * whole], value[:, 2 * whole :]


def own_kernel(start, own_ref, weight_ref, target_ref, filter_ref, *rest):
    early, out_ref = rest[:-1], rest[-1]
    rows, size, width = out_ref.shape
    per = own_ref.shape[0]
    accs = {t: split_tiles(jnp.zeros((size, width), jnp.float32)) for t in range(rows)}
    for row in range(rows):
        at = row + REACH
        targets = [t for t in range(rows) if abs(row - t) <= REACH]
        half = row // per
        spectrum = early[half][row % per, start : start + size, :] if half < len(early) else own_ref[row % per]
        add_row(accs, spectrum, weight_ref[...], target_ref[at : at + 1, :], filter_ref[at], targets)
    for t in range(rows):
        out_ref[t] = jnp.concatenate(accs[t], axis=1)


def own_terms(own, early, start, weight, target, filters):
    per, size, width = own.shape
    return pl.pallas_call(
        functools.partial(own_kernel, start),
        in_specs=[pl.BlockSpec(memory_space=VMEM)] * (4 + len(early)),
        out_specs=pl.BlockSpec(memory_space=VMEM),
        out_shape=jax.ShapeDtypeStruct((per * (1 + len(early)), size, width), jnp.float32),
        compiler_params=pltpu.CompilerParams(vmem_limit_bytes=12 * 2**20),
        cost_estimate=NO_COST,
        name="own_terms",
    )(own, weight, target, filters, *early)


def add_halo(accs, sides, rows, weight_ref, target_ref, filter_ref):
    for side, base in sides:
        for h in range(REACH):
            at = base + h + REACH
            targets = [t for t in range(rows) if abs(base + h - t) <= REACH]
            add_row(
                accs,
                side[h].astype(jnp.float32),
                weight_ref[...],
                target_ref[at : at + 1, :],
                filter_ref[at],
                targets,
            )


def side_kernel(part_ref, first_ref, weight_ref, target_ref, filter_ref, *rest):
    out_ref = rest[-1]
    rows = part_ref.shape[0]
    even = lax.rem(lax.axis_index("polar"), 2) == 0

    def combine(base):
        accs = {t: split_tiles(part_ref[t]) for t in range(rows)}
        add_halo(accs, [(first_ref, base)], rows, weight_ref, target_ref, filter_ref)
        for t in range(rows):
            out_ref[t] = jnp.concatenate(accs[t], axis=1)

    pl.when(even)(lambda: combine(rows))
    pl.when(jnp.logical_not(even))(lambda: combine(-REACH))


def side_terms(own, first, weight, target, filters, after):
    return pl.pallas_call(
        side_kernel,
        in_specs=[pl.BlockSpec(memory_space=VMEM)] * 5 + [pl.BlockSpec(memory_space=pl.ANY)] * len(after),
        out_specs=pl.BlockSpec(memory_space=VMEM),
        out_shape=jax.ShapeDtypeStruct(own.shape, jnp.float32),
        compiler_params=pltpu.CompilerParams(vmem_limit_bytes=12 * 2**20),
        cost_estimate=NO_COST,
        name="side_terms",
    )(own, first, weight, target, filters, *after)


def finish_kernel(count, swaps, part_ref, *refs):
    halos, (weight_ref, target_ref, filter_ref, table_ref) = refs[:swaps], refs[swaps : swaps + 4]
    outs, stacked_ref = refs[-count - 1 : -1], refs[-1]
    rows, size, width = part_ref.shape
    even = lax.rem(lax.axis_index("polar"), 2) == 0

    def combine(bases):
        accs = {t: split_tiles(part_ref[t]) for t in range(rows)}
        sides = list(zip(halos, bases[-swaps:]))
        add_halo(accs, sides, rows, weight_ref, target_ref, filter_ref)
        for t in range(rows):
            stacked_ref[t * size : (t + 1) * size, :] = jnp.concatenate(accs[t], axis=1).astype(jnp.bfloat16)

    pl.when(even)(lambda: combine((rows, -REACH)))
    pl.when(jnp.logical_not(even))(lambda: combine((-REACH, rows)))
    grid = dot_nt(table_ref[...], stacked_ref[...])
    wide = grid.shape[0] // count
    for k, out in enumerate(outs):
        out[...] = grid[k * wide : k * wide + out.shape[0]].astype(jnp.bfloat16)


def finish(own, halos, weight, target, filters, table, count, part):
    rows, size, width = own.shape
    return pl.pallas_call(
        functools.partial(finish_kernel, count, len(halos)),
        in_specs=[pl.BlockSpec(memory_space=VMEM)] * (5 + len(halos)),
        out_specs=[pl.BlockSpec(memory_space=VMEM)] * count,
        out_shape=[jax.ShapeDtypeStruct((part, rows * size), jnp.bfloat16)] * count,
        scratch_shapes=[pltpu.VMEM((rows * size, width), jnp.bfloat16)],
        compiler_params=pltpu.CompilerParams(vmem_limit_bytes=12 * 2**20),
        cost_estimate=NO_COST,
        name="finish",
    )(own, *halos, weight, target, filters, table)


def add_kernel(count, chunk, steps, grad_ref, *refs):
    out_ref, tall_ref, done_ref, sems = refs[-4:]
    pieces = dict(zip(steps, refs))
    tiles, part, rows, _ = done_ref.shape
    start, size = chunk
    me = lax.axis_index("azimuth")

    def add(tile, mine):
        order = [[k for k in range(count) if partner_static(mine, k, count, -1) == s][0] for s in range(count)]
        lanes = range(tile * LANES, (tile + 1) * LANES)
        for row in range(rows):
            parts = []
            for s in range(lanes[0] // size, lanes[-1] // size + 1):
                low, high = max(lanes[0], s * size) - s * size, min(lanes[-1] + 1, (s + 1) * size) - s * size
                parts.append(pieces[order[s]][:part, row * size + low : row * size + high])
            conv = jnp.concatenate(parts, axis=1).astype(jnp.float32)
            first = count * start + tile * LANES
            total = grad_ref[row, :, first : first + LANES].astype(jnp.float32) + conv
            tall_ref[tile, pl.ds(row, part, stride=rows), :] = total
        done_ref[tile] = tall_ref[tile].reshape(part, rows, LANES).astype(jnp.bfloat16)

    copies = []
    for tile in range(tiles):
        for mine in range(count):
            pl.when(me == mine)(functools.partial(add, tile, mine))
        lanes = pl.ds(count * start + tile * LANES, LANES)
        copies.append(pltpu.make_async_copy(done_ref.at[tile], out_ref.at[:, :, lanes], sems.at[tile]))
        copies[-1].start()
    for copy in copies:
        copy.wait()


def add_chunk(grad_out, pieces, chunk, count, before):
    rows, part, channels = grad_out.shape
    start, size = chunk
    tiles = count * size // LANES
    pieces = sorted(pieces.items(), key=lambda item: item[0] <= NEAR)
    vmem = pl.BlockSpec(memory_space=VMEM)
    anywhere = pl.BlockSpec(memory_space=pl.ANY)
    return pl.pallas_call(
        functools.partial(add_kernel, count, chunk, [k for k, _ in pieces]),
        in_specs=[vmem] * (1 + len(pieces)) + [anywhere] * len(before),
        out_specs=anywhere,
        out_shape=jax.ShapeDtypeStruct((part, rows, channels), jnp.bfloat16),
        scratch_shapes=[
            pltpu.VMEM((tiles, rows * part, LANES), jnp.float32),
            pltpu.VMEM((tiles, part, rows, LANES), jnp.bfloat16),
            pltpu.SemaphoreType.DMA((tiles,)),
        ],
        input_output_aliases={1 + len(pieces): 0} if before else {},
        compiler_params=pltpu.CompilerParams(vmem_limit_bytes=12 * 2**20),
        cost_estimate=NO_COST,
        name="add_chunk",
    )(grad_out, *(block for _, block in pieces), *before)


def prepare_kernel(count, chunks, weight_ref, filt_ref, offset_ref, forth_ref, back_ref, *outs):
    filter_out, target_out, forth_out, back_out = outs[:4]
    me = lax.axis_index("azimuth")
    wide = back_ref.shape[0] // count
    for k in range(count):
        forth_out[k] = forth_ref[partner(me, k, count, -1)]
        first = pl.multiple_of(partner(me, k, count, 1) * wide, HALF)
        back_out[k * wide : (k + 1) * wide, :] = back_ref[pl.ds(first, wide), :]
    bases, channels = weight_ref.shape
    lats, width = filt_ref.shape[1:]
    ext, depth = target_out.shape
    rows = ext - 2 * REACH
    modes = width // 2
    whole = modes // LANES * LANES
    used = TERMS * bases
    for (start, size), out in zip(chunks, outs[4:]):
        first = count * start + lax.axis_index("azimuth") * size
        weight = pltpu.roll(weight_ref[...], lax.rem(channels - first, channels), 1)[:, :size]
        parts = []
        for _ in range(TERMS):
            rounded = weight.astype(jnp.bfloat16).astype(jnp.float32)
            parts.append(rounded)
            weight = weight - rounded
        parts.append(jnp.zeros((depth - used, size), jnp.float32))
        out[...] = jnp.concatenate(parts, axis=0).T
    start_lat = lax.axis_index("polar") * rows
    table = filt_ref[...].reshape(bases * lats, width)
    base = lax.broadcasted_iota(jnp.int32, (depth, bases * lats), 0)
    valid = base < used
    for _ in range(TERMS - 1):
        base = jnp.where(base >= bases, base - bases, base)
    column = lax.broadcasted_iota(jnp.int32, (depth, bases * lats), 1)
    for i in range(ext):
        lat = start_lat + (i - REACH)
        inside = (lat >= 0) & (lat < lats)
        lat = jnp.clip(lat, 0, lats - 1)
        pick = jnp.where(valid & (column == base * lats + lat), 1.0, 0.0).astype(jnp.bfloat16)
        row = dot_nn(pick, table)
        real, imag = row[:, :modes], row[:, modes:]
        rest_re, rest_im = real[:, whole:], imag[:, whole:]
        filter_out[i] = jnp.concatenate(
            [real[:, :whole], rest_re, rest_re, imag[:, :whole], rest_im, -rest_im], axis=1
        ).astype(jnp.bfloat16)
        local = jnp.where(inside, offset_ref[pl.ds(lat, 1), :] - start_lat, -1)
        spare = jnp.full((1, depth - used), -1, jnp.int32)
        target_out[i : i + 1, :] = jnp.concatenate([local] * TERMS + [spare], axis=1)


def prepare(basis_weight, filt, offsets, forth, back, rows, count, chunks):
    bases = filt.shape[0]
    width = filt.shape[2]
    ext = rows + 2 * REACH
    depth = round_up(TERMS * bases, 16)
    shapes = [
        jax.ShapeDtypeStruct((ext, depth, width + LANES), jnp.bfloat16),
        jax.ShapeDtypeStruct((ext, depth), jnp.int32),
        jax.ShapeDtypeStruct(forth.shape, forth.dtype),
        jax.ShapeDtypeStruct(back.shape, back.dtype),
    ] + [jax.ShapeDtypeStruct((size, depth), jnp.float32) for _, size in chunks]
    return pl.pallas_call(
        functools.partial(prepare_kernel, count, chunks),
        in_specs=[pl.BlockSpec(memory_space=VMEM)] * 5,
        out_specs=[pl.BlockSpec(memory_space=VMEM)] * len(shapes),
        out_shape=shapes,
        compiler_params=pltpu.CompilerParams(vmem_limit_bytes=16 * 2**20),
        cost_estimate=NO_COST,
        name="prepare",
    )(basis_weight, filt, offsets, forth, back)


def halo(first, second):
    bands, count = lax.axis_size("polar"), lax.axis_size("azimuth")
    blocks = []
    for odd, block in ((0, first), (1, second)):
        pairs = []
        for a in range(bands):
            other = ((a + odd) ^ 1) - odd
            for b in range(count):
                paired = 0 <= other < bands
                target = (other, b) if paired else (a, b ^ 1 if b ^ 1 < count else b)
                pairs.append((a * count + b, target[0] * count + target[1]))
        blocks.append(lax.ppermute(block, ("polar", "azimuth"), pairs))
    return blocks


def on_device(chunks, conv_out, grad_out, w_in, b_in, w_out, basis_weight, filt, offsets):
    rows, part, channels = conv_out.shape
    count = lax.axis_size("azimuth")
    forth, back = tables(count, part, filt.shape[2] // 2)
    forth, back = jnp.asarray(forth), jnp.asarray(back)
    owned = channels // count
    halves = 2 if rows % 2 == 0 else 1
    wide = round_up(part, HALF)
    far = range(NEAR + 1, count)
    filters, target, forth, back, *weights = prepare(
        basis_weight, filt, offsets, forth, back, rows, count, chunks
    )
    early, order = [], []
    for half in range(halves):
        final = half == halves - 1
        sent = [(k, 0, owned) for k in range(count)]
        if final:
            sent[NEAR + 1 :] = [(k,) + chunk for chunk in chunks for k in far]
        blocks = mlp(conv_out, grad_out, w_in, b_in, w_out, count, half, halves, sent, chunks, order)
        order = blocks[:1]
        if not final:
            early.append(analyze_early([exchange(blocks[k], k, count) for k in range(count)], forth, wide))
    whole = [exchange(blocks[k], k, count) for k in range(NEAR + 1)]
    spectra, terms, returned = {}, {}, {}
    for q, (start, size) in enumerate(chunks):
        tail = [exchange(blocks[NEAR + 1 + q * len(far) + i], k, count) for i, k in enumerate(far)]
        after = [terms[q - 1]] if q else []
        own, first, second = analyze(whole + tail, forth, early, rows, wide, (start, size), after)
        spectra[q] = halo(first, second)
        terms[q] = own_terms(own, early, start, weights[q], target, filters)
    for q in range(len(chunks)):
        halos = spectra[q]
        if q == 0:
            others = [terms[other] for other in terms if other > q]
            terms[q] = side_terms(terms[q], halos[0], weights[q], target, filters, others)
            halos = halos[1:]
        grids = finish(terms[q], halos, weights[q], target, filters, back, count, part)
        returned[q] = {k: exchange(grids[k], k, count) for k in range(count)}
    total = []
    for q, chunk in enumerate(chunks):
        total = [add_chunk(grad_out, returned[q], chunk, count, total)]
    return jnp.transpose(total[0], (1, 0, 2))


def solution(mesh):
    grid = P(("member", "polar"), "azimuth", None)

    def run(conv_out, grad_out, *others):
        owned = conv_out.shape[2] // mesh.shape["azimuth"]
        sizes = [owned]
        if owned % 32 == 0 and owned >= 96:
            big = owned * 3 // 5 // 32 * 32
            sizes = [big, owned - big]
        chunks = tuple((sum(sizes[:q]), size) for q, size in enumerate(sizes))
        return jax.shard_map(
            functools.partial(on_device, chunks),
            mesh=mesh,
            in_specs=(grid, grid) + (P(),) * 6,
            out_specs=grid,
            check_vma=False,
        )(conv_out, grad_out, *others)

    return run
```

```python
import functools
import math

import jax
import jax.numpy as jnp
import ml_dtypes
import numpy as np
from jax import lax
from jax.experimental import pallas as pl
from jax.experimental.pallas import tpu as pltpu
from jax.sharding import PartitionSpec as P

REACH = 3
LANES = 128
HALF = 64
TERMS = 3
NEAR = 1
VMEM = pltpu.MemorySpace.VMEM
NO_COST = pl.CostEstimate(flops=0, bytes_accessed=0, transcendentals=0)


def round_up(value, unit):
    return -(-value // unit) * unit


def partner(me, step, count, sign):
    if count & (count - 1) == 0:
        return me ^ step
    return lax.rem(me + sign * step + count, count)


def far_first(number, count):
    return sorted(range(number), key=lambda i: (i // count, i % count <= NEAR))


def exchange(block, step, count):
    if step == 0:
        return block
    pairs = [(a, int(partner_static(a, step, count))) for a in range(count)]
    return lax.ppermute(block, "azimuth", pairs)


def partner_static(a, step, count, sign=1):
    return a ^ step if count & (count - 1) == 0 else (a + sign * step) % count


def tables(count, part, modes):
    length = count * part
    whole = modes // LANES * LANES
    order = np.concatenate(
        [
            np.arange(whole),
            modes + np.arange(whole),
            np.arange(whole, modes),
            modes + np.arange(whole, modes),
        ]
    )
    positions = np.arange(length)
    waves = np.arange(modes)
    phase = (positions[:, None] * waves[None, :]) % length
    angle = (2.0 * math.pi / length) * phase
    scale = 1.0 / math.sqrt(length)
    factor = np.where(waves == 0, 1.0, 2.0)
    analysis = np.concatenate([np.cos(angle), -np.sin(angle)], axis=1) * scale
    synth = np.concatenate([np.cos(angle) * factor, -np.sin(angle) * factor], axis=1) * scale
    analysis = analysis.astype(np.float32).astype(ml_dtypes.bfloat16)[:, order]
    synth = synth.astype(np.float32).astype(ml_dtypes.bfloat16)[:, order]
    wide = round_up(part, HALF)
    window = round_up(HALF + wide, LANES)
    forth = np.zeros((count, HALF + window, 2 * modes), ml_dtypes.bfloat16)
    back = np.zeros((count * wide, 2 * modes), ml_dtypes.bfloat16)
    for s in range(count):
        forth[s, HALF : HALF + part] = analysis[s * part : (s + 1) * part]
        back[s * wide : s * wide + part] = synth[s * part : (s + 1) * part]
    return forth, back


def twice_gelu_slope(scaled):
    power = math.log2(2.0 / math.sqrt(math.pi)) - (1.0 / math.log(2.0)) * (scaled * scaled)
    return (1.0 + lax.erf(scaled)) + scaled * jnp.exp2(power)


def dot_nt(left, right):
    return lax.dot_general(left, right, (((1,), (1,)), ((), ())), preferred_element_type=jnp.float32)


def dot_nn(left, right):
    return jnp.dot(left, right, preferred_element_type=jnp.float32)


def mlp_kernel(count, half, sent, chunks, conv_ref, grad_ref, win_ref, bias_ref, wout_ref, *rest):
    outs, (tall_conv, tall_grad, pre_ref, back_ref, slope_ref, total_ref) = rest[-6 - len(sent) : -6], rest[-6:]
    part, channels = conv_ref.shape[1:]
    wide = round_up(part, HALF)
    rows = tall_conv.shape[0] // wide
    owned = channels // count
    block = pre_ref.shape[2]
    steps = win_ref.shape[1] // block
    me = lax.axis_index("azimuth")
    def stack(tall, source):
        for row in range(rows):
            whole = part // 16 * 16
            tall[row * wide + whole : (row + 1) * wide, :] = jnp.zeros((wide - whole, channels), jnp.bfloat16)
            tall[row * wide : row * wide + part, :] = source[half * rows + row]

    group = 48
    groups = rows * wide // group

    def span(step):
        return slice(step * block, (step + 1) * block)

    def project_pre(step):
        pre_ref[step % 2] = dot_nn(tall_conv[...], win_ref[:, span(step)])

    def project_back(step):
        back_ref[step % 2] = dot_nt(tall_grad[...], wout_ref[span(step), :])

    def slope(step, first, last):
        root = math.sqrt(0.5)
        bias = bias_ref[span(step)].reshape(1, block) * root
        for g in range(first, last):
            some = slice(g * group, (g + 1) * group)
            value = back_ref[step % 2, some, :] * twice_gelu_slope(pre_ref[step % 2, some, :] * root + bias)
            slope_ref[some, span(step)] = value.astype(jnp.bfloat16)

    def gather(first, last):
        at = slice(first * block, last * block)
        term = dot_nt(win_ref[:, at], slope_ref[:, at])
        total_ref[...] = term if first == 0 else total_ref[...] + term

    stack(tall_conv, conv_ref)
    project_pre(0)
    stack(tall_grad, grad_ref)
    project_back(0)
    gathered = 0
    thirds = [groups * n // 3 for n in range(4)]
    for step in range(steps):
        if step + 1 < steps:
            project_pre(step + 1)
        slope(step, thirds[0], thirds[1])
        if step - gathered == 2:
            gather(gathered, step)
            gathered = step
        slope(step, thirds[1], thirds[2])
        if step + 1 < steps:
            project_back(step + 1)
        slope(step, thirds[2], thirds[3])
    gather(gathered, steps)
    for out, (k, start, size) in zip(outs, sent):
        target = partner(me, k, count, 1)
        for begin, width in chunks:
            if start <= begin < start + size:
                first = pl.multiple_of(count * begin + target * width, 32)
                value = 0.5 * total_ref[pl.ds(first, width), :]
                out[begin - start : begin - start + width, :] = value.astype(jnp.bfloat16)


def mlp(conv_out, grad_out, w_in, b_in, w_out, count, half, halves, sent, chunks, after):
    rows, part, channels = conv_out.shape
    rows //= halves
    block = 256
    wide = round_up(part, HALF)
    vmem = pl.BlockSpec(memory_space=VMEM)
    out_shape = [jax.ShapeDtypeStruct((size, rows * wide), jnp.bfloat16) for _, _, size in sent]
    return pl.pallas_call(
        functools.partial(mlp_kernel, count, half, sent, chunks),
        in_specs=[vmem] * 5 + [pl.BlockSpec(memory_space=pl.ANY)] * len(after),
        out_specs=[vmem] * len(out_shape),
        out_shape=out_shape,
        scratch_shapes=[
            pltpu.VMEM((rows * wide, channels), jnp.bfloat16),
            pltpu.VMEM((rows * wide, channels), jnp.bfloat16),
            pltpu.VMEM((2, rows * wide, block), jnp.float32),
            pltpu.VMEM((2, rows * wide, block), jnp.float32),
            pltpu.VMEM((rows * wide, w_in.shape[1]), jnp.bfloat16),
            pltpu.VMEM((channels, rows * wide), jnp.float32),
        ],
        compiler_params=pltpu.CompilerParams(vmem_limit_bytes=16 * 2**20),
        cost_estimate=NO_COST,
        name="mlp",
    )(conv_out, grad_out, w_in, b_in, w_out, *after)


def spectra_of(pieces, channels, table_ref, wide):
    size = channels[1]
    rows = pieces[0][0].shape[1] // wide
    window = table_ref.shape[1] - HALF
    shifts = [row * wide % LANES for row in range(rows)]
    spectra = [None] * rows
    for shift in sorted(set(shifts)):
        group = [row for row in range(rows) if shifts[row] == shift]
        total = None
        for k, (piece, base) in enumerate(pieces):
            windows = [row * wide // LANES * LANES for row in group]
            left = jnp.concatenate([piece[base : base + size, at : at + window] for at in windows], axis=0)
            term = dot_nn(left, table_ref[k, HALF - shift : HALF - shift + window, :])
            total = term if total is None else total + term
        for at, row in enumerate(group):
            spectra[row] = total[at * size : (at + 1) * size]
    return spectra


def early_kernel(count, wide, *refs):
    ranks = far_first(count, count)
    pieces = [(refs[ranks.index(k)], 0) for k in range(count)]
    table_ref, out_ref = refs[count], refs[-1]
    for row, spectrum in enumerate(spectra_of(pieces, (0, pieces[0][0].shape[0]), table_ref, wide)):
        out_ref[row] = spectrum


def analyze_early(pieces, table, wide):
    count = len(pieces)
    size, across = pieces[0].shape
    return pl.pallas_call(
        functools.partial(early_kernel, count, wide),
        in_specs=[pl.BlockSpec(memory_space=VMEM)] * (count + 1),
        out_specs=pl.BlockSpec(memory_space=VMEM),
        out_shape=jax.ShapeDtypeStruct((across // wide, size, table.shape[2]), jnp.float32),
        compiler_params=pltpu.CompilerParams(vmem_limit_bytes=12 * 2**20),
        cost_estimate=NO_COST,
        name="analysis_early",
    )(*(pieces[k] for k in far_first(count, count)), table)


def analysis_kernel(count, rows, wide, chunk, halves, *refs):
    own_ref, first_ref, second_ref = refs[-3:]
    start, size = chunk
    ranks = far_first(count, count)
    pieces = [(refs[ranks.index(k)], 0 if k else start) for k in range(count)]
    table_ref, early = refs[count], refs[count + 1 : count + halves]
    per = rows // halves
    even = lax.rem(lax.axis_index("polar"), 2) == 0
    for row, spectrum in enumerate(spectra_of(pieces, chunk, table_ref, wide)):
        own_ref[row] = spectrum

    def row_of(row):
        half, row = divmod(row, per)
        return own_ref[row] if half == halves - 1 else early[half][row, start : start + size, :]

    def share(above, below):
        for h in range(REACH):
            above[h] = row_of(rows - REACH + h).astype(jnp.bfloat16)
            below[h] = row_of(h).astype(jnp.bfloat16)

    pl.when(even)(lambda: share(first_ref, second_ref))
    pl.when(jnp.logical_not(even))(lambda: share(second_ref, first_ref))


def analyze(pieces, table, early, rows, wide, chunk, after):
    count = len(pieces)
    size = chunk[1]
    width = table.shape[2]
    halves = len(early) + 1
    halo = jax.ShapeDtypeStruct((REACH, size, width), jnp.bfloat16)
    return pl.pallas_call(
        functools.partial(analysis_kernel, count, rows, wide, chunk, halves),
        in_specs=[pl.BlockSpec(memory_space=VMEM)] * (count + halves)
        + [pl.BlockSpec(memory_space=pl.ANY)] * len(after),
        out_specs=[pl.BlockSpec(memory_space=VMEM)] * 3,
        out_shape=[jax.ShapeDtypeStruct((rows // halves, size, width), jnp.float32), halo, halo],
        compiler_params=pltpu.CompilerParams(vmem_limit_bytes=12 * 2**20),
        cost_estimate=NO_COST,
        name="analysis",
    )(*(pieces[k] for k in far_first(count, count)), table, *early, *after)


def add_row(accs, spectrum, weight, target_row, filter_row, targets):
    size = spectrum.shape[0]
    masked = jnp.concatenate([jnp.where(target_row == t, weight, 0.0) for t in targets], axis=0)
    gains = dot_nn(masked.astype(jnp.bfloat16), filter_row)
    whole = (gains.shape[1] // 2) // LANES * LANES - LANES
    spec_re = spectrum[:, :whole]
    spec_im = spectrum[:, whole : 2 * whole]
    spec_x = spectrum[:, 2 * whole :]
    swapped = pltpu.roll(spec_x, HALF, 1)
    for at, target in enumerate(targets):
        gain = gains[at * size : (at + 1) * size]
        gain_re = gain[:, :whole]
        gain_rx = gain[:, whole : whole + LANES]
        gain_im = gain[:, whole + LANES : 2 * whole + LANES]
        gain_ix = gain[:, 2 * whole + LANES :]
        acc_re, acc_im, acc_x = accs[target]
        acc_re = acc_re + (gain_re * spec_re + gain_im * spec_im)
        acc_im = acc_im + (gain_re * spec_im - gain_im * spec_re)
        acc_x = acc_x + (gain_rx * spec_x + gain_ix * swapped)
        accs[target] = acc_re, acc_im, acc_x


def split_tiles(value):
    whole = (value.shape[1] - LANES) // 2
    return value[:, :whole], value[:, whole : 2 * whole], value[:, 2 * whole :]


def own_kernel(start, own_ref, weight_ref, target_ref, filter_ref, *rest):
    early, out_ref = rest[:-1], rest[-1]
    rows, size, width = out_ref.shape
    per = own_ref.shape[0]
    accs = {t: split_tiles(jnp.zeros((size, width), jnp.float32)) for t in range(rows)}
    for row in range(rows):
        at = row + REACH
        targets = [t for t in range(rows) if abs(row - t) <= REACH]
        half = row // per
        spectrum = early[half][row % per, start : start + size, :] if half < len(early) else own_ref[row % per]
        add_row(accs, spectrum, weight_ref[...], target_ref[at : at + 1, :], filter_ref[at], targets)
    for t in range(rows):
        out_ref[t] = jnp.concatenate(accs[t], axis=1)


def own_terms(own, early, start, weight, target, filters):
    per, size, width = own.shape
    return pl.pallas_call(
        functools.partial(own_kernel, start),
        in_specs=[pl.BlockSpec(memory_space=VMEM)] * (4 + len(early)),
        out_specs=pl.BlockSpec(memory_space=VMEM),
        out_shape=jax.ShapeDtypeStruct((per * (1 + len(early)), size, width), jnp.float32),
        compiler_params=pltpu.CompilerParams(vmem_limit_bytes=12 * 2**20),
        cost_estimate=NO_COST,
        name="own_terms",
    )(own, weight, target, filters, *early)


def add_halo(accs, sides, rows, weight_ref, target_ref, filter_ref):
    for side, base in sides:
        for h in range(REACH):
            at = base + h + REACH
            targets = [t for t in range(rows) if abs(base + h - t) <= REACH]
            add_row(
                accs,
                side[h].astype(jnp.float32),
                weight_ref[...],
                target_ref[at : at + 1, :],
                filter_ref[at],
                targets,
            )


def side_kernel(part_ref, first_ref, weight_ref, target_ref, filter_ref, *rest):
    out_ref = rest[-1]
    rows = part_ref.shape[0]
    even = lax.rem(lax.axis_index("polar"), 2) == 0

    def combine(base):
        accs = {t: split_tiles(part_ref[t]) for t in range(rows)}
        add_halo(accs, [(first_ref, base)], rows, weight_ref, target_ref, filter_ref)
        for t in range(rows):
            out_ref[t] = jnp.concatenate(accs[t], axis=1)

    pl.when(even)(lambda: combine(rows))
    pl.when(jnp.logical_not(even))(lambda: combine(-REACH))


def side_terms(own, first, weight, target, filters, after):
    return pl.pallas_call(
        side_kernel,
        in_specs=[pl.BlockSpec(memory_space=VMEM)] * 5 + [pl.BlockSpec(memory_space=pl.ANY)] * len(after),
        out_specs=pl.BlockSpec(memory_space=VMEM),
        out_shape=jax.ShapeDtypeStruct(own.shape, jnp.float32),
        compiler_params=pltpu.CompilerParams(vmem_limit_bytes=12 * 2**20),
        cost_estimate=NO_COST,
        name="side_terms",
    )(own, first, weight, target, filters, *after)


def finish_kernel(count, swaps, part_ref, *refs):
    halos, (weight_ref, target_ref, filter_ref, table_ref) = refs[:swaps], refs[swaps : swaps + 4]
    outs, stacked_ref = refs[-count - 1 : -1], refs[-1]
    rows, size, width = part_ref.shape
    even = lax.rem(lax.axis_index("polar"), 2) == 0

    def combine(bases):
        accs = {t: split_tiles(part_ref[t]) for t in range(rows)}
        sides = list(zip(halos, bases[-swaps:]))
        add_halo(accs, sides, rows, weight_ref, target_ref, filter_ref)
        for t in range(rows):
            stacked_ref[t * size : (t + 1) * size, :] = jnp.concatenate(accs[t], axis=1).astype(jnp.bfloat16)

    pl.when(even)(lambda: combine((rows, -REACH)))
    pl.when(jnp.logical_not(even))(lambda: combine((-REACH, rows)))
    grid = dot_nt(table_ref[...], stacked_ref[...])
    wide = grid.shape[0] // count
    for k, out in enumerate(outs):
        out[...] = grid[k * wide : k * wide + out.shape[0]].astype(jnp.bfloat16)


def finish(own, halos, weight, target, filters, table, count, part):
    rows, size, width = own.shape
    return pl.pallas_call(
        functools.partial(finish_kernel, count, len(halos)),
        in_specs=[pl.BlockSpec(memory_space=VMEM)] * (5 + len(halos)),
        out_specs=[pl.BlockSpec(memory_space=VMEM)] * count,
        out_shape=[jax.ShapeDtypeStruct((part, rows * size), jnp.bfloat16)] * count,
        scratch_shapes=[pltpu.VMEM((rows * size, width), jnp.bfloat16)],
        compiler_params=pltpu.CompilerParams(vmem_limit_bytes=12 * 2**20),
        cost_estimate=NO_COST,
        name="finish",
    )(own, *halos, weight, target, filters, table)


def add_kernel(count, chunk, steps, grad_ref, *refs):
    out_ref, tall_ref, done_ref, sems = refs[-4:]
    pieces = dict(zip(steps, refs))
    tiles, part, rows, _ = done_ref.shape
    start, size = chunk
    me = lax.axis_index("azimuth")

    def add(tile, mine):
        order = [[k for k in range(count) if partner_static(mine, k, count, -1) == s][0] for s in range(count)]
        lanes = range(tile * LANES, (tile + 1) * LANES)
        for row in range(rows):
            parts = []
            for s in range(lanes[0] // size, lanes[-1] // size + 1):
                low, high = max(lanes[0], s * size) - s * size, min(lanes[-1] + 1, (s + 1) * size) - s * size
                parts.append(pieces[order[s]][:part, row * size + low : row * size + high])
            conv = jnp.concatenate(parts, axis=1).astype(jnp.float32)
            first = count * start + tile * LANES
            total = grad_ref[row, :, first : first + LANES].astype(jnp.float32) + conv
            tall_ref[tile, pl.ds(row, part, stride=rows), :] = total
        done_ref[tile] = tall_ref[tile].reshape(part, rows, LANES).astype(jnp.bfloat16)

    copies = []
    for tile in range(tiles):
        for mine in range(count):
            pl.when(me == mine)(functools.partial(add, tile, mine))
        lanes = pl.ds(count * start + tile * LANES, LANES)
        copies.append(pltpu.make_async_copy(done_ref.at[tile], out_ref.at[:, :, lanes], sems.at[tile]))
        copies[-1].start()
    for copy in copies:
        copy.wait()


def add_chunk(grad_out, pieces, chunk, count, before):
    rows, part, channels = grad_out.shape
    start, size = chunk
    tiles = count * size // LANES
    pieces = sorted(pieces.items(), key=lambda item: item[0] <= NEAR)
    vmem = pl.BlockSpec(memory_space=VMEM)
    anywhere = pl.BlockSpec(memory_space=pl.ANY)
    return pl.pallas_call(
        functools.partial(add_kernel, count, chunk, [k for k, _ in pieces]),
        in_specs=[vmem] * (1 + len(pieces)) + [anywhere] * len(before),
        out_specs=anywhere,
        out_shape=jax.ShapeDtypeStruct((part, rows, channels), jnp.bfloat16),
        scratch_shapes=[
            pltpu.VMEM((tiles, rows * part, LANES), jnp.float32),
            pltpu.VMEM((tiles, part, rows, LANES), jnp.bfloat16),
            pltpu.SemaphoreType.DMA((tiles,)),
        ],
        input_output_aliases={1 + len(pieces): 0} if before else {},
        compiler_params=pltpu.CompilerParams(vmem_limit_bytes=12 * 2**20),
        cost_estimate=NO_COST,
        name="add_chunk",
    )(grad_out, *(block for _, block in pieces), *before)


def prepare_kernel(count, chunks, weight_ref, filt_ref, offset_ref, forth_ref, back_ref, *outs):
    filter_out, target_out, forth_out, back_out = outs[:4]
    me = lax.axis_index("azimuth")
    wide = back_ref.shape[0] // count
    for k in range(count):
        forth_out[k] = forth_ref[partner(me, k, count, -1)]
        first = pl.multiple_of(partner(me, k, count, 1) * wide, HALF)
        back_out[k * wide : (k + 1) * wide, :] = back_ref[pl.ds(first, wide), :]
    bases, channels = weight_ref.shape
    lats, width = filt_ref.shape[1:]
    ext, depth = target_out.shape
    rows = ext - 2 * REACH
    modes = width // 2
    whole = modes // LANES * LANES
    used = TERMS * bases
    for (start, size), out in zip(chunks, outs[4:]):
        first = count * start + lax.axis_index("azimuth") * size
        weight = pltpu.roll(weight_ref[...], lax.rem(channels - first, channels), 1)[:, :size]
        parts = []
        for _ in range(TERMS):
            rounded = weight.astype(jnp.bfloat16).astype(jnp.float32)
            parts.append(rounded)
            weight = weight - rounded
        parts.append(jnp.zeros((depth - used, size), jnp.float32))
        out[...] = jnp.concatenate(parts, axis=0).T
    start_lat = lax.axis_index("polar") * rows
    table = filt_ref[...].reshape(bases * lats, width)
    base = lax.broadcasted_iota(jnp.int32, (depth, bases * lats), 0)
    valid = base < used
    for _ in range(TERMS - 1):
        base = jnp.where(base >= bases, base - bases, base)
    column = lax.broadcasted_iota(jnp.int32, (depth, bases * lats), 1)
    for i in range(ext):
        lat = start_lat + (i - REACH)
        inside = (lat >= 0) & (lat < lats)
        lat = jnp.clip(lat, 0, lats - 1)
        pick = jnp.where(valid & (column == base * lats + lat), 1.0, 0.0).astype(jnp.bfloat16)
        row = dot_nn(pick, table)
        real, imag = row[:, :modes], row[:, modes:]
        rest_re, rest_im = real[:, whole:], imag[:, whole:]
        filter_out[i] = jnp.concatenate(
            [real[:, :whole], rest_re, rest_re, imag[:, :whole], rest_im, -rest_im], axis=1
        ).astype(jnp.bfloat16)
        local = jnp.where(inside, offset_ref[pl.ds(lat, 1), :] - start_lat, -1)
        spare = jnp.full((1, depth - used), -1, jnp.int32)
        target_out[i : i + 1, :] = jnp.concatenate([local] * TERMS + [spare], axis=1)


def prepare(basis_weight, filt, offsets, forth, back, rows, count, chunks):
    bases = filt.shape[0]
    width = filt.shape[2]
    ext = rows + 2 * REACH
    depth = round_up(TERMS * bases, 16)
    shapes = [
        jax.ShapeDtypeStruct((ext, depth, width + LANES), jnp.bfloat16),
        jax.ShapeDtypeStruct((ext, depth), jnp.int32),
        jax.ShapeDtypeStruct(forth.shape, forth.dtype),
        jax.ShapeDtypeStruct(back.shape, back.dtype),
    ] + [jax.ShapeDtypeStruct((size, depth), jnp.float32) for _, size in chunks]
    return pl.pallas_call(
        functools.partial(prepare_kernel, count, chunks),
        in_specs=[pl.BlockSpec(memory_space=VMEM)] * 5,
        out_specs=[pl.BlockSpec(memory_space=VMEM)] * len(shapes),
        out_shape=shapes,
        compiler_params=pltpu.CompilerParams(vmem_limit_bytes=16 * 2**20),
        cost_estimate=NO_COST,
        name="prepare",
    )(basis_weight, filt, offsets, forth, back)


def halo(first, second):
    bands, count = lax.axis_size("polar"), lax.axis_size("azimuth")
    blocks = []
    for odd, block in ((0, first), (1, second)):
        pairs = []
        for a in range(bands):
            other = ((a + odd) ^ 1) - odd
            for b in range(count):
                paired = 0 <= other < bands
                target = (other, b) if paired else (a, b ^ 1 if b ^ 1 < count else b)
                pairs.append((a * count + b, target[0] * count + target[1]))
        blocks.append(lax.ppermute(block, ("polar", "azimuth"), pairs))
    return blocks


def on_device(chunks, conv_out, grad_out, w_in, b_in, w_out, basis_weight, filt, offsets):
    rows, part, channels = conv_out.shape
    count = lax.axis_size("azimuth")
    forth, back = tables(count, part, filt.shape[2] // 2)
    forth, back = jnp.asarray(forth), jnp.asarray(back)
    owned = channels // count
    halves = 2 if rows % 2 == 0 else 1
    wide = round_up(part, HALF)
    filters, target, forth, back, *weights = prepare(
        basis_weight, filt, offsets, forth, back, rows, count, chunks
    )
    early, order = [], []
    for half in range(halves):
        final = half == halves - 1
        sent = [(k, 0, owned) for k in range(count)]
        if final:
            sent[1:] = [(k,) + chunk for chunk in chunks for k in range(1, count)]
        blocks = mlp(conv_out, grad_out, w_in, b_in, w_out, count, half, halves, sent, chunks, order)
        order = blocks[:1]
        if not final:
            early.append(analyze_early([exchange(blocks[k], k, count) for k in range(count)], forth, wide))
    spectra, terms, returned = {}, {}, {}
    for q, (start, size) in enumerate(chunks):
        mine = blocks[1 + q * (count - 1) : 1 + (q + 1) * (count - 1)]
        pieces = [blocks[0]] + [exchange(block, k, count) for k, block in enumerate(mine, 1)]
        after = [terms[q - 1]] if q else []
        own, first, second = analyze(pieces, forth, early, rows, wide, (start, size), after)
        spectra[q] = halo(first, second)
        terms[q] = own_terms(own, early, start, weights[q], target, filters)
    for q in range(len(chunks)):
        halos = spectra[q]
        if q == 0:
            others = [terms[other] for other in terms if other > q]
            terms[q] = side_terms(terms[q], halos[0], weights[q], target, filters, others)
            halos = halos[1:]
        grids = finish(terms[q], halos, weights[q], target, filters, back, count, part)
        returned[q] = {k: exchange(grids[k], k, count) for k in range(count)}
    total = []
    for q, chunk in enumerate(chunks):
        total = [add_chunk(grad_out, returned[q], chunk, count, total)]
    return jnp.transpose(total[0], (1, 0, 2))


def solution(mesh):
    grid = P(("member", "polar"), "azimuth", None)

    def run(conv_out, grad_out, *others):
        owned = conv_out.shape[2] // mesh.shape["azimuth"]
        sizes = [owned]
        if owned % 32 == 0 and owned >= 96:
            big = owned * 3 // 5 // 32 * 32
            sizes = [big, owned - big]
        chunks = tuple((sum(sizes[:q]), size) for q, size in enumerate(sizes))
        return jax.shard_map(
            functools.partial(on_device, chunks),
            mesh=mesh,
            in_specs=(grid, grid) + (P(),) * 6,
            out_specs=grid,
            check_vma=False,
        )(conv_out, grad_out, *others)

    return run
```

```python
import functools
import math

import jax
import jax.numpy as jnp
import ml_dtypes
import numpy as np
from jax import lax
from jax.experimental import pallas as pl
from jax.experimental.pallas import tpu as pltpu
from jax.sharding import PartitionSpec as P

REACH = 3
LANES = 128
HALF = 64
TERMS = 3
NEAR = 1
VMEM = pltpu.MemorySpace.VMEM
NO_COST = pl.CostEstimate(flops=0, bytes_accessed=0, transcendentals=0)


def round_up(value, unit):
    return -(-value // unit) * unit


def partner(me, step, count, sign):
    if count & (count - 1) == 0:
        return me ^ step
    return lax.rem(me + sign * step + count, count)


def far_first(number, count):
    return sorted(range(number), key=lambda i: (i // count, i % count <= NEAR))


def exchange(block, step, count):
    if step == 0:
        return block
    pairs = [(a, int(partner_static(a, step, count))) for a in range(count)]
    return lax.ppermute(block, "azimuth", pairs)


def partner_static(a, step, count, sign=1):
    return a ^ step if count & (count - 1) == 0 else (a + sign * step) % count


def tables(count, part, modes):
    length = count * part
    whole = modes // LANES * LANES
    order = np.concatenate(
        [
            np.arange(whole),
            modes + np.arange(whole),
            np.arange(whole, modes),
            modes + np.arange(whole, modes),
        ]
    )
    positions = np.arange(length)
    waves = np.arange(modes)
    phase = (positions[:, None] * waves[None, :]) % length
    angle = (2.0 * math.pi / length) * phase
    scale = 1.0 / math.sqrt(length)
    factor = np.where(waves == 0, 1.0, 2.0)
    analysis = np.concatenate([np.cos(angle), -np.sin(angle)], axis=1) * scale
    synth = np.concatenate([np.cos(angle) * factor, -np.sin(angle) * factor], axis=1) * scale
    analysis = analysis.astype(np.float32).astype(ml_dtypes.bfloat16)[:, order]
    synth = synth.astype(np.float32).astype(ml_dtypes.bfloat16)[:, order]
    wide = round_up(part, HALF)
    window = round_up(HALF + wide, LANES)
    forth = np.zeros((count, HALF + window, 2 * modes), ml_dtypes.bfloat16)
    back = np.zeros((count * wide, 2 * modes), ml_dtypes.bfloat16)
    for s in range(count):
        forth[s, HALF : HALF + part] = analysis[s * part : (s + 1) * part]
        back[s * wide : s * wide + part] = synth[s * part : (s + 1) * part]
    return forth, back


def twice_gelu_slope(scaled):
    power = math.log2(2.0 / math.sqrt(math.pi)) - (1.0 / math.log(2.0)) * (scaled * scaled)
    return (1.0 + lax.erf(scaled)) + scaled * jnp.exp2(power)


def dot_nt(left, right):
    return lax.dot_general(left, right, (((1,), (1,)), ((), ())), preferred_element_type=jnp.float32)


def dot_nn(left, right):
    return jnp.dot(left, right, preferred_element_type=jnp.float32)


def mlp_kernel(count, half, sent, conv_ref, grad_ref, win_ref, bias_ref, wout_ref, *rest):
    outs, (tall_conv, tall_grad, pre_ref, back_ref, slope_ref, total_ref) = rest[-6 - len(sent) : -6], rest[-6:]
    earlier = iter(rest[: -6 - len(sent)])
    part, channels = conv_ref.shape[1:]
    wide = round_up(part, HALF)
    rows = tall_conv.shape[0] // wide
    owned = channels // count
    block = pre_ref.shape[2]
    steps = win_ref.shape[1] // block
    me = lax.axis_index("azimuth")
    def stack(tall, source):
        for row in range(rows):
            whole = part // 16 * 16
            tall[row * wide + whole : (row + 1) * wide, :] = jnp.zeros((wide - whole, channels), jnp.bfloat16)
            tall[row * wide : row * wide + part, :] = source[half * rows + row]

    group = 48
    groups = rows * wide // group

    def span(step):
        return slice(step * block, (step + 1) * block)

    def project_pre(step):
        pre_ref[step % 2] = dot_nn(tall_conv[...], win_ref[:, span(step)])

    def project_back(step):
        back_ref[step % 2] = dot_nt(tall_grad[...], wout_ref[span(step), :])

    def slope(step, first, last):
        root = math.sqrt(0.5)
        bias = bias_ref[span(step)].reshape(1, block) * root
        for g in range(first, last):
            some = slice(g * group, (g + 1) * group)
            value = back_ref[step % 2, some, :] * twice_gelu_slope(pre_ref[step % 2, some, :] * root + bias)
            slope_ref[some, span(step)] = value.astype(jnp.bfloat16)

    def gather(first, last):
        at = slice(first * block, last * block)
        term = dot_nt(win_ref[:, at], slope_ref[:, at])
        total_ref[...] = term if first == 0 else total_ref[...] + term

    stack(tall_conv, conv_ref)
    project_pre(0)
    stack(tall_grad, grad_ref)
    project_back(0)
    gathered = 0
    thirds = [groups * n // 3 for n in range(4)]
    for step in range(steps):
        if step + 1 < steps:
            project_pre(step + 1)
        slope(step, thirds[0], thirds[1])
        if step - gathered == 2:
            gather(gathered, step)
            gathered = step
        slope(step, thirds[1], thirds[2])
        if step + 1 < steps:
            project_back(step + 1)
        slope(step, thirds[2], thirds[3])
    gather(gathered, steps)
    for out, (k, start, size) in zip(outs, sent):
        first = pl.multiple_of(count * start + partner(me, k, count, 1) * size, 32)
        value = (0.5 * total_ref[pl.ds(first, size), :]).astype(jnp.bfloat16)
        before = out.shape[1] - rows * wide
        for at in range(0, before, rows * wide):
            out[:, at : at + rows * wide] = next(earlier)[...]
        out[:, before:] = value


def mlp(conv_out, grad_out, w_in, b_in, w_out, count, half, halves, sent, earlier):
    rows, part, channels = conv_out.shape
    rows //= halves
    block = 256
    wide = round_up(part, HALF)
    vmem = pl.BlockSpec(memory_space=VMEM)
    out_shape = [
        jax.ShapeDtypeStruct((size, rows * wide * (1 + len(blocks))), jnp.bfloat16)
        for (_, _, size), blocks in zip(sent, earlier)
    ]
    earlier = [block for blocks in earlier for block in blocks]
    return pl.pallas_call(
        functools.partial(mlp_kernel, count, half, sent),
        in_specs=[vmem] * (5 + len(earlier)),
        out_specs=[vmem] * len(out_shape),
        out_shape=out_shape,
        scratch_shapes=[
            pltpu.VMEM((rows * wide, channels), jnp.bfloat16),
            pltpu.VMEM((rows * wide, channels), jnp.bfloat16),
            pltpu.VMEM((2, rows * wide, block), jnp.float32),
            pltpu.VMEM((2, rows * wide, block), jnp.float32),
            pltpu.VMEM((rows * wide, w_in.shape[1]), jnp.bfloat16),
            pltpu.VMEM((channels, rows * wide), jnp.float32),
        ],
        compiler_params=pltpu.CompilerParams(vmem_limit_bytes=16 * 2**20),
        cost_estimate=NO_COST,
        name="mlp",
    )(conv_out, grad_out, w_in, b_in, w_out, *earlier)


def spectra_of(pieces, table_ref, wide):
    size, across = pieces[0].shape
    rows = across // wide
    window = table_ref.shape[1] - HALF
    shifts = [row * wide % LANES for row in range(rows)]
    spectra = [None] * rows
    for shift in sorted(set(shifts)):
        group = [row for row in range(rows) if shifts[row] == shift]
        total = None
        for k, piece in enumerate(pieces):
            windows = [row * wide // LANES * LANES for row in group]
            left = jnp.concatenate([piece[:, at : at + window] for at in windows], axis=0)
            term = dot_nn(left, table_ref[k, HALF - shift : HALF - shift + window, :])
            total = term if total is None else total + term
        for at, row in enumerate(group):
            spectra[row] = total[at * size : (at + 1) * size]
    return spectra


def row_in(row, early, own_ref):
    for ref in early:
        if row < ref.shape[0]:
            return ref[row]
        row -= ref.shape[0]
    return own_ref[row]


def early_kernel(count, wide, *refs):
    ranks = far_first(count, count)
    pieces = [refs[ranks.index(k)] for k in range(count)]
    table_ref, out_ref = refs[count], refs[-1]
    for row, spectrum in enumerate(spectra_of(pieces, table_ref, wide)):
        out_ref[row] = spectrum


def analyze_early(pieces, table, wide):
    count = len(pieces)
    size, across = pieces[0].shape
    return pl.pallas_call(
        functools.partial(early_kernel, count, wide),
        in_specs=[pl.BlockSpec(memory_space=VMEM)] * (count + 1),
        out_specs=pl.BlockSpec(memory_space=VMEM),
        out_shape=jax.ShapeDtypeStruct((across // wide, size, table.shape[2]), jnp.float32),
        compiler_params=pltpu.CompilerParams(vmem_limit_bytes=12 * 2**20),
        cost_estimate=NO_COST,
        name="analysis_early",
    )(*(pieces[k] for k in far_first(count, count)), table)


def analysis_kernel(count, rows, wide, early_halves, *refs):
    own_ref, first_ref, second_ref = refs[-3:]
    ranks = far_first(count, count)
    pieces = [refs[ranks.index(k)] for k in range(count)]
    table_ref, early = refs[count], refs[count + 1 : count + 1 + early_halves]
    even = lax.rem(lax.axis_index("polar"), 2) == 0
    for row, spectrum in enumerate(spectra_of(pieces, table_ref, wide)):
        own_ref[row] = spectrum

    def row_of(row):
        return row_in(row, early, own_ref)

    def share(above, below):
        for h in range(REACH):
            above[h] = row_of(rows - REACH + h).astype(jnp.bfloat16)
            below[h] = row_of(h).astype(jnp.bfloat16)

    pl.when(even)(lambda: share(first_ref, second_ref))
    pl.when(jnp.logical_not(even))(lambda: share(second_ref, first_ref))


def analyze(pieces, table, early, rows, wide, after):
    count = len(pieces)
    size, across = pieces[0].shape
    width = table.shape[2]
    halo = jax.ShapeDtypeStruct((REACH, size, width), jnp.bfloat16)
    return pl.pallas_call(
        functools.partial(analysis_kernel, count, rows, wide, len(early)),
        in_specs=[pl.BlockSpec(memory_space=VMEM)] * (count + 1 + len(early))
        + [pl.BlockSpec(memory_space=pl.ANY)] * len(after),
        out_specs=[pl.BlockSpec(memory_space=VMEM)] * 3,
        out_shape=[jax.ShapeDtypeStruct((across // wide, size, width), jnp.float32), halo, halo],
        compiler_params=pltpu.CompilerParams(vmem_limit_bytes=12 * 2**20),
        cost_estimate=NO_COST,
        name="analysis",
    )(*(pieces[k] for k in far_first(count, count)), table, *early, *after)


def add_row(accs, spectrum, weight, target_row, filter_row, targets):
    size = spectrum.shape[0]
    masked = jnp.concatenate([jnp.where(target_row == t, weight, 0.0) for t in targets], axis=0)
    gains = dot_nn(masked.astype(jnp.bfloat16), filter_row)
    whole = (gains.shape[1] // 2) // LANES * LANES - LANES
    spec_re = spectrum[:, :whole]
    spec_im = spectrum[:, whole : 2 * whole]
    spec_x = spectrum[:, 2 * whole :]
    swapped = pltpu.roll(spec_x, HALF, 1)
    for at, target in enumerate(targets):
        gain = gains[at * size : (at + 1) * size]
        gain_re = gain[:, :whole]
        gain_rx = gain[:, whole : whole + LANES]
        gain_im = gain[:, whole + LANES : 2 * whole + LANES]
        gain_ix = gain[:, 2 * whole + LANES :]
        acc_re, acc_im, acc_x = accs[target]
        acc_re = acc_re + (gain_re * spec_re + gain_im * spec_im)
        acc_im = acc_im + (gain_re * spec_im - gain_im * spec_re)
        acc_x = acc_x + (gain_rx * spec_x + gain_ix * swapped)
        accs[target] = acc_re, acc_im, acc_x


def split_tiles(value):
    whole = (value.shape[1] - LANES) // 2
    return value[:, :whole], value[:, whole : 2 * whole], value[:, 2 * whole :]


def own_kernel(own_ref, weight_ref, target_ref, filter_ref, *rest):
    early, out_ref = rest[:-1], rest[-1]
    rows, size, width = out_ref.shape
    accs = {t: split_tiles(jnp.zeros((size, width), jnp.float32)) for t in range(rows)}
    for row in range(rows):
        at = row + REACH
        targets = [t for t in range(rows) if abs(row - t) <= REACH]
        spectrum = row_in(row, early, own_ref)
        add_row(accs, spectrum, weight_ref[...], target_ref[at : at + 1, :], filter_ref[at], targets)
    for t in range(rows):
        out_ref[t] = jnp.concatenate(accs[t], axis=1)


def own_terms(own, early, weight, target, filters):
    rows, size, width = own.shape
    rows += sum(x.shape[0] for x in early)
    return pl.pallas_call(
        own_kernel,
        in_specs=[pl.BlockSpec(memory_space=VMEM)] * (4 + len(early)),
        out_specs=pl.BlockSpec(memory_space=VMEM),
        out_shape=jax.ShapeDtypeStruct((rows, size, width), jnp.float32),
        compiler_params=pltpu.CompilerParams(vmem_limit_bytes=12 * 2**20),
        cost_estimate=NO_COST,
        name="own_terms",
    )(own, weight, target, filters, *early)


def add_halo(accs, sides, rows, weight_ref, target_ref, filter_ref):
    for side, base in sides:
        for h in range(REACH):
            at = base + h + REACH
            targets = [t for t in range(rows) if abs(base + h - t) <= REACH]
            add_row(
                accs,
                side[h].astype(jnp.float32),
                weight_ref[...],
                target_ref[at : at + 1, :],
                filter_ref[at],
                targets,
            )


def side_kernel(part_ref, first_ref, weight_ref, target_ref, filter_ref, *rest):
    out_ref = rest[-1]
    rows = part_ref.shape[0]
    even = lax.rem(lax.axis_index("polar"), 2) == 0

    def combine(base):
        accs = {t: split_tiles(part_ref[t]) for t in range(rows)}
        add_halo(accs, [(first_ref, base)], rows, weight_ref, target_ref, filter_ref)
        for t in range(rows):
            out_ref[t] = jnp.concatenate(accs[t], axis=1)

    pl.when(even)(lambda: combine(rows))
    pl.when(jnp.logical_not(even))(lambda: combine(-REACH))


def side_terms(own, first, weight, target, filters, after):
    return pl.pallas_call(
        side_kernel,
        in_specs=[pl.BlockSpec(memory_space=VMEM)] * 5 + [pl.BlockSpec(memory_space=pl.ANY)] * len(after),
        out_specs=pl.BlockSpec(memory_space=VMEM),
        out_shape=jax.ShapeDtypeStruct(own.shape, jnp.float32),
        compiler_params=pltpu.CompilerParams(vmem_limit_bytes=12 * 2**20),
        cost_estimate=NO_COST,
        name="side_terms",
    )(own, first, weight, target, filters, *after)


def finish_kernel(count, swaps, part_ref, *refs):
    halos, (weight_ref, target_ref, filter_ref, table_ref) = refs[:swaps], refs[swaps : swaps + 4]
    outs, stacked_ref = refs[-count - 1 : -1], refs[-1]
    rows, size, width = part_ref.shape
    even = lax.rem(lax.axis_index("polar"), 2) == 0

    def combine(bases):
        accs = {t: split_tiles(part_ref[t]) for t in range(rows)}
        sides = list(zip(halos, bases[-swaps:]))
        add_halo(accs, sides, rows, weight_ref, target_ref, filter_ref)
        for t in range(rows):
            stacked_ref[t * size : (t + 1) * size, :] = jnp.concatenate(accs[t], axis=1).astype(jnp.bfloat16)

    pl.when(even)(lambda: combine((rows, -REACH)))
    pl.when(jnp.logical_not(even))(lambda: combine((-REACH, rows)))
    grid = dot_nt(table_ref[...], stacked_ref[...])
    wide = grid.shape[0] // count
    for k, out in enumerate(outs):
        out[...] = grid[k * wide : k * wide + out.shape[0]].astype(jnp.bfloat16)


def finish(own, halos, weight, target, filters, table, count, part):
    rows, size, width = own.shape
    return pl.pallas_call(
        functools.partial(finish_kernel, count, len(halos)),
        in_specs=[pl.BlockSpec(memory_space=VMEM)] * (5 + len(halos)),
        out_specs=[pl.BlockSpec(memory_space=VMEM)] * count,
        out_shape=[jax.ShapeDtypeStruct((part, rows * size), jnp.bfloat16)] * count,
        scratch_shapes=[pltpu.VMEM((rows * size, width), jnp.bfloat16)],
        compiler_params=pltpu.CompilerParams(vmem_limit_bytes=12 * 2**20),
        cost_estimate=NO_COST,
        name="finish",
    )(own, *halos, weight, target, filters, table)


def add_kernel(count, chunk, steps, grad_ref, *refs):
    out_ref, tall_ref, done_ref, sems = refs[-4:]
    pieces = dict(zip(steps, refs))
    tiles, part, rows, _ = done_ref.shape
    start, size = chunk
    me = lax.axis_index("azimuth")

    def add(tile, mine):
        order = [[k for k in range(count) if partner_static(mine, k, count, -1) == s][0] for s in range(count)]
        lanes = range(tile * LANES, (tile + 1) * LANES)
        for row in range(rows):
            parts = []
            for s in range(lanes[0] // size, lanes[-1] // size + 1):
                low, high = max(lanes[0], s * size) - s * size, min(lanes[-1] + 1, (s + 1) * size) - s * size
                parts.append(pieces[order[s]][:part, row * size + low : row * size + high])
            conv = jnp.concatenate(parts, axis=1).astype(jnp.float32)
            first = count * start + tile * LANES
            total = grad_ref[row, :, first : first + LANES].astype(jnp.float32) + conv
            tall_ref[tile, pl.ds(row, part, stride=rows), :] = total
        done_ref[tile] = tall_ref[tile].reshape(part, rows, LANES).astype(jnp.bfloat16)

    copies = []
    for tile in range(tiles):
        for mine in range(count):
            pl.when(me == mine)(functools.partial(add, tile, mine))
        lanes = pl.ds(count * start + tile * LANES, LANES)
        copies.append(pltpu.make_async_copy(done_ref.at[tile], out_ref.at[:, :, lanes], sems.at[tile]))
        copies[-1].start()
    for copy in copies:
        copy.wait()


def add_chunk(grad_out, pieces, chunk, count, before):
    rows, part, channels = grad_out.shape
    start, size = chunk
    tiles = count * size // LANES
    pieces = sorted(pieces.items(), key=lambda item: item[0] <= NEAR)
    vmem = pl.BlockSpec(memory_space=VMEM)
    anywhere = pl.BlockSpec(memory_space=pl.ANY)
    return pl.pallas_call(
        functools.partial(add_kernel, count, chunk, [k for k, _ in pieces]),
        in_specs=[vmem] * (1 + len(pieces)) + [anywhere] * len(before),
        out_specs=anywhere,
        out_shape=jax.ShapeDtypeStruct((part, rows, channels), jnp.bfloat16),
        scratch_shapes=[
            pltpu.VMEM((tiles, rows * part, LANES), jnp.float32),
            pltpu.VMEM((tiles, part, rows, LANES), jnp.bfloat16),
            pltpu.SemaphoreType.DMA((tiles,)),
        ],
        input_output_aliases={1 + len(pieces): 0} if before else {},
        compiler_params=pltpu.CompilerParams(vmem_limit_bytes=12 * 2**20),
        cost_estimate=NO_COST,
        name="add_chunk",
    )(grad_out, *(block for _, block in pieces), *before)


def prepare_kernel(count, chunks, weight_ref, filt_ref, offset_ref, forth_ref, back_ref, *outs):
    filter_out, target_out, forth_out, back_out = outs[:4]
    me = lax.axis_index("azimuth")
    wide = back_ref.shape[0] // count
    for k in range(count):
        forth_out[k] = forth_ref[partner(me, k, count, -1)]
        first = pl.multiple_of(partner(me, k, count, 1) * wide, HALF)
        back_out[k * wide : (k + 1) * wide, :] = back_ref[pl.ds(first, wide), :]
    bases, channels = weight_ref.shape
    lats, width = filt_ref.shape[1:]
    ext, depth = target_out.shape
    rows = ext - 2 * REACH
    modes = width // 2
    whole = modes // LANES * LANES
    used = TERMS * bases
    for (start, size), out in zip(chunks, outs[4:]):
        first = count * start + lax.axis_index("azimuth") * size
        weight = pltpu.roll(weight_ref[...], lax.rem(channels - first, channels), 1)[:, :size]
        parts = []
        for _ in range(TERMS):
            rounded = weight.astype(jnp.bfloat16).astype(jnp.float32)
            parts.append(rounded)
            weight = weight - rounded
        parts.append(jnp.zeros((depth - used, size), jnp.float32))
        out[...] = jnp.concatenate(parts, axis=0).T
    start_lat = lax.axis_index("polar") * rows
    table = filt_ref[...].reshape(bases * lats, width)
    base = lax.broadcasted_iota(jnp.int32, (depth, bases * lats), 0)
    valid = base < used
    for _ in range(TERMS - 1):
        base = jnp.where(base >= bases, base - bases, base)
    column = lax.broadcasted_iota(jnp.int32, (depth, bases * lats), 1)
    for i in range(ext):
        lat = start_lat + (i - REACH)
        inside = (lat >= 0) & (lat < lats)
        lat = jnp.clip(lat, 0, lats - 1)
        pick = jnp.where(valid & (column == base * lats + lat), 1.0, 0.0).astype(jnp.bfloat16)
        row = dot_nn(pick, table)
        real, imag = row[:, :modes], row[:, modes:]
        rest_re, rest_im = real[:, whole:], imag[:, whole:]
        filter_out[i] = jnp.concatenate(
            [real[:, :whole], rest_re, rest_re, imag[:, :whole], rest_im, -rest_im], axis=1
        ).astype(jnp.bfloat16)
        local = jnp.where(inside, offset_ref[pl.ds(lat, 1), :] - start_lat, -1)
        spare = jnp.full((1, depth - used), -1, jnp.int32)
        target_out[i : i + 1, :] = jnp.concatenate([local] * TERMS + [spare], axis=1)


def prepare(basis_weight, filt, offsets, forth, back, rows, count, chunks):
    bases = filt.shape[0]
    width = filt.shape[2]
    ext = rows + 2 * REACH
    depth = round_up(TERMS * bases, 16)
    shapes = [
        jax.ShapeDtypeStruct((ext, depth, width + LANES), jnp.bfloat16),
        jax.ShapeDtypeStruct((ext, depth), jnp.int32),
        jax.ShapeDtypeStruct(forth.shape, forth.dtype),
        jax.ShapeDtypeStruct(back.shape, back.dtype),
    ] + [jax.ShapeDtypeStruct((size, depth), jnp.float32) for _, size in chunks]
    return pl.pallas_call(
        functools.partial(prepare_kernel, count, chunks),
        in_specs=[pl.BlockSpec(memory_space=VMEM)] * 5,
        out_specs=[pl.BlockSpec(memory_space=VMEM)] * len(shapes),
        out_shape=shapes,
        compiler_params=pltpu.CompilerParams(vmem_limit_bytes=16 * 2**20),
        cost_estimate=NO_COST,
        name="prepare",
    )(basis_weight, filt, offsets, forth, back)


def halo(first, second):
    bands, count = lax.axis_size("polar"), lax.axis_size("azimuth")
    blocks = []
    for odd, block in ((0, first), (1, second)):
        pairs = []
        for a in range(bands):
            other = ((a + odd) ^ 1) - odd
            for b in range(count):
                paired = 0 <= other < bands
                target = (other, b) if paired else (a, b ^ 1 if b ^ 1 < count else b)
                pairs.append((a * count + b, target[0] * count + target[1]))
        blocks.append(lax.ppermute(block, ("polar", "azimuth"), pairs))
    return blocks


def on_device(chunks, conv_out, grad_out, w_in, b_in, w_out, basis_weight, filt, offsets):
    rows, part, channels = conv_out.shape
    count = lax.axis_size("azimuth")
    forth, back = tables(count, part, filt.shape[2] // 2)
    forth, back = jnp.asarray(forth), jnp.asarray(back)
    owned = channels // count
    halves = 2 if rows % 2 == 0 else 1
    wide = round_up(part, HALF)
    filters, target, forth, back, *weights = prepare(
        basis_weight, filt, offsets, forth, back, rows, count, chunks
    )
    sent = [(k,) + chunk for chunk in chunks for k in range(count)]
    early, kept = [], [[] for _ in sent]
    for half in range(halves):
        final = half == halves - 1
        blocks = mlp(
            conv_out, grad_out, w_in, b_in, w_out, count, half, halves, sent, kept if final else [[] for _ in sent]
        )
        if not final:
            early.append(analyze_early([exchange(blocks[k], k, count) for k in range(count)], forth, wide))
            for i in range(count, len(sent)):
                kept[i].append(blocks[i])
    spectra, terms, returned = {}, {}, {}
    for q in range(len(chunks)):
        pieces = [exchange(blocks[q * count + k], k, count) for k in range(count)]
        ahead = early if q == 0 else []
        after = [terms[q - 1]] if q else []
        own, first, second = analyze(pieces, forth, ahead, rows, wide, after)
        spectra[q] = halo(first, second)
        terms[q] = own_terms(own, ahead, weights[q], target, filters)
    for q in range(len(chunks)):
        halos = spectra[q]
        if q == 0:
            others = [terms[other] for other in terms if other > q]
            terms[q] = side_terms(terms[q], halos[0], weights[q], target, filters, others)
            halos = halos[1:]
        grids = finish(terms[q], halos, weights[q], target, filters, back, count, part)
        returned[q] = {k: exchange(grids[k], k, count) for k in range(count)}
    total = []
    for q, chunk in enumerate(chunks):
        total = [add_chunk(grad_out, returned[q], chunk, count, total)]
    return jnp.transpose(total[0], (1, 0, 2))


def solution(mesh):
    grid = P(("member", "polar"), "azimuth", None)

    def run(conv_out, grad_out, *others):
        owned = conv_out.shape[2] // mesh.shape["azimuth"]
        sizes = [owned]
        if owned % 32 == 0 and owned >= 96:
            big = owned * 3 // 5 // 32 * 32
            sizes = [big, owned - big]
        chunks = tuple((sum(sizes[:q]), size) for q, size in enumerate(sizes))
        return jax.shard_map(
            functools.partial(on_device, chunks),
            mesh=mesh,
            in_specs=(grid, grid) + (P(),) * 6,
            out_specs=grid,
            check_vma=False,
        )(conv_out, grad_out, *others)

    return run
```

```python
import functools
import math

import jax
import jax.numpy as jnp
import ml_dtypes
import numpy as np
from jax import lax
from jax.experimental import pallas as pl
from jax.experimental.pallas import tpu as pltpu
from jax.sharding import PartitionSpec as P

REACH = 3
LANES = 128
HALF = 64
TERMS = 3
NEAR = 1
VMEM = pltpu.MemorySpace.VMEM
NO_COST = pl.CostEstimate(flops=0, bytes_accessed=0, transcendentals=0)


def round_up(value, unit):
    return -(-value // unit) * unit


def partner(me, step, count, sign):
    if count & (count - 1) == 0:
        return me ^ step
    return lax.rem(me + sign * step + count, count)


def far_first(number, count):
    return sorted(range(number), key=lambda i: (i // count, i % count <= NEAR))


def exchange(block, step, count):
    if step == 0:
        return block
    pairs = [(a, int(partner_static(a, step, count))) for a in range(count)]
    return lax.ppermute(block, "azimuth", pairs)


def partner_static(a, step, count, sign=1):
    return a ^ step if count & (count - 1) == 0 else (a + sign * step) % count


def tables(count, part, modes):
    length = count * part
    whole = modes // LANES * LANES
    order = np.concatenate(
        [
            np.arange(whole),
            modes + np.arange(whole),
            np.arange(whole, modes),
            modes + np.arange(whole, modes),
        ]
    )
    positions = np.arange(length)
    waves = np.arange(modes)
    phase = (positions[:, None] * waves[None, :]) % length
    angle = (2.0 * math.pi / length) * phase
    scale = 1.0 / math.sqrt(length)
    factor = np.where(waves == 0, 1.0, 2.0)
    analysis = np.concatenate([np.cos(angle), -np.sin(angle)], axis=1) * scale
    synth = np.concatenate([np.cos(angle) * factor, -np.sin(angle) * factor], axis=1) * scale
    analysis = analysis.astype(np.float32).astype(ml_dtypes.bfloat16)[:, order]
    synth = synth.astype(np.float32).astype(ml_dtypes.bfloat16)[:, order]
    wide = round_up(part, HALF)
    window = round_up(HALF + wide, LANES)
    forth = np.zeros((count, HALF + window, 2 * modes), ml_dtypes.bfloat16)
    back = np.zeros((count * wide, 2 * modes), ml_dtypes.bfloat16)
    for s in range(count):
        forth[s, HALF : HALF + part] = analysis[s * part : (s + 1) * part]
        back[s * wide : s * wide + part] = synth[s * part : (s + 1) * part]
    return forth, back


def twice_gelu_slope(scaled):
    power = math.log2(2.0 / math.sqrt(math.pi)) - (1.0 / math.log(2.0)) * (scaled * scaled)
    return (1.0 + lax.erf(scaled)) + scaled * jnp.exp2(power)


def dot_nt(left, right):
    return lax.dot_general(left, right, (((1,), (1,)), ((), ())), preferred_element_type=jnp.float32)


def dot_nn(left, right):
    return jnp.dot(left, right, preferred_element_type=jnp.float32)


def mlp_kernel(count, half, sent, chunks, conv_ref, grad_ref, win_ref, bias_ref, wout_ref, *rest):
    outs, (tall_conv, tall_grad, pre_ref, back_ref, slope_ref, total_ref) = rest[-6 - len(sent) : -6], rest[-6:]
    part, channels = conv_ref.shape[1:]
    wide = round_up(part, HALF)
    rows = tall_conv.shape[0] // wide
    owned = channels // count
    block = pre_ref.shape[2]
    steps = win_ref.shape[1] // block
    me = lax.axis_index("azimuth")
    def stack(tall, source):
        for row in range(rows):
            whole = part // 16 * 16
            tall[row * wide + whole : (row + 1) * wide, :] = jnp.zeros((wide - whole, channels), jnp.bfloat16)
            tall[row * wide : row * wide + part, :] = source[half * rows + row]

    group = 48
    groups = rows * wide // group

    def span(step):
        return slice(step * block, (step + 1) * block)

    def project_pre(step):
        pre_ref[step % 2] = dot_nn(tall_conv[...], win_ref[:, span(step)])

    def project_back(step):
        back_ref[step % 2] = dot_nt(tall_grad[...], wout_ref[span(step), :])

    def slope(step, first, last):
        root = math.sqrt(0.5)
        bias = bias_ref[span(step)].reshape(1, block) * root
        for g in range(first, last):
            some = slice(g * group, (g + 1) * group)
            value = back_ref[step % 2, some, :] * twice_gelu_slope(pre_ref[step % 2, some, :] * root + bias)
            slope_ref[some, span(step)] = value.astype(jnp.bfloat16)

    def gather(first, last):
        at = slice(first * block, last * block)
        term = dot_nt(win_ref[:, at], slope_ref[:, at])
        total_ref[...] = term if first == 0 else total_ref[...] + term

    stack(tall_conv, conv_ref)
    project_pre(0)
    stack(tall_grad, grad_ref)
    project_back(0)
    gathered = 0
    thirds = [groups * n // 3 for n in range(4)]
    for step in range(steps):
        if step + 1 < steps:
            project_pre(step + 1)
        slope(step, thirds[0], thirds[1])
        if step - gathered == 3:
            gather(gathered, step)
            gathered = step
        slope(step, thirds[1], thirds[2])
        if step + 1 < steps:
            project_back(step + 1)
        slope(step, thirds[2], thirds[3])
    gather(gathered, steps)
    for out, (k, start, size) in zip(outs, sent):
        target = partner(me, k, count, 1)
        for begin, width in chunks:
            if start <= begin < start + size:
                first = pl.multiple_of(count * begin + target * width, 32)
                value = 0.5 * total_ref[pl.ds(first, width), :]
                out[begin - start : begin - start + width, :] = value.astype(jnp.bfloat16)


def mlp(conv_out, grad_out, w_in, b_in, w_out, count, half, halves, sent, chunks, after):
    rows, part, channels = conv_out.shape
    rows //= halves
    block = 256
    wide = round_up(part, HALF)
    vmem = pl.BlockSpec(memory_space=VMEM)
    out_shape = [jax.ShapeDtypeStruct((size, rows * wide), jnp.bfloat16) for _, _, size in sent]
    return pl.pallas_call(
        functools.partial(mlp_kernel, count, half, sent, chunks),
        in_specs=[vmem] * 5 + [pl.BlockSpec(memory_space=pl.ANY)] * len(after),
        out_specs=[vmem] * len(out_shape),
        out_shape=out_shape,
        scratch_shapes=[
            pltpu.VMEM((rows * wide, channels), jnp.bfloat16),
            pltpu.VMEM((rows * wide, channels), jnp.bfloat16),
            pltpu.VMEM((2, rows * wide, block), jnp.float32),
            pltpu.VMEM((2, rows * wide, block), jnp.float32),
            pltpu.VMEM((rows * wide, w_in.shape[1]), jnp.bfloat16),
            pltpu.VMEM((channels, rows * wide), jnp.float32),
        ],
        compiler_params=pltpu.CompilerParams(vmem_limit_bytes=16 * 2**20),
        cost_estimate=NO_COST,
        name="mlp",
    )(conv_out, grad_out, w_in, b_in, w_out, *after)


def spectra_of(pieces, channels, table_ref, wide):
    size = channels[1]
    rows = pieces[0][0].shape[1] // wide
    window = table_ref.shape[1] - HALF
    shifts = [row * wide % LANES for row in range(rows)]
    spectra = [None] * rows
    for shift in sorted(set(shifts)):
        group = [row for row in range(rows) if shifts[row] == shift]
        total = None
        for k, (piece, base) in enumerate(pieces):
            windows = [row * wide // LANES * LANES for row in group]
            left = jnp.concatenate([piece[base : base + size, at : at + window] for at in windows], axis=0)
            term = dot_nn(left, table_ref[k, HALF - shift : HALF - shift + window, :])
            total = term if total is None else total + term
        for at, row in enumerate(group):
            spectra[row] = total[at * size : (at + 1) * size]
    return spectra


def early_kernel(count, wide, *refs):
    ranks = far_first(count, count)
    pieces = [(refs[ranks.index(k)], 0) for k in range(count)]
    table_ref, (out_ref, sent_ref) = refs[count], refs[-2:]
    for row, spectrum in enumerate(spectra_of(pieces, (0, pieces[0][0].shape[0]), table_ref, wide)):
        out_ref[row] = spectrum
        sent_ref[row] = spectrum.astype(jnp.bfloat16)


def analyze_early(pieces, table, wide):
    count = len(pieces)
    size, across = pieces[0].shape
    return pl.pallas_call(
        functools.partial(early_kernel, count, wide),
        in_specs=[pl.BlockSpec(memory_space=VMEM)] * (count + 1),
        out_specs=[pl.BlockSpec(memory_space=VMEM)] * 2,
        out_shape=[
            jax.ShapeDtypeStruct((across // wide, size, table.shape[2]), kind) for kind in (jnp.float32, jnp.bfloat16)
        ],
        compiler_params=pltpu.CompilerParams(vmem_limit_bytes=12 * 2**20),
        cost_estimate=NO_COST,
        name="analysis_early",
    )(*(pieces[k] for k in far_first(count, count)), table)


def analysis_kernel(count, rows, wide, chunk, halves, *refs):
    own_ref, first_ref, second_ref, sent_ref = refs[-4:]
    start, size = chunk
    ranks = far_first(count, count)
    pieces = [(refs[ranks.index(k)], 0 if k else start) for k in range(count)]
    table_ref, early = refs[count], refs[count + 1 : count + halves]
    per = rows // halves
    even = lax.rem(lax.axis_index("polar"), 2) == 0
    for row, spectrum in enumerate(spectra_of(pieces, chunk, table_ref, wide)):
        own_ref[row] = spectrum
        sent_ref[row] = spectrum.astype(jnp.bfloat16)

    def row_of(row):
        half, row = divmod(row, per)
        return sent_ref[row] if half == halves - 1 else early[half][row, start : start + size, :]

    def share(above, below):
        for h in range(REACH):
            above[h] = row_of(rows - REACH + h)
            below[h] = row_of(h)

    pl.when(even)(lambda: share(first_ref, second_ref))
    pl.when(jnp.logical_not(even))(lambda: share(second_ref, first_ref))


def analyze(pieces, table, early, rows, wide, chunk, after):
    count = len(pieces)
    size = chunk[1]
    width = table.shape[2]
    halves = len(early) + 1
    halo = jax.ShapeDtypeStruct((REACH, size, width), jnp.bfloat16)
    return pl.pallas_call(
        functools.partial(analysis_kernel, count, rows, wide, chunk, halves),
        in_specs=[pl.BlockSpec(memory_space=VMEM)] * (count + halves)
        + [pl.BlockSpec(memory_space=pl.ANY)] * len(after),
        out_specs=[pl.BlockSpec(memory_space=VMEM)] * 3,
        out_shape=[jax.ShapeDtypeStruct((rows // halves, size, width), jnp.float32), halo, halo],
        scratch_shapes=[pltpu.VMEM((rows // halves, size, width), jnp.bfloat16)],
        compiler_params=pltpu.CompilerParams(vmem_limit_bytes=12 * 2**20),
        cost_estimate=NO_COST,
        name="analysis",
    )(*(pieces[k] for k in far_first(count, count)), table, *early, *after)


def add_row(accs, spectrum, weight, target_row, filter_row, targets):
    size = spectrum.shape[0]
    masked = jnp.concatenate([jnp.where(target_row == t, weight, 0.0) for t in targets], axis=0)
    gains = dot_nn(masked.astype(jnp.bfloat16), filter_row)
    whole = (gains.shape[1] // 2) // LANES * LANES - LANES
    spec_re = spectrum[:, :whole]
    spec_im = spectrum[:, whole : 2 * whole]
    spec_x = spectrum[:, 2 * whole :]
    swapped = pltpu.roll(spec_x, HALF, 1)
    for at, target in enumerate(targets):
        gain = gains[at * size : (at + 1) * size]
        gain_re = gain[:, :whole]
        gain_rx = gain[:, whole : whole + LANES]
        gain_im = gain[:, whole + LANES : 2 * whole + LANES]
        gain_ix = gain[:, 2 * whole + LANES :]
        acc_re, acc_im, acc_x = accs[target]
        acc_re = acc_re + (gain_re * spec_re + gain_im * spec_im)
        acc_im = acc_im + (gain_re * spec_im - gain_im * spec_re)
        acc_x = acc_x + (gain_rx * spec_x + gain_ix * swapped)
        accs[target] = acc_re, acc_im, acc_x


def split_tiles(value):
    whole = (value.shape[1] - LANES) // 2
    return value[:, :whole], value[:, whole : 2 * whole], value[:, 2 * whole :]


def own_kernel(start, own_ref, weight_ref, target_ref, filter_ref, *rest):
    early, out_ref = rest[:-1], rest[-1]
    rows, size, width = out_ref.shape
    per = own_ref.shape[0]
    accs = {t: split_tiles(jnp.zeros((size, width), jnp.float32)) for t in range(rows)}
    for row in range(rows):
        at = row + REACH
        targets = [t for t in range(rows) if abs(row - t) <= REACH]
        half = row // per
        spectrum = early[half][row % per, start : start + size, :] if half < len(early) else own_ref[row % per]
        add_row(accs, spectrum, weight_ref[...], target_ref[at : at + 1, :], filter_ref[at], targets)
    for t in range(rows):
        out_ref[t] = jnp.concatenate(accs[t], axis=1)


def own_terms(own, early, start, weight, target, filters):
    per, size, width = own.shape
    return pl.pallas_call(
        functools.partial(own_kernel, start),
        in_specs=[pl.BlockSpec(memory_space=VMEM)] * (4 + len(early)),
        out_specs=pl.BlockSpec(memory_space=VMEM),
        out_shape=jax.ShapeDtypeStruct((per * (1 + len(early)), size, width), jnp.float32),
        compiler_params=pltpu.CompilerParams(vmem_limit_bytes=12 * 2**20),
        cost_estimate=NO_COST,
        name="own_terms",
    )(own, weight, target, filters, *early)


def add_halo(accs, sides, rows, weight_ref, target_ref, filter_ref):
    for side, base in sides:
        for h in range(REACH):
            at = base + h + REACH
            targets = [t for t in range(rows) if abs(base + h - t) <= REACH]
            add_row(
                accs,
                side[h].astype(jnp.float32),
                weight_ref[...],
                target_ref[at : at + 1, :],
                filter_ref[at],
                targets,
            )


def side_kernel(part_ref, first_ref, weight_ref, target_ref, filter_ref, *rest):
    out_ref = rest[-1]
    rows = part_ref.shape[0]
    even = lax.rem(lax.axis_index("polar"), 2) == 0

    def combine(base):
        accs = {t: split_tiles(part_ref[t]) for t in range(rows)}
        add_halo(accs, [(first_ref, base)], rows, weight_ref, target_ref, filter_ref)
        for t in range(rows):
            out_ref[t] = jnp.concatenate(accs[t], axis=1)

    pl.when(even)(lambda: combine(rows))
    pl.when(jnp.logical_not(even))(lambda: combine(-REACH))


def side_terms(own, first, weight, target, filters, after):
    return pl.pallas_call(
        side_kernel,
        in_specs=[pl.BlockSpec(memory_space=VMEM)] * 5 + [pl.BlockSpec(memory_space=pl.ANY)] * len(after),
        out_specs=pl.BlockSpec(memory_space=VMEM),
        out_shape=jax.ShapeDtypeStruct(own.shape, jnp.float32),
        compiler_params=pltpu.CompilerParams(vmem_limit_bytes=12 * 2**20),
        cost_estimate=NO_COST,
        name="side_terms",
    )(own, first, weight, target, filters, *after)


def finish_kernel(count, swaps, part_ref, *refs):
    halos, (weight_ref, target_ref, filter_ref, table_ref) = refs[:swaps], refs[swaps : swaps + 4]
    outs, stacked_ref = refs[-count - 1 : -1], refs[-1]
    rows, size, width = part_ref.shape
    even = lax.rem(lax.axis_index("polar"), 2) == 0

    def combine(bases):
        accs = {t: split_tiles(part_ref[t]) for t in range(rows)}
        sides = list(zip(halos, bases[-swaps:]))
        add_halo(accs, sides, rows, weight_ref, target_ref, filter_ref)
        for t in range(rows):
            stacked_ref[t * size : (t + 1) * size, :] = jnp.concatenate(accs[t], axis=1).astype(jnp.bfloat16)

    pl.when(even)(lambda: combine((rows, -REACH)))
    pl.when(jnp.logical_not(even))(lambda: combine((-REACH, rows)))
    grid = dot_nt(table_ref[...], stacked_ref[...])
    wide = grid.shape[0] // count
    for k, out in enumerate(outs):
        out[...] = grid[k * wide : k * wide + out.shape[0]].astype(jnp.bfloat16)


def finish(own, halos, weight, target, filters, table, count, part):
    rows, size, width = own.shape
    return pl.pallas_call(
        functools.partial(finish_kernel, count, len(halos)),
        in_specs=[pl.BlockSpec(memory_space=VMEM)] * (5 + len(halos)),
        out_specs=[pl.BlockSpec(memory_space=VMEM)] * count,
        out_shape=[jax.ShapeDtypeStruct((part, rows * size), jnp.bfloat16)] * count,
        scratch_shapes=[pltpu.VMEM((rows * size, width), jnp.bfloat16)],
        compiler_params=pltpu.CompilerParams(vmem_limit_bytes=12 * 2**20),
        cost_estimate=NO_COST,
        name="finish",
    )(own, *halos, weight, target, filters, table)


def add_kernel(count, chunk, steps, grad_ref, *refs):
    out_ref, tall_ref, done_ref, sems = refs[-4:]
    pieces = dict(zip(steps, refs))
    tiles, part, rows, _ = done_ref.shape
    start, size = chunk
    me = lax.axis_index("azimuth")

    def add(tile, mine):
        order = [[k for k in range(count) if partner_static(mine, k, count, -1) == s][0] for s in range(count)]
        lanes = range(tile * LANES, (tile + 1) * LANES)
        for row in range(rows):
            parts = []
            for s in range(lanes[0] // size, lanes[-1] // size + 1):
                low, high = max(lanes[0], s * size) - s * size, min(lanes[-1] + 1, (s + 1) * size) - s * size
                parts.append(pieces[order[s]][:part, row * size + low : row * size + high])
            conv = jnp.concatenate(parts, axis=1).astype(jnp.float32)
            first = count * start + tile * LANES
            total = grad_ref[row, :, first : first + LANES].astype(jnp.float32) + conv
            tall_ref[tile, pl.ds(row, part, stride=rows), :] = total
        done_ref[tile] = tall_ref[tile].reshape(part, rows, LANES).astype(jnp.bfloat16)

    copies = []
    for tile in range(tiles):
        for mine in range(count):
            pl.when(me == mine)(functools.partial(add, tile, mine))
        lanes = pl.ds(count * start + tile * LANES, LANES)
        copies.append(pltpu.make_async_copy(done_ref.at[tile], out_ref.at[:, :, lanes], sems.at[tile]))
        copies[-1].start()
    for copy in copies:
        copy.wait()


def add_chunk(grad_out, pieces, chunk, count, before):
    rows, part, channels = grad_out.shape
    start, size = chunk
    tiles = count * size // LANES
    pieces = sorted(pieces.items(), key=lambda item: item[0] <= NEAR)
    vmem = pl.BlockSpec(memory_space=VMEM)
    anywhere = pl.BlockSpec(memory_space=pl.ANY)
    return pl.pallas_call(
        functools.partial(add_kernel, count, chunk, [k for k, _ in pieces]),
        in_specs=[vmem] * (1 + len(pieces)) + [anywhere] * len(before),
        out_specs=anywhere,
        out_shape=jax.ShapeDtypeStruct((part, rows, channels), jnp.bfloat16),
        scratch_shapes=[
            pltpu.VMEM((tiles, rows * part, LANES), jnp.float32),
            pltpu.VMEM((tiles, part, rows, LANES), jnp.bfloat16),
            pltpu.SemaphoreType.DMA((tiles,)),
        ],
        input_output_aliases={1 + len(pieces): 0} if before else {},
        compiler_params=pltpu.CompilerParams(vmem_limit_bytes=12 * 2**20),
        cost_estimate=NO_COST,
        name="add_chunk",
    )(grad_out, *(block for _, block in pieces), *before)


def prepare_kernel(count, chunks, weight_ref, filt_ref, offset_ref, forth_ref, back_ref, *outs):
    filter_out, target_out, forth_out, back_out = outs[:4]
    me = lax.axis_index("azimuth")
    wide = back_ref.shape[0] // count
    for k in range(count):
        forth_out[k] = forth_ref[partner(me, k, count, -1)]
        first = pl.multiple_of(partner(me, k, count, 1) * wide, HALF)
        back_out[k * wide : (k + 1) * wide, :] = back_ref[pl.ds(first, wide), :]
    bases, channels = weight_ref.shape
    lats, width = filt_ref.shape[1:]
    ext, depth = target_out.shape
    rows = ext - 2 * REACH
    modes = width // 2
    whole = modes // LANES * LANES
    used = TERMS * bases
    for (start, size), out in zip(chunks, outs[4:]):
        first = count * start + lax.axis_index("azimuth") * size
        weight = pltpu.roll(weight_ref[...], lax.rem(channels - first, channels), 1)[:, :size]
        parts = []
        for _ in range(TERMS):
            rounded = weight.astype(jnp.bfloat16).astype(jnp.float32)
            parts.append(rounded)
            weight = weight - rounded
        parts.append(jnp.zeros((depth - used, size), jnp.float32))
        out[...] = jnp.concatenate(parts, axis=0).T
    start_lat = lax.axis_index("polar") * rows
    table = filt_ref[...].reshape(bases * lats, width)
    base = lax.broadcasted_iota(jnp.int32, (depth, bases * lats), 0)
    valid = base < used
    for _ in range(TERMS - 1):
        base = jnp.where(base >= bases, base - bases, base)
    column = lax.broadcasted_iota(jnp.int32, (depth, bases * lats), 1)
    for i in range(ext):
        lat = start_lat + (i - REACH)
        inside = (lat >= 0) & (lat < lats)
        lat = jnp.clip(lat, 0, lats - 1)
        pick = jnp.where(valid & (column == base * lats + lat), 1.0, 0.0).astype(jnp.bfloat16)
        row = dot_nn(pick, table)
        real, imag = row[:, :modes], row[:, modes:]
        rest_re, rest_im = real[:, whole:], imag[:, whole:]
        filter_out[i] = jnp.concatenate(
            [real[:, :whole], rest_re, rest_re, imag[:, :whole], rest_im, -rest_im], axis=1
        ).astype(jnp.bfloat16)
        local = jnp.where(inside, offset_ref[pl.ds(lat, 1), :] - start_lat, -1)
        spare = jnp.full((1, depth - used), -1, jnp.int32)
        target_out[i : i + 1, :] = jnp.concatenate([local] * TERMS + [spare], axis=1)


def prepare(basis_weight, filt, offsets, forth, back, rows, count, chunks):
    bases = filt.shape[0]
    width = filt.shape[2]
    ext = rows + 2 * REACH
    depth = round_up(TERMS * bases, 16)
    shapes = [
        jax.ShapeDtypeStruct((ext, depth, width + LANES), jnp.bfloat16),
        jax.ShapeDtypeStruct((ext, depth), jnp.int32),
        jax.ShapeDtypeStruct(forth.shape, forth.dtype),
        jax.ShapeDtypeStruct(back.shape, back.dtype),
    ] + [jax.ShapeDtypeStruct((size, depth), jnp.float32) for _, size in chunks]
    return pl.pallas_call(
        functools.partial(prepare_kernel, count, chunks),
        in_specs=[pl.BlockSpec(memory_space=VMEM)] * 5,
        out_specs=[pl.BlockSpec(memory_space=VMEM)] * len(shapes),
        out_shape=shapes,
        compiler_params=pltpu.CompilerParams(vmem_limit_bytes=16 * 2**20),
        cost_estimate=NO_COST,
        name="prepare",
    )(basis_weight, filt, offsets, forth, back)


def halo(first, second):
    bands, count = lax.axis_size("polar"), lax.axis_size("azimuth")
    blocks = []
    for odd, block in ((0, first), (1, second)):
        pairs = []
        for a in range(bands):
            other = ((a + odd) ^ 1) - odd
            for b in range(count):
                paired = 0 <= other < bands
                target = (other, b) if paired else (a, b ^ 1 if b ^ 1 < count else b)
                pairs.append((a * count + b, target[0] * count + target[1]))
        blocks.append(lax.ppermute(block, ("polar", "azimuth"), pairs))
    return blocks


def on_device(chunks, conv_out, grad_out, w_in, b_in, w_out, basis_weight, filt, offsets):
    rows, part, channels = conv_out.shape
    count = lax.axis_size("azimuth")
    forth, back = tables(count, part, filt.shape[2] // 2)
    forth, back = jnp.asarray(forth), jnp.asarray(back)
    owned = channels // count
    halves = 2 if rows % 2 == 0 else 1
    wide = round_up(part, HALF)
    filters, target, forth, back, *weights = prepare(
        basis_weight, filt, offsets, forth, back, rows, count, chunks
    )
    early, order = [], []
    for half in range(halves):
        final = half == halves - 1
        sent = [(k, 0, owned) for k in range(count)]
        if final:
            sent[1:] = [(k,) + chunk for chunk in chunks for k in range(1, count)]
        blocks = mlp(conv_out, grad_out, w_in, b_in, w_out, count, half, halves, sent, chunks, order)
        order = blocks[:1]
        if not final:
            early.append(analyze_early([exchange(blocks[k], k, count) for k in range(count)], forth, wide))
    spectra, terms, returned = {}, {}, {}
    for q, (start, size) in enumerate(chunks):
        mine = blocks[1 + q * (count - 1) : 1 + (q + 1) * (count - 1)]
        pieces = [blocks[0]] + [exchange(block, k, count) for k, block in enumerate(mine, 1)]
        after = [terms[q - 1]] if q else []
        own, first, second = analyze(pieces, forth, [sent for _, sent in early], rows, wide, (start, size), after)
        spectra[q] = halo(first, second)
        terms[q] = own_terms(own, [spectrum for spectrum, _ in early], start, weights[q], target, filters)
    for q in range(len(chunks)):
        halos = spectra[q]
        if q == 0:
            others = [terms[other] for other in terms if other > q]
            terms[q] = side_terms(terms[q], halos[0], weights[q], target, filters, others)
            halos = halos[1:]
        grids = finish(terms[q], halos, weights[q], target, filters, back, count, part)
        returned[q] = {k: exchange(grids[k], k, count) for k in range(count)}
    total = []
    for q, chunk in enumerate(chunks):
        total = [add_chunk(grad_out, returned[q], chunk, count, total)]
    return jnp.transpose(total[0], (1, 0, 2))


def solution(mesh):
    grid = P(("member", "polar"), "azimuth", None)

    def run(conv_out, grad_out, *others):
        owned = conv_out.shape[2] // mesh.shape["azimuth"]
        sizes = [owned]
        if owned % 32 == 0 and owned >= 96:
            big = owned * 3 // 5 // 32 * 32
            sizes = [big, owned - big]
        chunks = tuple((sum(sizes[:q]), size) for q, size in enumerate(sizes))
        return jax.shard_map(
            functools.partial(on_device, chunks),
            mesh=mesh,
            in_specs=(grid, grid) + (P(),) * 6,
            out_specs=grid,
            check_vma=False,
        )(conv_out, grad_out, *others)

    return run
```

```python
import functools
import math

import jax
import jax.numpy as jnp
import ml_dtypes
import numpy as np
from jax import lax
from jax.experimental import pallas as pl
from jax.experimental.pallas import tpu as pltpu
from jax.sharding import PartitionSpec as P

REACH = 3
LANES = 128
HALF = 64
TERMS = 3
NEAR = 1
VMEM = pltpu.MemorySpace.VMEM
NO_COST = pl.CostEstimate(flops=0, bytes_accessed=0, transcendentals=0)


def round_up(value, unit):
    return -(-value // unit) * unit


def partner(me, step, count, sign):
    if count & (count - 1) == 0:
        return me ^ step
    return lax.rem(me + sign * step + count, count)


def far_first(number, count):
    return sorted(range(number), key=lambda i: (i // count, i % count <= NEAR))


def exchange(block, step, count):
    if step == 0:
        return block
    pairs = [(a, int(partner_static(a, step, count))) for a in range(count)]
    return lax.ppermute(block, "azimuth", pairs)


def partner_static(a, step, count, sign=1):
    return a ^ step if count & (count - 1) == 0 else (a + sign * step) % count


def tables(count, part, modes):
    length = count * part
    whole = modes // LANES * LANES
    order = np.concatenate(
        [
            np.arange(whole),
            modes + np.arange(whole),
            np.arange(whole, modes),
            modes + np.arange(whole, modes),
        ]
    )
    positions = np.arange(length)
    waves = np.arange(modes)
    phase = (positions[:, None] * waves[None, :]) % length
    angle = (2.0 * math.pi / length) * phase
    scale = 1.0 / math.sqrt(length)
    factor = np.where(waves == 0, 1.0, 2.0)
    analysis = np.concatenate([np.cos(angle), -np.sin(angle)], axis=1) * scale
    synth = np.concatenate([np.cos(angle) * factor, -np.sin(angle) * factor], axis=1) * scale
    analysis = analysis.astype(np.float32).astype(ml_dtypes.bfloat16)[:, order]
    synth = synth.astype(np.float32).astype(ml_dtypes.bfloat16)[:, order]
    wide = round_up(part, HALF)
    window = round_up(HALF + wide, LANES)
    forth = np.zeros((count, HALF + window, 2 * modes), ml_dtypes.bfloat16)
    back = np.zeros((count * wide, 2 * modes), ml_dtypes.bfloat16)
    for s in range(count):
        forth[s, HALF : HALF + part] = analysis[s * part : (s + 1) * part]
        back[s * wide : s * wide + part] = synth[s * part : (s + 1) * part]
    return forth, back


def twice_gelu_slope(scaled):
    power = math.log2(2.0 / math.sqrt(math.pi)) - (1.0 / math.log(2.0)) * (scaled * scaled)
    return (1.0 + lax.erf(scaled)) + scaled * jnp.exp2(power)


def dot_nt(left, right):
    return lax.dot_general(left, right, (((1,), (1,)), ((), ())), preferred_element_type=jnp.float32)


def dot_nn(left, right):
    return jnp.dot(left, right, preferred_element_type=jnp.float32)


def mlp_kernel(count, half, sent, chunks, conv_ref, grad_ref, win_ref, bias_ref, wout_ref, *rest):
    outs, (tall_conv, tall_grad, pre_ref, back_ref, slope_ref, total_ref) = rest[-6 - len(sent) : -6], rest[-6:]
    part, channels = conv_ref.shape[1:]
    wide = round_up(part, HALF)
    rows = tall_conv.shape[0] // wide
    owned = channels // count
    block = pre_ref.shape[2]
    steps = win_ref.shape[1] // block
    me = lax.axis_index("azimuth")
    def stack(tall, source):
        for row in range(rows):
            whole = part // 16 * 16
            tall[row * wide + whole : (row + 1) * wide, :] = jnp.zeros((wide - whole, channels), jnp.bfloat16)
            tall[row * wide : row * wide + part, :] = source[half * rows + row]

    group = 48
    groups = rows * wide // group

    def span(step):
        return slice(step * block, (step + 1) * block)

    def project_pre(step):
        pre_ref[step % 2] = dot_nn(tall_conv[...], win_ref[:, span(step)])

    def project_back(step):
        back_ref[step % 2] = dot_nt(tall_grad[...], wout_ref[span(step), :])

    def slope(step, first, last):
        root = math.sqrt(0.5)
        bias = bias_ref[span(step)].reshape(1, block) * root
        for g in range(first, last):
            some = slice(g * group, (g + 1) * group)
            value = back_ref[step % 2, some, :] * twice_gelu_slope(pre_ref[step % 2, some, :] * root + bias)
            slope_ref[some, span(step)] = value.astype(jnp.bfloat16)

    def gather(first, last):
        at = slice(first * block, last * block)
        term = dot_nt(win_ref[:, at], slope_ref[:, at])
        total_ref[...] = term if first == 0 else total_ref[...] + term

    stack(tall_conv, conv_ref)
    project_pre(0)
    stack(tall_grad, grad_ref)
    project_back(0)
    gathered = 0
    thirds = [groups * n // 3 for n in range(4)]
    for step in range(steps):
        if step + 1 < steps:
            project_pre(step + 1)
        slope(step, thirds[0], thirds[1])
        if step - gathered == 2:
            gather(gathered, step)
            gathered = step
        slope(step, thirds[1], thirds[2])
        if step + 1 < steps:
            project_back(step + 1)
        slope(step, thirds[2], thirds[3])
    gather(gathered, steps)
    for out, (k, start, size) in zip(outs, sent):
        target = partner(me, k, count, 1)
        for begin, width in chunks:
            if start <= begin < start + size:
                first = pl.multiple_of(count * begin + target * width, 32)
                value = 0.5 * total_ref[pl.ds(first, width), :]
                out[begin - start : begin - start + width, :] = value.astype(jnp.bfloat16)


def mlp(conv_out, grad_out, w_in, b_in, w_out, count, half, halves, sent, chunks, after):
    rows, part, channels = conv_out.shape
    rows //= halves
    block = 256
    wide = round_up(part, HALF)
    vmem = pl.BlockSpec(memory_space=VMEM)
    out_shape = [jax.ShapeDtypeStruct((size, rows * wide), jnp.bfloat16) for _, _, size in sent]
    return pl.pallas_call(
        functools.partial(mlp_kernel, count, half, sent, chunks),
        in_specs=[vmem] * 5 + [pl.BlockSpec(memory_space=pl.ANY)] * len(after),
        out_specs=[vmem] * len(out_shape),
        out_shape=out_shape,
        scratch_shapes=[
            pltpu.VMEM((rows * wide, channels), jnp.bfloat16),
            pltpu.VMEM((rows * wide, channels), jnp.bfloat16),
            pltpu.VMEM((2, rows * wide, block), jnp.float32),
            pltpu.VMEM((2, rows * wide, block), jnp.float32),
            pltpu.VMEM((rows * wide, w_in.shape[1]), jnp.bfloat16),
            pltpu.VMEM((channels, rows * wide), jnp.float32),
        ],
        compiler_params=pltpu.CompilerParams(vmem_limit_bytes=16 * 2**20),
        cost_estimate=NO_COST,
        name="mlp",
    )(conv_out, grad_out, w_in, b_in, w_out, *after)


def spectra_of(pieces, channels, table_ref, wide):
    size = channels[1]
    rows = pieces[0][0].shape[1] // wide
    window = table_ref.shape[1] - HALF
    shifts = [row * wide % LANES for row in range(rows)]
    spectra = [None] * rows
    for shift in sorted(set(shifts)):
        group = [row for row in range(rows) if shifts[row] == shift]
        total = None
        for k, (piece, base) in enumerate(pieces):
            windows = [row * wide // LANES * LANES for row in group]
            left = jnp.concatenate([piece[base : base + size, at : at + window] for at in windows], axis=0)
            term = dot_nn(left, table_ref[k, HALF - shift : HALF - shift + window, :])
            total = term if total is None else total + term
        for at, row in enumerate(group):
            spectra[row] = total[at * size : (at + 1) * size]
    return spectra


def early_kernel(count, wide, *refs):
    ranks = far_first(count, count)
    pieces = [(refs[ranks.index(k)], 0) for k in range(count)]
    table_ref, out_ref = refs[count], refs[-1]
    for row, spectrum in enumerate(spectra_of(pieces, (0, pieces[0][0].shape[0]), table_ref, wide)):
        out_ref[row] = spectrum


def analyze_early(pieces, table, wide):
    count = len(pieces)
    size, across = pieces[0].shape
    return pl.pallas_call(
        functools.partial(early_kernel, count, wide),
        in_specs=[pl.BlockSpec(memory_space=VMEM)] * (count + 1),
        out_specs=pl.BlockSpec(memory_space=VMEM),
        out_shape=jax.ShapeDtypeStruct((across // wide, size, table.shape[2]), jnp.float32),
        compiler_params=pltpu.CompilerParams(vmem_limit_bytes=12 * 2**20),
        cost_estimate=NO_COST,
        name="analysis_early",
    )(*(pieces[k] for k in far_first(count, count)), table)


def analysis_kernel(count, rows, wide, chunk, halves, *refs):
    own_ref, first_ref, second_ref = refs[-3:]
    start, size = chunk
    ranks = far_first(count, count)
    pieces = [(refs[ranks.index(k)], 0 if k else start) for k in range(count)]
    table_ref, early = refs[count], refs[count + 1 : count + halves]
    per = rows // halves
    even = lax.rem(lax.axis_index("polar"), 2) == 0
    for row, spectrum in enumerate(spectra_of(pieces, chunk, table_ref, wide)):
        own_ref[row] = spectrum

    def row_of(row):
        half, row = divmod(row, per)
        return own_ref[row] if half == halves - 1 else early[half][row, start : start + size, :]

    def share(above, below):
        for h in range(REACH):
            above[h] = row_of(rows - REACH + h).astype(jnp.bfloat16)
            below[h] = row_of(h).astype(jnp.bfloat16)

    pl.when(even)(lambda: share(first_ref, second_ref))
    pl.when(jnp.logical_not(even))(lambda: share(second_ref, first_ref))


def analyze(pieces, table, early, rows, wide, chunk, after):
    count = len(pieces)
    size = chunk[1]
    width = table.shape[2]
    halves = len(early) + 1
    halo = jax.ShapeDtypeStruct((REACH, size, width), jnp.bfloat16)
    return pl.pallas_call(
        functools.partial(analysis_kernel, count, rows, wide, chunk, halves),
        in_specs=[pl.BlockSpec(memory_space=VMEM)] * (count + halves)
        + [pl.BlockSpec(memory_space=pl.ANY)] * len(after),
        out_specs=[pl.BlockSpec(memory_space=VMEM)] * 3,
        out_shape=[jax.ShapeDtypeStruct((rows // halves, size, width), jnp.float32), halo, halo],
        compiler_params=pltpu.CompilerParams(vmem_limit_bytes=12 * 2**20),
        cost_estimate=NO_COST,
        name="analysis",
    )(*(pieces[k] for k in far_first(count, count)), table, *early, *after)


def add_row(accs, spectrum, weight, target_row, filter_row, targets):
    size = spectrum.shape[0]
    masked = jnp.concatenate([jnp.where(target_row == t, weight, 0.0) for t in targets], axis=0)
    gains = dot_nn(masked.astype(jnp.bfloat16), filter_row)
    whole = (gains.shape[1] // 2) // LANES * LANES - LANES
    spec_re = spectrum[:, :whole]
    spec_im = spectrum[:, whole : 2 * whole]
    spec_x = spectrum[:, 2 * whole :]
    swapped = pltpu.roll(spec_x, HALF, 1)
    for at, target in enumerate(targets):
        gain = gains[at * size : (at + 1) * size]
        gain_re = gain[:, :whole]
        gain_rx = gain[:, whole : whole + LANES]
        gain_im = gain[:, whole + LANES : 2 * whole + LANES]
        gain_ix = gain[:, 2 * whole + LANES :]
        acc_re, acc_im, acc_x = accs[target]
        acc_re = acc_re + (gain_re * spec_re + gain_im * spec_im)
        acc_im = acc_im + (gain_re * spec_im - gain_im * spec_re)
        acc_x = acc_x + (gain_rx * spec_x + gain_ix * swapped)
        accs[target] = acc_re, acc_im, acc_x


def split_tiles(value):
    whole = (value.shape[1] - LANES) // 2
    return value[:, :whole], value[:, whole : 2 * whole], value[:, 2 * whole :]


def own_kernel(start, own_ref, weight_ref, target_ref, filter_ref, *rest):
    early, out_ref = rest[:-1], rest[-1]
    rows, size, width = out_ref.shape
    per = own_ref.shape[0]
    accs = {t: split_tiles(jnp.zeros((size, width), jnp.float32)) for t in range(rows)}
    for row in range(rows):
        at = row + REACH
        targets = [t for t in range(rows) if abs(row - t) <= REACH]
        half = row // per
        spectrum = early[half][row % per, start : start + size, :] if half < len(early) else own_ref[row % per]
        add_row(accs, spectrum, weight_ref[...], target_ref[at : at + 1, :], filter_ref[at], targets)
    for t in range(rows):
        out_ref[t] = jnp.concatenate(accs[t], axis=1)


def own_terms(own, early, start, weight, target, filters):
    per, size, width = own.shape
    return pl.pallas_call(
        functools.partial(own_kernel, start),
        in_specs=[pl.BlockSpec(memory_space=VMEM)] * (4 + len(early)),
        out_specs=pl.BlockSpec(memory_space=VMEM),
        out_shape=jax.ShapeDtypeStruct((per * (1 + len(early)), size, width), jnp.float32),
        compiler_params=pltpu.CompilerParams(vmem_limit_bytes=12 * 2**20),
        cost_estimate=NO_COST,
        name="own_terms",
    )(own, weight, target, filters, *early)


def add_halo(accs, sides, rows, weight_ref, target_ref, filter_ref):
    for side, base in sides:
        for h in range(REACH):
            at = base + h + REACH
            targets = [t for t in range(rows) if abs(base + h - t) <= REACH]
            add_row(
                accs,
                side[h].astype(jnp.float32),
                weight_ref[...],
                target_ref[at : at + 1, :],
                filter_ref[at],
                targets,
            )


def side_kernel(part_ref, first_ref, weight_ref, target_ref, filter_ref, *rest):
    out_ref = rest[-1]
    rows = part_ref.shape[0]
    even = lax.rem(lax.axis_index("polar"), 2) == 0

    def combine(base):
        accs = {t: split_tiles(part_ref[t]) for t in range(rows)}
        add_halo(accs, [(first_ref, base)], rows, weight_ref, target_ref, filter_ref)
        for t in range(rows):
            out_ref[t] = jnp.concatenate(accs[t], axis=1)

    pl.when(even)(lambda: combine(rows))
    pl.when(jnp.logical_not(even))(lambda: combine(-REACH))


def side_terms(own, first, weight, target, filters, after):
    return pl.pallas_call(
        side_kernel,
        in_specs=[pl.BlockSpec(memory_space=VMEM)] * 5 + [pl.BlockSpec(memory_space=pl.ANY)] * len(after),
        out_specs=pl.BlockSpec(memory_space=VMEM),
        out_shape=jax.ShapeDtypeStruct(own.shape, jnp.float32),
        compiler_params=pltpu.CompilerParams(vmem_limit_bytes=12 * 2**20),
        cost_estimate=NO_COST,
        name="side_terms",
    )(own, first, weight, target, filters, *after)


def finish_kernel(count, swaps, part_ref, *refs):
    halos, (weight_ref, target_ref, filter_ref, table_ref) = refs[:swaps], refs[swaps : swaps + 4]
    outs, stacked_ref = refs[-count - 1 : -1], refs[-1]
    rows, size, width = part_ref.shape
    even = lax.rem(lax.axis_index("polar"), 2) == 0

    def combine(bases):
        accs = {t: split_tiles(part_ref[t]) for t in range(rows)}
        sides = list(zip(halos, bases[-swaps:]))
        add_halo(accs, sides, rows, weight_ref, target_ref, filter_ref)
        for t in range(rows):
            stacked_ref[t * size : (t + 1) * size, :] = jnp.concatenate(accs[t], axis=1).astype(jnp.bfloat16)

    pl.when(even)(lambda: combine((rows, -REACH)))
    pl.when(jnp.logical_not(even))(lambda: combine((-REACH, rows)))
    grid = dot_nt(table_ref[...], stacked_ref[...])
    wide = grid.shape[0] // count
    for k, out in enumerate(outs):
        out[...] = grid[k * wide : k * wide + out.shape[0]].astype(jnp.bfloat16)


def finish(own, halos, weight, target, filters, table, count, part):
    rows, size, width = own.shape
    return pl.pallas_call(
        functools.partial(finish_kernel, count, len(halos)),
        in_specs=[pl.BlockSpec(memory_space=VMEM)] * (5 + len(halos)),
        out_specs=[pl.BlockSpec(memory_space=VMEM)] * count,
        out_shape=[jax.ShapeDtypeStruct((part, rows * size), jnp.bfloat16)] * count,
        scratch_shapes=[pltpu.VMEM((rows * size, width), jnp.bfloat16)],
        compiler_params=pltpu.CompilerParams(vmem_limit_bytes=12 * 2**20),
        cost_estimate=NO_COST,
        name="finish",
    )(own, *halos, weight, target, filters, table)


def add_kernel(count, chunk, steps, tiles, grad_ref, *refs):
    out_ref, tall_ref, done_ref, sems = refs[-4:]
    pieces = dict(zip(steps, refs))
    _, part, rows, _ = done_ref.shape
    start, size = chunk
    me = lax.axis_index("azimuth")

    def add(mine):
        order = [[k for k in range(count) if partner_static(mine, k, count, -1) == s][0] for s in range(count)]
        copies = []
        for at, tile in enumerate(tiles[mine]):
            lanes = range(tile * LANES, (tile + 1) * LANES)
            first = count * start + tile * LANES
            for row in range(rows):
                parts = []
                for s in owners(tile, size):
                    low, high = max(lanes[0], s * size) - s * size, min(lanes[-1] + 1, (s + 1) * size) - s * size
                    parts.append(pieces[order[s]][:, row * size + low : row * size + high])
                conv = jnp.concatenate(parts, axis=1).astype(jnp.float32)
                total = grad_ref[row, :, first : first + LANES].astype(jnp.float32) + conv
                tall_ref[at, pl.ds(row, part, stride=rows), :] = total
            done_ref[at] = tall_ref[at].reshape(part, rows, LANES).astype(jnp.bfloat16)
            copies.append(pltpu.make_async_copy(done_ref.at[at], out_ref.at[:, :, pl.ds(first, LANES)], sems.at[at]))
            copies[-1].start()
        for copy in copies:
            copy.wait()

    for mine in range(count):
        pl.when(me == mine)(functools.partial(add, mine))


def owners(tile, size):
    return range(tile * LANES // size, ((tile + 1) * LANES - 1) // size + 1)


def add_chunk(grad_out, pieces, chunk, count, tiles, before):
    rows, part, channels = grad_out.shape
    number = max(len(some) for some in tiles)
    needed = {
        k
        for mine in range(count)
        for tile in tiles[mine]
        for s in owners(tile, chunk[1])
        for k in range(count)
        if partner_static(mine, k, count, -1) == s
    }
    pieces = sorted(((k, pieces[k]) for k in needed), key=lambda item: item[0] <= NEAR)
    vmem = pl.BlockSpec(memory_space=VMEM)
    anywhere = pl.BlockSpec(memory_space=pl.ANY)
    return pl.pallas_call(
        functools.partial(add_kernel, count, chunk, [k for k, _ in pieces], tiles),
        in_specs=[vmem] * (1 + len(pieces)) + [anywhere] * len(before),
        out_specs=anywhere,
        out_shape=jax.ShapeDtypeStruct((part, rows, channels), jnp.bfloat16),
        scratch_shapes=[
            pltpu.VMEM((number, rows * part, LANES), jnp.float32),
            pltpu.VMEM((number, part, rows, LANES), jnp.bfloat16),
            pltpu.SemaphoreType.DMA((number,)),
        ],
        input_output_aliases={1 + len(pieces): 0} if before else {},
        compiler_params=pltpu.CompilerParams(vmem_limit_bytes=12 * 2**20),
        cost_estimate=NO_COST,
        name="add_chunk",
    )(grad_out, *(block for _, block in pieces), *before)


def prepare_kernel(count, chunks, weight_ref, filt_ref, offset_ref, forth_ref, back_ref, *outs):
    filter_out, target_out, forth_out, back_out = outs[:4]
    me = lax.axis_index("azimuth")
    wide = back_ref.shape[0] // count
    for k in range(count):
        forth_out[k] = forth_ref[partner(me, k, count, -1)]
        first = pl.multiple_of(partner(me, k, count, 1) * wide, HALF)
        back_out[k * wide : (k + 1) * wide, :] = back_ref[pl.ds(first, wide), :]
    bases, channels = weight_ref.shape
    lats, width = filt_ref.shape[1:]
    ext, depth = target_out.shape
    rows = ext - 2 * REACH
    modes = width // 2
    whole = modes // LANES * LANES
    used = TERMS * bases
    for (start, size), out in zip(chunks, outs[4:]):
        first = count * start + lax.axis_index("azimuth") * size
        weight = pltpu.roll(weight_ref[...], lax.rem(channels - first, channels), 1)[:, :size]
        parts = []
        for _ in range(TERMS):
            rounded = weight.astype(jnp.bfloat16).astype(jnp.float32)
            parts.append(rounded)
            weight = weight - rounded
        parts.append(jnp.zeros((depth - used, size), jnp.float32))
        out[...] = jnp.concatenate(parts, axis=0).T
    start_lat = lax.axis_index("polar") * rows
    table = filt_ref[...].reshape(bases * lats, width)
    base = lax.broadcasted_iota(jnp.int32, (depth, bases * lats), 0)
    valid = base < used
    for _ in range(TERMS - 1):
        base = jnp.where(base >= bases, base - bases, base)
    column = lax.broadcasted_iota(jnp.int32, (depth, bases * lats), 1)
    for i in range(ext):
        lat = start_lat + (i - REACH)
        inside = (lat >= 0) & (lat < lats)
        lat = jnp.clip(lat, 0, lats - 1)
        pick = jnp.where(valid & (column == base * lats + lat), 1.0, 0.0).astype(jnp.bfloat16)
        row = dot_nn(pick, table)
        real, imag = row[:, :modes], row[:, modes:]
        rest_re, rest_im = real[:, whole:], imag[:, whole:]
        filter_out[i] = jnp.concatenate(
            [real[:, :whole], rest_re, rest_re, imag[:, :whole], rest_im, -rest_im], axis=1
        ).astype(jnp.bfloat16)
        local = jnp.where(inside, offset_ref[pl.ds(lat, 1), :] - start_lat, -1)
        spare = jnp.full((1, depth - used), -1, jnp.int32)
        target_out[i : i + 1, :] = jnp.concatenate([local] * TERMS + [spare], axis=1)


def prepare(basis_weight, filt, offsets, forth, back, rows, count, chunks):
    bases = filt.shape[0]
    width = filt.shape[2]
    ext = rows + 2 * REACH
    depth = round_up(TERMS * bases, 16)
    shapes = [
        jax.ShapeDtypeStruct((ext, depth, width + LANES), jnp.bfloat16),
        jax.ShapeDtypeStruct((ext, depth), jnp.int32),
        jax.ShapeDtypeStruct(forth.shape, forth.dtype),
        jax.ShapeDtypeStruct(back.shape, back.dtype),
    ] + [jax.ShapeDtypeStruct((size, depth), jnp.float32) for _, size in chunks]
    return pl.pallas_call(
        functools.partial(prepare_kernel, count, chunks),
        in_specs=[pl.BlockSpec(memory_space=VMEM)] * 5,
        out_specs=[pl.BlockSpec(memory_space=VMEM)] * len(shapes),
        out_shape=shapes,
        compiler_params=pltpu.CompilerParams(vmem_limit_bytes=16 * 2**20),
        cost_estimate=NO_COST,
        name="prepare",
    )(basis_weight, filt, offsets, forth, back)


def halo(first, second):
    bands, count = lax.axis_size("polar"), lax.axis_size("azimuth")
    blocks = []
    for odd, block in ((0, first), (1, second)):
        pairs = []
        for a in range(bands):
            other = ((a + odd) ^ 1) - odd
            for b in range(count):
                paired = 0 <= other < bands
                target = (other, b) if paired else (a, b ^ 1 if b ^ 1 < count else b)
                pairs.append((a * count + b, target[0] * count + target[1]))
        blocks.append(lax.ppermute(block, ("polar", "azimuth"), pairs))
    return blocks


def on_device(chunks, conv_out, grad_out, w_in, b_in, w_out, basis_weight, filt, offsets):
    rows, part, channels = conv_out.shape
    count = lax.axis_size("azimuth")
    forth, back = tables(count, part, filt.shape[2] // 2)
    forth, back = jnp.asarray(forth), jnp.asarray(back)
    owned = channels // count
    halves = 2 if rows % 2 == 0 else 1
    wide = round_up(part, HALF)
    filters, target, forth, back, *weights = prepare(
        basis_weight, filt, offsets, forth, back, rows, count, chunks
    )
    early, order = [], []
    for half in range(halves):
        final = half == halves - 1
        sent = [(k, 0, owned) for k in range(count)]
        if final:
            sent[1:] = [(k,) + chunk for chunk in chunks for k in range(1, count)]
        blocks = mlp(conv_out, grad_out, w_in, b_in, w_out, count, half, halves, sent, chunks, order)
        order = blocks[:1]
        if not final:
            early.append(analyze_early([exchange(blocks[k], k, count) for k in range(count)], forth, wide))
    spectra, terms, returned = {}, {}, {}
    for q, (start, size) in enumerate(chunks):
        mine = blocks[1 + q * (count - 1) : 1 + (q + 1) * (count - 1)]
        pieces = [blocks[0]] + [exchange(block, k, count) for k, block in enumerate(mine, 1)]
        after = [terms[q - 1]] if q else []
        own, first, second = analyze(pieces, forth, early, rows, wide, (start, size), after)
        spectra[q] = halo(first, second)
        terms[q] = own_terms(own, early, start, weights[q], target, filters)
    for q in range(len(chunks)):
        halos = spectra[q]
        if q == 0:
            others = [terms[other] for other in terms if other > q]
            terms[q] = side_terms(terms[q], halos[0], weights[q], target, filters, others)
            halos = halos[1:]
        grids = finish(terms[q], halos, weights[q], target, filters, back, count, part)
        returned[q] = {k: exchange(grids[k], k, count) for k in range(count)}
    total = []
    for q, chunk in enumerate(chunks):
        tiles = [list(range(count * chunk[1] // LANES)) for _ in range(count)]
        if q == len(chunks) - 1:
            chip = [{mine, partner_static(mine, NEAR, count, -1)} for mine in range(count)]
            close = [[t for t in tiles[mine] if set(owners(t, chunk[1])) <= chip[mine]] for mine in range(count)]
            if any(close):
                total = [add_chunk(grad_out, returned[q], chunk, count, close, total)]
                tiles = [[t for t in tiles[mine] if t not in close[mine]] for mine in range(count)]
        total = [add_chunk(grad_out, returned[q], chunk, count, tiles, total)]
    return jnp.transpose(total[0], (1, 0, 2))


def solution(mesh):
    grid = P(("member", "polar"), "azimuth", None)

    def run(conv_out, grad_out, *others):
        owned = conv_out.shape[2] // mesh.shape["azimuth"]
        sizes = [owned]
        if owned % 32 == 0 and owned >= 96:
            big = owned * 3 // 5 // 32 * 32
            sizes = [big, owned - big]
        chunks = tuple((sum(sizes[:q]), size) for q, size in enumerate(sizes))
        return jax.shard_map(
            functools.partial(on_device, chunks),
            mesh=mesh,
            in_specs=(grid, grid) + (P(),) * 6,
            out_specs=grid,
            check_vma=False,
        )(conv_out, grad_out, *others)

    return run
```

```python
import functools
import math

import jax
import jax.numpy as jnp
import ml_dtypes
import numpy as np
from jax import lax
from jax.experimental import pallas as pl
from jax.experimental.pallas import tpu as pltpu
from jax.sharding import PartitionSpec as P

REACH = 3
LANES = 128
HALF = 64
TERMS = 3
NEAR = 1
VMEM = pltpu.MemorySpace.VMEM
NO_COST = pl.CostEstimate(flops=0, bytes_accessed=0, transcendentals=0)


def round_up(value, unit):
    return -(-value // unit) * unit


def partner(me, step, count, sign):
    if count & (count - 1) == 0:
        return me ^ step
    return lax.rem(me + sign * step + count, count)


def far_first(number, count):
    return sorted(range(number), key=lambda i: (i // count, i % count <= NEAR))


def exchange(block, step, count):
    if step == 0:
        return block
    pairs = [(a, int(partner_static(a, step, count))) for a in range(count)]
    return lax.ppermute(block, "azimuth", pairs)


def partner_static(a, step, count, sign=1):
    return a ^ step if count & (count - 1) == 0 else (a + sign * step) % count


def tables(count, part, modes):
    length = count * part
    whole = modes // LANES * LANES
    order = np.concatenate(
        [
            np.arange(whole),
            modes + np.arange(whole),
            np.arange(whole, modes),
            modes + np.arange(whole, modes),
        ]
    )
    positions = np.arange(length)
    waves = np.arange(modes)
    phase = (positions[:, None] * waves[None, :]) % length
    angle = (2.0 * math.pi / length) * phase
    scale = 1.0 / math.sqrt(length)
    factor = np.where(waves == 0, 1.0, 2.0)
    analysis = np.concatenate([np.cos(angle), -np.sin(angle)], axis=1) * scale
    synth = np.concatenate([np.cos(angle) * factor, -np.sin(angle) * factor], axis=1) * scale
    analysis = analysis.astype(np.float32).astype(ml_dtypes.bfloat16)[:, order]
    synth = synth.astype(np.float32).astype(ml_dtypes.bfloat16)[:, order]
    wide = round_up(part, HALF)
    window = round_up(HALF + wide, LANES)
    forth = np.zeros((count, HALF + window, 2 * modes), ml_dtypes.bfloat16)
    back = np.zeros((count * wide, 2 * modes), ml_dtypes.bfloat16)
    for s in range(count):
        forth[s, HALF : HALF + part] = analysis[s * part : (s + 1) * part]
        back[s * wide : s * wide + part] = synth[s * part : (s + 1) * part]
    return forth, back


def twice_gelu_slope(scaled):
    power = math.log2(2.0 / math.sqrt(math.pi)) - (1.0 / math.log(2.0)) * (scaled * scaled)
    return (1.0 + lax.erf(scaled)) + scaled * jnp.exp2(power)


def dot_nt(left, right):
    return lax.dot_general(left, right, (((1,), (1,)), ((), ())), preferred_element_type=jnp.float32)


def dot_nn(left, right):
    return jnp.dot(left, right, preferred_element_type=jnp.float32)


def mlp_kernel(count, half, sent, chunks, conv_ref, grad_ref, win_ref, bias_ref, wout_ref, *rest):
    outs, (tall_conv, tall_grad, pre_ref, back_ref, slope_ref, total_ref) = rest[-6 - len(sent) : -6], rest[-6:]
    part, channels = conv_ref.shape[1:]
    wide = round_up(part, HALF)
    rows = tall_conv.shape[0] // wide
    owned = channels // count
    block = pre_ref.shape[2]
    steps = win_ref.shape[1] // block
    me = lax.axis_index("azimuth")
    def stack(tall, source):
        for row in range(rows):
            whole = part // 16 * 16
            tall[row * wide + whole : (row + 1) * wide, :] = jnp.zeros((wide - whole, channels), jnp.bfloat16)
            tall[row * wide : row * wide + part, :] = source[half * rows + row]

    group = 32
    groups = rows * wide // group

    def span(step):
        return slice(step * block, (step + 1) * block)

    def project_pre(step):
        pre_ref[step % 2] = dot_nn(tall_conv[...], win_ref[:, span(step)])

    def project_back(step):
        back_ref[step % 2] = dot_nt(tall_grad[...], wout_ref[span(step), :])

    def slope(step, first, last):
        root = math.sqrt(0.5)
        bias = bias_ref[span(step)].reshape(1, block) * root
        for g in range(first, last):
            some = slice(g * group, (g + 1) * group)
            value = back_ref[step % 2, some, :] * twice_gelu_slope(pre_ref[step % 2, some, :] * root + bias)
            slope_ref[some, span(step)] = value.astype(jnp.bfloat16)

    def gather(first, last, part):
        at = slice(first * block, last * block)
        some = slice(part * channels // 2, (part + 1) * channels // 2)
        term = dot_nt(win_ref[some, at], slope_ref[:, at])
        total_ref[some] = term if first == 0 else total_ref[some] + term

    stack(tall_conv, conv_ref)
    project_pre(0)
    stack(tall_grad, grad_ref)
    project_back(0)
    gathered = 0
    ends = [groups * n // 4 for n in range(5)]
    for step in range(steps):
        ready = step - gathered == 2
        if step + 1 < steps:
            project_pre(step + 1)
        slope(step, ends[0], ends[1])
        if ready:
            gather(gathered, step, 0)
        slope(step, ends[1], ends[2])
        if ready:
            gather(gathered, step, 1)
            gathered = step
        slope(step, ends[2], ends[3])
        if step + 1 < steps:
            project_back(step + 1)
        slope(step, ends[3], ends[4])
    for part_at in range(2):
        gather(gathered, steps, part_at)
    for out, (k, start, size) in zip(outs, sent):
        target = partner(me, k, count, 1)
        for begin, width in chunks:
            if start <= begin < start + size:
                first = pl.multiple_of(count * begin + target * width, 32)
                value = 0.5 * total_ref[pl.ds(first, width), :]
                out[begin - start : begin - start + width, :] = value.astype(jnp.bfloat16)


def mlp(conv_out, grad_out, w_in, b_in, w_out, count, half, halves, sent, chunks, after):
    rows, part, channels = conv_out.shape
    rows //= halves
    block = 256
    wide = round_up(part, HALF)
    vmem = pl.BlockSpec(memory_space=VMEM)
    out_shape = [jax.ShapeDtypeStruct((size, rows * wide), jnp.bfloat16) for _, _, size in sent]
    return pl.pallas_call(
        functools.partial(mlp_kernel, count, half, sent, chunks),
        in_specs=[vmem] * 5 + [pl.BlockSpec(memory_space=pl.ANY)] * len(after),
        out_specs=[vmem] * len(out_shape),
        out_shape=out_shape,
        scratch_shapes=[
            pltpu.VMEM((rows * wide, channels), jnp.bfloat16),
            pltpu.VMEM((rows * wide, channels), jnp.bfloat16),
            pltpu.VMEM((2, rows * wide, block), jnp.float32),
            pltpu.VMEM((2, rows * wide, block), jnp.float32),
            pltpu.VMEM((rows * wide, w_in.shape[1]), jnp.bfloat16),
            pltpu.VMEM((channels, rows * wide), jnp.float32),
        ],
        compiler_params=pltpu.CompilerParams(vmem_limit_bytes=16 * 2**20),
        cost_estimate=NO_COST,
        name="mlp",
    )(conv_out, grad_out, w_in, b_in, w_out, *after)


def spectra_of(pieces, channels, table_ref, wide):
    size = channels[1]
    rows = pieces[0][0].shape[1] // wide
    window = table_ref.shape[1] - HALF
    shifts = [row * wide % LANES for row in range(rows)]
    spectra = [None] * rows
    for shift in sorted(set(shifts)):
        group = [row for row in range(rows) if shifts[row] == shift]
        total = None
        for k, (piece, base) in enumerate(pieces):
            windows = [row * wide // LANES * LANES for row in group]
            left = jnp.concatenate([piece[base : base + size, at : at + window] for at in windows], axis=0)
            term = dot_nn(left, table_ref[k, HALF - shift : HALF - shift + window, :])
            total = term if total is None else total + term
        for at, row in enumerate(group):
            spectra[row] = total[at * size : (at + 1) * size]
    return spectra


def early_kernel(count, wide, *refs):
    ranks = far_first(count, count)
    pieces = [(refs[ranks.index(k)], 0) for k in range(count)]
    table_ref, out_ref = refs[count], refs[-1]
    for row, spectrum in enumerate(spectra_of(pieces, (0, pieces[0][0].shape[0]), table_ref, wide)):
        out_ref[row] = spectrum


def analyze_early(pieces, table, wide):
    count = len(pieces)
    size, across = pieces[0].shape
    return pl.pallas_call(
        functools.partial(early_kernel, count, wide),
        in_specs=[pl.BlockSpec(memory_space=VMEM)] * (count + 1),
        out_specs=pl.BlockSpec(memory_space=VMEM),
        out_shape=jax.ShapeDtypeStruct((across // wide, size, table.shape[2]), jnp.float32),
        compiler_params=pltpu.CompilerParams(vmem_limit_bytes=12 * 2**20),
        cost_estimate=NO_COST,
        name="analysis_early",
    )(*(pieces[k] for k in far_first(count, count)), table)


def analysis_kernel(count, rows, wide, chunk, halves, *refs):
    own_ref, first_ref, second_ref = refs[-3:]
    start, size = chunk
    ranks = far_first(count, count)
    pieces = [(refs[ranks.index(k)], 0 if k else start) for k in range(count)]
    table_ref, early = refs[count], refs[count + 1 : count + halves]
    per = rows // halves
    even = lax.rem(lax.axis_index("polar"), 2) == 0
    for row, spectrum in enumerate(spectra_of(pieces, chunk, table_ref, wide)):
        own_ref[row] = spectrum

    def row_of(row):
        half, row = divmod(row, per)
        return own_ref[row] if half == halves - 1 else early[half][row, start : start + size, :]

    def share(above, below):
        for h in range(REACH):
            above[h] = row_of(rows - REACH + h).astype(jnp.bfloat16)
            below[h] = row_of(h).astype(jnp.bfloat16)

    pl.when(even)(lambda: share(first_ref, second_ref))
    pl.when(jnp.logical_not(even))(lambda: share(second_ref, first_ref))


def analyze(pieces, table, early, rows, wide, chunk, after):
    count = len(pieces)
    size = chunk[1]
    width = table.shape[2]
    halves = len(early) + 1
    halo = jax.ShapeDtypeStruct((REACH, size, width), jnp.bfloat16)
    return pl.pallas_call(
        functools.partial(analysis_kernel, count, rows, wide, chunk, halves),
        in_specs=[pl.BlockSpec(memory_space=VMEM)] * (count + halves)
        + [pl.BlockSpec(memory_space=pl.ANY)] * len(after),
        out_specs=[pl.BlockSpec(memory_space=VMEM)] * 3,
        out_shape=[jax.ShapeDtypeStruct((rows // halves, size, width), jnp.float32), halo, halo],
        compiler_params=pltpu.CompilerParams(vmem_limit_bytes=12 * 2**20),
        cost_estimate=NO_COST,
        name="analysis",
    )(*(pieces[k] for k in far_first(count, count)), table, *early, *after)


def add_row(accs, spectrum, weight, target_row, filter_row, targets):
    size = spectrum.shape[0]
    masked = jnp.concatenate([jnp.where(target_row == t, weight, 0.0) for t in targets], axis=0)
    gains = dot_nn(masked.astype(jnp.bfloat16), filter_row)
    whole = (gains.shape[1] // 2) // LANES * LANES - LANES
    spec_re = spectrum[:, :whole]
    spec_im = spectrum[:, whole : 2 * whole]
    spec_x = spectrum[:, 2 * whole :]
    swapped = pltpu.roll(spec_x, HALF, 1)
    for at, target in enumerate(targets):
        gain = gains[at * size : (at + 1) * size]
        gain_re = gain[:, :whole]
        gain_rx = gain[:, whole : whole + LANES]
        gain_im = gain[:, whole + LANES : 2 * whole + LANES]
        gain_ix = gain[:, 2 * whole + LANES :]
        acc_re, acc_im, acc_x = accs[target]
        acc_re = acc_re + (gain_re * spec_re + gain_im * spec_im)
        acc_im = acc_im + (gain_re * spec_im - gain_im * spec_re)
        acc_x = acc_x + (gain_rx * spec_x + gain_ix * swapped)
        accs[target] = acc_re, acc_im, acc_x


def split_tiles(value):
    whole = (value.shape[1] - LANES) // 2
    return value[:, :whole], value[:, whole : 2 * whole], value[:, 2 * whole :]


def own_kernel(start, own_ref, weight_ref, target_ref, filter_ref, *rest):
    early, out_ref = rest[:-1], rest[-1]
    rows, size, width = out_ref.shape
    per = own_ref.shape[0]
    accs = {t: split_tiles(jnp.zeros((size, width), jnp.float32)) for t in range(rows)}
    for row in range(rows):
        at = row + REACH
        targets = [t for t in range(rows) if abs(row - t) <= REACH]
        half = row // per
        spectrum = early[half][row % per, start : start + size, :] if half < len(early) else own_ref[row % per]
        add_row(accs, spectrum, weight_ref[...], target_ref[at : at + 1, :], filter_ref[at], targets)
    for t in range(rows):
        out_ref[t] = jnp.concatenate(accs[t], axis=1)


def own_terms(own, early, start, weight, target, filters):
    per, size, width = own.shape
    return pl.pallas_call(
        functools.partial(own_kernel, start),
        in_specs=[pl.BlockSpec(memory_space=VMEM)] * (4 + len(early)),
        out_specs=pl.BlockSpec(memory_space=VMEM),
        out_shape=jax.ShapeDtypeStruct((per * (1 + len(early)), size, width), jnp.float32),
        compiler_params=pltpu.CompilerParams(vmem_limit_bytes=12 * 2**20),
        cost_estimate=NO_COST,
        name="own_terms",
    )(own, weight, target, filters, *early)


def add_halo(accs, sides, rows, weight_ref, target_ref, filter_ref):
    for side, base in sides:
        for h in range(REACH):
            at = base + h + REACH
            targets = [t for t in range(rows) if abs(base + h - t) <= REACH]
            add_row(
                accs,
                side[h].astype(jnp.float32),
                weight_ref[...],
                target_ref[at : at + 1, :],
                filter_ref[at],
                targets,
            )


def side_kernel(part_ref, first_ref, weight_ref, target_ref, filter_ref, *rest):
    out_ref = rest[-1]
    rows = part_ref.shape[0]
    even = lax.rem(lax.axis_index("polar"), 2) == 0

    def combine(base):
        accs = {t: split_tiles(part_ref[t]) for t in range(rows)}
        add_halo(accs, [(first_ref, base)], rows, weight_ref, target_ref, filter_ref)
        for t in range(rows):
            out_ref[t] = jnp.concatenate(accs[t], axis=1)

    pl.when(even)(lambda: combine(rows))
    pl.when(jnp.logical_not(even))(lambda: combine(-REACH))


def side_terms(own, first, weight, target, filters, after):
    return pl.pallas_call(
        side_kernel,
        in_specs=[pl.BlockSpec(memory_space=VMEM)] * 5 + [pl.BlockSpec(memory_space=pl.ANY)] * len(after),
        out_specs=pl.BlockSpec(memory_space=VMEM),
        out_shape=jax.ShapeDtypeStruct(own.shape, jnp.float32),
        compiler_params=pltpu.CompilerParams(vmem_limit_bytes=12 * 2**20),
        cost_estimate=NO_COST,
        name="side_terms",
    )(own, first, weight, target, filters, *after)


def finish_kernel(count, swaps, part_ref, *refs):
    halos, (weight_ref, target_ref, filter_ref, table_ref) = refs[:swaps], refs[swaps : swaps + 4]
    outs, stacked_ref = refs[-count - 1 : -1], refs[-1]
    rows, size, width = part_ref.shape
    even = lax.rem(lax.axis_index("polar"), 2) == 0

    def combine(bases):
        accs = {t: split_tiles(part_ref[t]) for t in range(rows)}
        sides = list(zip(halos, bases[-swaps:]))
        add_halo(accs, sides, rows, weight_ref, target_ref, filter_ref)
        for t in range(rows):
            stacked_ref[t * size : (t + 1) * size, :] = jnp.concatenate(accs[t], axis=1).astype(jnp.bfloat16)

    pl.when(even)(lambda: combine((rows, -REACH)))
    pl.when(jnp.logical_not(even))(lambda: combine((-REACH, rows)))
    grid = dot_nt(table_ref[...], stacked_ref[...])
    wide = grid.shape[0] // count
    for k, out in enumerate(outs):
        out[...] = grid[k * wide : k * wide + out.shape[0]].astype(jnp.bfloat16)


def finish(own, halos, weight, target, filters, table, count, part):
    rows, size, width = own.shape
    return pl.pallas_call(
        functools.partial(finish_kernel, count, len(halos)),
        in_specs=[pl.BlockSpec(memory_space=VMEM)] * (5 + len(halos)),
        out_specs=[pl.BlockSpec(memory_space=VMEM)] * count,
        out_shape=[jax.ShapeDtypeStruct((part, rows * size), jnp.bfloat16)] * count,
        scratch_shapes=[pltpu.VMEM((rows * size, width), jnp.bfloat16)],
        compiler_params=pltpu.CompilerParams(vmem_limit_bytes=12 * 2**20),
        cost_estimate=NO_COST,
        name="finish",
    )(own, *halos, weight, target, filters, table)


def add_kernel(count, chunk, steps, tiles, grad_ref, *refs):
    out_ref, tall_ref, done_ref, sems = refs[-4:]
    pieces = dict(zip(steps, refs))
    _, part, rows, _ = done_ref.shape
    start, size = chunk
    me = lax.axis_index("azimuth")

    def add(mine):
        order = [[k for k in range(count) if partner_static(mine, k, count, -1) == s][0] for s in range(count)]
        copies = []
        for at, tile in enumerate(tiles[mine]):
            lanes = range(tile * LANES, (tile + 1) * LANES)
            first = count * start + tile * LANES
            for row in range(rows):
                parts = []
                for s in owners(tile, size):
                    low, high = max(lanes[0], s * size) - s * size, min(lanes[-1] + 1, (s + 1) * size) - s * size
                    parts.append(pieces[order[s]][:, row * size + low : row * size + high])
                conv = jnp.concatenate(parts, axis=1).astype(jnp.float32)
                total = grad_ref[row, :, first : first + LANES].astype(jnp.float32) + conv
                tall_ref[at, pl.ds(row, part, stride=rows), :] = total
            done_ref[at] = tall_ref[at].reshape(part, rows, LANES).astype(jnp.bfloat16)
            copies.append(pltpu.make_async_copy(done_ref.at[at], out_ref.at[:, :, pl.ds(first, LANES)], sems.at[at]))
            copies[-1].start()
        for copy in copies:
            copy.wait()

    for mine in range(count):
        pl.when(me == mine)(functools.partial(add, mine))


def owners(tile, size):
    return range(tile * LANES // size, ((tile + 1) * LANES - 1) // size + 1)


def add_chunk(grad_out, pieces, chunk, count, tiles, before):
    rows, part, channels = grad_out.shape
    number = max(len(some) for some in tiles)
    needed = {
        k
        for mine in range(count)
        for tile in tiles[mine]
        for s in owners(tile, chunk[1])
        for k in range(count)
        if partner_static(mine, k, count, -1) == s
    }
    pieces = sorted(((k, pieces[k]) for k in needed), key=lambda item: item[0] <= NEAR)
    vmem = pl.BlockSpec(memory_space=VMEM)
    anywhere = pl.BlockSpec(memory_space=pl.ANY)
    return pl.pallas_call(
        functools.partial(add_kernel, count, chunk, [k for k, _ in pieces], tiles),
        in_specs=[vmem] * (1 + len(pieces)) + [anywhere] * len(before),
        out_specs=anywhere,
        out_shape=jax.ShapeDtypeStruct((part, rows, channels), jnp.bfloat16),
        scratch_shapes=[
            pltpu.VMEM((number, rows * part, LANES), jnp.float32),
            pltpu.VMEM((number, part, rows, LANES), jnp.bfloat16),
            pltpu.SemaphoreType.DMA((number,)),
        ],
        input_output_aliases={1 + len(pieces): 0} if before else {},
        compiler_params=pltpu.CompilerParams(vmem_limit_bytes=12 * 2**20),
        cost_estimate=NO_COST,
        name="add_chunk",
    )(grad_out, *(block for _, block in pieces), *before)


def prepare_kernel(count, chunks, weight_ref, filt_ref, offset_ref, forth_ref, back_ref, *outs):
    filter_out, target_out, forth_out, back_out = outs[:4]
    me = lax.axis_index("azimuth")
    wide = back_ref.shape[0] // count
    for k in range(count):
        forth_out[k] = forth_ref[partner(me, k, count, -1)]
        first = pl.multiple_of(partner(me, k, count, 1) * wide, HALF)
        back_out[k * wide : (k + 1) * wide, :] = back_ref[pl.ds(first, wide), :]
    bases, channels = weight_ref.shape
    lats, width = filt_ref.shape[1:]
    ext, depth = target_out.shape
    rows = ext - 2 * REACH
    modes = width // 2
    whole = modes // LANES * LANES
    used = TERMS * bases
    for (start, size), out in zip(chunks, outs[4:]):
        first = count * start + lax.axis_index("azimuth") * size
        weight = pltpu.roll(weight_ref[...], lax.rem(channels - first, channels), 1)[:, :size]
        parts = []
        for _ in range(TERMS):
            rounded = weight.astype(jnp.bfloat16).astype(jnp.float32)
            parts.append(rounded)
            weight = weight - rounded
        parts.append(jnp.zeros((depth - used, size), jnp.float32))
        out[...] = jnp.concatenate(parts, axis=0).T
    start_lat = lax.axis_index("polar") * rows
    table = filt_ref[...].reshape(bases * lats, width)
    base = lax.broadcasted_iota(jnp.int32, (depth, bases * lats), 0)
    valid = base < used
    for _ in range(TERMS - 1):
        base = jnp.where(base >= bases, base - bases, base)
    column = lax.broadcasted_iota(jnp.int32, (depth, bases * lats), 1)
    for i in range(ext):
        lat = start_lat + (i - REACH)
        inside = (lat >= 0) & (lat < lats)
        lat = jnp.clip(lat, 0, lats - 1)
        pick = jnp.where(valid & (column == base * lats + lat), 1.0, 0.0).astype(jnp.bfloat16)
        row = dot_nn(pick, table)
        real, imag = row[:, :modes], row[:, modes:]
        rest_re, rest_im = real[:, whole:], imag[:, whole:]
        filter_out[i] = jnp.concatenate(
            [real[:, :whole], rest_re, rest_re, imag[:, :whole], rest_im, -rest_im], axis=1
        ).astype(jnp.bfloat16)
        local = jnp.where(inside, offset_ref[pl.ds(lat, 1), :] - start_lat, -1)
        spare = jnp.full((1, depth - used), -1, jnp.int32)
        target_out[i : i + 1, :] = jnp.concatenate([local] * TERMS + [spare], axis=1)


def prepare(basis_weight, filt, offsets, forth, back, rows, count, chunks):
    bases = filt.shape[0]
    width = filt.shape[2]
    ext = rows + 2 * REACH
    depth = round_up(TERMS * bases, 16)
    shapes = [
        jax.ShapeDtypeStruct((ext, depth, width + LANES), jnp.bfloat16),
        jax.ShapeDtypeStruct((ext, depth), jnp.int32),
        jax.ShapeDtypeStruct(forth.shape, forth.dtype),
        jax.ShapeDtypeStruct(back.shape, back.dtype),
    ] + [jax.ShapeDtypeStruct((size, depth), jnp.float32) for _, size in chunks]
    return pl.pallas_call(
        functools.partial(prepare_kernel, count, chunks),
        in_specs=[pl.BlockSpec(memory_space=VMEM)] * 5,
        out_specs=[pl.BlockSpec(memory_space=VMEM)] * len(shapes),
        out_shape=shapes,
        compiler_params=pltpu.CompilerParams(vmem_limit_bytes=16 * 2**20),
        cost_estimate=NO_COST,
        name="prepare",
    )(basis_weight, filt, offsets, forth, back)


def halo(first, second):
    bands, count = lax.axis_size("polar"), lax.axis_size("azimuth")
    blocks = []
    for odd, block in ((0, first), (1, second)):
        pairs = []
        for a in range(bands):
            other = ((a + odd) ^ 1) - odd
            for b in range(count):
                paired = 0 <= other < bands
                target = (other, b) if paired else (a, b ^ 1 if b ^ 1 < count else b)
                pairs.append((a * count + b, target[0] * count + target[1]))
        blocks.append(lax.ppermute(block, ("polar", "azimuth"), pairs))
    return blocks


def on_device(chunks, conv_out, grad_out, w_in, b_in, w_out, basis_weight, filt, offsets):
    rows, part, channels = conv_out.shape
    count = lax.axis_size("azimuth")
    forth, back = tables(count, part, filt.shape[2] // 2)
    forth, back = jnp.asarray(forth), jnp.asarray(back)
    owned = channels // count
    halves = 2 if rows % 2 == 0 else 1
    wide = round_up(part, HALF)
    filters, target, forth, back, *weights = prepare(
        basis_weight, filt, offsets, forth, back, rows, count, chunks
    )
    early, order = [], []
    for half in range(halves):
        final = half == halves - 1
        sent = [(k, 0, owned) for k in range(count)]
        if final:
            sent[1:] = [(k,) + chunk for chunk in chunks for k in range(1, count)]
        blocks = mlp(conv_out, grad_out, w_in, b_in, w_out, count, half, halves, sent, chunks, order)
        order = blocks[:1]
        if not final:
            early.append(analyze_early([exchange(blocks[k], k, count) for k in range(count)], forth, wide))
    spectra, terms, returned = {}, {}, {}
    for q, (start, size) in enumerate(chunks):
        mine = blocks[1 + q * (count - 1) : 1 + (q + 1) * (count - 1)]
        pieces = [blocks[0]] + [exchange(block, k, count) for k, block in enumerate(mine, 1)]
        after = [terms[q - 1]] if q else []
        own, first, second = analyze(pieces, forth, early, rows, wide, (start, size), after)
        spectra[q] = halo(first, second)
        terms[q] = own_terms(own, early, start, weights[q], target, filters)
    for q in range(len(chunks)):
        halos = spectra[q]
        if q == 0:
            others = [terms[other] for other in terms if other > q]
            terms[q] = side_terms(terms[q], halos[0], weights[q], target, filters, others)
            halos = halos[1:]
        grids = finish(terms[q], halos, weights[q], target, filters, back, count, part)
        returned[q] = {k: exchange(grids[k], k, count) for k in range(count)}
    total = []
    for q, chunk in enumerate(chunks):
        tiles = [list(range(count * chunk[1] // LANES)) for _ in range(count)]
        if q == len(chunks) - 1:
            chip = [{mine, partner_static(mine, NEAR, count, -1)} for mine in range(count)]
            close = [[t for t in tiles[mine] if set(owners(t, chunk[1])) <= chip[mine]] for mine in range(count)]
            if any(close):
                total = [add_chunk(grad_out, returned[q], chunk, count, close, total)]
                tiles = [[t for t in tiles[mine] if t not in close[mine]] for mine in range(count)]
        total = [add_chunk(grad_out, returned[q], chunk, count, tiles, total)]
    return jnp.transpose(total[0], (1, 0, 2))


def solution(mesh):
    grid = P(("member", "polar"), "azimuth", None)

    def run(conv_out, grad_out, *others):
        owned = conv_out.shape[2] // mesh.shape["azimuth"]
        sizes = [owned]
        if owned % 32 == 0 and owned >= 96:
            big = owned * 3 // 5 // 32 * 32
            sizes = [big, owned - big]
        chunks = tuple((sum(sizes[:q]), size) for q, size in enumerate(sizes))
        return jax.shard_map(
            functools.partial(on_device, chunks),
            mesh=mesh,
            in_specs=(grid, grid) + (P(),) * 6,
            out_specs=grid,
            check_vma=False,
        )(conv_out, grad_out, *others)

    return run
```

```python
import functools
import math

import jax
import jax.numpy as jnp
import ml_dtypes
import numpy as np
from jax import lax
from jax.experimental import pallas as pl
from jax.experimental.pallas import tpu as pltpu
from jax.sharding import PartitionSpec as P

REACH = 3
LANES = 128
HALF = 64
TERMS = 3
NEAR = 1
VMEM = pltpu.MemorySpace.VMEM
NO_COST = pl.CostEstimate(flops=0, bytes_accessed=0, transcendentals=0)


def round_up(value, unit):
    return -(-value // unit) * unit


def partner(me, step, count, sign):
    if count & (count - 1) == 0:
        return me ^ step
    return lax.rem(me + sign * step + count, count)


def far_first(number, count):
    return sorted(range(number), key=lambda i: (i // count, i % count <= NEAR))


def exchange(block, step, count):
    if step == 0:
        return block
    pairs = [(a, int(partner_static(a, step, count))) for a in range(count)]
    return lax.ppermute(block, "azimuth", pairs)


def partner_static(a, step, count, sign=1):
    return a ^ step if count & (count - 1) == 0 else (a + sign * step) % count


def tables(count, part, modes):
    length = count * part
    whole = modes // LANES * LANES
    order = np.concatenate(
        [
            np.arange(whole),
            modes + np.arange(whole),
            np.arange(whole, modes),
            modes + np.arange(whole, modes),
        ]
    )
    positions = np.arange(length)
    waves = np.arange(modes)
    phase = (positions[:, None] * waves[None, :]) % length
    angle = (2.0 * math.pi / length) * phase
    scale = 1.0 / math.sqrt(length)
    factor = np.where(waves == 0, 1.0, 2.0)
    analysis = np.concatenate([np.cos(angle), -np.sin(angle)], axis=1) * scale
    synth = np.concatenate([np.cos(angle) * factor, -np.sin(angle) * factor], axis=1) * scale
    analysis = analysis.astype(np.float32).astype(ml_dtypes.bfloat16)[:, order]
    synth = synth.astype(np.float32).astype(ml_dtypes.bfloat16)[:, order]
    wide = round_up(part, HALF)
    window = round_up(HALF + wide, LANES)
    forth = np.zeros((count, HALF + window, 2 * modes), ml_dtypes.bfloat16)
    back = np.zeros((count * wide, 2 * modes), ml_dtypes.bfloat16)
    for s in range(count):
        forth[s, HALF : HALF + part] = analysis[s * part : (s + 1) * part]
        back[s * wide : s * wide + part] = synth[s * part : (s + 1) * part]
    return forth, back


def twice_gelu_slope(scaled):
    power = math.log2(2.0 / math.sqrt(math.pi)) - (1.0 / math.log(2.0)) * (scaled * scaled)
    return (1.0 + lax.erf(scaled)) + scaled * jnp.exp2(power)


def dot_nt(left, right):
    return lax.dot_general(left, right, (((1,), (1,)), ((), ())), preferred_element_type=jnp.float32)


def dot_nn(left, right):
    return jnp.dot(left, right, preferred_element_type=jnp.float32)


def mlp_kernel(count, half, sent, chunks, conv_ref, grad_ref, win_ref, bias_ref, wout_ref, *rest):
    outs, (tall_conv, tall_grad, pre_ref, back_ref, slope_ref, total_ref) = rest[-6 - len(sent) : -6], rest[-6:]
    part, channels = conv_ref.shape[1:]
    wide = round_up(part, HALF)
    rows = tall_conv.shape[0] // wide
    owned = channels // count
    block = pre_ref.shape[2]
    steps = win_ref.shape[1] // block
    me = lax.axis_index("azimuth")
    def stack(tall, source):
        for row in range(rows):
            whole = part // 16 * 16
            tall[row * wide + whole : (row + 1) * wide, :] = jnp.zeros((wide - whole, channels), jnp.bfloat16)
            tall[row * wide : row * wide + part, :] = source[half * rows + row]

    group = 96
    groups = rows * wide // group

    def span(step):
        return slice(step * block, (step + 1) * block)

    def project_pre(step):
        pre_ref[step % 2] = dot_nn(tall_conv[...], win_ref[:, span(step)])

    def project_back(step):
        back_ref[step % 2] = dot_nt(tall_grad[...], wout_ref[span(step), :])

    def slope(step, first, last):
        root = math.sqrt(0.5)
        bias = bias_ref[span(step)].reshape(1, block) * root
        for g in range(first, last):
            some = slice(g * group, (g + 1) * group)
            value = back_ref[step % 2, some, :] * twice_gelu_slope(pre_ref[step % 2, some, :] * root + bias)
            slope_ref[some, span(step)] = value.astype(jnp.bfloat16)

    def gather(first, last):
        at = slice(first * block, last * block)
        term = dot_nt(win_ref[:, at], slope_ref[:, at])
        total_ref[...] = term if first == 0 else total_ref[...] + term

    stack(tall_conv, conv_ref)
    project_pre(0)
    stack(tall_grad, grad_ref)
    project_back(0)
    gathered = 0
    thirds = [groups * n // 4 for n in (0, 1, 3, 4)]
    for step in range(steps):
        if step + 1 < steps:
            project_pre(step + 1)
        slope(step, thirds[0], thirds[1])
        if step - gathered == 2:
            gather(gathered, step)
            gathered = step
        slope(step, thirds[1], thirds[2])
        if step + 1 < steps:
            project_back(step + 1)
        slope(step, thirds[2], thirds[3])
    gather(gathered, steps)
    for out, (k, start, size) in zip(outs, sent):
        target = partner(me, k, count, 1)
        for begin, width in chunks:
            if start <= begin < start + size:
                first = pl.multiple_of(count * begin + target * width, 32)
                value = 0.5 * total_ref[pl.ds(first, width), :]
                out[begin - start : begin - start + width, :] = value.astype(jnp.bfloat16)


def mlp(conv_out, grad_out, w_in, b_in, w_out, count, half, halves, sent, chunks, after):
    rows, part, channels = conv_out.shape
    rows //= halves
    block = 256
    wide = round_up(part, HALF)
    vmem = pl.BlockSpec(memory_space=VMEM)
    out_shape = [jax.ShapeDtypeStruct((size, rows * wide), jnp.bfloat16) for _, _, size in sent]
    return pl.pallas_call(
        functools.partial(mlp_kernel, count, half, sent, chunks),
        in_specs=[vmem] * 5 + [pl.BlockSpec(memory_space=pl.ANY)] * len(after),
        out_specs=[vmem] * len(out_shape),
        out_shape=out_shape,
        scratch_shapes=[
            pltpu.VMEM((rows * wide, channels), jnp.bfloat16),
            pltpu.VMEM((rows * wide, channels), jnp.bfloat16),
            pltpu.VMEM((2, rows * wide, block), jnp.float32),
            pltpu.VMEM((2, rows * wide, block), jnp.float32),
            pltpu.VMEM((rows * wide, w_in.shape[1]), jnp.bfloat16),
            pltpu.VMEM((channels, rows * wide), jnp.float32),
        ],
        compiler_params=pltpu.CompilerParams(vmem_limit_bytes=16 * 2**20),
        cost_estimate=NO_COST,
        name="mlp",
    )(conv_out, grad_out, w_in, b_in, w_out, *after)


def spectra_of(pieces, channels, table_ref, wide):
    size = channels[1]
    rows = pieces[0][0].shape[1] // wide
    window = table_ref.shape[1] - HALF
    shifts = [row * wide % LANES for row in range(rows)]
    spectra = [None] * rows
    for shift in sorted(set(shifts)):
        group = [row for row in range(rows) if shifts[row] == shift]
        total = None
        for k, (piece, base) in enumerate(pieces):
            windows = [row * wide // LANES * LANES for row in group]
            left = jnp.concatenate([piece[base : base + size, at : at + window] for at in windows], axis=0)
            term = dot_nn(left, table_ref[k, HALF - shift : HALF - shift + window, :])
            total = term if total is None else total + term
        for at, row in enumerate(group):
            spectra[row] = total[at * size : (at + 1) * size]
    return spectra


def early_kernel(count, wide, *refs):
    ranks = far_first(count, count)
    pieces = [(refs[ranks.index(k)], 0) for k in range(count)]
    table_ref, out_ref = refs[count], refs[-1]
    for row, spectrum in enumerate(spectra_of(pieces, (0, pieces[0][0].shape[0]), table_ref, wide)):
        out_ref[row] = spectrum


def analyze_early(pieces, table, wide):
    count = len(pieces)
    size, across = pieces[0].shape
    return pl.pallas_call(
        functools.partial(early_kernel, count, wide),
        in_specs=[pl.BlockSpec(memory_space=VMEM)] * (count + 1),
        out_specs=pl.BlockSpec(memory_space=VMEM),
        out_shape=jax.ShapeDtypeStruct((across // wide, size, table.shape[2]), jnp.float32),
        compiler_params=pltpu.CompilerParams(vmem_limit_bytes=12 * 2**20),
        cost_estimate=NO_COST,
        name="analysis_early",
    )(*(pieces[k] for k in far_first(count, count)), table)


def analysis_kernel(count, rows, wide, chunk, halves, *refs):
    own_ref, first_ref, second_ref = refs[-3:]
    start, size = chunk
    ranks = far_first(count, count)
    pieces = [(refs[ranks.index(k)], 0 if k else start) for k in range(count)]
    table_ref, early = refs[count], refs[count + 1 : count + halves]
    per = rows // halves
    even = lax.rem(lax.axis_index("polar"), 2) == 0
    for row, spectrum in enumerate(spectra_of(pieces, chunk, table_ref, wide)):
        own_ref[row] = spectrum

    def row_of(row):
        half, row = divmod(row, per)
        return own_ref[row] if half == halves - 1 else early[half][row, start : start + size, :]

    def share(above, below):
        for h in range(REACH):
            above[h] = row_of(rows - REACH + h).astype(jnp.bfloat16)
            below[h] = row_of(h).astype(jnp.bfloat16)

    pl.when(even)(lambda: share(first_ref, second_ref))
    pl.when(jnp.logical_not(even))(lambda: share(second_ref, first_ref))


def analyze(pieces, table, early, rows, wide, chunk, after):
    count = len(pieces)
    size = chunk[1]
    width = table.shape[2]
    halves = len(early) + 1
    halo = jax.ShapeDtypeStruct((REACH, size, width), jnp.bfloat16)
    return pl.pallas_call(
        functools.partial(analysis_kernel, count, rows, wide, chunk, halves),
        in_specs=[pl.BlockSpec(memory_space=VMEM)] * (count + halves)
        + [pl.BlockSpec(memory_space=pl.ANY)] * len(after),
        out_specs=[pl.BlockSpec(memory_space=VMEM)] * 3,
        out_shape=[jax.ShapeDtypeStruct((rows // halves, size, width), jnp.float32), halo, halo],
        compiler_params=pltpu.CompilerParams(vmem_limit_bytes=12 * 2**20),
        cost_estimate=NO_COST,
        name="analysis",
    )(*(pieces[k] for k in far_first(count, count)), table, *early, *after)


def add_row(accs, spectrum, weight, target_row, filter_row, targets):
    size = spectrum.shape[0]
    masked = jnp.concatenate([jnp.where(target_row == t, weight, 0.0) for t in targets], axis=0)
    gains = dot_nn(masked.astype(jnp.bfloat16), filter_row)
    whole = (gains.shape[1] // 2) // LANES * LANES - LANES
    spec_re = spectrum[:, :whole]
    spec_im = spectrum[:, whole : 2 * whole]
    spec_x = spectrum[:, 2 * whole :]
    swapped = pltpu.roll(spec_x, HALF, 1)
    for at, target in enumerate(targets):
        gain = gains[at * size : (at + 1) * size]
        gain_re = gain[:, :whole]
        gain_rx = gain[:, whole : whole + LANES]
        gain_im = gain[:, whole + LANES : 2 * whole + LANES]
        gain_ix = gain[:, 2 * whole + LANES :]
        acc_re, acc_im, acc_x = accs[target]
        acc_re = acc_re + (gain_re * spec_re + gain_im * spec_im)
        acc_im = acc_im + (gain_re * spec_im - gain_im * spec_re)
        acc_x = acc_x + (gain_rx * spec_x + gain_ix * swapped)
        accs[target] = acc_re, acc_im, acc_x


def split_tiles(value):
    whole = (value.shape[1] - LANES) // 2
    return value[:, :whole], value[:, whole : 2 * whole], value[:, 2 * whole :]


def own_kernel(start, own_ref, weight_ref, target_ref, filter_ref, *rest):
    early, out_ref = rest[:-1], rest[-1]
    rows, size, width = out_ref.shape
    per = own_ref.shape[0]
    accs = {t: split_tiles(jnp.zeros((size, width), jnp.float32)) for t in range(rows)}
    for row in range(rows):
        at = row + REACH
        targets = [t for t in range(rows) if abs(row - t) <= REACH]
        half = row // per
        spectrum = early[half][row % per, start : start + size, :] if half < len(early) else own_ref[row % per]
        add_row(accs, spectrum, weight_ref[...], target_ref[at : at + 1, :], filter_ref[at], targets)
    for t in range(rows):
        out_ref[t] = jnp.concatenate(accs[t], axis=1)


def own_terms(own, early, start, weight, target, filters):
    per, size, width = own.shape
    return pl.pallas_call(
        functools.partial(own_kernel, start),
        in_specs=[pl.BlockSpec(memory_space=VMEM)] * (4 + len(early)),
        out_specs=pl.BlockSpec(memory_space=VMEM),
        out_shape=jax.ShapeDtypeStruct((per * (1 + len(early)), size, width), jnp.float32),
        compiler_params=pltpu.CompilerParams(vmem_limit_bytes=12 * 2**20),
        cost_estimate=NO_COST,
        name="own_terms",
    )(own, weight, target, filters, *early)


def add_halo(accs, sides, rows, weight_ref, target_ref, filter_ref):
    for side, base in sides:
        for h in range(REACH):
            at = base + h + REACH
            targets = [t for t in range(rows) if abs(base + h - t) <= REACH]
            add_row(
                accs,
                side[h].astype(jnp.float32),
                weight_ref[...],
                target_ref[at : at + 1, :],
                filter_ref[at],
                targets,
            )


def side_kernel(part_ref, first_ref, weight_ref, target_ref, filter_ref, *rest):
    out_ref = rest[-1]
    rows = part_ref.shape[0]
    even = lax.rem(lax.axis_index("polar"), 2) == 0

    def combine(base):
        accs = {t: split_tiles(part_ref[t]) for t in range(rows)}
        add_halo(accs, [(first_ref, base)], rows, weight_ref, target_ref, filter_ref)
        for t in range(rows):
            out_ref[t] = jnp.concatenate(accs[t], axis=1)

    pl.when(even)(lambda: combine(rows))
    pl.when(jnp.logical_not(even))(lambda: combine(-REACH))


def side_terms(own, first, weight, target, filters, after):
    return pl.pallas_call(
        side_kernel,
        in_specs=[pl.BlockSpec(memory_space=VMEM)] * 5 + [pl.BlockSpec(memory_space=pl.ANY)] * len(after),
        out_specs=pl.BlockSpec(memory_space=VMEM),
        out_shape=jax.ShapeDtypeStruct(own.shape, jnp.float32),
        compiler_params=pltpu.CompilerParams(vmem_limit_bytes=12 * 2**20),
        cost_estimate=NO_COST,
        name="side_terms",
    )(own, first, weight, target, filters, *after)


def finish_kernel(count, swaps, part_ref, *refs):
    halos, (weight_ref, target_ref, filter_ref, table_ref) = refs[:swaps], refs[swaps : swaps + 4]
    outs, stacked_ref = refs[-count - 1 : -1], refs[-1]
    rows, size, width = part_ref.shape
    even = lax.rem(lax.axis_index("polar"), 2) == 0

    def combine(bases):
        accs = {t: split_tiles(part_ref[t]) for t in range(rows)}
        sides = list(zip(halos, bases[-swaps:]))
        add_halo(accs, sides, rows, weight_ref, target_ref, filter_ref)
        for t in range(rows):
            stacked_ref[t * size : (t + 1) * size, :] = jnp.concatenate(accs[t], axis=1).astype(jnp.bfloat16)

    pl.when(even)(lambda: combine((rows, -REACH)))
    pl.when(jnp.logical_not(even))(lambda: combine((-REACH, rows)))
    grid = dot_nt(table_ref[...], stacked_ref[...])
    wide = grid.shape[0] // count
    for k, out in enumerate(outs):
        out[...] = grid[k * wide : k * wide + out.shape[0]].astype(jnp.bfloat16)


def finish(own, halos, weight, target, filters, table, count, part):
    rows, size, width = own.shape
    return pl.pallas_call(
        functools.partial(finish_kernel, count, len(halos)),
        in_specs=[pl.BlockSpec(memory_space=VMEM)] * (5 + len(halos)),
        out_specs=[pl.BlockSpec(memory_space=VMEM)] * count,
        out_shape=[jax.ShapeDtypeStruct((part, rows * size), jnp.bfloat16)] * count,
        scratch_shapes=[pltpu.VMEM((rows * size, width), jnp.bfloat16)],
        compiler_params=pltpu.CompilerParams(vmem_limit_bytes=12 * 2**20),
        cost_estimate=NO_COST,
        name="finish",
    )(own, *halos, weight, target, filters, table)


def add_kernel(count, chunk, steps, tiles, grad_ref, *refs):
    out_ref, tall_ref, done_ref, sems = refs[-4:]
    pieces = dict(zip(steps, refs))
    _, part, rows, _ = done_ref.shape
    start, size = chunk
    me = lax.axis_index("azimuth")

    def add(mine):
        order = [[k for k in range(count) if partner_static(mine, k, count, -1) == s][0] for s in range(count)]
        copies = []
        for at, tile in enumerate(tiles[mine]):
            lanes = range(tile * LANES, (tile + 1) * LANES)
            first = count * start + tile * LANES
            for row in range(rows):
                parts = []
                for s in owners(tile, size):
                    low, high = max(lanes[0], s * size) - s * size, min(lanes[-1] + 1, (s + 1) * size) - s * size
                    parts.append(pieces[order[s]][:, row * size + low : row * size + high])
                conv = jnp.concatenate(parts, axis=1).astype(jnp.float32)
                total = grad_ref[row, :, first : first + LANES].astype(jnp.float32) + conv
                tall_ref[at, pl.ds(row, part, stride=rows), :] = total
            done_ref[at] = tall_ref[at].reshape(part, rows, LANES).astype(jnp.bfloat16)
            copies.append(pltpu.make_async_copy(done_ref.at[at], out_ref.at[:, :, pl.ds(first, LANES)], sems.at[at]))
            copies[-1].start()
        for copy in copies:
            copy.wait()

    for mine in range(count):
        pl.when(me == mine)(functools.partial(add, mine))


def owners(tile, size):
    return range(tile * LANES // size, ((tile + 1) * LANES - 1) // size + 1)


def add_chunk(grad_out, pieces, chunk, count, tiles, before):
    rows, part, channels = grad_out.shape
    number = max(len(some) for some in tiles)
    needed = {
        k
        for mine in range(count)
        for tile in tiles[mine]
        for s in owners(tile, chunk[1])
        for k in range(count)
        if partner_static(mine, k, count, -1) == s
    }
    pieces = sorted(((k, pieces[k]) for k in needed), key=lambda item: item[0] <= NEAR)
    vmem = pl.BlockSpec(memory_space=VMEM)
    anywhere = pl.BlockSpec(memory_space=pl.ANY)
    return pl.pallas_call(
        functools.partial(add_kernel, count, chunk, [k for k, _ in pieces], tiles),
        in_specs=[vmem] * (1 + len(pieces)) + [anywhere] * len(before),
        out_specs=anywhere,
        out_shape=jax.ShapeDtypeStruct((part, rows, channels), jnp.bfloat16),
        scratch_shapes=[
            pltpu.VMEM((number, rows * part, LANES), jnp.float32),
            pltpu.VMEM((number, part, rows, LANES), jnp.bfloat16),
            pltpu.SemaphoreType.DMA((number,)),
        ],
        input_output_aliases={1 + len(pieces): 0} if before else {},
        compiler_params=pltpu.CompilerParams(vmem_limit_bytes=12 * 2**20),
        cost_estimate=NO_COST,
        name="add_chunk",
    )(grad_out, *(block for _, block in pieces), *before)


def prepare_kernel(count, chunks, weight_ref, filt_ref, offset_ref, forth_ref, back_ref, *outs):
    filter_out, target_out, forth_out, back_out = outs[:4]
    me = lax.axis_index("azimuth")
    wide = back_ref.shape[0] // count
    for k in range(count):
        forth_out[k] = forth_ref[partner(me, k, count, -1)]
        first = pl.multiple_of(partner(me, k, count, 1) * wide, HALF)
        back_out[k * wide : (k + 1) * wide, :] = back_ref[pl.ds(first, wide), :]
    bases, channels = weight_ref.shape
    lats, width = filt_ref.shape[1:]
    ext, depth = target_out.shape
    rows = ext - 2 * REACH
    modes = width // 2
    whole = modes // LANES * LANES
    used = TERMS * bases
    for (start, size), out in zip(chunks, outs[4:]):
        first = count * start + lax.axis_index("azimuth") * size
        weight = pltpu.roll(weight_ref[...], lax.rem(channels - first, channels), 1)[:, :size]
        parts = []
        for _ in range(TERMS):
            rounded = weight.astype(jnp.bfloat16).astype(jnp.float32)
            parts.append(rounded)
            weight = weight - rounded
        parts.append(jnp.zeros((depth - used, size), jnp.float32))
        out[...] = jnp.concatenate(parts, axis=0).T
    start_lat = lax.axis_index("polar") * rows
    table = filt_ref[...].reshape(bases * lats, width)
    base = lax.broadcasted_iota(jnp.int32, (depth, bases * lats), 0)
    valid = base < used
    for _ in range(TERMS - 1):
        base = jnp.where(base >= bases, base - bases, base)
    column = lax.broadcasted_iota(jnp.int32, (depth, bases * lats), 1)
    for i in range(ext):
        lat = start_lat + (i - REACH)
        inside = (lat >= 0) & (lat < lats)
        lat = jnp.clip(lat, 0, lats - 1)
        pick = jnp.where(valid & (column == base * lats + lat), 1.0, 0.0).astype(jnp.bfloat16)
        row = dot_nn(pick, table)
        real, imag = row[:, :modes], row[:, modes:]
        rest_re, rest_im = real[:, whole:], imag[:, whole:]
        filter_out[i] = jnp.concatenate(
            [real[:, :whole], rest_re, rest_re, imag[:, :whole], rest_im, -rest_im], axis=1
        ).astype(jnp.bfloat16)
        local = jnp.where(inside, offset_ref[pl.ds(lat, 1), :] - start_lat, -1)
        spare = jnp.full((1, depth - used), -1, jnp.int32)
        target_out[i : i + 1, :] = jnp.concatenate([local] * TERMS + [spare], axis=1)


def prepare(basis_weight, filt, offsets, forth, back, rows, count, chunks):
    bases = filt.shape[0]
    width = filt.shape[2]
    ext = rows + 2 * REACH
    depth = round_up(TERMS * bases, 16)
    shapes = [
        jax.ShapeDtypeStruct((ext, depth, width + LANES), jnp.bfloat16),
        jax.ShapeDtypeStruct((ext, depth), jnp.int32),
        jax.ShapeDtypeStruct(forth.shape, forth.dtype),
        jax.ShapeDtypeStruct(back.shape, back.dtype),
    ] + [jax.ShapeDtypeStruct((size, depth), jnp.float32) for _, size in chunks]
    return pl.pallas_call(
        functools.partial(prepare_kernel, count, chunks),
        in_specs=[pl.BlockSpec(memory_space=VMEM)] * 5,
        out_specs=[pl.BlockSpec(memory_space=VMEM)] * len(shapes),
        out_shape=shapes,
        compiler_params=pltpu.CompilerParams(vmem_limit_bytes=16 * 2**20),
        cost_estimate=NO_COST,
        name="prepare",
    )(basis_weight, filt, offsets, forth, back)


def halo(first, second):
    bands, count = lax.axis_size("polar"), lax.axis_size("azimuth")
    blocks = []
    for odd, block in ((0, first), (1, second)):
        pairs = []
        for a in range(bands):
            other = ((a + odd) ^ 1) - odd
            for b in range(count):
                paired = 0 <= other < bands
                target = (other, b) if paired else (a, b ^ 1 if b ^ 1 < count else b)
                pairs.append((a * count + b, target[0] * count + target[1]))
        blocks.append(lax.ppermute(block, ("polar", "azimuth"), pairs))
    return blocks


def on_device(chunks, conv_out, grad_out, w_in, b_in, w_out, basis_weight, filt, offsets):
    rows, part, channels = conv_out.shape
    count = lax.axis_size("azimuth")
    forth, back = tables(count, part, filt.shape[2] // 2)
    forth, back = jnp.asarray(forth), jnp.asarray(back)
    owned = channels // count
    halves = 2 if rows % 2 == 0 else 1
    wide = round_up(part, HALF)
    filters, target, forth, back, *weights = prepare(
        basis_weight, filt, offsets, forth, back, rows, count, chunks
    )
    early, order = [], []
    for half in range(halves):
        final = half == halves - 1
        sent = [(k, 0, owned) for k in range(count)]
        if final:
            sent[1:] = [(k,) + chunk for chunk in chunks for k in range(1, count)]
        blocks = mlp(conv_out, grad_out, w_in, b_in, w_out, count, half, halves, sent, chunks, order)
        order = blocks[:1]
        if not final:
            early.append(analyze_early([exchange(blocks[k], k, count) for k in range(count)], forth, wide))
    spectra, terms, returned = {}, {}, {}
    for q, (start, size) in enumerate(chunks):
        mine = blocks[1 + q * (count - 1) : 1 + (q + 1) * (count - 1)]
        pieces = [blocks[0]] + [exchange(block, k, count) for k, block in enumerate(mine, 1)]
        after = [terms[q - 1]] if q else []
        own, first, second = analyze(pieces, forth, early, rows, wide, (start, size), after)
        spectra[q] = halo(first, second)
        terms[q] = own_terms(own, early, start, weights[q], target, filters)
    for q in range(len(chunks)):
        halos = spectra[q]
        if q == 0:
            others = [terms[other] for other in terms if other > q]
            terms[q] = side_terms(terms[q], halos[0], weights[q], target, filters, others)
            halos = halos[1:]
        grids = finish(terms[q], halos, weights[q], target, filters, back, count, part)
        returned[q] = {k: exchange(grids[k], k, count) for k in range(count)}
    total = []
    for q, chunk in enumerate(chunks):
        tiles = [list(range(count * chunk[1] // LANES)) for _ in range(count)]
        if q == len(chunks) - 1:
            chip = [{mine, partner_static(mine, NEAR, count, -1)} for mine in range(count)]
            close = [[t for t in tiles[mine] if set(owners(t, chunk[1])) <= chip[mine]] for mine in range(count)]
            if any(close):
                total = [add_chunk(grad_out, returned[q], chunk, count, close, total)]
                tiles = [[t for t in tiles[mine] if t not in close[mine]] for mine in range(count)]
        total = [add_chunk(grad_out, returned[q], chunk, count, tiles, total)]
    return jnp.transpose(total[0], (1, 0, 2))


def solution(mesh):
    grid = P(("member", "polar"), "azimuth", None)

    def run(conv_out, grad_out, *others):
        owned = conv_out.shape[2] // mesh.shape["azimuth"]
        sizes = [owned]
        if owned % 32 == 0 and owned >= 96:
            big = owned * 3 // 5 // 32 * 32
            sizes = [big, owned - big]
        chunks = tuple((sum(sizes[:q]), size) for q, size in enumerate(sizes))
        return jax.shard_map(
            functools.partial(on_device, chunks),
            mesh=mesh,
            in_specs=(grid, grid) + (P(),) * 6,
            out_specs=grid,
            check_vma=False,
        )(conv_out, grad_out, *others)

    return run
```

```python
import functools
import math

import jax
import jax.numpy as jnp
import ml_dtypes
import numpy as np
from jax import lax
from jax.experimental import pallas as pl
from jax.experimental.pallas import tpu as pltpu
from jax.sharding import PartitionSpec as P

REACH = 3
LANES = 128
HALF = 64
TERMS = 3
NEAR = 1
VMEM = pltpu.MemorySpace.VMEM
NO_COST = pl.CostEstimate(flops=0, bytes_accessed=0, transcendentals=0)


def round_up(value, unit):
    return -(-value // unit) * unit


def partner(me, step, count, sign):
    if count & (count - 1) == 0:
        return me ^ step
    return lax.rem(me + sign * step + count, count)


def far_first(number, count):
    return sorted(range(number), key=lambda i: (i // count, i % count <= NEAR))


def exchange(block, step, count):
    if step == 0:
        return block
    pairs = [(a, int(partner_static(a, step, count))) for a in range(count)]
    return lax.ppermute(block, "azimuth", pairs)


def partner_static(a, step, count, sign=1):
    return a ^ step if count & (count - 1) == 0 else (a + sign * step) % count


def tables(count, part, modes):
    length = count * part
    whole = modes // LANES * LANES
    order = np.concatenate(
        [
            np.arange(whole),
            modes + np.arange(whole),
            np.arange(whole, modes),
            modes + np.arange(whole, modes),
        ]
    )
    positions = np.arange(length)
    waves = np.arange(modes)
    phase = (positions[:, None] * waves[None, :]) % length
    angle = (2.0 * math.pi / length) * phase
    scale = 1.0 / math.sqrt(length)
    factor = np.where(waves == 0, 1.0, 2.0)
    analysis = np.concatenate([np.cos(angle), -np.sin(angle)], axis=1) * scale
    synth = np.concatenate([np.cos(angle) * factor, -np.sin(angle) * factor], axis=1) * scale
    analysis = analysis.astype(np.float32).astype(ml_dtypes.bfloat16)[:, order]
    synth = synth.astype(np.float32).astype(ml_dtypes.bfloat16)[:, order]
    wide = round_up(part, HALF)
    window = round_up(HALF + wide, LANES)
    forth = np.zeros((count, HALF + window, 2 * modes), ml_dtypes.bfloat16)
    back = np.zeros((count * wide, 2 * modes), ml_dtypes.bfloat16)
    for s in range(count):
        forth[s, HALF : HALF + part] = analysis[s * part : (s + 1) * part]
        back[s * wide : s * wide + part] = synth[s * part : (s + 1) * part]
    return forth, back


def twice_gelu_slope(scaled):
    power = math.log2(2.0 / math.sqrt(math.pi)) - (1.0 / math.log(2.0)) * (scaled * scaled)
    return (1.0 + lax.erf(scaled)) + scaled * jnp.exp2(power)


def dot_nt(left, right):
    return lax.dot_general(left, right, (((1,), (1,)), ((), ())), preferred_element_type=jnp.float32)


def dot_nn(left, right):
    return jnp.dot(left, right, preferred_element_type=jnp.float32)


def mlp_kernel(count, half, sent, chunks, conv_ref, grad_ref, win_ref, bias_ref, wout_ref, *rest):
    outs, (tall_conv, tall_grad, pre_ref, back_ref, slope_ref, total_ref) = rest[-6 - len(sent) : -6], rest[-6:]
    part, channels = conv_ref.shape[1:]
    wide = round_up(part, HALF)
    rows = tall_conv.shape[0] // wide
    owned = channels // count
    block = pre_ref.shape[2]
    steps = win_ref.shape[1] // block
    me = lax.axis_index("azimuth")
    def stack(tall, source):
        for row in range(rows):
            whole = part // 16 * 16
            tall[row * wide + whole : (row + 1) * wide, :] = jnp.zeros((wide - whole, channels), jnp.bfloat16)
            tall[row * wide : row * wide + part, :] = source[half * rows + row]

    group = 96
    groups = rows * wide // group

    def span(step):
        return slice(step * block, (step + 1) * block)

    def project_pre(step):
        pre_ref[step % 2] = dot_nn(tall_conv[...], win_ref[:, span(step)])

    def project_back(step):
        back_ref[step % 2] = dot_nt(tall_grad[...], wout_ref[span(step), :])

    def slope(step, first, last):
        root = math.sqrt(0.5)
        bias = bias_ref[span(step)].reshape(1, block) * root
        for g in range(first, last):
            some = slice(g * group, (g + 1) * group)
            value = back_ref[step % 2, some, :] * twice_gelu_slope(pre_ref[step % 2, some, :] * root + bias)
            slope_ref[some, span(step)] = value.astype(jnp.bfloat16)

    def gather(first, last):
        at = slice(first * block, last * block)
        term = dot_nt(win_ref[:, at], slope_ref[:, at])
        total_ref[...] = term if first == 0 else total_ref[...] + term

    stack(tall_conv, conv_ref)
    project_pre(0)
    stack(tall_grad, grad_ref)
    project_back(0)
    gathered = 0
    thirds = [groups * n // 4 for n in (0, 1, 3, 4)]
    for step in range(steps):
        if step + 1 < steps:
            project_pre(step + 1)
        slope(step, thirds[0], thirds[1])
        if step - gathered == 2:
            gather(gathered, step)
            gathered = step
        slope(step, thirds[1], thirds[2])
        if step + 1 < steps:
            project_back(step + 1)
        slope(step, thirds[2], thirds[3])
    gather(gathered, steps)
    for out, (k, start, size) in zip(outs, sent):
        target = partner(me, k, count, 1)
        for begin, width in chunks:
            if start <= begin < start + size:
                first = pl.multiple_of(count * begin + target * width, 32)
                value = 0.5 * total_ref[pl.ds(first, width), :]
                out[begin - start : begin - start + width, :] = value.astype(jnp.bfloat16)


def mlp(conv_out, grad_out, w_in, b_in, w_out, count, half, halves, sent, chunks, after):
    rows, part, channels = conv_out.shape
    rows //= halves
    block = 256
    wide = round_up(part, HALF)
    vmem = pl.BlockSpec(memory_space=VMEM)
    out_shape = [jax.ShapeDtypeStruct((size, rows * wide), jnp.bfloat16) for _, _, size in sent]
    return pl.pallas_call(
        functools.partial(mlp_kernel, count, half, sent, chunks),
        in_specs=[vmem] * 5 + [pl.BlockSpec(memory_space=pl.ANY)] * len(after),
        out_specs=[vmem] * len(out_shape),
        out_shape=out_shape,
        scratch_shapes=[
            pltpu.VMEM((rows * wide, channels), jnp.bfloat16),
            pltpu.VMEM((rows * wide, channels), jnp.bfloat16),
            pltpu.VMEM((2, rows * wide, block), jnp.float32),
            pltpu.VMEM((2, rows * wide, block), jnp.float32),
            pltpu.VMEM((rows * wide, w_in.shape[1]), jnp.bfloat16),
            pltpu.VMEM((channels, rows * wide), jnp.float32),
        ],
        compiler_params=pltpu.CompilerParams(vmem_limit_bytes=16 * 2**20),
        cost_estimate=NO_COST,
        name="mlp",
    )(conv_out, grad_out, w_in, b_in, w_out, *after)


def spectra_of(pieces, channels, table_ref, wide):
    size = channels[1]
    rows = pieces[0][0].shape[1] // wide
    window = table_ref.shape[1] - HALF
    shifts = [row * wide % LANES for row in range(rows)]
    spectra = [None] * rows
    for shift in sorted(set(shifts)):
        group = [row for row in range(rows) if shifts[row] == shift]
        total = None
        for k, (piece, base) in enumerate(pieces):
            windows = [row * wide // LANES * LANES for row in group]
            left = jnp.concatenate([piece[base : base + size, at : at + window] for at in windows], axis=0)
            term = dot_nn(left, table_ref[k, HALF - shift : HALF - shift + window, :])
            total = term if total is None else total + term
        for at, row in enumerate(group):
            spectra[row] = total[at * size : (at + 1) * size]
    return spectra


def early_kernel(count, wide, *refs):
    ranks = far_first(count, count)
    pieces = [(refs[ranks.index(k)], 0) for k in range(count)]
    table_ref, out_ref = refs[count], refs[-1]
    for row, spectrum in enumerate(spectra_of(pieces, (0, pieces[0][0].shape[0]), table_ref, wide)):
        out_ref[row] = spectrum


def analyze_early(pieces, table, wide):
    count = len(pieces)
    size, across = pieces[0].shape
    return pl.pallas_call(
        functools.partial(early_kernel, count, wide),
        in_specs=[pl.BlockSpec(memory_space=VMEM)] * (count + 1),
        out_specs=pl.BlockSpec(memory_space=VMEM),
        out_shape=jax.ShapeDtypeStruct((across // wide, size, table.shape[2]), jnp.float32),
        compiler_params=pltpu.CompilerParams(vmem_limit_bytes=12 * 2**20),
        cost_estimate=NO_COST,
        name="analysis_early",
    )(*(pieces[k] for k in far_first(count, count)), table)


def analysis_kernel(count, rows, wide, chunk, halves, *refs):
    own_ref, first_ref, second_ref = refs[-3:]
    start, size = chunk
    ranks = far_first(count, count)
    pieces = [(refs[ranks.index(k)], 0 if k else start) for k in range(count)]
    table_ref, early = refs[count], refs[count + 1 : count + halves]
    per = rows // halves
    even = lax.rem(lax.axis_index("polar"), 2) == 0
    for row, spectrum in enumerate(spectra_of(pieces, chunk, table_ref, wide)):
        own_ref[row] = spectrum

    def row_of(row):
        half, row = divmod(row, per)
        return own_ref[row] if half == halves - 1 else early[half][row, start : start + size, :]

    def share(above, below):
        for h in range(REACH):
            above[h] = row_of(rows - REACH + h).astype(jnp.bfloat16)
            below[h] = row_of(h).astype(jnp.bfloat16)

    pl.when(even)(lambda: share(first_ref, second_ref))
    pl.when(jnp.logical_not(even))(lambda: share(second_ref, first_ref))


def analyze(pieces, table, early, rows, wide, chunk, after):
    count = len(pieces)
    size = chunk[1]
    width = table.shape[2]
    halves = len(early) + 1
    halo = jax.ShapeDtypeStruct((REACH, size, width), jnp.bfloat16)
    return pl.pallas_call(
        functools.partial(analysis_kernel, count, rows, wide, chunk, halves),
        in_specs=[pl.BlockSpec(memory_space=VMEM)] * (count + halves)
        + [pl.BlockSpec(memory_space=pl.ANY)] * len(after),
        out_specs=[pl.BlockSpec(memory_space=VMEM)] * 3,
        out_shape=[jax.ShapeDtypeStruct((rows // halves, size, width), jnp.float32), halo, halo],
        compiler_params=pltpu.CompilerParams(vmem_limit_bytes=12 * 2**20),
        cost_estimate=NO_COST,
        name="analysis",
    )(*(pieces[k] for k in far_first(count, count)), table, *early, *after)


def add_row(accs, spectrum, weight, target_row, filter_row, targets):
    size = spectrum.shape[0]
    masked = jnp.concatenate([jnp.where(target_row == t, weight, 0.0) for t in targets], axis=0)
    gains = dot_nn(masked.astype(jnp.bfloat16), filter_row)
    whole = (gains.shape[1] // 2) // LANES * LANES - LANES
    spec_re = spectrum[:, :whole]
    spec_im = spectrum[:, whole : 2 * whole]
    spec_x = spectrum[:, 2 * whole :]
    swapped = pltpu.roll(spec_x, HALF, 1)
    for at, target in enumerate(targets):
        gain = gains[at * size : (at + 1) * size]
        gain_re = gain[:, :whole]
        gain_rx = gain[:, whole : whole + LANES]
        gain_im = gain[:, whole + LANES : 2 * whole + LANES]
        gain_ix = gain[:, 2 * whole + LANES :]
        acc_re, acc_im, acc_x = accs[target]
        acc_re = acc_re + (gain_re * spec_re + gain_im * spec_im)
        acc_im = acc_im + (gain_re * spec_im - gain_im * spec_re)
        acc_x = acc_x + (gain_rx * spec_x + gain_ix * swapped)
        accs[target] = acc_re, acc_im, acc_x


def split_tiles(value):
    whole = (value.shape[1] - LANES) // 2
    return value[:, :whole], value[:, whole : 2 * whole], value[:, 2 * whole :]


def own_kernel(start, own_ref, weight_ref, target_ref, filter_ref, *rest):
    early, out_ref = rest[:-1], rest[-1]
    rows, size, width = out_ref.shape
    per = own_ref.shape[0]
    accs = {t: split_tiles(jnp.zeros((size, width), jnp.float32)) for t in range(rows)}
    for row in range(rows):
        at = row + REACH
        targets = [t for t in range(rows) if abs(row - t) <= REACH]
        half = row // per
        spectrum = early[half][row % per, start : start + size, :] if half < len(early) else own_ref[row % per]
        add_row(accs, spectrum, weight_ref[...], target_ref[at : at + 1, :], filter_ref[at], targets)
    for t in range(rows):
        out_ref[t] = jnp.concatenate(accs[t], axis=1)


def own_terms(own, early, start, weight, target, filters):
    per, size, width = own.shape
    return pl.pallas_call(
        functools.partial(own_kernel, start),
        in_specs=[pl.BlockSpec(memory_space=VMEM)] * (4 + len(early)),
        out_specs=pl.BlockSpec(memory_space=VMEM),
        out_shape=jax.ShapeDtypeStruct((per * (1 + len(early)), size, width), jnp.float32),
        compiler_params=pltpu.CompilerParams(vmem_limit_bytes=12 * 2**20),
        cost_estimate=NO_COST,
        name="own_terms",
    )(own, weight, target, filters, *early)


def add_halo(accs, sides, rows, weight_ref, target_ref, filter_ref):
    for side, base in sides:
        for h in range(REACH):
            at = base + h + REACH
            targets = [t for t in range(rows) if abs(base + h - t) <= REACH]
            add_row(
                accs,
                side[h].astype(jnp.float32),
                weight_ref[...],
                target_ref[at : at + 1, :],
                filter_ref[at],
                targets,
            )


def side_kernel(part_ref, first_ref, weight_ref, target_ref, filter_ref, *rest):
    out_ref = rest[-1]
    rows = part_ref.shape[0]
    even = lax.rem(lax.axis_index("polar"), 2) == 0

    def combine(base):
        accs = {t: split_tiles(part_ref[t]) for t in range(rows)}
        add_halo(accs, [(first_ref, base)], rows, weight_ref, target_ref, filter_ref)
        for t in range(rows):
            out_ref[t] = jnp.concatenate(accs[t], axis=1)

    pl.when(even)(lambda: combine(rows))
    pl.when(jnp.logical_not(even))(lambda: combine(-REACH))


def side_terms(own, first, weight, target, filters, after):
    return pl.pallas_call(
        side_kernel,
        in_specs=[pl.BlockSpec(memory_space=VMEM)] * 5 + [pl.BlockSpec(memory_space=pl.ANY)] * len(after),
        out_specs=pl.BlockSpec(memory_space=VMEM),
        out_shape=jax.ShapeDtypeStruct(own.shape, jnp.float32),
        compiler_params=pltpu.CompilerParams(vmem_limit_bytes=12 * 2**20),
        cost_estimate=NO_COST,
        name="side_terms",
    )(own, first, weight, target, filters, *after)


def finish_kernel(count, swaps, part_ref, *refs):
    halos, (weight_ref, target_ref, filter_ref, table_ref) = refs[:swaps], refs[swaps : swaps + 4]
    outs, stacked_ref = refs[-count - 1 : -1], refs[-1]
    rows, size, width = part_ref.shape
    even = lax.rem(lax.axis_index("polar"), 2) == 0

    def combine(bases):
        accs = {t: split_tiles(part_ref[t]) for t in range(rows)}
        sides = list(zip(halos, bases[-swaps:]))
        add_halo(accs, sides, rows, weight_ref, target_ref, filter_ref)
        for t in range(rows):
            stacked_ref[t * size : (t + 1) * size, :] = jnp.concatenate(accs[t], axis=1).astype(jnp.bfloat16)

    pl.when(even)(lambda: combine((rows, -REACH)))
    pl.when(jnp.logical_not(even))(lambda: combine((-REACH, rows)))
    grid = dot_nt(table_ref[...], stacked_ref[...])
    wide = grid.shape[0] // count
    for k, out in enumerate(outs):
        out[...] = grid[k * wide : k * wide + out.shape[0]].astype(jnp.bfloat16)


def finish(own, halos, weight, target, filters, table, count, part):
    rows, size, width = own.shape
    return pl.pallas_call(
        functools.partial(finish_kernel, count, len(halos)),
        in_specs=[pl.BlockSpec(memory_space=VMEM)] * (5 + len(halos)),
        out_specs=[pl.BlockSpec(memory_space=VMEM)] * count,
        out_shape=[jax.ShapeDtypeStruct((part, rows * size), jnp.bfloat16)] * count,
        scratch_shapes=[pltpu.VMEM((rows * size, width), jnp.bfloat16)],
        compiler_params=pltpu.CompilerParams(vmem_limit_bytes=12 * 2**20),
        cost_estimate=NO_COST,
        name="finish",
    )(own, *halos, weight, target, filters, table)


def add_kernel(count, chunk, steps, tiles, grad_ref, *refs):
    out_ref, tall_ref, done_ref, sems = refs[-4:]
    pieces = dict(zip(steps, refs))
    _, part, rows, _ = done_ref.shape
    start, size = chunk
    me = lax.axis_index("azimuth")

    def add(mine):
        order = [[k for k in range(count) if partner_static(mine, k, count, -1) == s][0] for s in range(count)]
        copies = []
        for at, tile in enumerate(tiles[mine]):
            lanes = range(tile * LANES, (tile + 1) * LANES)
            first = count * start + tile * LANES
            cut = round_up(part, 32) // 2
            for side, (low, high) in enumerate(((0, cut), (cut, part))):
                for row in range(rows):
                    parts = []
                    for s in owners(tile, size):
                        left, right = max(lanes[0], s * size), min(lanes[-1] + 1, (s + 1) * size)
                        base = (row - s) * size
                        parts.append(pieces[order[s]][low:high, base + left : base + right])
                    conv = jnp.concatenate(parts, axis=1).astype(jnp.float32)
                    total = grad_ref[row, low:high, first : first + LANES].astype(jnp.float32) + conv
                    tall_ref[at, pl.ds(low * rows + row, high - low, stride=rows), :] = total
                block = tall_ref[at, low * rows : high * rows, :].reshape(high - low, rows, LANES)
                done_ref[at, low:high] = block.astype(jnp.bfloat16)
                copies.append(
                    pltpu.make_async_copy(
                        done_ref.at[at, low:high],
                        out_ref.at[low:high, :, pl.ds(first, LANES)],
                        sems.at[2 * at + side],
                    )
                )
                copies[-1].start()
        for copy in copies:
            copy.wait()

    for mine in range(count):
        pl.when(me == mine)(functools.partial(add, mine))


def owners(tile, size):
    return range(tile * LANES // size, ((tile + 1) * LANES - 1) // size + 1)


def add_chunk(grad_out, pieces, chunk, count, tiles, before):
    rows, part, channels = grad_out.shape
    number = max(len(some) for some in tiles)
    needed = {
        k
        for mine in range(count)
        for tile in tiles[mine]
        for s in owners(tile, chunk[1])
        for k in range(count)
        if partner_static(mine, k, count, -1) == s
    }
    pieces = sorted(((k, pieces[k]) for k in needed), key=lambda item: item[0] <= NEAR)
    vmem = pl.BlockSpec(memory_space=VMEM)
    anywhere = pl.BlockSpec(memory_space=pl.ANY)
    return pl.pallas_call(
        functools.partial(add_kernel, count, chunk, [k for k, _ in pieces], tiles),
        in_specs=[vmem] * (1 + len(pieces)) + [anywhere] * len(before),
        out_specs=anywhere,
        out_shape=jax.ShapeDtypeStruct((part, rows, channels), jnp.bfloat16),
        scratch_shapes=[
            pltpu.VMEM((number, rows * part, LANES), jnp.float32),
            pltpu.VMEM((number, part, rows, LANES), jnp.bfloat16),
            pltpu.SemaphoreType.DMA((2 * number,)),
        ],
        input_output_aliases={1 + len(pieces): 0} if before else {},
        compiler_params=pltpu.CompilerParams(vmem_limit_bytes=12 * 2**20),
        cost_estimate=NO_COST,
        name="add_chunk",
    )(grad_out, *(block for _, block in pieces), *before)


def prepare_kernel(count, chunks, weight_ref, filt_ref, offset_ref, forth_ref, back_ref, *outs):
    filter_out, target_out, forth_out, back_out = outs[:4]
    me = lax.axis_index("azimuth")
    wide = back_ref.shape[0] // count
    for k in range(count):
        forth_out[k] = forth_ref[partner(me, k, count, -1)]
        first = pl.multiple_of(partner(me, k, count, 1) * wide, HALF)
        back_out[k * wide : (k + 1) * wide, :] = back_ref[pl.ds(first, wide), :]
    bases, channels = weight_ref.shape
    lats, width = filt_ref.shape[1:]
    ext, depth = target_out.shape
    rows = ext - 2 * REACH
    modes = width // 2
    whole = modes // LANES * LANES
    used = TERMS * bases
    for (start, size), out in zip(chunks, outs[4:]):
        first = count * start + lax.axis_index("azimuth") * size
        weight = pltpu.roll(weight_ref[...], lax.rem(channels - first, channels), 1)[:, :size]
        parts = []
        for _ in range(TERMS):
            rounded = weight.astype(jnp.bfloat16).astype(jnp.float32)
            parts.append(rounded)
            weight = weight - rounded
        parts.append(jnp.zeros((depth - used, size), jnp.float32))
        out[...] = jnp.concatenate(parts, axis=0).T
    start_lat = lax.axis_index("polar") * rows
    table = filt_ref[...].reshape(bases * lats, width)
    base = lax.broadcasted_iota(jnp.int32, (depth, bases * lats), 0)
    valid = base < used
    for _ in range(TERMS - 1):
        base = jnp.where(base >= bases, base - bases, base)
    column = lax.broadcasted_iota(jnp.int32, (depth, bases * lats), 1)
    for i in range(ext):
        lat = start_lat + (i - REACH)
        inside = (lat >= 0) & (lat < lats)
        lat = jnp.clip(lat, 0, lats - 1)
        pick = jnp.where(valid & (column == base * lats + lat), 1.0, 0.0).astype(jnp.bfloat16)
        row = dot_nn(pick, table)
        real, imag = row[:, :modes], row[:, modes:]
        rest_re, rest_im = real[:, whole:], imag[:, whole:]
        filter_out[i] = jnp.concatenate(
            [real[:, :whole], rest_re, rest_re, imag[:, :whole], rest_im, -rest_im], axis=1
        ).astype(jnp.bfloat16)
        local = jnp.where(inside, offset_ref[pl.ds(lat, 1), :] - start_lat, -1)
        spare = jnp.full((1, depth - used), -1, jnp.int32)
        target_out[i : i + 1, :] = jnp.concatenate([local] * TERMS + [spare], axis=1)


def prepare(basis_weight, filt, offsets, forth, back, rows, count, chunks):
    bases = filt.shape[0]
    width = filt.shape[2]
    ext = rows + 2 * REACH
    depth = round_up(TERMS * bases, 16)
    shapes = [
        jax.ShapeDtypeStruct((ext, depth, width + LANES), jnp.bfloat16),
        jax.ShapeDtypeStruct((ext, depth), jnp.int32),
        jax.ShapeDtypeStruct(forth.shape, forth.dtype),
        jax.ShapeDtypeStruct(back.shape, back.dtype),
    ] + [jax.ShapeDtypeStruct((size, depth), jnp.float32) for _, size in chunks]
    return pl.pallas_call(
        functools.partial(prepare_kernel, count, chunks),
        in_specs=[pl.BlockSpec(memory_space=VMEM)] * 5,
        out_specs=[pl.BlockSpec(memory_space=VMEM)] * len(shapes),
        out_shape=shapes,
        compiler_params=pltpu.CompilerParams(vmem_limit_bytes=16 * 2**20),
        cost_estimate=NO_COST,
        name="prepare",
    )(basis_weight, filt, offsets, forth, back)


def halo(first, second):
    bands, count = lax.axis_size("polar"), lax.axis_size("azimuth")
    blocks = []
    for odd, block in ((0, first), (1, second)):
        pairs = []
        for a in range(bands):
            other = ((a + odd) ^ 1) - odd
            for b in range(count):
                paired = 0 <= other < bands
                target = (other, b) if paired else (a, b ^ 1 if b ^ 1 < count else b)
                pairs.append((a * count + b, target[0] * count + target[1]))
        blocks.append(lax.ppermute(block, ("polar", "azimuth"), pairs))
    return blocks


def on_device(chunks, conv_out, grad_out, w_in, b_in, w_out, basis_weight, filt, offsets):
    rows, part, channels = conv_out.shape
    count = lax.axis_size("azimuth")
    forth, back = tables(count, part, filt.shape[2] // 2)
    forth, back = jnp.asarray(forth), jnp.asarray(back)
    owned = channels // count
    halves = 2 if rows % 2 == 0 else 1
    wide = round_up(part, HALF)
    filters, target, forth, back, *weights = prepare(
        basis_weight, filt, offsets, forth, back, rows, count, chunks
    )
    early, order = [], []
    for half in range(halves):
        final = half == halves - 1
        sent = [(k, 0, owned) for k in range(count)]
        if final:
            sent[1:] = [(k,) + chunk for chunk in chunks for k in range(1, count)]
        blocks = mlp(conv_out, grad_out, w_in, b_in, w_out, count, half, halves, sent, chunks, order)
        order = blocks[:1]
        if not final:
            early.append(analyze_early([exchange(blocks[k], k, count) for k in range(count)], forth, wide))
    spectra, terms, returned = {}, {}, {}
    for q, (start, size) in enumerate(chunks):
        mine = blocks[1 + q * (count - 1) : 1 + (q + 1) * (count - 1)]
        pieces = [blocks[0]] + [exchange(block, k, count) for k, block in enumerate(mine, 1)]
        after = [terms[q - 1]] if q else []
        own, first, second = analyze(pieces, forth, early, rows, wide, (start, size), after)
        spectra[q] = halo(first, second)
        terms[q] = own_terms(own, early, start, weights[q], target, filters)
    for q in range(len(chunks)):
        halos = spectra[q]
        if q == 0:
            others = [terms[other] for other in terms if other > q]
            terms[q] = side_terms(terms[q], halos[0], weights[q], target, filters, others)
            halos = halos[1:]
        grids = finish(terms[q], halos, weights[q], target, filters, back, count, part)
        returned[q] = {k: exchange(grids[k], k, count) for k in range(count)}
    total = []
    for q, chunk in enumerate(chunks):
        tiles = [list(range(count * chunk[1] // LANES)) for _ in range(count)]
        if q == len(chunks) - 1:
            chip = [{mine, partner_static(mine, NEAR, count, -1)} for mine in range(count)]
            close = [[t for t in tiles[mine] if set(owners(t, chunk[1])) <= chip[mine]] for mine in range(count)]
            if any(close):
                total = [add_chunk(grad_out, returned[q], chunk, count, close, total)]
                tiles = [[t for t in tiles[mine] if t not in close[mine]] for mine in range(count)]
        total = [add_chunk(grad_out, returned[q], chunk, count, tiles, total)]
    return jnp.transpose(total[0], (1, 0, 2))


def solution(mesh):
    grid = P(("member", "polar"), "azimuth", None)

    def run(conv_out, grad_out, *others):
        owned = conv_out.shape[2] // mesh.shape["azimuth"]
        sizes = [owned]
        if owned % 32 == 0 and owned >= 96:
            big = owned * 3 // 5 // 32 * 32
            sizes = [big, owned - big]
        chunks = tuple((sum(sizes[:q]), size) for q, size in enumerate(sizes))
        return jax.shard_map(
            functools.partial(on_device, chunks),
            mesh=mesh,
            in_specs=(grid, grid) + (P(),) * 6,
            out_specs=grid,
            check_vma=False,
        )(conv_out, grad_out, *others)

    return run
```

```python
import functools
import math

import jax
import jax.numpy as jnp
import ml_dtypes
import numpy as np
from jax import lax
from jax.experimental import pallas as pl
from jax.experimental.pallas import tpu as pltpu
from jax.sharding import PartitionSpec as P

REACH = 3
LANES = 128
HALF = 64
TERMS = 3
NEAR = 1
VMEM = pltpu.MemorySpace.VMEM
NO_COST = pl.CostEstimate(flops=0, bytes_accessed=0, transcendentals=0)


def round_up(value, unit):
    return -(-value // unit) * unit


def partner(me, step, count, sign):
    if count & (count - 1) == 0:
        return me ^ step
    return lax.rem(me + sign * step + count, count)


def far_first(number, count):
    return sorted(range(number), key=lambda i: (i // count, i % count <= NEAR))


def exchange(block, step, count):
    if step == 0:
        return block
    pairs = [(a, int(partner_static(a, step, count))) for a in range(count)]
    return lax.ppermute(block, "azimuth", pairs)


def partner_static(a, step, count, sign=1):
    return a ^ step if count & (count - 1) == 0 else (a + sign * step) % count


def tables(count, part, modes):
    length = count * part
    whole = modes // LANES * LANES
    order = np.concatenate(
        [
            np.arange(whole),
            modes + np.arange(whole),
            np.arange(whole, modes),
            modes + np.arange(whole, modes),
        ]
    )
    positions = np.arange(length)
    waves = np.arange(modes)
    phase = (positions[:, None] * waves[None, :]) % length
    angle = (2.0 * math.pi / length) * phase
    scale = 1.0 / math.sqrt(length)
    factor = np.where(waves == 0, 1.0, 2.0)
    analysis = np.concatenate([np.cos(angle), -np.sin(angle)], axis=1) * scale
    synth = np.concatenate([np.cos(angle) * factor, -np.sin(angle) * factor], axis=1) * scale
    analysis = analysis.astype(np.float32).astype(ml_dtypes.bfloat16)[:, order]
    synth = synth.astype(np.float32).astype(ml_dtypes.bfloat16)[:, order]
    wide = round_up(part, HALF)
    window = round_up(HALF + wide, LANES)
    forth = np.zeros((count, HALF + window, 2 * modes), ml_dtypes.bfloat16)
    back = np.zeros((count * wide, 2 * modes), ml_dtypes.bfloat16)
    for s in range(count):
        forth[s, HALF : HALF + part] = analysis[s * part : (s + 1) * part]
        back[s * wide : s * wide + part] = synth[s * part : (s + 1) * part]
    return forth, back


def twice_gelu_slope(scaled):
    power = math.log2(2.0 / math.sqrt(math.pi)) - (1.0 / math.log(2.0)) * (scaled * scaled)
    return (1.0 + lax.erf(scaled)) + scaled * jnp.exp2(power)


def dot_nt(left, right):
    return lax.dot_general(left, right, (((1,), (1,)), ((), ())), preferred_element_type=jnp.float32)


def dot_nn(left, right):
    return jnp.dot(left, right, preferred_element_type=jnp.float32)


def mlp_kernel(count, half, sent, chunks, conv_ref, grad_ref, win_ref, bias_ref, wout_ref, *rest):
    outs, (tall_conv, tall_grad, pre_ref, back_ref, slope_ref, total_ref) = rest[-6 - len(sent) : -6], rest[-6:]
    part, channels = conv_ref.shape[1:]
    wide = round_up(part, HALF)
    rows = tall_conv.shape[0] // wide
    owned = channels // count
    block = pre_ref.shape[2]
    steps = win_ref.shape[1] // block
    me = lax.axis_index("azimuth")
    def stack(tall, source):
        for row in range(rows):
            whole = part // 16 * 16
            tall[row * wide + whole : (row + 1) * wide, :] = jnp.zeros((wide - whole, channels), jnp.bfloat16)
            tall[row * wide : row * wide + part, :] = source[half * rows + row]

    group = 96
    groups = rows * wide // group

    def span(step):
        return slice(step * block, (step + 1) * block)

    def project_pre(step):
        pre_ref[step % 2] = dot_nn(tall_conv[...], win_ref[:, span(step)])

    def project_back(step):
        back_ref[step % 2] = dot_nt(tall_grad[...], wout_ref[span(step), :])

    def slope(step, first, last):
        root = math.sqrt(0.5)
        bias = bias_ref[span(step)].reshape(1, block) * root
        for g in range(first, last):
            some = slice(g * group, (g + 1) * group)
            value = back_ref[step % 2, some, :] * twice_gelu_slope(pre_ref[step % 2, some, :] * root + bias)
            slope_ref[some, span(step)] = value.astype(jnp.bfloat16)

    def gather(first, last):
        at = slice(first * block, last * block)
        term = dot_nt(win_ref[:, at], slope_ref[:, at])
        total_ref[...] = term if first == 0 else total_ref[...] + term

    stack(tall_conv, conv_ref)
    project_pre(0)
    stack(tall_grad, grad_ref)
    project_back(0)
    gathered = 0
    thirds = [groups * n // 4 for n in (0, 1, 3, 4)]
    for step in range(steps):
        if step + 1 < steps:
            project_pre(step + 1)
        slope(step, thirds[0], thirds[1])
        if step - gathered == 2:
            gather(gathered, step)
            gathered = step
        slope(step, thirds[1], thirds[2])
        if step + 1 < steps:
            project_back(step + 1)
        slope(step, thirds[2], thirds[3])
    gather(gathered, steps)
    for out, (k, start, size) in zip(outs, sent):
        target = partner(me, k, count, 1)
        for begin, width in chunks:
            if start <= begin < start + size:
                first = pl.multiple_of(count * begin + target * width, 32)
                value = 0.5 * total_ref[pl.ds(first, width), :]
                out[begin - start : begin - start + width, :] = value.astype(jnp.bfloat16)


def mlp(conv_out, grad_out, w_in, b_in, w_out, count, half, halves, sent, chunks, after):
    rows, part, channels = conv_out.shape
    rows //= halves
    block = 256
    wide = round_up(part, HALF)
    vmem = pl.BlockSpec(memory_space=VMEM)
    out_shape = [jax.ShapeDtypeStruct((size, rows * wide), jnp.bfloat16) for _, _, size in sent]
    return pl.pallas_call(
        functools.partial(mlp_kernel, count, half, sent, chunks),
        in_specs=[vmem] * 5 + [pl.BlockSpec(memory_space=pl.ANY)] * len(after),
        out_specs=[vmem] * len(out_shape),
        out_shape=out_shape,
        scratch_shapes=[
            pltpu.VMEM((rows * wide, channels), jnp.bfloat16),
            pltpu.VMEM((rows * wide, channels), jnp.bfloat16),
            pltpu.VMEM((2, rows * wide, block), jnp.float32),
            pltpu.VMEM((2, rows * wide, block), jnp.float32),
            pltpu.VMEM((rows * wide, w_in.shape[1]), jnp.bfloat16),
            pltpu.VMEM((channels, rows * wide), jnp.float32),
        ],
        compiler_params=pltpu.CompilerParams(vmem_limit_bytes=16 * 2**20),
        cost_estimate=NO_COST,
        name="mlp",
    )(conv_out, grad_out, w_in, b_in, w_out, *after)


def spectra_of(pieces, channels, table_ref, wide):
    size = channels[1]
    rows = pieces[0][0].shape[1] // wide
    window = table_ref.shape[1] - HALF
    shifts = [row * wide % LANES for row in range(rows)]
    spectra = [None] * rows
    for shift in sorted(set(shifts)):
        group = [row for row in range(rows) if shifts[row] == shift]
        total = None
        for k, (piece, base) in enumerate(pieces):
            windows = [row * wide // LANES * LANES for row in group]
            left = jnp.concatenate([piece[base : base + size, at : at + window] for at in windows], axis=0)
            term = dot_nn(left, table_ref[k, HALF - shift : HALF - shift + window, :])
            total = term if total is None else total + term
        for at, row in enumerate(group):
            spectra[row] = total[at * size : (at + 1) * size]
    return spectra


def early_kernel(count, wide, *refs):
    ranks = far_first(count, count)
    pieces = [(refs[ranks.index(k)], 0) for k in range(count)]
    table_ref, out_ref = refs[count], refs[-1]
    for row, spectrum in enumerate(spectra_of(pieces, (0, pieces[0][0].shape[0]), table_ref, wide)):
        out_ref[row] = spectrum


def analyze_early(pieces, table, wide):
    count = len(pieces)
    size, across = pieces[0].shape
    return pl.pallas_call(
        functools.partial(early_kernel, count, wide),
        in_specs=[pl.BlockSpec(memory_space=VMEM)] * (count + 1),
        out_specs=pl.BlockSpec(memory_space=VMEM),
        out_shape=jax.ShapeDtypeStruct((across // wide, size, table.shape[2]), jnp.float32),
        compiler_params=pltpu.CompilerParams(vmem_limit_bytes=12 * 2**20),
        cost_estimate=NO_COST,
        name="analysis_early",
    )(*(pieces[k] for k in far_first(count, count)), table)


def analysis_kernel(count, rows, wide, chunk, halves, *refs):
    own_ref, first_ref, second_ref = refs[-3:]
    start, size = chunk
    ranks = far_first(count, count)
    pieces = [(refs[ranks.index(k)], 0 if k else start) for k in range(count)]
    table_ref, early = refs[count], refs[count + 1 : count + halves]
    per = rows // halves
    even = lax.rem(lax.axis_index("polar"), 2) == 0
    for row, spectrum in enumerate(spectra_of(pieces, chunk, table_ref, wide)):
        own_ref[row] = spectrum

    def row_of(row):
        half, row = divmod(row, per)
        return own_ref[row] if half == halves - 1 else early[half][row, start : start + size, :]

    def share(above, below):
        for h in range(REACH):
            above[h] = row_of(rows - REACH + h).astype(jnp.bfloat16)
            below[h] = row_of(h).astype(jnp.bfloat16)

    pl.when(even)(lambda: share(first_ref, second_ref))
    pl.when(jnp.logical_not(even))(lambda: share(second_ref, first_ref))


def analyze(pieces, table, early, rows, wide, chunk, after):
    count = len(pieces)
    size = chunk[1]
    width = table.shape[2]
    halves = len(early) + 1
    halo = jax.ShapeDtypeStruct((REACH, size, width), jnp.bfloat16)
    return pl.pallas_call(
        functools.partial(analysis_kernel, count, rows, wide, chunk, halves),
        in_specs=[pl.BlockSpec(memory_space=VMEM)] * (count + halves)
        + [pl.BlockSpec(memory_space=pl.ANY)] * len(after),
        out_specs=[pl.BlockSpec(memory_space=VMEM)] * 3,
        out_shape=[jax.ShapeDtypeStruct((rows // halves, size, width), jnp.float32), halo, halo],
        compiler_params=pltpu.CompilerParams(vmem_limit_bytes=12 * 2**20),
        cost_estimate=NO_COST,
        name="analysis",
    )(*(pieces[k] for k in far_first(count, count)), table, *early, *after)


def add_row(accs, spectrum, weight, target_row, filter_row, targets):
    masked = jnp.concatenate([jnp.where(target_row == t, weight, 0.0) for t in targets], axis=0)
    add_gains(accs, spectrum, dot_nn(masked.astype(jnp.bfloat16), filter_row), targets)


def add_gains(accs, spectrum, gains, targets):
    size = spectrum.shape[0]
    whole = (gains.shape[1] // 2) // LANES * LANES - LANES
    spec_re = spectrum[:, :whole]
    spec_im = spectrum[:, whole : 2 * whole]
    spec_x = spectrum[:, 2 * whole :]
    swapped = pltpu.roll(spec_x, HALF, 1)
    for at, target in enumerate(targets):
        gain = gains[at * size : (at + 1) * size]
        gain_re = gain[:, :whole]
        gain_rx = gain[:, whole : whole + LANES]
        gain_im = gain[:, whole + LANES : 2 * whole + LANES]
        gain_ix = gain[:, 2 * whole + LANES :]
        acc_re, acc_im, acc_x = accs[target]
        acc_re = acc_re + (gain_re * spec_re + gain_im * spec_im)
        acc_im = acc_im + (gain_re * spec_im - gain_im * spec_re)
        acc_x = acc_x + (gain_rx * spec_x + gain_ix * swapped)
        accs[target] = acc_re, acc_im, acc_x


def split_tiles(value):
    whole = (value.shape[1] - LANES) // 2
    return value[:, :whole], value[:, whole : 2 * whole], value[:, 2 * whole :]


def own_kernel(start, own_ref, weight_ref, target_ref, filter_ref, *rest):
    early, out_ref = rest[:-1], rest[-1]
    rows, size, width = out_ref.shape
    per = own_ref.shape[0]
    accs = {t: split_tiles(jnp.zeros((size, width), jnp.float32)) for t in range(rows)}
    for row in range(rows):
        at = row + REACH
        targets = [t for t in range(rows) if abs(row - t) <= REACH]
        half = row // per
        spectrum = early[half][row % per, start : start + size, :] if half < len(early) else own_ref[row % per]
        add_row(accs, spectrum, weight_ref[...], target_ref[at : at + 1, :], filter_ref[at], targets)
    for t in range(rows):
        out_ref[t] = jnp.concatenate(accs[t], axis=1)


def own_terms(own, early, start, weight, target, filters):
    per, size, width = own.shape
    return pl.pallas_call(
        functools.partial(own_kernel, start),
        in_specs=[pl.BlockSpec(memory_space=VMEM)] * (4 + len(early)),
        out_specs=pl.BlockSpec(memory_space=VMEM),
        out_shape=jax.ShapeDtypeStruct((per * (1 + len(early)), size, width), jnp.float32),
        compiler_params=pltpu.CompilerParams(vmem_limit_bytes=12 * 2**20),
        cost_estimate=NO_COST,
        name="own_terms",
    )(own, weight, target, filters, *early)


def add_halo(accs, sides, rows, weight_ref, target_ref, filter_ref):
    rows_at = [(side, h, base + h) for side, base in sides for h in range(REACH)]
    size, depth = weight_ref.shape
    number = len(rows_at)
    weight = jnp.concatenate([weight_ref[...]] * number, axis=1)
    wanted = jnp.concatenate([target_ref[row + REACH : row + REACH + 1, :] for _, _, row in rows_at], axis=1)
    lane = lax.broadcasted_iota(jnp.int32, wanted.shape, 1)
    left, reached = [], []
    for i, (_, _, row) in enumerate(rows_at):
        reached.append([t for t in range(rows) if abs(row - t) <= REACH])
        mine = jnp.where((lane >= i * depth) & (lane < (i + 1) * depth), wanted, -1)
        left += [jnp.where(mine == t, weight, 0.0).astype(jnp.bfloat16) for t in reached[i]]
    filters = jnp.concatenate([filter_ref[row + REACH] for _, _, row in rows_at], axis=0)
    gains = dot_nn(jnp.concatenate(left, axis=0), filters)
    first = 0
    for (side, h, _), targets in zip(rows_at, reached):
        last = first + len(targets) * size
        add_gains(accs, side[h].astype(jnp.float32), gains[first:last], targets)
        first = last


def side_kernel(part_ref, first_ref, weight_ref, target_ref, filter_ref, *rest):
    out_ref = rest[-1]
    rows = part_ref.shape[0]
    even = lax.rem(lax.axis_index("polar"), 2) == 0

    def combine(base):
        accs = {t: split_tiles(part_ref[t]) for t in range(rows)}
        add_halo(accs, [(first_ref, base)], rows, weight_ref, target_ref, filter_ref)
        for t in range(rows):
            out_ref[t] = jnp.concatenate(accs[t], axis=1)

    pl.when(even)(lambda: combine(rows))
    pl.when(jnp.logical_not(even))(lambda: combine(-REACH))


def side_terms(own, first, weight, target, filters, after):
    return pl.pallas_call(
        side_kernel,
        in_specs=[pl.BlockSpec(memory_space=VMEM)] * 5 + [pl.BlockSpec(memory_space=pl.ANY)] * len(after),
        out_specs=pl.BlockSpec(memory_space=VMEM),
        out_shape=jax.ShapeDtypeStruct(own.shape, jnp.float32),
        compiler_params=pltpu.CompilerParams(vmem_limit_bytes=12 * 2**20),
        cost_estimate=NO_COST,
        name="side_terms",
    )(own, first, weight, target, filters, *after)


def finish_kernel(count, swaps, part_ref, *refs):
    halos, (weight_ref, target_ref, filter_ref, table_ref) = refs[:swaps], refs[swaps : swaps + 4]
    outs, stacked_ref = refs[-count - 1 : -1], refs[-1]
    rows, size, width = part_ref.shape
    even = lax.rem(lax.axis_index("polar"), 2) == 0

    def combine(bases):
        accs = {t: split_tiles(part_ref[t]) for t in range(rows)}
        sides = list(zip(halos, bases[-swaps:]))
        add_halo(accs, sides, rows, weight_ref, target_ref, filter_ref)
        for t in range(rows):
            stacked_ref[t * size : (t + 1) * size, :] = jnp.concatenate(accs[t], axis=1).astype(jnp.bfloat16)

    pl.when(even)(lambda: combine((rows, -REACH)))
    pl.when(jnp.logical_not(even))(lambda: combine((-REACH, rows)))
    grid = dot_nt(table_ref[...], stacked_ref[...])
    wide = grid.shape[0] // count
    for k, out in enumerate(outs):
        out[...] = grid[k * wide : k * wide + out.shape[0]].astype(jnp.bfloat16)


def finish(own, halos, weight, target, filters, table, count, part):
    rows, size, width = own.shape
    return pl.pallas_call(
        functools.partial(finish_kernel, count, len(halos)),
        in_specs=[pl.BlockSpec(memory_space=VMEM)] * (5 + len(halos)),
        out_specs=[pl.BlockSpec(memory_space=VMEM)] * count,
        out_shape=[jax.ShapeDtypeStruct((part, rows * size), jnp.bfloat16)] * count,
        scratch_shapes=[pltpu.VMEM((rows * size, width), jnp.bfloat16)],
        compiler_params=pltpu.CompilerParams(vmem_limit_bytes=12 * 2**20),
        cost_estimate=NO_COST,
        name="finish",
    )(own, *halos, weight, target, filters, table)


def add_kernel(count, chunk, steps, tiles, grad_ref, *refs):
    out_ref, tall_ref, done_ref, sems = refs[-4:]
    pieces = dict(zip(steps, refs))
    _, part, rows, _ = done_ref.shape
    start, size = chunk
    me = lax.axis_index("azimuth")

    def add(mine):
        order = [[k for k in range(count) if partner_static(mine, k, count, -1) == s][0] for s in range(count)]
        copies = []
        for at, tile in enumerate(tiles[mine]):
            lanes = range(tile * LANES, (tile + 1) * LANES)
            first = count * start + tile * LANES
            cut = round_up(part, 32) // 2
            for side, (low, high) in enumerate(((0, cut), (cut, part))):
                for row in range(rows):
                    parts = []
                    for s in owners(tile, size):
                        left, right = max(lanes[0], s * size), min(lanes[-1] + 1, (s + 1) * size)
                        base = (row - s) * size
                        parts.append(pieces[order[s]][low:high, base + left : base + right])
                    conv = jnp.concatenate(parts, axis=1).astype(jnp.float32)
                    total = grad_ref[row, low:high, first : first + LANES].astype(jnp.float32) + conv
                    tall_ref[at, pl.ds(low * rows + row, high - low, stride=rows), :] = total
                block = tall_ref[at, low * rows : high * rows, :].reshape(high - low, rows, LANES)
                done_ref[at, low:high] = block.astype(jnp.bfloat16)
                copies.append(
                    pltpu.make_async_copy(
                        done_ref.at[at, low:high],
                        out_ref.at[low:high, :, pl.ds(first, LANES)],
                        sems.at[2 * at + side],
                    )
                )
                copies[-1].start()
        for copy in copies:
            copy.wait()

    for mine in range(count):
        pl.when(me == mine)(functools.partial(add, mine))


def owners(tile, size):
    return range(tile * LANES // size, ((tile + 1) * LANES - 1) // size + 1)


def add_chunk(grad_out, pieces, chunk, count, tiles, before):
    rows, part, channels = grad_out.shape
    number = max(len(some) for some in tiles)
    needed = {
        k
        for mine in range(count)
        for tile in tiles[mine]
        for s in owners(tile, chunk[1])
        for k in range(count)
        if partner_static(mine, k, count, -1) == s
    }
    pieces = sorted(((k, pieces[k]) for k in needed), key=lambda item: item[0] <= NEAR)
    vmem = pl.BlockSpec(memory_space=VMEM)
    anywhere = pl.BlockSpec(memory_space=pl.ANY)
    return pl.pallas_call(
        functools.partial(add_kernel, count, chunk, [k for k, _ in pieces], tiles),
        in_specs=[vmem] * (1 + len(pieces)) + [anywhere] * len(before),
        out_specs=anywhere,
        out_shape=jax.ShapeDtypeStruct((part, rows, channels), jnp.bfloat16),
        scratch_shapes=[
            pltpu.VMEM((number, rows * part, LANES), jnp.float32),
            pltpu.VMEM((number, part, rows, LANES), jnp.bfloat16),
            pltpu.SemaphoreType.DMA((2 * number,)),
        ],
        input_output_aliases={1 + len(pieces): 0} if before else {},
        compiler_params=pltpu.CompilerParams(vmem_limit_bytes=12 * 2**20),
        cost_estimate=NO_COST,
        name="add_chunk",
    )(grad_out, *(block for _, block in pieces), *before)


def prepare_kernel(count, chunks, weight_ref, filt_ref, offset_ref, forth_ref, back_ref, *outs):
    filter_out, target_out, forth_out, back_out = outs[:4]
    me = lax.axis_index("azimuth")
    wide = back_ref.shape[0] // count
    for k in range(count):
        forth_out[k] = forth_ref[partner(me, k, count, -1)]
        first = pl.multiple_of(partner(me, k, count, 1) * wide, HALF)
        back_out[k * wide : (k + 1) * wide, :] = back_ref[pl.ds(first, wide), :]
    bases, channels = weight_ref.shape
    lats, width = filt_ref.shape[1:]
    ext, depth = target_out.shape
    rows = ext - 2 * REACH
    modes = width // 2
    whole = modes // LANES * LANES
    used = TERMS * bases
    for (start, size), out in zip(chunks, outs[4:]):
        first = count * start + lax.axis_index("azimuth") * size
        weight = pltpu.roll(weight_ref[...], lax.rem(channels - first, channels), 1)[:, :size]
        parts = []
        for _ in range(TERMS):
            rounded = weight.astype(jnp.bfloat16).astype(jnp.float32)
            parts.append(rounded)
            weight = weight - rounded
        parts.append(jnp.zeros((depth - used, size), jnp.float32))
        out[...] = jnp.concatenate(parts, axis=0).T
    start_lat = lax.axis_index("polar") * rows
    table = filt_ref[...].reshape(bases * lats, width)
    base = lax.broadcasted_iota(jnp.int32, (depth, bases * lats), 0)
    valid = base < used
    for _ in range(TERMS - 1):
        base = jnp.where(base >= bases, base - bases, base)
    column = lax.broadcasted_iota(jnp.int32, (depth, bases * lats), 1)
    for i in range(ext):
        lat = start_lat + (i - REACH)
        inside = (lat >= 0) & (lat < lats)
        lat = jnp.clip(lat, 0, lats - 1)
        pick = jnp.where(valid & (column == base * lats + lat), 1.0, 0.0).astype(jnp.bfloat16)
        row = dot_nn(pick, table)
        real, imag = row[:, :modes], row[:, modes:]
        rest_re, rest_im = real[:, whole:], imag[:, whole:]
        filter_out[i] = jnp.concatenate(
            [real[:, :whole], rest_re, rest_re, imag[:, :whole], rest_im, -rest_im], axis=1
        ).astype(jnp.bfloat16)
        local = jnp.where(inside, offset_ref[pl.ds(lat, 1), :] - start_lat, -1)
        spare = jnp.full((1, depth - used), -1, jnp.int32)
        target_out[i : i + 1, :] = jnp.concatenate([local] * TERMS + [spare], axis=1)


def prepare(basis_weight, filt, offsets, forth, back, rows, count, chunks):
    bases = filt.shape[0]
    width = filt.shape[2]
    ext = rows + 2 * REACH
    depth = round_up(TERMS * bases, 16)
    shapes = [
        jax.ShapeDtypeStruct((ext, depth, width + LANES), jnp.bfloat16),
        jax.ShapeDtypeStruct((ext, depth), jnp.int32),
        jax.ShapeDtypeStruct(forth.shape, forth.dtype),
        jax.ShapeDtypeStruct(back.shape, back.dtype),
    ] + [jax.ShapeDtypeStruct((size, depth), jnp.float32) for _, size in chunks]
    return pl.pallas_call(
        functools.partial(prepare_kernel, count, chunks),
        in_specs=[pl.BlockSpec(memory_space=VMEM)] * 5,
        out_specs=[pl.BlockSpec(memory_space=VMEM)] * len(shapes),
        out_shape=shapes,
        compiler_params=pltpu.CompilerParams(vmem_limit_bytes=16 * 2**20),
        cost_estimate=NO_COST,
        name="prepare",
    )(basis_weight, filt, offsets, forth, back)


def halo(first, second):
    bands, count = lax.axis_size("polar"), lax.axis_size("azimuth")
    blocks = []
    for odd, block in ((0, first), (1, second)):
        pairs = []
        for a in range(bands):
            other = ((a + odd) ^ 1) - odd
            for b in range(count):
                paired = 0 <= other < bands
                target = (other, b) if paired else (a, b ^ 1 if b ^ 1 < count else b)
                pairs.append((a * count + b, target[0] * count + target[1]))
        blocks.append(lax.ppermute(block, ("polar", "azimuth"), pairs))
    return blocks


def on_device(chunks, conv_out, grad_out, w_in, b_in, w_out, basis_weight, filt, offsets):
    rows, part, channels = conv_out.shape
    count = lax.axis_size("azimuth")
    forth, back = tables(count, part, filt.shape[2] // 2)
    forth, back = jnp.asarray(forth), jnp.asarray(back)
    owned = channels // count
    halves = 2 if rows % 2 == 0 else 1
    wide = round_up(part, HALF)
    filters, target, forth, back, *weights = prepare(
        basis_weight, filt, offsets, forth, back, rows, count, chunks
    )
    early, order = [], []
    for half in range(halves):
        final = half == halves - 1
        sent = [(k, 0, owned) for k in range(count)]
        if final:
            sent[1:] = [(k,) + chunk for chunk in chunks for k in range(1, count)]
        blocks = mlp(conv_out, grad_out, w_in, b_in, w_out, count, half, halves, sent, chunks, order)
        order = blocks[:1]
        if not final:
            early.append(analyze_early([exchange(blocks[k], k, count) for k in range(count)], forth, wide))
    spectra, terms, returned = {}, {}, {}
    for q, (start, size) in enumerate(chunks):
        mine = blocks[1 + q * (count - 1) : 1 + (q + 1) * (count - 1)]
        pieces = [blocks[0]] + [exchange(block, k, count) for k, block in enumerate(mine, 1)]
        after = [terms[q - 1]] if q else []
        own, first, second = analyze(pieces, forth, early, rows, wide, (start, size), after)
        spectra[q] = halo(first, second)
        terms[q] = own_terms(own, early, start, weights[q], target, filters)
    for q in range(len(chunks)):
        halos = spectra[q]
        if q == 0:
            others = [terms[other] for other in terms if other > q]
            terms[q] = side_terms(terms[q], halos[0], weights[q], target, filters, others)
            halos = halos[1:]
        grids = finish(terms[q], halos, weights[q], target, filters, back, count, part)
        returned[q] = {k: exchange(grids[k], k, count) for k in range(count)}
    total = []
    for q, chunk in enumerate(chunks):
        tiles = [list(range(count * chunk[1] // LANES)) for _ in range(count)]
        if q == len(chunks) - 1:
            chip = [{mine, partner_static(mine, NEAR, count, -1)} for mine in range(count)]
            close = [[t for t in tiles[mine] if set(owners(t, chunk[1])) <= chip[mine]] for mine in range(count)]
            if any(close):
                total = [add_chunk(grad_out, returned[q], chunk, count, close, total)]
                tiles = [[t for t in tiles[mine] if t not in close[mine]] for mine in range(count)]
        total = [add_chunk(grad_out, returned[q], chunk, count, tiles, total)]
    return jnp.transpose(total[0], (1, 0, 2))


def solution(mesh):
    grid = P(("member", "polar"), "azimuth", None)

    def run(conv_out, grad_out, *others):
        owned = conv_out.shape[2] // mesh.shape["azimuth"]
        sizes = [owned]
        if owned % 32 == 0 and owned >= 96:
            big = owned * 3 // 5 // 32 * 32
            sizes = [big, owned - big]
        chunks = tuple((sum(sizes[:q]), size) for q, size in enumerate(sizes))
        return jax.shard_map(
            functools.partial(on_device, chunks),
            mesh=mesh,
            in_specs=(grid, grid) + (P(),) * 6,
            out_specs=grid,
            check_vma=False,
        )(conv_out, grad_out, *others)

    return run
```

```python
import functools
import math

import jax
import jax.numpy as jnp
import ml_dtypes
import numpy as np
from jax import lax
from jax.experimental import pallas as pl
from jax.experimental.pallas import tpu as pltpu
from jax.sharding import PartitionSpec as P

REACH = 3
LANES = 128
HALF = 64
TERMS = 3
NEAR = 1
VMEM = pltpu.MemorySpace.VMEM
NO_COST = pl.CostEstimate(flops=0, bytes_accessed=0, transcendentals=0)


def round_up(value, unit):
    return -(-value // unit) * unit


def partner(me, step, count, sign):
    if count & (count - 1) == 0:
        return me ^ step
    return lax.rem(me + sign * step + count, count)


def far_first(number, count):
    return sorted(range(number), key=lambda i: (i // count, i % count <= NEAR))


def exchange(block, step, count):
    if step == 0:
        return block
    pairs = [(a, int(partner_static(a, step, count))) for a in range(count)]
    return lax.ppermute(block, "azimuth", pairs)


def partner_static(a, step, count, sign=1):
    return a ^ step if count & (count - 1) == 0 else (a + sign * step) % count


def tables(count, part, modes):
    length = count * part
    whole = modes // LANES * LANES
    order = np.concatenate(
        [
            np.arange(whole),
            modes + np.arange(whole),
            np.arange(whole, modes),
            modes + np.arange(whole, modes),
        ]
    )
    positions = np.arange(length)
    waves = np.arange(modes)
    phase = (positions[:, None] * waves[None, :]) % length
    angle = (2.0 * math.pi / length) * phase
    scale = 1.0 / math.sqrt(length)
    factor = np.where(waves == 0, 1.0, 2.0)
    analysis = np.concatenate([np.cos(angle), -np.sin(angle)], axis=1) * scale
    synth = np.concatenate([np.cos(angle) * factor, -np.sin(angle) * factor], axis=1) * scale
    analysis = analysis.astype(np.float32).astype(ml_dtypes.bfloat16)[:, order]
    synth = synth.astype(np.float32).astype(ml_dtypes.bfloat16)[:, order]
    wide = round_up(part, HALF)
    window = round_up(HALF + wide, LANES)
    forth = np.zeros((count, HALF + window, 2 * modes), ml_dtypes.bfloat16)
    back = np.zeros((count * wide, 2 * modes), ml_dtypes.bfloat16)
    for s in range(count):
        forth[s, HALF : HALF + part] = analysis[s * part : (s + 1) * part]
        back[s * wide : s * wide + part] = synth[s * part : (s + 1) * part]
    return forth, back


def twice_gelu_slope(scaled):
    power = math.log2(2.0 / math.sqrt(math.pi)) - (1.0 / math.log(2.0)) * (scaled * scaled)
    return (1.0 + lax.erf(scaled)) + scaled * jnp.exp2(power)


def dot_nt(left, right):
    return lax.dot_general(left, right, (((1,), (1,)), ((), ())), preferred_element_type=jnp.float32)


def dot_nn(left, right):
    return jnp.dot(left, right, preferred_element_type=jnp.float32)


def mlp_kernel(count, half, sent, chunks, conv_ref, grad_ref, win_ref, bias_ref, wout_ref, *rest):
    outs, (tall_conv, tall_grad, pre_ref, back_ref, slope_ref, total_ref) = rest[-6 - len(sent) : -6], rest[-6:]
    part, channels = conv_ref.shape[1:]
    wide = round_up(part, HALF)
    rows = tall_conv.shape[0] // wide
    owned = channels // count
    block = pre_ref.shape[2]
    steps = win_ref.shape[1] // block
    me = lax.axis_index("azimuth")
    def stack(tall, source):
        for row in range(rows):
            whole = part // 16 * 16
            tall[row * wide + whole : (row + 1) * wide, :] = jnp.zeros((wide - whole, channels), jnp.bfloat16)
            tall[row * wide : row * wide + part, :] = source[half * rows + row]

    group = 96
    groups = rows * wide // group

    def span(step):
        return slice(step * block, (step + 1) * block)

    def project_pre(step):
        pre_ref[step % 2] = dot_nn(tall_conv[...], win_ref[:, span(step)])

    def project_back(step):
        back_ref[step % 2] = dot_nt(tall_grad[...], wout_ref[span(step), :])

    def slope(step, first, last):
        root = math.sqrt(0.5)
        bias = bias_ref[span(step)].reshape(1, block) * root
        for g in range(first, last):
            some = slice(g * group, (g + 1) * group)
            value = back_ref[step % 2, some, :] * twice_gelu_slope(pre_ref[step % 2, some, :] * root + bias)
            slope_ref[some, span(step)] = value.astype(jnp.bfloat16)

    def gather(first, last):
        at = slice(first * block, last * block)
        term = dot_nt(win_ref[:, at], slope_ref[:, at])
        total_ref[...] = term if first == 0 else total_ref[...] + term

    stack(tall_conv, conv_ref)
    project_pre(0)
    stack(tall_grad, grad_ref)
    project_back(0)
    gathered = 0
    thirds = [groups * n // 4 for n in (0, 1, 3, 4)]
    for step in range(steps):
        if step + 1 < steps:
            project_pre(step + 1)
        slope(step, thirds[0], thirds[1])
        if step - gathered == 2:
            gather(gathered, step)
            gathered = step
        slope(step, thirds[1], thirds[2])
        if step + 1 < steps:
            project_back(step + 1)
        slope(step, thirds[2], thirds[3])
    gather(gathered, steps)
    for out, (k, start, size) in zip(outs, sent):
        target = partner(me, k, count, 1)
        for begin, width in chunks:
            if start <= begin < start + size:
                first = pl.multiple_of(count * begin + target * width, 32)
                value = 0.5 * total_ref[pl.ds(first, width), :]
                out[begin - start : begin - start + width, :] = value.astype(jnp.bfloat16)


def mlp(conv_out, grad_out, w_in, b_in, w_out, count, half, halves, sent, chunks, after):
    rows, part, channels = conv_out.shape
    rows //= halves
    block = 256
    wide = round_up(part, HALF)
    vmem = pl.BlockSpec(memory_space=VMEM)
    out_shape = [jax.ShapeDtypeStruct((size, rows * wide), jnp.bfloat16) for _, _, size in sent]
    return pl.pallas_call(
        functools.partial(mlp_kernel, count, half, sent, chunks),
        in_specs=[vmem] * 5 + [pl.BlockSpec(memory_space=pl.ANY)] * len(after),
        out_specs=[vmem] * len(out_shape),
        out_shape=out_shape,
        scratch_shapes=[
            pltpu.VMEM((rows * wide, channels), jnp.bfloat16),
            pltpu.VMEM((rows * wide, channels), jnp.bfloat16),
            pltpu.VMEM((2, rows * wide, block), jnp.float32),
            pltpu.VMEM((2, rows * wide, block), jnp.float32),
            pltpu.VMEM((rows * wide, w_in.shape[1]), jnp.bfloat16),
            pltpu.VMEM((channels, rows * wide), jnp.float32),
        ],
        compiler_params=pltpu.CompilerParams(vmem_limit_bytes=16 * 2**20),
        cost_estimate=NO_COST,
        name="mlp",
    )(conv_out, grad_out, w_in, b_in, w_out, *after)


def spectra_of(pieces, channels, table_ref, wide):
    size = channels[1]
    rows = pieces[0][0].shape[1] // wide
    window = table_ref.shape[1] - HALF
    shifts = [row * wide % LANES for row in range(rows)]
    spectra = [None] * rows
    for shift in sorted(set(shifts)):
        group = [row for row in range(rows) if shifts[row] == shift]
        total = None
        for k, (piece, base) in enumerate(pieces):
            windows = [row * wide // LANES * LANES for row in group]
            left = jnp.concatenate([piece[base : base + size, at : at + window] for at in windows], axis=0)
            term = dot_nn(left, table_ref[k, HALF - shift : HALF - shift + window, :])
            total = term if total is None else total + term
        for at, row in enumerate(group):
            spectra[row] = total[at * size : (at + 1) * size]
    return spectra


def early_kernel(count, wide, *refs):
    ranks = far_first(count, count)
    pieces = [(refs[ranks.index(k)], 0) for k in range(count)]
    table_ref, out_ref = refs[count], refs[-1]
    for row, spectrum in enumerate(spectra_of(pieces, (0, pieces[0][0].shape[0]), table_ref, wide)):
        out_ref[row] = spectrum


def analyze_early(pieces, table, wide):
    count = len(pieces)
    size, across = pieces[0].shape
    return pl.pallas_call(
        functools.partial(early_kernel, count, wide),
        in_specs=[pl.BlockSpec(memory_space=VMEM)] * (count + 1),
        out_specs=pl.BlockSpec(memory_space=VMEM),
        out_shape=jax.ShapeDtypeStruct((across // wide, size, table.shape[2]), jnp.float32),
        compiler_params=pltpu.CompilerParams(vmem_limit_bytes=12 * 2**20),
        cost_estimate=NO_COST,
        name="analysis_early",
    )(*(pieces[k] for k in far_first(count, count)), table)


def analysis_kernel(count, rows, wide, chunk, halves, *refs):
    own_ref, first_ref, second_ref = refs[-3:]
    start, size = chunk
    ranks = far_first(count, count)
    pieces = [(refs[ranks.index(k)], 0 if k else start) for k in range(count)]
    table_ref, early = refs[count], refs[count + 1 : count + halves]
    per = rows // halves
    even = lax.rem(lax.axis_index("polar"), 2) == 0
    for row, spectrum in enumerate(spectra_of(pieces, chunk, table_ref, wide)):
        own_ref[row] = spectrum

    def row_of(row):
        half, row = divmod(row, per)
        return own_ref[row] if half == halves - 1 else early[half][row, start : start + size, :]

    def share(above, below):
        for h in range(REACH):
            above[h] = row_of(rows - REACH + h).astype(jnp.bfloat16)
            below[h] = row_of(h).astype(jnp.bfloat16)

    pl.when(even)(lambda: share(first_ref, second_ref))
    pl.when(jnp.logical_not(even))(lambda: share(second_ref, first_ref))


def analyze(pieces, table, early, rows, wide, chunk, after):
    count = len(pieces)
    size = chunk[1]
    width = table.shape[2]
    halves = len(early) + 1
    halo = jax.ShapeDtypeStruct((REACH, size, width), jnp.bfloat16)
    return pl.pallas_call(
        functools.partial(analysis_kernel, count, rows, wide, chunk, halves),
        in_specs=[pl.BlockSpec(memory_space=VMEM)] * (count + halves)
        + [pl.BlockSpec(memory_space=pl.ANY)] * len(after),
        out_specs=[pl.BlockSpec(memory_space=VMEM)] * 3,
        out_shape=[jax.ShapeDtypeStruct((rows // halves, size, width), jnp.float32), halo, halo],
        compiler_params=pltpu.CompilerParams(vmem_limit_bytes=12 * 2**20),
        cost_estimate=NO_COST,
        name="analysis",
    )(*(pieces[k] for k in far_first(count, count)), table, *early, *after)


def add_row(accs, spectrum, weight, target_row, filter_row, targets):
    size = spectrum.shape[0]
    masked = jnp.concatenate([jnp.where(target_row == t, weight, 0.0) for t in targets], axis=0)
    gains = dot_nn(masked.astype(jnp.bfloat16), filter_row)
    whole = (gains.shape[1] // 2) // LANES * LANES - LANES
    spec_re = spectrum[:, :whole]
    spec_im = spectrum[:, whole : 2 * whole]
    spec_x = spectrum[:, 2 * whole :]
    swapped = pltpu.roll(spec_x, HALF, 1)
    for at, target in enumerate(targets):
        gain = gains[at * size : (at + 1) * size]
        gain_re = gain[:, :whole]
        gain_rx = gain[:, whole : whole + LANES]
        gain_im = gain[:, whole + LANES : 2 * whole + LANES]
        gain_ix = gain[:, 2 * whole + LANES :]
        acc_re, acc_im, acc_x = accs[target]
        acc_re = acc_re + (gain_re * spec_re + gain_im * spec_im)
        acc_im = acc_im + (gain_re * spec_im - gain_im * spec_re)
        acc_x = acc_x + (gain_rx * spec_x + gain_ix * swapped)
        accs[target] = acc_re, acc_im, acc_x


def split_tiles(value):
    whole = (value.shape[1] - LANES) // 2
    return value[:, :whole], value[:, whole : 2 * whole], value[:, 2 * whole :]


def own_kernel(start, own_ref, weight_ref, target_ref, filter_ref, *rest):
    early, out_ref = rest[:-1], rest[-1]
    rows, size, width = out_ref.shape
    per = own_ref.shape[0]
    accs = {t: split_tiles(jnp.zeros((size, width), jnp.float32)) for t in range(rows)}
    for row in range(rows):
        at = row + REACH
        targets = [t for t in range(rows) if abs(row - t) <= REACH]
        half = row // per
        spectrum = early[half][row % per, start : start + size, :] if half < len(early) else own_ref[row % per]
        add_row(accs, spectrum, weight_ref[...], target_ref[at : at + 1, :], filter_ref[at], targets)
    for t in range(rows):
        out_ref[t] = jnp.concatenate(accs[t], axis=1)


def own_terms(own, early, start, weight, target, filters):
    per, size, width = own.shape
    return pl.pallas_call(
        functools.partial(own_kernel, start),
        in_specs=[pl.BlockSpec(memory_space=VMEM)] * (4 + len(early)),
        out_specs=pl.BlockSpec(memory_space=VMEM),
        out_shape=jax.ShapeDtypeStruct((per * (1 + len(early)), size, width), jnp.float32),
        compiler_params=pltpu.CompilerParams(vmem_limit_bytes=12 * 2**20),
        cost_estimate=NO_COST,
        name="own_terms",
    )(own, weight, target, filters, *early)


def add_halo(accs, sides, rows, weight_ref, target_ref, filter_ref):
    for side, base in sides:
        for h in range(REACH):
            at = base + h + REACH
            targets = [t for t in range(rows) if abs(base + h - t) <= REACH]
            add_row(
                accs,
                side[h].astype(jnp.float32),
                weight_ref[...],
                target_ref[at : at + 1, :],
                filter_ref[at],
                targets,
            )


def side_kernel(part_ref, first_ref, weight_ref, target_ref, filter_ref, *rest):
    out_ref = rest[-1]
    rows = part_ref.shape[0]
    even = lax.rem(lax.axis_index("polar"), 2) == 0

    def combine(base):
        accs = {t: split_tiles(part_ref[t]) for t in range(rows)}
        add_halo(accs, [(first_ref, base)], rows, weight_ref, target_ref, filter_ref)
        for t in range(rows):
            out_ref[t] = jnp.concatenate(accs[t], axis=1)

    pl.when(even)(lambda: combine(rows))
    pl.when(jnp.logical_not(even))(lambda: combine(-REACH))


def side_terms(own, first, weight, target, filters, after):
    return pl.pallas_call(
        side_kernel,
        in_specs=[pl.BlockSpec(memory_space=VMEM)] * 5 + [pl.BlockSpec(memory_space=pl.ANY)] * len(after),
        out_specs=pl.BlockSpec(memory_space=VMEM),
        out_shape=jax.ShapeDtypeStruct(own.shape, jnp.float32),
        compiler_params=pltpu.CompilerParams(vmem_limit_bytes=12 * 2**20),
        cost_estimate=NO_COST,
        name="side_terms",
    )(own, first, weight, target, filters, *after)


def finish_kernel(count, swaps, part_ref, *refs):
    halos, (weight_ref, target_ref, filter_ref, table_ref) = refs[:swaps], refs[swaps : swaps + 4]
    outs, stacked_ref = refs[-count - 1 : -1], refs[-1]
    rows, size, width = part_ref.shape
    even = lax.rem(lax.axis_index("polar"), 2) == 0

    def combine(bases):
        accs = {t: split_tiles(part_ref[t]) for t in range(rows)}
        sides = list(zip(halos, bases[-swaps:]))
        add_halo(accs, sides, rows, weight_ref, target_ref, filter_ref)
        for t in range(rows):
            stacked_ref[t * size : (t + 1) * size, :] = jnp.concatenate(accs[t], axis=1).astype(jnp.bfloat16)

    pl.when(even)(lambda: combine((rows, -REACH)))
    pl.when(jnp.logical_not(even))(lambda: combine((-REACH, rows)))
    grid = dot_nt(table_ref[...], stacked_ref[...])
    wide = grid.shape[0] // count
    for k, out in enumerate(outs):
        out[...] = grid[k * wide : k * wide + out.shape[0]].astype(jnp.bfloat16)


def finish(own, halos, weight, target, filters, table, count, part):
    rows, size, width = own.shape
    return pl.pallas_call(
        functools.partial(finish_kernel, count, len(halos)),
        in_specs=[pl.BlockSpec(memory_space=VMEM)] * (5 + len(halos)),
        out_specs=[pl.BlockSpec(memory_space=VMEM)] * count,
        out_shape=[jax.ShapeDtypeStruct((part, rows * size), jnp.bfloat16)] * count,
        scratch_shapes=[pltpu.VMEM((rows * size, width), jnp.bfloat16)],
        compiler_params=pltpu.CompilerParams(vmem_limit_bytes=12 * 2**20),
        cost_estimate=NO_COST,
        name="finish",
    )(own, *halos, weight, target, filters, table)


def add_kernel(count, chunk, steps, tiles, grad_ref, *refs):
    out_ref, tall_ref, done_ref, sems = refs[-4:]
    pieces = dict(zip(steps, refs))
    _, part, rows, _ = done_ref.shape
    start, size = chunk
    me = lax.axis_index("azimuth")

    def add(mine):
        order = [[k for k in range(count) if partner_static(mine, k, count, -1) == s][0] for s in range(count)]
        copies = []
        for at, tile in enumerate(tiles[mine]):
            lanes = range(tile * LANES, (tile + 1) * LANES)
            first = count * start + tile * LANES
            cut = round_up(part, 32) // 2
            for side, (low, high) in enumerate(((0, cut), (cut, part))):
                for row in range(rows):
                    parts = []
                    for s in owners(tile, size):
                        left, right = max(lanes[0], s * size), min(lanes[-1] + 1, (s + 1) * size)
                        base = (row - s) * size
                        parts.append(pieces[order[s]][low:high, base + left : base + right])
                    conv = jnp.concatenate(parts, axis=1).astype(jnp.float32)
                    total = grad_ref[row, low:high, first : first + LANES].astype(jnp.float32) + conv
                    tall_ref[at, pl.ds(low * rows + row, high - low, stride=rows), :] = total
                block = tall_ref[at, low * rows : high * rows, :].reshape(high - low, rows, LANES)
                done_ref[at, low:high] = block.astype(jnp.bfloat16)
                copies.append(
                    pltpu.make_async_copy(
                        done_ref.at[at, low:high],
                        out_ref.at[low:high, :, pl.ds(first, LANES)],
                        sems.at[2 * at + side],
                    )
                )
                copies[-1].start()
        for copy in copies:
            copy.wait()

    for mine in range(count):
        pl.when(me == mine)(functools.partial(add, mine))


def owners(tile, size):
    return range(tile * LANES // size, ((tile + 1) * LANES - 1) // size + 1)


def add_chunk(grad_out, pieces, chunk, count, tiles, before):
    rows, part, channels = grad_out.shape
    number = max(len(some) for some in tiles)
    needed = {
        k
        for mine in range(count)
        for tile in tiles[mine]
        for s in owners(tile, chunk[1])
        for k in range(count)
        if partner_static(mine, k, count, -1) == s
    }
    pieces = sorted(((k, pieces[k]) for k in needed), key=lambda item: item[0] <= NEAR)
    vmem = pl.BlockSpec(memory_space=VMEM)
    anywhere = pl.BlockSpec(memory_space=pl.ANY)
    return pl.pallas_call(
        functools.partial(add_kernel, count, chunk, [k for k, _ in pieces], tiles),
        in_specs=[vmem] * (1 + len(pieces)) + [anywhere] * len(before),
        out_specs=anywhere,
        out_shape=jax.ShapeDtypeStruct((part, rows, channels), jnp.bfloat16),
        scratch_shapes=[
            pltpu.VMEM((number, rows * part, LANES), jnp.float32),
            pltpu.VMEM((number, part, rows, LANES), jnp.bfloat16),
            pltpu.SemaphoreType.DMA((2 * number,)),
        ],
        input_output_aliases={1 + len(pieces): 0} if before else {},
        compiler_params=pltpu.CompilerParams(vmem_limit_bytes=12 * 2**20),
        cost_estimate=NO_COST,
        name="add_chunk",
    )(grad_out, *(block for _, block in pieces), *before)


def prepare_kernel(count, chunks, weight_ref, filt_ref, offset_ref, forth_ref, back_ref, *outs):
    filter_out, target_out, forth_out, back_out = outs[:4]
    me = lax.axis_index("azimuth")
    wide = back_ref.shape[0] // count
    for k in range(count):
        forth_out[k] = forth_ref[partner(me, k, count, -1)]
        first = pl.multiple_of(partner(me, k, count, 1) * wide, HALF)
        back_out[k * wide : (k + 1) * wide, :] = back_ref[pl.ds(first, wide), :]
    bases, channels = weight_ref.shape
    lats, width = filt_ref.shape[1:]
    ext, depth = target_out.shape
    rows = ext - 2 * REACH
    modes = width // 2
    whole = modes // LANES * LANES
    used = TERMS * bases
    for (start, size), out in zip(chunks, outs[4:]):
        first = count * start + lax.axis_index("azimuth") * size
        weight = pltpu.roll(weight_ref[...], lax.rem(channels - first, channels), 1)[:, :size]
        parts = []
        for _ in range(TERMS):
            rounded = weight.astype(jnp.bfloat16).astype(jnp.float32)
            parts.append(rounded)
            weight = weight - rounded
        parts.append(jnp.zeros((depth - used, size), jnp.float32))
        out[...] = jnp.concatenate(parts, axis=0).T
    start_lat = lax.axis_index("polar") * rows
    table = filt_ref[...].reshape(bases * lats, width)
    base = lax.broadcasted_iota(jnp.int32, (depth, bases * lats), 0)
    valid = base < used
    for _ in range(TERMS - 1):
        base = jnp.where(base >= bases, base - bases, base)
    column = lax.broadcasted_iota(jnp.int32, (depth, bases * lats), 1)
    for i in range(ext):
        lat = start_lat + (i - REACH)
        inside = (lat >= 0) & (lat < lats)
        lat = jnp.clip(lat, 0, lats - 1)
        pick = jnp.where(valid & (column == base * lats + lat), 1.0, 0.0).astype(jnp.bfloat16)
        row = dot_nn(pick, table)
        real, imag = row[:, :modes], row[:, modes:]
        rest_re, rest_im = real[:, whole:], imag[:, whole:]
        filter_out[i] = jnp.concatenate(
            [real[:, :whole], rest_re, rest_re, imag[:, :whole], rest_im, -rest_im], axis=1
        ).astype(jnp.bfloat16)
        local = jnp.where(inside, offset_ref[pl.ds(lat, 1), :] - start_lat, -1)
        spare = jnp.full((1, depth - used), -1, jnp.int32)
        target_out[i : i + 1, :] = jnp.concatenate([local] * TERMS + [spare], axis=1)


def prepare(basis_weight, filt, offsets, forth, back, rows, count, chunks):
    bases = filt.shape[0]
    width = filt.shape[2]
    ext = rows + 2 * REACH
    depth = round_up(TERMS * bases, 16)
    shapes = [
        jax.ShapeDtypeStruct((ext, depth, width + LANES), jnp.bfloat16),
        jax.ShapeDtypeStruct((ext, depth), jnp.int32),
        jax.ShapeDtypeStruct(forth.shape, forth.dtype),
        jax.ShapeDtypeStruct(back.shape, back.dtype),
    ] + [jax.ShapeDtypeStruct((size, depth), jnp.float32) for _, size in chunks]
    return pl.pallas_call(
        functools.partial(prepare_kernel, count, chunks),
        in_specs=[pl.BlockSpec(memory_space=VMEM)] * 5,
        out_specs=[pl.BlockSpec(memory_space=VMEM)] * len(shapes),
        out_shape=shapes,
        compiler_params=pltpu.CompilerParams(vmem_limit_bytes=16 * 2**20),
        cost_estimate=NO_COST,
        name="prepare",
    )(basis_weight, filt, offsets, forth, back)


def halo(first, second):
    bands, count = lax.axis_size("polar"), lax.axis_size("azimuth")
    blocks = []
    for odd, block in ((0, first), (1, second)):
        pairs = []
        for a in range(bands):
            other = ((a + odd) ^ 1) - odd
            for b in range(count):
                paired = 0 <= other < bands
                target = (other, b) if paired else (a, b ^ 1 if b ^ 1 < count else b)
                pairs.append((a * count + b, target[0] * count + target[1]))
        blocks.append(lax.ppermute(block, ("polar", "azimuth"), pairs))
    return blocks


def on_device(chunks, conv_out, grad_out, w_in, b_in, w_out, basis_weight, filt, offsets):
    rows, part, channels = conv_out.shape
    count = lax.axis_size("azimuth")
    forth, back = tables(count, part, filt.shape[2] // 2)
    forth, back = jnp.asarray(forth), jnp.asarray(back)
    owned = channels // count
    halves = 2 if rows % 2 == 0 else 1
    wide = round_up(part, HALF)
    filters, target, forth, back, *weights = prepare(
        basis_weight, filt, offsets, forth, back, rows, count, chunks
    )
    early, order = [], []
    for half in range(halves):
        final = half == halves - 1
        sent = [(k, 0, owned) for k in range(count)]
        if final:
            sent[1:] = [(k,) + chunk for chunk in chunks for k in range(1, count)]
        blocks = mlp(conv_out, grad_out, w_in, b_in, w_out, count, half, halves, sent, chunks, order)
        order = blocks[:1]
        if not final:
            early.append(analyze_early([exchange(blocks[k], k, count) for k in range(count)], forth, wide))
    spectra, terms, returned = {}, {}, {}
    for q, (start, size) in enumerate(chunks):
        mine = blocks[1 + q * (count - 1) : 1 + (q + 1) * (count - 1)]
        pieces = [blocks[0]] + [exchange(block, k, count) for k, block in enumerate(mine, 1)]
        after = [terms[q - 1]] if q else []
        own, first, second = analyze(pieces, forth, early, rows, wide, (start, size), after)
        spectra[q] = halo(first, second)
        terms[q] = own_terms(own, early, start, weights[q], target, filters)
    for q in range(len(chunks)):
        halos = spectra[q]
        if q == 0:
            others = []
            terms[q] = side_terms(terms[q], halos[0], weights[q], target, filters, others)
            halos = halos[1:]
        grids = finish(terms[q], halos, weights[q], target, filters, back, count, part)
        returned[q] = {k: exchange(grids[k], k, count) for k in range(count)}
    total = []
    for q, chunk in enumerate(chunks):
        tiles = [list(range(count * chunk[1] // LANES)) for _ in range(count)]
        if q == len(chunks) - 1:
            chip = [{mine, partner_static(mine, NEAR, count, -1)} for mine in range(count)]
            close = [[t for t in tiles[mine] if set(owners(t, chunk[1])) <= chip[mine]] for mine in range(count)]
            if any(close):
                total = [add_chunk(grad_out, returned[q], chunk, count, close, total)]
                tiles = [[t for t in tiles[mine] if t not in close[mine]] for mine in range(count)]
        total = [add_chunk(grad_out, returned[q], chunk, count, tiles, total)]
    return jnp.transpose(total[0], (1, 0, 2))


def solution(mesh):
    grid = P(("member", "polar"), "azimuth", None)

    def run(conv_out, grad_out, *others):
        owned = conv_out.shape[2] // mesh.shape["azimuth"]
        sizes = [owned]
        if owned % 32 == 0 and owned >= 96:
            big = owned * 3 // 5 // 32 * 32
            sizes = [big, owned - big]
        chunks = tuple((sum(sizes[:q]), size) for q, size in enumerate(sizes))
        return jax.shard_map(
            functools.partial(on_device, chunks),
            mesh=mesh,
            in_specs=(grid, grid) + (P(),) * 6,
            out_specs=grid,
            check_vma=False,
        )(conv_out, grad_out, *others)

    return run
```
